32 devices in a mesh: dp: 8 (over z, x), mp: 4 (over y, core).
Axes of the slice: x: 2, y: 2, z: 4, core: 2. Of those that a mesh axis runs over, the one named last changes fastest.
Arguments:
- tokens: bfloat16 [6144, 1472], P(('dp', 'mp')), may hold values from -6 to 6
- cotangent: bfloat16 [6144, 1472], P(('dp', 'mp')), may hold values from -9 to 9
- lengths: int32 [8, 2], P('dp'), may hold values from 1 to 672, as said below
- heads_in: float32 [3, 1472, 384], P(None, 'dp'), may hold values from -0.0546875 to 0.0546875
- heads_out: float32 [384, 1472], P(None, 'dp'), may hold values from -6 to 6
- expand_in: float32 [2, 1472, 3584], P(None, 'dp', 'mp'), may hold values from -0.15625 to 0.15625
- expand_out: float32 [3584, 1472], P('mp', 'dp'), may hold values from -0.09375 to 0.09375
- norm_gains: float32 [2, 1472], P(None, 'dp'), may hold values from 0.4 to 3.2
- bias_table: float32 [32, 6], replicated, may hold values from -4 to 4
- heads_in_first: float32 [3, 1472, 384], P(None, 'dp'), may hold values from -160 to 160
- heads_out_first: float32 [384, 1472], P(None, 'dp'), may hold values from -2.5 to 2.5
- expand_in_first: float32 [2, 1472, 3584], P(None, 'dp', 'mp'), may hold values from -28 to 28
- expand_out_first: float32 [3584, 1472], P('mp', 'dp'), may hold values from -40 to 40
- gains_first: float32 [2, 1472], P(None, 'dp'), may hold values from -56 to 56
- table_first: float32 [32, 6], replicated, may hold values from -40 to 40
- heads_in_second: float32 [3, 1472, 384], P(None, 'dp'), may hold values from 55.296 to 221.184
- heads_out_second: float32 [384, 1472], P(None, 'dp'), may hold values from 0.01536 to 0.06144
- expand_in_second: float32 [2, 1472, 3584], P(None, 'dp', 'mp'), may hold values from 1.536 to 6.144
- expand_out_second: float32 [3584, 1472], P('mp', 'dp'), may hold values from 3.93216 to 15.9744
- gains_second: float32 [2, 1472], P(None, 'dp'), may hold values from 6.144 to 24.576
- table_second: float32 [32, 6], replicated, may hold values from 4.2467327 to 16.98693
Outputs:
- layer_out: bfloat16 [6144, 1472], P(('dp', 'mp'))
- tokens_grad: float32 [6144, 1472], P(('dp', 'mp'))
- heads_in_moment: float32 [3, 1472, 384], P(None, 'dp')
- heads_in_square: float32 [3, 1472, 384], P(None, 'dp')
- heads_in_new: float32 [3, 1472, 384], P(None, 'dp')
- heads_in_copy: bfloat16 [3, 1472, 384], P(None, 'dp')
- heads_out_moment: float32 [384, 1472], P(None, 'dp')
- heads_out_square: float32 [384, 1472], P(None, 'dp')
- heads_out_new: float32 [384, 1472], P(None, 'dp')
- heads_out_copy: bfloat16 [384, 1472], P(None, 'dp')
- expand_in_moment: float32 [2, 1472, 3584], P(None, 'dp', 'mp')
- expand_in_square: float32 [2, 1472, 3584], P(None, 'dp', 'mp')
- expand_in_new: float32 [2, 1472, 3584], P(None, 'dp', 'mp')
- expand_in_copy: bfloat16 [2, 1472, 3584], P(None, 'dp', 'mp')
- expand_out_moment: float32 [3584, 1472], P('mp', 'dp')
- expand_out_square: float32 [3584, 1472], P('mp', 'dp')
- expand_out_new: float32 [3584, 1472], P('mp', 'dp')
- expand_out_copy: bfloat16 [3584, 1472], P('mp', 'dp')
- gains_moment: float32 [2, 1472], P(None, 'dp')
- gains_square: float32 [2, 1472], P(None, 'dp')
- gains_new: float32 [2, 1472], P(None, 'dp')
- gains_copy: bfloat16 [2, 1472], P(None, 'dp')
- table_moment: float32 [32, 6], replicated
- table_square: float32 [32, 6], replicated
- table_new: float32 [32, 6], replicated
- table_copy: bfloat16 [32, 6], replicated
- weight_norms: float32 [2, 10], replicated
The draws below stay inside these ranges and needn't reach their ends.
Inputs may be any that keep to these rules, and one draw needn't show every extreme that they name: Group g's two items fill positions 0 to lengths[g, 0] + lengths[g, 1] - 1 of the group, the rest being padding; the sum is at most 768. Each group's longer item has more than 576 positions, and some group's has exactly 672.
All inputs are finite; a program needn't handle non-finite values.
Results may differ from the reference program's by a relative error of at most 0.024.
The reference program's roundings to bfloat16 on the way count: a program that leaves them out, or rounds other values in their place, can miss the bound.
Values may be sent and summed in bfloat16 or wider, within the bound.
A program may use at most 192 MiB of HBM per device.

```python
import math
import jax
import jax.numpy as jnp
from jax import lax

D = 1472
FF = 3584
HEADS = 6
HEAD_DIM = 64
BUCKETS = 32
STEP = 10
TOK_GRP = 768
GROUPS = 8
TOKENS = 6144
INNER = 384
LONGEST = 672


def rising_scale(key, length_total, start_value, ratio):
    position_ramp = jnp.arange(length_total, dtype=jnp.float32) / (length_total - 1)
    jitter = jax.random.uniform(key, (length_total,), jnp.float32, 0.8, 1.25)
    return start_value * ratio ** position_ramp * jitter


def draw_norm_gains(key, part):
    key = jax.random.fold_in(key, 11)
    first_key, second_key = jax.random.split(key)
    start_value, ratio = (0.6, 3.0)
    return jnp.stack([rising_scale(first_key, D, start_value, ratio), rising_scale(second_key, D, start_value, ratio)])


def draw_cotangent(key, part):
    key = jax.random.fold_in(key, 12)
    scale_key, entry_key = jax.random.split(key)
    column = rising_scale(scale_key, D, 0.6, 3.0)
    entries = jax.random.truncated_normal(entry_key, -4.0, 4.0, (TOKENS, D), jnp.float32)
    return (entries * column[None, :]).astype(jnp.bfloat16)


def draw_lengths(key, part):
    key = jax.random.fold_in(key, 13)
    long_key, pick_key, short_key, order_key = jax.random.split(key, 4)
    long_low = TOK_GRP * 3 // 4 + 1
    longer = jax.random.randint(long_key, (GROUPS,), long_low, LONGEST + 1)
    chosen = jax.random.randint(pick_key, (), 0, GROUPS)
    longer = jnp.where(jnp.arange(GROUPS) == chosen, LONGEST, longer)
    shorter = jax.random.randint(short_key, (GROUPS,), 1, TOK_GRP - longer + 1)
    swapped = jax.random.randint(order_key, (GROUPS,), 0, 2)
    leading = jnp.where(swapped == 1, shorter, longer)
    trailing = jnp.where(swapped == 1, longer, shorter)
    return jnp.stack([leading, trailing], axis=1).astype(jnp.int32)


def level_of(rng, dims, cuts, smallest, largest):
    gain, own = 1.0, jax.random.fold_in(rng, 6)
    for dim, shards_of in cuts:
        steps = jnp.exp(jax.random.uniform(jax.random.fold_in(own, dim), (shards_of,), jnp.float32, smallest / len(cuts), largest / len(cuts)))
        gain = gain * jnp.repeat(steps, dims[dim] // shards_of).reshape([-1 if axis == dim else 1 for axis in range(len(dims))])
    return gain


def centred(key, dims, width, limit, cuts=(), held_as=jnp.bfloat16):
    array = jax.random.normal(key, dims, jnp.float32) * width
    if len(cuts) > 0:
        array = level_of(key, dims, cuts, -0.22, 0.18) * array
    return jnp.clip(array, min=-limit, max=limit).astype(held_as)


def setup_inputs(seed: int = 0) -> dict:
    key_list = jax.random.split(jax.random.key(seed), 22)
    return {
        "tokens": centred(key_list[0], (TOKENS, D), 1.0, 6.0, ((0, 32),)),
        "cotangent": draw_cotangent(jax.random.fold_in(key_list[21], 71), 0),
        "lengths": draw_lengths(jax.random.fold_in(key_list[21], 71), 0),
        "heads_in": centred(key_list[3], (3, D, INNER), (8 * D) ** -0.5, 0.0546875, ((1, 8),), jnp.float32),
        "heads_out": centred(key_list[4], (INNER, D), 1 ** -0.5, 6.0, ((1, 8),), jnp.float32),
        "expand_in": centred(key_list[5], (2, D, FF), D ** -0.5, 0.15625, ((1, 8), (2, 4)), jnp.float32),
        "expand_out": centred(key_list[6], (FF, D), FF ** -0.5, 0.09375, ((0, 4), (1, 8)), jnp.float32),
        "norm_gains": draw_norm_gains(jax.random.fold_in(key_list[21], 71), 0),
        "bias_table": centred(key_list[8], (BUCKETS, HEADS), 1.0, 4.0, (), jnp.float32),
        "heads_in_first": centred(key_list[9], (3, D, INNER), (0.33 * TOKENS ** 0.5), 160.0, ((1, 8),), jnp.float32),
        "heads_out_first": centred(key_list[10], (INNER, D), (0.0055 * TOKENS ** 0.5), 2.5, ((1, 8),), jnp.float32),
        "expand_in_first": centred(key_list[11], (2, D, FF), (0.055 * TOKENS ** 0.5), 28.0, ((1, 8), (2, 4)), jnp.float32),
        "expand_out_first": centred(key_list[12], (FF, D), (0.09 * TOKENS ** 0.5), 40.0, ((0, 4), (1, 8)), jnp.float32),
        "gains_first": centred(key_list[13], (2, D), (0.11 * TOKENS ** 0.5), 56.0, ((1, 8),), jnp.float32),
        "table_first": centred(key_list[14], (BUCKETS, HEADS), (0.0033 * (TOKENS * TOK_GRP) ** 0.5), 40.0, (), jnp.float32),
        "heads_in_second": jnp.clip(jnp.exp(math.log(221.184) - 1.3862944 * jax.random.uniform(key_list[15], (3, D, INNER), jnp.float32) ** level_of(key_list[15], (3, D, INNER), ((1, 8),), -0.2, 0.2)), 55.296, 221.184),
        "heads_out_second": jnp.clip(jnp.exp(math.log(0.06144) - 1.3862944 * jax.random.uniform(key_list[16], (INNER, D), jnp.float32) ** level_of(key_list[16], (INNER, D), ((1, 8),), -0.2, 0.2)), 0.01536, 0.06144),
        "expand_in_second": jnp.clip(jnp.exp(math.log(6.144) - 1.3862944 * jax.random.uniform(key_list[17], (2, D, FF), jnp.float32) ** level_of(key_list[17], (2, D, FF), ((1, 8), (2, 4)), -0.2, 0.2)), 1.536, 6.144),
        "expand_out_second": jnp.clip(jnp.exp(math.log(15.9744) - 1.4017985 * jax.random.uniform(key_list[18], (FF, D), jnp.float32) ** level_of(key_list[18], (FF, D), ((0, 4), (1, 8)), -0.2, 0.2)), 3.93216, 15.9744),
        "gains_second": jnp.clip(jnp.exp(math.log(24.576) - 1.3862944 * jax.random.uniform(key_list[19], (2, D), jnp.float32) ** level_of(key_list[19], (2, D), ((1, 8),), -0.2, 0.2)), 6.144, 24.576),
        "table_second": jnp.clip(jnp.exp(jax.random.uniform(key_list[20], (BUCKETS, HEADS), jnp.float32, math.log(4.2467327), math.log(16.98693))), 4.2467327, 16.98693),
    }


norm_eps = 1e-06
beta_first = 0.9
beta_second = 0.999
adam_eps = 1e-06
weight_decay = 0.01
learn_rate = 0.4
masked_fill = -1000000000.0
bucket_edges = (12, 16, 23, 32, 46, 64, 91)
highest = lax.Precision.HIGHEST

@jax.custom_vjp
def low(v):
    return lax.optimization_barrier(v.astype(jnp.bfloat16)).astype(jnp.float32)

@jax.custom_vjp
def low_back(v):
    return v

def low_keep(v):
    return (low(v), None)

def low_pass(kept, grad):
    return (grad,)

def back_keep(v):
    return (v, None)

def back_low(kept, grad):
    return (low(grad),)
low.defvjp(low_keep, low_pass)
low_back.defvjp(back_keep, back_low)

def bucket_ids(offsets):
    distance = jnp.abs(offsets)
    coarse = jnp.full_like(distance, 8)
    for edge_value in bucket_edges:
        coarse = coarse + (distance >= edge_value).astype(jnp.int32)
    nearby = jnp.where(distance < 8, distance, coarse)
    return (nearby + 16 * (offsets > 0).astype(jnp.int32)).astype(jnp.int32)

def rms_scale(hidden_rows, gain_vector):
    return hidden_rows * lax.rsqrt(lax.optimization_barrier(jnp.mean(hidden_rows * hidden_rows, axis=-1, keepdims=True)) + norm_eps) * gain_vector

def mat_prod(left_side, right_side):
    return jnp.dot(left_side, right_side, precision=highest)

def segment_of(positions, item_lengths):
    first_end = item_lengths[0]
    second_end = item_lengths[0] + item_lengths[1]
    return (positions >= first_end).astype(jnp.int32) + (positions >= second_end).astype(jnp.int32)

def group_layer(group_rows, item_lengths, weights):
    heads_in, heads_out, expand_in, expand_out, norm_gains, bias_table = weights
    seq_len = group_rows.shape[0]
    positions = jnp.arange(seq_len, dtype=jnp.int32)
    segments = segment_of(positions, item_lengths)
    normed = low(rms_scale(group_rows, norm_gains[0]))
    queries = low_back(low(mat_prod(normed, heads_in[0]))).reshape(seq_len, HEADS, HEAD_DIM)
    keys_all = low_back(low(mat_prod(normed, heads_in[1]))).reshape(seq_len, HEADS, HEAD_DIM)
    values_all = low_back(low(mat_prod(normed, heads_in[2]))).reshape(seq_len, HEADS, HEAD_DIM)
    scores = jnp.einsum('qhd,khd->hqk', queries, keys_all, precision=highest)
    offsets = positions[None, :] - positions[:, None]
    position_bias = jnp.transpose(jnp.take(bias_table, bucket_ids(offsets), axis=0), (2, 0, 1))
    allowed = segments[:, None] == segments[None, :]
    scores = low_back(jnp.where(allowed[None], scores + position_bias, masked_fill))
    soft_weights = low(jax.nn.softmax(scores, axis=-1))
    mixed_heads = jnp.einsum('hqk,khd->qhd', soft_weights, values_all, precision=highest).reshape(seq_len, INNER)
    mixed_heads = low_back(low(mixed_heads))
    attended = low_back(mat_prod(mixed_heads, heads_out))
    residual_one = group_rows + attended
    normed_two = low(rms_scale(residual_one, norm_gains[1]))
    gate_pre = low_back(mat_prod(normed_two, expand_in[0]))
    up_pre = low_back(mat_prod(normed_two, expand_in[1]))
    hidden_units = low(jax.nn.gelu(gate_pre, approximate=True) * up_pre)
    feed_out = low_back(mat_prod(hidden_units, expand_out))
    return residual_one + feed_out

def lamb_update(weight, gradient, first_moment, second, decay_rate, sub_count):
    new_first = beta_first * first_moment + (1.0 - beta_first) * gradient
    new_second = beta_second * second + (1.0 - beta_second) * gradient * gradient
    first_fix = 1.0 - beta_first ** STEP
    second_fix = 1.0 - beta_second ** STEP
    step_dir = new_first / first_fix / (jnp.sqrt(new_second / second_fix) + adam_eps) + decay_rate * weight
    flat_weight = weight.reshape(sub_count, -1)
    flat_step = step_dir.reshape(sub_count, -1)
    weight_norm = jnp.sqrt(lax.optimization_barrier(jnp.sum(flat_weight * flat_weight, axis=1)))
    step_norm = jnp.sqrt(lax.optimization_barrier(jnp.sum(flat_step * flat_step, axis=1)))
    new_weight = (flat_weight - learn_rate * (weight_norm / step_norm)[:, None] * flat_step).reshape(weight.shape)
    return (new_first, new_second, new_weight, weight_norm, step_norm)

def reference(tokens, cotangent, lengths, heads_in, heads_out, expand_in, expand_out, norm_gains, bias_table, heads_in_first, heads_out_first, expand_in_first, expand_out_first, gains_first, table_first, heads_in_second, heads_out_second, expand_in_second, expand_out_second, gains_second, table_second):
    inputs = tokens.astype(jnp.float32).reshape(GROUPS, TOK_GRP, D)
    positions = jnp.arange(TOK_GRP, dtype=jnp.int32)
    used_rows = (positions[None, :] < (lengths[:, 0] + lengths[:, 1])[:, None]).astype(jnp.float32)
    upstream = cotangent.astype(jnp.float32).reshape(GROUPS, TOK_GRP, D) * used_rows[:, :, None]

    def whole_layer(layer_in, w_heads_in, w_heads_out, w_expand_in, w_expand_out, w_gains, w_table):
        rounded = (low(w_heads_in), low(w_heads_out), low(w_expand_in), low(w_expand_out), low(w_gains), w_table)

        def one_group(group_pair):
            return group_layer(group_pair[0], group_pair[1], rounded)
        return lax.map(jax.checkpoint(one_group), (layer_in, lengths))
    outputs, pullback = jax.vjp(whole_layer, inputs, heads_in, heads_out, expand_in, expand_out, norm_gains, bias_table)
    gradients = pullback(upstream)
    layer_out = outputs.reshape(TOKENS, D).astype(jnp.bfloat16)
    tokens_grad = gradients[0].reshape(TOKENS, D)
    upd_a = lamb_update(heads_in, gradients[1], heads_in_first, heads_in_second, weight_decay, 3)
    upd_b = lamb_update(heads_out, gradients[2], heads_out_first, heads_out_second, weight_decay, 1)
    upd_c = lamb_update(expand_in, gradients[3], expand_in_first, expand_in_second, weight_decay, 2)
    upd_d = lamb_update(expand_out, gradients[4], expand_out_first, expand_out_second, weight_decay, 1)
    upd_e = lamb_update(norm_gains, gradients[5], gains_first, gains_second, 0.0, 2)
    upd_f = lamb_update(bias_table, gradients[6], table_first, table_second, 0.0, 1)
    weight_norms = jnp.stack([jnp.concatenate([upd_a[3], upd_b[3], upd_c[3], upd_d[3], upd_e[3], upd_f[3]]), jnp.concatenate([upd_a[4], upd_b[4], upd_c[4], upd_d[4], upd_e[4], upd_f[4]])])
    return (layer_out, tokens_grad, upd_a[0], upd_a[1], upd_a[2], upd_a[2].astype(jnp.bfloat16), upd_b[0], upd_b[1], upd_b[2], upd_b[2].astype(jnp.bfloat16), upd_c[0], upd_c[1], upd_c[2], upd_c[2].astype(jnp.bfloat16), upd_d[0], upd_d[1], upd_d[2], upd_d[2].astype(jnp.bfloat16), upd_e[0], upd_e[1], upd_e[2], upd_e[2].astype(jnp.bfloat16), upd_f[0], upd_f[1], upd_f[2], upd_f[2].astype(jnp.bfloat16), weight_norms)
```

```python
from functools import partial

import jax
import jax.numpy as jnp
from jax import lax
from jax.experimental import pallas as pl
from jax.experimental.pallas import tpu as pltpu
from jax.sharding import PartitionSpec as P

HEADS = 6
HEAD_DIM = 64
STEP = 10
INNER = 384
LANES = 128
PAIRS = INNER // LANES
MESH = pl.DeviceIdType.MESH
VMEM_BYTES = 56 * 2**20
RING_LIMIT = 8


norm_eps = 1e-06
beta_first = 0.9
beta_second = 0.999
adam_eps = 1e-06
weight_decay = 0.01
learn_rate = 0.4
masked_fill = -1000000000.0
bucket_edges = (12, 16, 23, 32, 46, 64, 91)
highest = lax.Precision.HIGHEST
f32 = jnp.float32
bf16 = jnp.bfloat16


def bucket_ids(offsets):
    distance = jnp.abs(offsets)
    coarse = jnp.full_like(distance, 8)
    for edge_value in bucket_edges:
        coarse = coarse + (distance >= edge_value).astype(jnp.int32)
    nearby = jnp.where(distance < 8, distance, coarse)
    return nearby + 16 * (offsets > 0).astype(jnp.int32)


def rms_scale(hidden_rows, gain_vector):
    return (
        hidden_rows
        * lax.rsqrt(jnp.mean(hidden_rows * hidden_rows, axis=-1, keepdims=True) + norm_eps)
        * gain_vector
    )


def contract_rows(left_side, right_side):
    return lax.dot_general(
        left_side, right_side, (((0,), (0,)), ((), ())), preferred_element_type=f32
    )


def contract_cols(left_side, right_side):
    return lax.dot_general(
        left_side, right_side, (((1,), (1,)), ((), ())), preferred_element_type=f32
    )


def matmul(left_side, right_side):
    return jnp.dot(left_side, right_side, preferred_element_type=f32)


def ring_order(size):
    return list(range(0, size, 2)) + list(range(size - 1, 0, -2))


def ring_pairs(size):
    order = ring_order(size)
    forward = [(order[spot], order[(spot + 1) % size]) for spot in range(size)]
    return forward, [(target, source) for source, target in forward]


def ring_owner(spot, size):
    late = (spot >= size // 2).astype(jnp.int32)
    return 2 * spot + late * (2 * size - 1 - 4 * spot)


def ring_spot(index, size):
    return index // 2 + lax.rem(index, 2) * (size - 1 - 2 * (index // 2))


def cut_of(width):
    return ((width // LANES + 1) // 2) * LANES


def assemble_kernel(size, cut, *refs):
    slabs, (left, right, out, sems) = refs[:-4], refs[-4:]
    spot = ring_spot(lax.axis_index("dp"), size)
    copies = []
    for number, slab in enumerate(slabs):
        shift = number if number < size // 2 else number + 1
        owner = ring_owner(lax.rem(spot + shift, size), size)
        copies.append(pltpu.make_async_copy(slab, out.at[:, owner], sems.at[number]))
    owner = ring_owner(lax.rem(spot + size // 2, size), size)
    width = out.shape[-1]
    copies.append(
        pltpu.make_async_copy(left, out.at[:, owner, :, pl.ds(0, cut)], sems.at[size - 1])
    )
    copies.append(
        pltpu.make_async_copy(right, out.at[:, owner, :, pl.ds(cut, width - cut)], sems.at[size])
    )
    for copy in copies:
        copy.start()
    for copy in copies:
        copy.wait()


def gather_dp(part):
    size = lax.axis_size("dp")
    if size > RING_LIMIT:
        return lax.all_gather(part, "dp", axis=1, tiled=True)
    forward, backward = ring_pairs(size)
    count, rows, width = part.shape
    cut = cut_of(width)
    slabs = [None] * size
    slabs[0] = ahead = behind = part
    for hop in range(1, size // 2):
        ahead = lax.ppermute(ahead, "dp", forward)
        behind = lax.ppermute(behind, "dp", backward)
        slabs[size - hop] = ahead
        slabs[hop] = behind
    left = lax.ppermute(ahead[..., :cut], "dp", forward)
    right = lax.ppermute(behind[..., cut:], "dp", backward)
    operands = [slab for slab in slabs if slab is not None] + [left, right]
    total = count * size * rows * width * part.dtype.itemsize
    whole = pl.pallas_call(
        partial(assemble_kernel, size, cut),
        out_shape=jax.ShapeDtypeStruct((count, size, rows, width), part.dtype),
        in_specs=[pl.BlockSpec(memory_space=pl.ANY)] * len(operands),
        out_specs=pl.BlockSpec(memory_space=pltpu.VMEM),
        scratch_shapes=[pltpu.SemaphoreType.DMA((size + 1,))],
        compiler_params=pltpu.CompilerParams(vmem_limit_bytes=VMEM_BYTES),
        cost_estimate=pl.CostEstimate(flops=0, bytes_accessed=2 * total, transcendentals=0),
        name="assemble",
    )(*operands)
    return whole.reshape(count, size * rows, width)


def scatter_dp(whole):
    size = lax.axis_size("dp")
    if size > RING_LIMIT:
        return lax.psum_scatter(whole.astype(f32), "dp", scatter_dimension=1, tiled=True)
    forward, backward = ring_pairs(size)
    count, depth, width = whole.shape
    rows = depth // size
    cut = cut_of(width)
    spot = ring_spot(lax.axis_index("dp"), size)

    def term(shift):
        owner = ring_owner(lax.rem(spot + size + shift, size), size)
        return lax.dynamic_slice_in_dim(whole, owner * rows, rows, axis=1)

    far = term(size // 2)
    ahead = lax.ppermute(far[..., :cut], "dp", forward)
    behind = lax.ppermute(far[..., cut:], "dp", backward)
    for hop in range(size // 2 - 1, 0, -1):
        mine = term(hop).astype(f32)
        other = term(-hop).astype(f32)
        if hop == size // 2 - 1:
            ahead = jnp.concatenate([mine[..., :cut] + ahead.astype(f32), mine[..., cut:]], -1)
            behind = jnp.concatenate([other[..., :cut], other[..., cut:] + behind.astype(f32)], -1)
        else:
            ahead = mine + ahead.astype(f32)
            behind = other + behind.astype(f32)
        ahead = lax.ppermute(ahead.astype(bf16), "dp", forward)
        behind = lax.ppermute(behind.astype(bf16), "dp", backward)
    return term(0).astype(f32) + ahead.astype(f32) + behind.astype(f32)


def swap(part, bit):
    size = lax.axis_size("mp")
    return lax.ppermute(part, "mp", [(index, index ^ bit) for index in range(size)])


def gather_mp(part):
    across = swap(part, 2)
    beside = swap(part, 1)
    return part, across, beside, swap(across, 1)


def offset_values(table_ref, first_row, rows, span):
    offsets = lax.broadcasted_iota(jnp.int32, (8, span), 1) - (rows - 1) - first_row
    buckets = bucket_ids(offsets)
    table = table_ref[...]
    values = jnp.zeros((8, span), f32)
    for number in range(table.shape[1]):
        values = jnp.where(buckets == number, table[:, number : number + 1], values)
    return values


def segments_at(positions, first_len, second_len):
    return (positions >= first_len).astype(jnp.int32) + (
        positions >= first_len + second_len
    ).astype(jnp.int32)


def allowed_pairs(lens_ref, first_row, rows, keys):
    query = segments_at(
        first_row + lax.broadcasted_iota(jnp.int32, (rows, 1), 0), lens_ref[0, 0], lens_ref[0, 1]
    )
    key = segments_at(
        lax.broadcasted_iota(jnp.int32, (1, keys), 1), lens_ref[0, 0], lens_ref[0, 1]
    )
    return query == key


def skewed_bias(values, head, rows, keys, span):
    wide = jnp.broadcast_to(values[head : head + 1, :], (rows, span))
    return pltpu.roll(wide, span - (rows - 1), 1, stride=1, stride_axis=0)[:, :keys]


def forward_kernel(
    span,
    lens_ref,
    own_ref,
    across_ref,
    beside_ref,
    corner_ref,
    heads_ref,
    table_ref,
    tokens_ref,
    gain_ref,
    mixed_ref,
    query_ref,
    key_ref,
    value_ref,
    log_ref,
    residual_ref,
    normed_ref,
):
    rows = own_ref.shape[0]
    keys = key_ref.shape[0]
    spot = lax.axis_index("mp")
    first_row = spot * rows
    for block_ref, bit in ((own_ref, 0), (across_ref, 2), (beside_ref, 1), (corner_ref, 3)):
        place = pl.ds(pl.multiple_of((spot ^ bit) * rows, rows), rows)
        block = block_ref[...]
        key_ref[place, :] = matmul(block, heads_ref[1]).astype(bf16)
        value_ref[place, :] = matmul(block, heads_ref[2]).astype(bf16)
    query_ref[...] = matmul(own_ref[...], heads_ref[0]).astype(bf16)
    values = offset_values(table_ref, first_row, rows, span)
    allowed = allowed_pairs(lens_ref, first_row, rows, keys)
    lane = lax.broadcasted_iota(jnp.int32, (1, LANES), 1)
    logs = jnp.zeros((rows, LANES), f32)
    for pair in range(PAIRS):
        part = slice(pair * LANES, (pair + 1) * LANES)
        query = query_ref[:, part]
        key = key_ref[:, part]
        value = value_ref[:, part]
        mixed = jnp.zeros((rows, LANES), f32)
        for half in range(2):
            head = 2 * pair + half
            mask = (lane // HEAD_DIM) == half
            scores = contract_cols(jnp.where(mask, query, jnp.zeros_like(query)), key)
            scores = jnp.where(
                allowed, scores + skewed_bias(values, head, rows, keys, span), masked_fill
            )
            top = jnp.max(scores, axis=-1, keepdims=True)
            powers = jnp.exp(scores - top)
            total = jnp.sum(powers, axis=-1, keepdims=True)
            soft = (powers * (1.0 / total)).astype(bf16)
            mixed = jnp.where(mask, matmul(soft, value), mixed)
            logs = jnp.where(lane == head, top + jnp.log(total), logs)
        mixed_ref[:, part] = mixed.astype(bf16)
    log_ref[...] = logs
    residual = tokens_ref[...].astype(f32) + contract_cols(mixed_ref[...], heads_ref[3])
    residual_ref[...] = residual
    normed_ref[...] = rms_scale(residual, gain_ref[...]).astype(bf16)


def norm_backward(rows_in, gain, grad):
    scale = lax.rsqrt(jnp.mean(rows_in * rows_in, axis=-1, keepdims=True) + norm_eps)
    unit = rows_in * scale
    inner = grad * gain
    out = scale * (inner - unit * jnp.mean(inner * unit, axis=-1, keepdims=True))
    return out, jnp.sum(grad * unit, axis=0, keepdims=True)


def backward_kernel(
    span,
    lens_ref,
    part_ref,
    across_ref,
    residual_ref,
    upstream_ref,
    gain_ref,
    heads_ref,
    query_ref,
    key_ref,
    value_ref,
    log_ref,
    table_ref,
    residual_grad_ref,
    attended_ref,
    query_grad_ref,
    near_ref,
    far_ref,
    offset_ref,
    gain_grad_ref,
    whole_ref,
):
    rows = query_ref.shape[0]
    keys = key_ref.shape[0]
    spot = lax.axis_index("mp")
    first_row = spot * rows
    grad = part_ref[...].astype(f32) + across_ref[...].astype(f32)
    through, gain_grad = norm_backward(residual_ref[...], gain_ref[...], grad)
    gain_grad_ref[...] = gain_grad
    residual_grad = upstream_ref[...].astype(f32) + through
    residual_grad_ref[...] = residual_grad
    attended = residual_grad.astype(bf16)
    attended_ref[...] = attended
    mixed_grad_all = matmul(attended, heads_ref[3]).astype(bf16)
    values = offset_values(table_ref, first_row, rows, span)
    allowed = allowed_pairs(lens_ref, first_row, rows, keys)
    lane = lax.broadcasted_iota(jnp.int32, (1, LANES), 1)
    flip = (
        lax.broadcasted_iota(jnp.int32, (rows, rows), 0)
        + lax.broadcasted_iota(jnp.int32, (rows, rows), 1)
        == rows - 1
    ).astype(bf16)
    for pair in range(PAIRS):
        part = slice(pair * LANES, (pair + 1) * LANES)
        query = query_ref[:, part]
        key = key_ref[:, part]
        value = value_ref[:, part]
        mixed_grad = mixed_grad_all[:, part]
        query_grad = jnp.zeros((rows, LANES), f32)
        key_grad = jnp.zeros((keys, LANES), f32)
        value_grad = jnp.zeros((keys, LANES), f32)
        for half in range(2):
            head = 2 * pair + half
            mask = (lane // HEAD_DIM) == half
            query_own = jnp.where(mask, query, jnp.zeros_like(query))
            mixed_own = jnp.where(mask, mixed_grad, jnp.zeros_like(mixed_grad))
            scores = contract_cols(query_own, key)
            scores = jnp.where(
                allowed, scores + skewed_bias(values, head, rows, keys, span), masked_fill
            )
            soft = jnp.exp(scores - log_ref[:, head : head + 1])
            soft_grad = contract_cols(mixed_own, value)
            corr = jnp.sum(soft * soft_grad, axis=-1, keepdims=True)
            scores_grad = (soft * (soft_grad - corr)).astype(bf16)
            query_grad = jnp.where(mask, matmul(scores_grad, key), query_grad)
            key_grad = key_grad + contract_rows(scores_grad, query_own)
            value_grad = value_grad + contract_rows(soft.astype(bf16), mixed_own)
            flipped = matmul(flip, scores_grad)
            flipped = jnp.concatenate([flipped, jnp.zeros((rows, span - keys), f32)], axis=1)
            skewed = pltpu.roll(flipped, 0, 1, stride=1, stride_axis=0)
            offset_ref[head : head + 1, :] = jnp.sum(skewed, axis=0, keepdims=True)
        query_grad_ref[:, part] = query_grad.astype(bf16)
        whole_ref[:, part] = key_grad
        whole_ref[:, INNER + pair * LANES : INNER + (pair + 1) * LANES] = value_grad
    offset_ref[HEADS:, :] = jnp.zeros((8 - HEADS, span), f32)
    for number, bit in enumerate((0, 2)):
        place = pl.ds(pl.multiple_of((spot ^ bit) * rows, rows), rows)
        near_ref[number * rows : (number + 1) * rows, :] = whole_ref[place, :]
    for number, bit in enumerate((1, 3)):
        place = pl.ds(pl.multiple_of((spot ^ bit) * rows, rows), rows)
        far_ref[number * rows : (number + 1) * rows, :] = whole_ref[place, :].astype(bf16)


def input_kernel(
    own_ref,
    beside_ref,
    across_ref,
    query_grad_ref,
    heads_ref,
    tokens_ref,
    gain_ref,
    residual_grad_ref,
    tokens_grad_ref,
    both_ref,
    gain_grad_ref,
):
    rows = query_grad_ref.shape[0]
    both = (
        own_ref[:rows, :]
        + beside_ref[:rows, :].astype(f32)
        + across_ref[...].astype(f32)
    ).astype(bf16)
    both_ref[...] = both
    grad = (
        contract_cols(query_grad_ref[...], heads_ref[0])
        + contract_cols(both[:, :INNER], heads_ref[1])
        + contract_cols(both[:, INNER:], heads_ref[2])
    )
    through, gain_grad = norm_backward(tokens_ref[...].astype(f32), gain_ref[...], grad)
    gain_grad_ref[...] = gain_grad
    tokens_grad_ref[...] = residual_grad_ref[...] + through


def vmem_call(body, outs, cost, scratch=(), name=None, smem_first=False):
    def run(*operands):
        specs = [pl.BlockSpec(memory_space=pltpu.VMEM)] * len(operands)
        if smem_first:
            specs[0] = pl.BlockSpec(memory_space=pltpu.SMEM)
        return pl.pallas_call(
            body,
            out_shape=[jax.ShapeDtypeStruct(shape, kind) for shape, kind in outs],
            in_specs=specs,
            out_specs=[pl.BlockSpec(memory_space=pltpu.VMEM)] * len(outs),
            scratch_shapes=list(scratch),
            compiler_params=pltpu.CompilerParams(vmem_limit_bytes=VMEM_BYTES),
            cost_estimate=pl.CostEstimate(
                flops=cost[0], bytes_accessed=cost[1], transcendentals=cost[2]
            ),
            name=name,
        )(*operands)

    return run


def total_kernel(sizes, part_ref, out_ref, line_ref, plane_ref, line_send, line_recv, plane_send, plane_recv):
    plane, line = sizes
    dp_spot, mp_spot = lax.axis_index("dp"), lax.axis_index("mp")
    barrier = pltpu.get_barrier_semaphore()
    for step in range(1, line):
        pl.semaphore_signal(
            barrier, 1, device_id=(dp_spot, lax.rem(mp_spot + step, line)), device_id_type=MESH
        )
    for step in range(1, plane):
        pl.semaphore_signal(
            barrier, 1, device_id=(lax.rem(dp_spot + step, plane), mp_spot), device_id_type=MESH
        )
    pl.semaphore_wait(barrier, line + plane - 2)

    def exchange(source, slots, size, spot, send, recv, target):
        slots[spot] = source[...]
        copies = [
            pltpu.make_async_remote_copy(
                src_ref=source,
                dst_ref=slots.at[spot],
                send_sem=send.at[step],
                recv_sem=recv.at[step],
                device_id=target(lax.rem(spot + step, size)),
                device_id_type=MESH,
            )
            for step in range(1, size)
        ]
        for copy in copies:
            copy.start()
        for copy in copies:
            copy.wait()
        total = slots[0]
        for index in range(1, size):
            total = total + slots[index]
        out_ref[...] = total

    exchange(part_ref, line_ref, line, mp_spot, line_send, line_recv, lambda to: (dp_spot, to))
    exchange(out_ref, plane_ref, plane, dp_spot, plane_send, plane_recv, lambda to: (to, mp_spot))


def total_all(part, number):
    plane, line = lax.axis_size("dp"), lax.axis_size("mp")
    if plane > RING_LIMIT:
        return lax.psum(part, ("dp", "mp"))
    return pl.pallas_call(
        partial(total_kernel, (plane, line)),
        out_shape=jax.ShapeDtypeStruct(part.shape, part.dtype),
        in_specs=[pl.BlockSpec(memory_space=pltpu.VMEM)],
        out_specs=pl.BlockSpec(memory_space=pltpu.VMEM),
        scratch_shapes=[
            pltpu.VMEM((line,) + part.shape, f32),
            pltpu.VMEM((plane,) + part.shape, f32),
            pltpu.SemaphoreType.DMA((line,)),
            pltpu.SemaphoreType.DMA((line,)),
            pltpu.SemaphoreType.DMA((plane,)),
            pltpu.SemaphoreType.DMA((plane,)),
        ],
        compiler_params=pltpu.CompilerParams(collective_id=number, has_side_effects=True),
        name="total",
    )(part)


def small_gather_kernel(size, part_ref, out_ref, send, recv):
    dp_spot, mp_spot = lax.axis_index("dp"), lax.axis_index("mp")
    barrier = pltpu.get_barrier_semaphore()
    for step in range(1, size):
        pl.semaphore_signal(
            barrier, 1, device_id=(lax.rem(dp_spot + step, size), mp_spot), device_id_type=MESH
        )
    pl.semaphore_wait(barrier, size - 1)
    out_ref[dp_spot] = part_ref[...]
    copies = [
        pltpu.make_async_remote_copy(
            src_ref=part_ref,
            dst_ref=out_ref.at[dp_spot],
            send_sem=send.at[step],
            recv_sem=recv.at[step],
            device_id=(lax.rem(dp_spot + step, size), mp_spot),
            device_id_type=MESH,
        )
        for step in range(1, size)
    ]
    for copy in copies:
        copy.start()
    for copy in copies:
        copy.wait()


def gather_gains(gains):
    size = lax.axis_size("dp")
    if size > RING_LIMIT:
        return lax.all_gather(gains, "dp", axis=1, tiled=True)
    count, width = gains.shape
    wide = -(-width // LANES) * LANES
    part = jnp.pad(gains, ((0, 8 - count), (0, wide - width)))
    whole = pl.pallas_call(
        partial(small_gather_kernel, size),
        out_shape=jax.ShapeDtypeStruct((size,) + part.shape, part.dtype),
        in_specs=[pl.BlockSpec(memory_space=pltpu.VMEM)],
        out_specs=pl.BlockSpec(memory_space=pltpu.VMEM),
        scratch_shapes=[pltpu.SemaphoreType.DMA((size,)), pltpu.SemaphoreType.DMA((size,))],
        compiler_params=pltpu.CompilerParams(collective_id=3, has_side_effects=True),
        name="gather_gains",
    )(part)
    return jnp.concatenate([whole[index, :count, :width] for index in range(size)], axis=1)


def pack_rows(parts):
    flat = jnp.concatenate([part.reshape(-1) for part in parts])
    count = -(-flat.shape[0] // (8 * LANES)) * 8
    return jnp.pad(flat, (0, count * LANES - flat.shape[0])).reshape(count, LANES)


def lamb_parts(weight, gradient, first_moment, second, decay_rate):
    new_first = beta_first * first_moment + (1.0 - beta_first) * gradient
    new_second = beta_second * second + (1.0 - beta_second) * gradient * gradient
    first_fix = 1.0 - beta_first**STEP
    second_fix = 1.0 - beta_second**STEP
    step_dir = (
        new_first / first_fix / (jnp.sqrt(new_second / second_fix) + adam_eps) + decay_rate * weight
    )
    return (new_first, new_second, step_dir)


def sub_squares(values, sub_count):
    flat_values = values.reshape(sub_count, -1)
    return jnp.sum(flat_values * flat_values, axis=1)


def shards(
    tokens,
    cotangent,
    lengths,
    heads_in,
    heads_out,
    expand_in,
    expand_out,
    norm_gains,
    bias_table,
    heads_in_first,
    heads_out_first,
    expand_in_first,
    expand_out_first,
    gains_first,
    table_first,
    heads_in_second,
    heads_out_second,
    expand_in_second,
    expand_out_second,
    gains_second,
    table_second,
):
    rows, depth = tokens.shape
    mp_size = lax.axis_size("mp")
    mp_spot = lax.axis_index("mp")
    keys = rows * mp_size
    span = -(-(keys + rows - 1) // LANES) * LANES
    first_row = mp_spot * rows
    shard_width = norm_gains.shape[1]
    buckets = bias_table.shape[0]

    four = jnp.concatenate([heads_in, heads_out.T[None]], axis=0).astype(bf16)
    mine = lax.dynamic_slice_in_dim(four, mp_spot, 1, axis=0)
    mine_all = gather_dp(mine)
    full_gains = gather_gains(norm_gains.astype(bf16).astype(f32))
    gain_one, gain_two = full_gains[0:1], full_gains[1:2]
    inputs = tokens.astype(f32)
    normed = rms_scale(inputs, gain_one).astype(bf16)
    normed_parts = gather_mp(normed)
    used = first_row + jnp.arange(rows, dtype=jnp.int32) < lengths[0, 0] + lengths[0, 1]
    upstream = jnp.where(used[:, None], cotangent, jnp.zeros_like(cotangent))
    upstream_parts = gather_mp(upstream)

    mine_parts = gather_mp(mine_all)
    by_bit = jnp.concatenate([mine_parts[0], mine_parts[2], mine_parts[1], mine_parts[3]], axis=0)
    full_heads = jnp.concatenate(
        [lax.dynamic_slice_in_dim(by_bit, mp_spot ^ number, 1, axis=0) for number in range(mp_size)],
        axis=0,
    )
    wide_in = gather_dp(expand_in.astype(bf16))
    wide_out = gather_dp(expand_out.T.astype(bf16)[None])[0]

    table = jnp.pad(bias_table.T, ((0, 8 - HEADS), (0, 0)))
    attention_flops = rows * keys * LANES * HEADS
    mixed, query, key, value, logs, residual, normed_two = vmem_call(
        partial(forward_kernel, span),
        [
            ((rows, INNER), bf16),
            ((rows, INNER), bf16),
            ((keys, INNER), bf16),
            ((keys, INNER), bf16),
            ((rows, LANES), f32),
            ((rows, depth), f32),
            ((rows, depth), bf16),
        ],
        (
            2 * depth * INNER * (2 * keys + 2 * rows) + 4 * attention_flops,
            2 * (4 * depth * INNER + 2 * keys * depth),
            rows * keys * HEADS,
        ),
        name="attention_forward",
        smem_first=True,
    )(lengths, *normed_parts, full_heads, table, tokens, gain_two)

    normed_all = jnp.concatenate(gather_mp(normed_two), axis=0)
    upstream_all = jnp.concatenate(upstream_parts, axis=0)
    gate_pre = matmul(normed_all, wide_in[0])
    up_pre = matmul(normed_all, wide_in[1])
    gelu_gate, gelu_pull = jax.vjp(partial(jax.nn.gelu, approximate=True), gate_pre)
    hidden = (gelu_gate * up_pre).astype(bf16)
    expand_out_grad = scatter_dp(contract_rows(upstream_all, hidden).astype(bf16)[None])[0].T
    feed_part = contract_cols(hidden, wide_out).astype(bf16)
    feed_near = feed_part[: 2 * rows].astype(f32) + swap(feed_part[2 * rows :], 1).astype(f32)
    feed_out = feed_near[:rows] + swap(feed_near[rows:].astype(bf16), 2).astype(f32)
    layer_out = (residual + feed_out).astype(bf16)

    hidden_grad = matmul(upstream_all, wide_out)
    up_grad = (hidden_grad * gelu_gate).astype(bf16)
    gate_grad = gelu_pull(hidden_grad * up_pre)[0].astype(bf16)
    normed_part = contract_cols(gate_grad, wide_in[0]) + contract_cols(up_grad, wide_in[1])
    normed_near = normed_part[: 2 * rows] + swap(normed_part[2 * rows :].astype(bf16), 1).astype(f32)
    normed_across = swap(normed_near[rows:].astype(bf16), 2)
    expand_in_grad = scatter_dp(
        jnp.stack(
            [
                contract_rows(normed_all, gate_grad).astype(bf16),
                contract_rows(normed_all, up_grad).astype(bf16),
            ]
        )
    )

    residual_grad, attended_grad, query_grad, near, far, offset_grad, gain_two_grad = vmem_call(
        partial(backward_kernel, span),
        [
            ((rows, depth), f32),
            ((rows, depth), bf16),
            ((rows, INNER), bf16),
            ((2 * rows, 2 * INNER), f32),
            ((2 * rows, 2 * INNER), bf16),
            ((8, span), f32),
            ((1, depth), f32),
        ],
        (
            2 * depth * INNER * rows + 10 * attention_flops,
            rows * depth * 16 + 2 * (4 * depth * INNER + 2 * keys * INNER),
            rows * keys * HEADS,
        ),
        scratch=[pltpu.VMEM((keys, 2 * INNER), f32)],
        name="attention_backward",
        smem_first=True,
    )(
        lengths,
        normed_near[:rows],
        normed_across,
        residual,
        upstream,
        gain_two,
        full_heads,
        query,
        key,
        value,
        logs,
        table,
    )
    attended_parts = gather_mp(attended_grad)
    beside = swap(far, 1)
    across = swap((near[rows:] + beside[rows:].astype(f32)).astype(bf16), 2)
    tokens_grad, both, gain_one_grad = vmem_call(
        input_kernel,
        [((rows, depth), f32), ((rows, 2 * INNER), bf16), ((1, depth), f32)],
        (6 * rows * depth * INNER, rows * depth * 14 + 8 * depth * INNER, 0),
        name="input_backward",
    )(near, beside, across, query_grad, full_heads, tokens, gain_one, residual_grad)

    offered = jnp.stack([query_grad, both[:, :INNER], both[:, INNER:], mixed])

    def for_bit(bit):
        return lax.dynamic_slice_in_dim(offered, mp_spot ^ bit, 1, axis=0)

    from_beside = swap(jnp.concatenate([for_bit(1), for_bit(3)], axis=0), 1)
    from_across = swap(jnp.concatenate([for_bit(2), from_beside[1:]], axis=0), 2)
    right = jnp.concatenate(
        [for_bit(0)[0], from_across[0], from_beside[0], from_across[1]], axis=0
    )
    left = jnp.where(
        mp_spot == mp_size - 1,
        jnp.concatenate(attended_parts, axis=0),
        jnp.concatenate(normed_parts, axis=0),
    )
    mine_grad = scatter_dp(contract_rows(left, right).astype(bf16)[None]).astype(bf16)
    grad_parts = gather_mp(mine_grad)
    grads_by_bit = jnp.concatenate(
        [grad_parts[0], grad_parts[2], grad_parts[1], grad_parts[3]], axis=0
    )
    heads_grad = [
        lax.dynamic_slice_in_dim(grads_by_bit, mp_spot ^ number, 1, axis=0)
        for number in range(mp_size)
    ]
    head_in_grad = jnp.concatenate(heads_grad[:3], axis=0).astype(f32)
    head_out_grad = heads_grad[3][0].T.astype(f32)

    reach = jnp.arange(span, dtype=jnp.int32) - (rows - 1) - first_row
    onehot = (bucket_ids(reach)[:, None] == jnp.arange(buckets, dtype=jnp.int32)[None, :]).astype(f32)
    table_part = jnp.dot(offset_grad, onehot, precision=highest)[:HEADS].T
    gain_parts = jnp.concatenate([gain_one_grad, gain_two_grad], axis=0)
    small = total_all(pack_rows([gain_parts, table_part]), 1).reshape(-1)
    gains_total = small[: 2 * depth].reshape(2, depth)
    table_grad = small[2 * depth : 2 * depth + buckets * HEADS].reshape(buckets, HEADS)
    gains_grad = lax.dynamic_slice_in_dim(
        gains_total, lax.axis_index("dp") * shard_width, shard_width, 1
    )

    weight_list = (heads_in, heads_out, expand_in, expand_out, norm_gains, bias_table)
    grad_list = (
        head_in_grad,
        head_out_grad,
        expand_in_grad,
        expand_out_grad,
        gains_grad,
        table_grad,
    )
    first_list = (
        heads_in_first,
        heads_out_first,
        expand_in_first,
        expand_out_first,
        gains_first,
        table_first,
    )
    second_list = (
        heads_in_second,
        heads_out_second,
        expand_in_second,
        expand_out_second,
        gains_second,
        table_second,
    )
    decay_list = (weight_decay, weight_decay, weight_decay, weight_decay, 0.0, 0.0)
    sub_list = (3, 1, 2, 1, 2, 1)
    results = [
        lamb_parts(
            weight_list[number],
            grad_list[number],
            first_list[number],
            second_list[number],
            decay_list[number],
        )
        for number in range(6)
    ]
    shared_scale = 1.0 / mp_size
    share_list = (shared_scale, shared_scale, 1.0, 1.0, shared_scale)
    weight_sq = [sub_squares(weight_list[number], sub_list[number]) for number in range(6)]
    step_sq = [sub_squares(results[number][2], sub_list[number]) for number in range(6)]
    sums = total_all(
        pack_rows(
            [weight_sq[number] * share_list[number] for number in range(5)]
            + [step_sq[number] * share_list[number] for number in range(5)]
        ),
        2,
    )[0]
    count = sum(sub_list[:5])
    weight_norm = jnp.sqrt(jnp.concatenate([sums[:count], weight_sq[5]]))
    step_norm = jnp.sqrt(jnp.concatenate([sums[count : 2 * count], step_sq[5]]))
    ratios = weight_norm / step_norm
    starts = (0, 3, 4, 6, 7, 9)
    outputs = [layer_out, tokens_grad]
    for number in range(6):
        weight = weight_list[number]
        sub_count = sub_list[number]
        ratio_part = ratios[starts[number] : starts[number] + sub_count]
        shape = (sub_count,) + (1,) * (weight.ndim - 1) if sub_count > 1 else (1,) * weight.ndim
        new_weight = weight - learn_rate * ratio_part.reshape(shape) * results[number][2]
        outputs = outputs + [
            results[number][0],
            results[number][1],
            new_weight,
            new_weight.astype(bf16),
        ]
    outputs = outputs + [jnp.stack([weight_norm, step_norm])]
    return tuple(outputs)


def solution(mesh):
    return jax.shard_map(
        shards,
        mesh=mesh,
        in_specs=(
            P(("dp", "mp"), None),
            P(("dp", "mp"), None),
            P("dp", None),
            P(None, "dp", None),
            P(None, "dp"),
            P(None, "dp", "mp"),
            P("mp", "dp"),
            P(None, "dp"),
            P(),
            P(None, "dp", None),
            P(None, "dp"),
            P(None, "dp", "mp"),
            P("mp", "dp"),
            P(None, "dp"),
            P(),
            P(None, "dp", None),
            P(None, "dp"),
            P(None, "dp", "mp"),
            P("mp", "dp"),
            P(None, "dp"),
            P(),
        ),
        out_specs=(
            P(("dp", "mp"), None),
            P(("dp", "mp"), None),
            P(None, "dp", None),
            P(None, "dp", None),
            P(None, "dp", None),
            P(None, "dp", None),
            P(None, "dp"),
            P(None, "dp"),
            P(None, "dp"),
            P(None, "dp"),
            P(None, "dp", "mp"),
            P(None, "dp", "mp"),
            P(None, "dp", "mp"),
            P(None, "dp", "mp"),
            P("mp", "dp"),
            P("mp", "dp"),
            P("mp", "dp"),
            P("mp", "dp"),
            P(None, "dp"),
            P(None, "dp"),
            P(None, "dp"),
            P(None, "dp"),
            P(),
            P(),
            P(),
            P(),
            P(),
        ),
        check_vma=False,
    )
```

```python
from functools import partial
from typing import NamedTuple

import jax
import jax.numpy as jnp
from jax import lax
from jax.experimental import pallas as pl
from jax.experimental.pallas import tpu as pltpu
from jax.sharding import PartitionSpec as P

HEADS = 6
HEAD_DIM = 64
STEP = 10
INNER = 384
LANES = 128
PAIRS = INNER // LANES
MESH = pl.DeviceIdType.MESH
VMEM_BYTES = 56 * 2**20
RING_LIMIT = 8


norm_eps = 1e-06
beta_first = 0.9
beta_second = 0.999
adam_eps = 1e-06
weight_decay = 0.01
learn_rate = 0.4
masked_fill = -1000000000.0
bucket_edges = (12, 16, 23, 32, 46, 64, 91)
highest = lax.Precision.HIGHEST
f32 = jnp.float32
bf16 = jnp.bfloat16


def bucket_ids(offsets):
    distance = jnp.abs(offsets)
    coarse = jnp.full_like(distance, 8)
    for edge_value in bucket_edges:
        coarse = coarse + (distance >= edge_value).astype(jnp.int32)
    nearby = jnp.where(distance < 8, distance, coarse)
    return nearby + 16 * (offsets > 0).astype(jnp.int32)


def row_mean(values, depth):
    return jnp.sum(values, axis=-1, keepdims=True) * (1.0 / depth)


def rms_scale(hidden_rows, gain_vector, depth):
    return (
        hidden_rows
        * lax.rsqrt(row_mean(hidden_rows * hidden_rows, depth) + norm_eps)
        * gain_vector
    )


def contract_rows(left_side, right_side):
    return lax.dot_general(
        left_side, right_side, (((0,), (0,)), ((), ())), preferred_element_type=f32
    )


def contract_cols(left_side, right_side):
    return lax.dot_general(
        left_side, right_side, (((1,), (1,)), ((), ())), preferred_element_type=f32
    )


def matmul(left_side, right_side):
    return jnp.dot(left_side, right_side, preferred_element_type=f32)


def ring_order(size):
    return list(range(0, size, 2)) + list(range(size - 1, 0, -2))


def ring_pairs(size):
    order = ring_order(size)
    forward = [(order[spot], order[(spot + 1) % size]) for spot in range(size)]
    return forward, [(target, source) for source, target in forward]


def ring_owner(spot, size):
    late = (spot >= size // 2).astype(jnp.int32)
    return 2 * spot + late * (2 * size - 1 - 4 * spot)


def ring_spot(index, size):
    return index // 2 + lax.rem(index, 2) * (size - 1 - 2 * (index // 2))


def cut_of(width):
    return ((width // LANES + 1) // 2) * LANES


def assemble_kernel(size, cut, *refs):
    slabs, (left, right, out, sems) = refs[:-4], refs[-4:]
    spot = ring_spot(lax.axis_index("dp"), size)
    copies = []
    for number, slab in enumerate(slabs):
        shift = number if number < size // 2 else number + 1
        owner = ring_owner(lax.rem(spot + shift, size), size)
        copies.append(pltpu.make_async_copy(slab, out.at[:, owner], sems.at[number]))
    owner = ring_owner(lax.rem(spot + size // 2, size), size)
    width = out.shape[-1]
    copies.append(
        pltpu.make_async_copy(left, out.at[:, owner, :, pl.ds(0, cut)], sems.at[size - 1])
    )
    copies.append(
        pltpu.make_async_copy(right, out.at[:, owner, :, pl.ds(cut, width - cut)], sems.at[size])
    )
    for copy in copies:
        copy.start()
    for copy in copies:
        copy.wait()


def gather_dp(part):
    size = lax.axis_size("dp")
    if size > RING_LIMIT:
        return lax.all_gather(part, "dp", axis=1, tiled=True)
    forward, backward = ring_pairs(size)
    count, rows, width = part.shape
    cut = cut_of(width)
    slabs = [None] * size
    slabs[0] = ahead = behind = part
    for hop in range(1, size // 2):
        ahead = lax.ppermute(ahead, "dp", forward)
        behind = lax.ppermute(behind, "dp", backward)
        slabs[size - hop] = ahead
        slabs[hop] = behind
    left = lax.ppermute(ahead[..., :cut], "dp", forward)
    right = lax.ppermute(behind[..., cut:], "dp", backward)
    operands = [slab for slab in slabs if slab is not None] + [left, right]
    total = count * size * rows * width * part.dtype.itemsize
    whole = pl.pallas_call(
        partial(assemble_kernel, size, cut),
        out_shape=jax.ShapeDtypeStruct((count, size, rows, width), part.dtype),
        in_specs=[pl.BlockSpec(memory_space=pl.ANY)] * len(operands),
        out_specs=pl.BlockSpec(memory_space=pltpu.VMEM),
        scratch_shapes=[pltpu.SemaphoreType.DMA((size + 1,))],
        compiler_params=pltpu.CompilerParams(vmem_limit_bytes=VMEM_BYTES),
        cost_estimate=pl.CostEstimate(flops=0, bytes_accessed=2 * total, transcendentals=0),
        name="assemble",
    )(*operands)
    return whole.reshape(count, size * rows, width)


def scatter_dp(whole):
    size = lax.axis_size("dp")
    if size > RING_LIMIT:
        return lax.psum_scatter(whole.astype(f32), "dp", scatter_dimension=1, tiled=True)
    forward, backward = ring_pairs(size)
    count, depth, width = whole.shape
    rows = depth // size
    cut = cut_of(width)
    spot = ring_spot(lax.axis_index("dp"), size)

    def term(shift):
        owner = ring_owner(lax.rem(spot + size + shift, size), size)
        return lax.dynamic_slice_in_dim(whole, owner * rows, rows, axis=1)

    far = term(size // 2)
    ahead = lax.ppermute(far[..., :cut], "dp", forward)
    behind = lax.ppermute(far[..., cut:], "dp", backward)
    for hop in range(size // 2 - 1, 0, -1):
        mine = term(hop).astype(f32)
        other = term(-hop).astype(f32)
        if hop == size // 2 - 1:
            ahead = jnp.concatenate([mine[..., :cut] + ahead.astype(f32), mine[..., cut:]], -1)
            behind = jnp.concatenate([other[..., :cut], other[..., cut:] + behind.astype(f32)], -1)
        else:
            ahead = mine + ahead.astype(f32)
            behind = other + behind.astype(f32)
        ahead = lax.ppermute(ahead.astype(bf16), "dp", forward)
        behind = lax.ppermute(behind.astype(bf16), "dp", backward)
    return term(0).astype(f32) + ahead.astype(f32) + behind.astype(f32)


def swap(part, bit):
    size = lax.axis_size("mp")
    return lax.ppermute(part, "mp", [(index, index ^ bit) for index in range(size)])


def gather_mp(part):
    across = swap(part, 2)
    beside = swap(part, 1)
    return part, across, beside, swap(across, 1)


def offset_values(table_ref, first_row, rows, span):
    offsets = lax.broadcasted_iota(jnp.int32, (8, span), 1) - (rows - 1) - first_row
    buckets = bucket_ids(offsets)
    table = table_ref[...]
    values = jnp.zeros((8, span), f32)
    for number in range(table.shape[1]):
        values = jnp.where(buckets == number, table[:, number : number + 1], values)
    return values


def segments_at(positions, first_len, second_len):
    return (positions >= first_len).astype(jnp.int32) + (
        positions >= first_len + second_len
    ).astype(jnp.int32)


def allowed_pairs(lens_ref, first_row, rows, keys):
    query = segments_at(
        first_row + lax.broadcasted_iota(jnp.int32, (rows, 1), 0), lens_ref[0, 0], lens_ref[0, 1]
    )
    key = segments_at(
        lax.broadcasted_iota(jnp.int32, (1, keys), 1), lens_ref[0, 0], lens_ref[0, 1]
    )
    return query == key


def skewed_bias(values, head, rows, keys, span):
    wide = jnp.broadcast_to(values[head : head + 1, :], (rows, span))
    return pltpu.roll(wide, span - (rows - 1), 1, stride=1, stride_axis=0)[:, :keys]


def attend_pair(pair, query_ref, key_ref, value_ref, mixed_ref, logs, values, allowed, lane, span):
    rows, keys = query_ref.shape[0], key_ref.shape[0]
    part = slice(pair * LANES, (pair + 1) * LANES)
    query, key, value = query_ref[:, part], key_ref[:, part], value_ref[:, part]
    mixed = jnp.zeros((rows, LANES), f32)
    for half in range(2):
        head = 2 * pair + half
        mask = (lane // HEAD_DIM) == half
        scores = contract_cols(jnp.where(mask, query, jnp.zeros_like(query)), key)
        scores = jnp.where(
            allowed, scores + skewed_bias(values, head, rows, keys, span), masked_fill
        )
        top = jnp.max(scores, axis=-1, keepdims=True)
        powers = jnp.exp(scores - top)
        total = jnp.sum(powers, axis=-1, keepdims=True)
        soft = (powers * (1.0 / total)).astype(bf16)
        mixed = jnp.where(mask, matmul(soft, value), mixed)
        logs = jnp.where(lane == head, top + jnp.log(total), logs)
    mixed_ref[:, part] = mixed.astype(bf16)
    return logs


def forward_kernel(
    span,
    depth,
    lens_ref,
    own_ref,
    across_ref,
    beside_ref,
    corner_ref,
    heads_ref,
    table_ref,
    tokens_ref,
    gain_ref,
    mixed_ref,
    query_ref,
    key_ref,
    value_ref,
    log_ref,
    residual_ref,
    normed_ref,
):
    rows = own_ref.shape[0]
    keys = key_ref.shape[0]
    spot = lax.axis_index("mp")
    first_row = spot * rows
    for block_ref, bit in ((own_ref, 0), (across_ref, 2), (beside_ref, 1), (corner_ref, 3)):
        place = pl.ds(pl.multiple_of((spot ^ bit) * rows, rows), rows)
        block = block_ref[...]
        key_ref[place, :] = matmul(block, heads_ref[1]).astype(bf16)
        value_ref[place, :] = matmul(block, heads_ref[2]).astype(bf16)
    query_ref[...] = matmul(own_ref[...], heads_ref[0]).astype(bf16)
    values = offset_values(table_ref, first_row, rows, span)
    allowed = allowed_pairs(lens_ref, first_row, rows, keys)
    lane = lax.broadcasted_iota(jnp.int32, (1, LANES), 1)
    logs = jnp.zeros((rows, LANES), f32)
    for pair in range(PAIRS):
        logs = attend_pair(
            pair, query_ref, key_ref, value_ref, mixed_ref, logs, values, allowed, lane, span
        )
    log_ref[...] = logs
    residual = tokens_ref[...].astype(f32) + contract_cols(mixed_ref[...], heads_ref[3])
    residual_ref[...] = residual
    normed_ref[...] = rms_scale(residual, gain_ref[...], depth).astype(bf16)


def norm_backward(rows_in, gain, grad, depth):
    scale = lax.rsqrt(row_mean(rows_in * rows_in, depth) + norm_eps)
    unit = rows_in * scale
    inner = grad * gain
    out = scale * (inner - unit * row_mean(inner * unit, depth))
    return out, jnp.sum(grad * unit, axis=0, keepdims=True)


def attend_pair_backward(
    pair, query_ref, key_ref, value_ref, log_ref, mixed_grad, values, allowed, span
):
    rows, keys = query_ref.shape[0], key_ref.shape[0]
    lane = lax.broadcasted_iota(jnp.int32, (1, LANES), 1)
    flip = (
        lax.broadcasted_iota(jnp.int32, (rows, rows), 0)
        + lax.broadcasted_iota(jnp.int32, (rows, rows), 1)
        == rows - 1
    ).astype(bf16)
    part = slice(pair * LANES, (pair + 1) * LANES)
    query, key, value = query_ref[:, part], key_ref[:, part], value_ref[:, part]
    query_grad = jnp.zeros((rows, LANES), f32)
    key_grad = jnp.zeros((keys, LANES), f32)
    value_grad = jnp.zeros((keys, LANES), f32)
    offsets = []
    for half in range(2):
        head = 2 * pair + half
        mask = (lane // HEAD_DIM) == half
        query_own = jnp.where(mask, query, jnp.zeros_like(query))
        mixed_own = jnp.where(mask, mixed_grad, jnp.zeros_like(mixed_grad))
        scores = contract_cols(query_own, key)
        scores = jnp.where(
            allowed, scores + skewed_bias(values, head, rows, keys, span), masked_fill
        )
        soft = jnp.exp(scores - log_ref[:, head : head + 1])
        soft_grad = contract_cols(mixed_own, value)
        corr = jnp.sum(soft * soft_grad, axis=-1, keepdims=True)
        scores_grad = (soft * (soft_grad - corr)).astype(bf16)
        query_grad = jnp.where(mask, matmul(scores_grad, key), query_grad)
        key_grad = key_grad + contract_rows(scores_grad, query_own)
        value_grad = value_grad + contract_rows(soft.astype(bf16), mixed_own)
        flipped = matmul(flip, scores_grad)
        flipped = jnp.concatenate([flipped, jnp.zeros((rows, span - keys), f32)], axis=1)
        skewed = pltpu.roll(flipped, 0, 1, stride=1, stride_axis=0)
        offsets.append(jnp.sum(skewed, axis=0, keepdims=True))
    return query_grad, key_grad, value_grad, offsets


def backward_kernel(
    span,
    depth,
    lens_ref,
    part_ref,
    across_ref,
    residual_ref,
    upstream_ref,
    gain_ref,
    heads_ref,
    query_ref,
    key_ref,
    value_ref,
    log_ref,
    table_ref,
    residual_grad_ref,
    attended_ref,
    query_grad_ref,
    near_ref,
    far_ref,
    offset_ref,
    gain_grad_ref,
    whole_ref,
):
    rows = query_ref.shape[0]
    keys = key_ref.shape[0]
    spot = lax.axis_index("mp")
    first_row = spot * rows
    grad = part_ref[...].astype(f32) + across_ref[...].astype(f32)
    through, gain_grad = norm_backward(residual_ref[...], gain_ref[...], grad, depth)
    gain_grad_ref[...] = gain_grad
    residual_grad = upstream_ref[...].astype(f32) + through
    residual_grad_ref[...] = residual_grad
    attended = residual_grad.astype(bf16)
    attended_ref[...] = attended
    mixed_grad_all = matmul(attended, heads_ref[3]).astype(bf16)
    values = offset_values(table_ref, first_row, rows, span)
    allowed = allowed_pairs(lens_ref, first_row, rows, keys)
    for pair in range(PAIRS):
        part = slice(pair * LANES, (pair + 1) * LANES)
        query_grad, key_grad, value_grad, offsets = attend_pair_backward(
            pair, query_ref, key_ref, value_ref, log_ref, mixed_grad_all[:, part], values, allowed,
            span,
        )
        for half in range(2):
            offset_ref[2 * pair + half : 2 * pair + half + 1, :] = offsets[half]
        query_grad_ref[:, part] = query_grad.astype(bf16)
        whole_ref[:, part] = key_grad
        whole_ref[:, INNER + pair * LANES : INNER + (pair + 1) * LANES] = value_grad
    offset_ref[HEADS:, :] = jnp.zeros((8 - HEADS, span), f32)
    for number, bit in enumerate((0, 2)):
        place = pl.ds(pl.multiple_of((spot ^ bit) * rows, rows), rows)
        near_ref[number * rows : (number + 1) * rows, :] = whole_ref[place, :]
    for number, bit in enumerate((1, 3)):
        place = pl.ds(pl.multiple_of((spot ^ bit) * rows, rows), rows)
        far_ref[number * rows : (number + 1) * rows, :] = whole_ref[place, :].astype(bf16)


def input_kernel(
    depth,
    own_ref,
    beside_ref,
    across_ref,
    query_grad_ref,
    heads_ref,
    tokens_ref,
    gain_ref,
    residual_grad_ref,
    tokens_grad_ref,
    both_ref,
    gain_grad_ref,
):
    rows = query_grad_ref.shape[0]
    both = (
        own_ref[:rows, :]
        + beside_ref[:rows, :].astype(f32)
        + across_ref[...].astype(f32)
    ).astype(bf16)
    both_ref[...] = both
    grad = (
        contract_cols(query_grad_ref[...], heads_ref[0])
        + contract_cols(both[:, :INNER], heads_ref[1])
        + contract_cols(both[:, INNER:], heads_ref[2])
    )
    through, gain_grad = norm_backward(tokens_ref[...].astype(f32), gain_ref[...], grad, depth)
    gain_grad_ref[...] = gain_grad
    tokens_grad_ref[...] = residual_grad_ref[...] + through


def vmem_call(body, outs, cost, scratch=(), name=None, smem_first=False):
    def run(*operands):
        specs = [pl.BlockSpec(memory_space=pltpu.VMEM)] * len(operands)
        if smem_first:
            specs[0] = pl.BlockSpec(memory_space=pltpu.SMEM)
        return pl.pallas_call(
            body,
            out_shape=[jax.ShapeDtypeStruct(shape, kind) for shape, kind in outs],
            in_specs=specs,
            out_specs=[pl.BlockSpec(memory_space=pltpu.VMEM)] * len(outs),
            scratch_shapes=list(scratch),
            compiler_params=pltpu.CompilerParams(vmem_limit_bytes=VMEM_BYTES),
            cost_estimate=pl.CostEstimate(
                flops=cost[0], bytes_accessed=cost[1], transcendentals=cost[2]
            ),
            name=name,
        )(*operands)

    return run


def total_kernel(sizes, part_ref, out_ref, line_ref, plane_ref, line_send, line_recv, plane_send, plane_recv):
    plane, line = sizes
    dp_spot, mp_spot = lax.axis_index("dp"), lax.axis_index("mp")
    barrier = pltpu.get_barrier_semaphore()
    for step in range(1, line):
        pl.semaphore_signal(
            barrier, 1, device_id=(dp_spot, lax.rem(mp_spot + step, line)), device_id_type=MESH
        )
    for step in range(1, plane):
        pl.semaphore_signal(
            barrier, 1, device_id=(lax.rem(dp_spot + step, plane), mp_spot), device_id_type=MESH
        )
    pl.semaphore_wait(barrier, line + plane - 2)

    def exchange(source, slots, size, spot, send, recv, target):
        slots[spot] = source[...]
        copies = [
            pltpu.make_async_remote_copy(
                src_ref=source,
                dst_ref=slots.at[spot],
                send_sem=send.at[step],
                recv_sem=recv.at[step],
                device_id=target(lax.rem(spot + step, size)),
                device_id_type=MESH,
            )
            for step in range(1, size)
        ]
        for copy in copies:
            copy.start()
        for copy in copies:
            copy.wait()
        total = slots[0]
        for index in range(1, size):
            total = total + slots[index]
        out_ref[...] = total

    exchange(part_ref, line_ref, line, mp_spot, line_send, line_recv, lambda to: (dp_spot, to))
    exchange(out_ref, plane_ref, plane, dp_spot, plane_send, plane_recv, lambda to: (to, mp_spot))


def total_all(part, number):
    plane, line = lax.axis_size("dp"), lax.axis_size("mp")
    if plane > RING_LIMIT:
        return lax.psum(part, ("dp", "mp"))
    return pl.pallas_call(
        partial(total_kernel, (plane, line)),
        out_shape=jax.ShapeDtypeStruct(part.shape, part.dtype),
        in_specs=[pl.BlockSpec(memory_space=pltpu.VMEM)],
        out_specs=pl.BlockSpec(memory_space=pltpu.VMEM),
        scratch_shapes=[
            pltpu.VMEM((line,) + part.shape, f32),
            pltpu.VMEM((plane,) + part.shape, f32),
            pltpu.SemaphoreType.DMA((line,)),
            pltpu.SemaphoreType.DMA((line,)),
            pltpu.SemaphoreType.DMA((plane,)),
            pltpu.SemaphoreType.DMA((plane,)),
        ],
        compiler_params=pltpu.CompilerParams(collective_id=number, has_side_effects=True),
        name="total",
    )(part)


def small_gather_kernel(size, part_ref, out_ref, send, recv):
    dp_spot, mp_spot = lax.axis_index("dp"), lax.axis_index("mp")
    barrier = pltpu.get_barrier_semaphore()
    for step in range(1, size):
        pl.semaphore_signal(
            barrier, 1, device_id=(lax.rem(dp_spot + step, size), mp_spot), device_id_type=MESH
        )
    pl.semaphore_wait(barrier, size - 1)
    out_ref[dp_spot] = part_ref[...]
    copies = [
        pltpu.make_async_remote_copy(
            src_ref=part_ref,
            dst_ref=out_ref.at[dp_spot],
            send_sem=send.at[step],
            recv_sem=recv.at[step],
            device_id=(lax.rem(dp_spot + step, size), mp_spot),
            device_id_type=MESH,
        )
        for step in range(1, size)
    ]
    for copy in copies:
        copy.start()
    for copy in copies:
        copy.wait()


def gather_gains(gains):
    size = lax.axis_size("dp")
    if size > RING_LIMIT:
        return lax.all_gather(gains, "dp", axis=1, tiled=True)
    count, width = gains.shape
    wide = -(-width // LANES) * LANES
    part = jnp.pad(gains, ((0, 8 - count), (0, wide - width)))
    whole = pl.pallas_call(
        partial(small_gather_kernel, size),
        out_shape=jax.ShapeDtypeStruct((size,) + part.shape, part.dtype),
        in_specs=[pl.BlockSpec(memory_space=pltpu.VMEM)],
        out_specs=pl.BlockSpec(memory_space=pltpu.VMEM),
        scratch_shapes=[pltpu.SemaphoreType.DMA((size,)), pltpu.SemaphoreType.DMA((size,))],
        compiler_params=pltpu.CompilerParams(collective_id=3, has_side_effects=True),
        name="gather_gains",
    )(part)
    return jnp.concatenate([whole[index, :count, :width] for index in range(size)], axis=1)


def pack_rows(parts):
    flat = jnp.concatenate([part.reshape(-1) for part in parts])
    count = -(-flat.shape[0] // (8 * LANES)) * 8
    return jnp.pad(flat, (0, count * LANES - flat.shape[0])).reshape(count, LANES)


def lamb_parts(weight, gradient, first_moment, second, decay_rate):
    new_first = beta_first * first_moment + (1.0 - beta_first) * gradient
    new_second = beta_second * second + (1.0 - beta_second) * gradient * gradient
    first_fix = 1.0 - beta_first**STEP
    second_fix = 1.0 - beta_second**STEP
    step_dir = (
        new_first / first_fix / (jnp.sqrt(new_second / second_fix) + adam_eps) + decay_rate * weight
    )
    return (new_first, new_second, step_dir)


def sub_squares(values, sub_count):
    flat_values = values.reshape(sub_count, -1)
    return jnp.sum(flat_values * flat_values, axis=1)


def gelu_parts(gate):
    root = (2.0 / 3.141592653589793) ** 0.5
    square = gate * gate
    curve = jnp.tanh(root * (gate + 0.044715 * gate * square))
    value = 0.5 * gate * (1.0 + curve)
    slope = 0.5 * (1.0 + curve) + 0.5 * gate * (1.0 - curve * curve) * root * (
        1.0 + 3.0 * 0.044715 * square
    )
    return value, slope


class Places:
    def __init__(self, size):
        self.size, self.half = size, size // 2
        self.dp, self.mp = lax.axis_index("dp"), lax.axis_index("mp")
        self.spot = ring_spot(self.dp, size)
        self.sides = (
            ring_owner(lax.rem(self.spot + 1, size), size),
            ring_owner(lax.rem(self.spot + size - 1, size), size),
        )

    def owner(self, shift):
        return ring_owner(lax.rem(self.spot + self.size + shift, self.size), self.size)

    def sent(self, side, hop):
        return self.owner(-hop if side == 0 else hop)

    def came(self, side, hop):
        return self.sent(side, hop + 1)


def remote(source, target, send, recv, dp, mp):
    return pltpu.make_async_remote_copy(
        src_ref=source,
        dst_ref=target,
        send_sem=send,
        recv_sem=recv,
        device_id=(dp, mp),
        device_id_type=MESH,
    )


class ForwardOut(NamedTuple):
    heads: object
    gate_up: object
    down: object
    normed: object
    upstream: object
    normed_two: object
    gelu: object
    slope: object
    hidden: object
    hidden_grad_out: object
    query: object
    key: object
    value: object
    mixed: object
    logs: object
    residual: object
    full_gains: object


class ForwardRefs(NamedTuple):
    lens: object
    tokens: object
    cotangent: object
    gains: object
    table: object
    mine: object
    wide_in: object
    wide_out: object
    heads: object
    gate_up: object
    down: object
    normed: object
    upstream: object
    normed_two: object
    gelu: object
    slope: object
    hidden: object
    hidden_grad_out: object
    query: object
    key: object
    value: object
    mixed: object
    logs: object
    residual: object
    full_gains: object
    gain_slots: object
    gain_send: object
    gain_recv: object
    head_send: object
    head_recv: object
    wide_send: object
    wide_recv: object
    line_send: object
    line_recv: object
    slab_send: object
    slab_recv: object
    store_sems: object


def forward_shapes(rows, line, size, slot, width, span):
    wide, keys = size * slot, rows * line
    return ForwardOut(
        heads=((4, wide, INNER), bf16),
        gate_up=((2, wide, width), bf16),
        down=((wide, width), bf16),
        normed=((keys, wide), bf16),
        upstream=((keys, wide), bf16),
        normed_two=((keys, wide), bf16),
        gelu=((keys, width), f32),
        slope=((keys, width), f32),
        hidden=((keys, width), bf16),
        hidden_grad_out=((wide, width), bf16),
        query=((rows, INNER), bf16),
        key=((keys, INNER), bf16),
        value=((keys, INNER), bf16),
        mixed=((rows, INNER), bf16),
        logs=((rows, LANES), f32),
        residual=((rows, wide), f32),
        full_gains=((8, wide), f32),
    )


def ring_forward_kernel(size, depth, span, *refs):
    count = len(ForwardOut._fields)
    inputs = len(refs) - 2 * count - 12
    stores = refs[inputs : inputs + count]
    r = ForwardRefs(*refs[:inputs], *refs[inputs + count :])
    kept = refs[inputs + count : inputs + 2 * count]

    def store_copy(number):
        return pltpu.make_async_copy(kept[number], stores[number], r.store_sems.at[number])

    def store(*which):
        for number in range(count):
            if any(kept[number] is ref for ref in which):
                store_copy(number).start()

    at = Places(size)
    half = at.half
    rows, wide = r.tokens.shape
    keys = r.key.shape[0]
    slot = wide // size
    width = r.down.shape[1]
    cut, head_cut = cut_of(width), cut_of(INNER)
    first_row = at.mp * rows
    across, beside = at.mp ^ 2, at.mp ^ 1

    barrier = pltpu.get_barrier_semaphore()
    for step in range(1, size):
        pl.semaphore_signal(
            barrier, 1, device_id=(lax.rem(at.dp + step, size), at.mp), device_id_type=MESH
        )
    for partner in (across, beside):
        pl.semaphore_signal(barrier, 1, device_id=(at.dp, partner), device_id_type=MESH)
    pl.semaphore_wait(barrier, size + 1)

    def slab_rows(owner):
        return pl.ds(pl.multiple_of(owner * slot, slot), slot)

    def head_lanes(side, hop):
        if hop < half - 1:
            return pl.ds(0, INNER)
        return pl.ds(0, head_cut) if side == 0 else pl.ds(head_cut, INNER - head_cut)

    def head_hop(side, hop):
        lanes = head_lanes(side, hop)
        target = r.heads.at[at.mp, slab_rows(at.sent(side, hop)), lanes]
        source = r.mine.at[:, lanes] if hop == 0 else target
        return remote(
            source, target, r.head_send.at[side, hop], r.head_recv.at[side, hop],
            at.sides[side], at.mp,
        )

    def head_came(side, hop):
        target = r.heads.at[at.mp, slab_rows(at.came(side, hop)), head_lanes(side, hop)]
        return remote(
            target, target, r.head_send.at[side, hop], r.head_recv.at[side, hop],
            at.sides[side], at.mp,
        )

    def piece_view(piece, owner):
        lanes = pl.ds(0, cut) if piece % 2 == 0 else pl.ds(cut, width - cut)
        if piece < 4:
            return r.gate_up.at[piece // 2, slab_rows(owner), lanes]
        return r.down.at[slab_rows(owner), lanes]

    def piece_source(piece):
        lanes = pl.ds(0, cut) if piece % 2 == 0 else pl.ds(cut, width - cut)
        if piece < 4:
            return r.wide_in.at[piece // 2, :, lanes]
        return r.wide_out.at[:, lanes]

    def piece_goes(piece, side, hop):
        return hop < half - 1 or piece in ((0, 3, 4), (1, 2, 5))[side]

    def piece_hop(piece, side, hop):
        target = piece_view(piece, at.sent(side, hop))
        source = piece_source(piece) if hop == 0 else target
        return remote(
            source, target, r.wide_send.at[piece, side, hop], r.wide_recv.at[piece, side, hop],
            at.sides[side], at.mp,
        )

    def piece_came(piece, side, hop):
        target = piece_view(piece, at.came(side, hop))
        return remote(
            target, target, r.wide_send.at[piece, side, hop], r.wide_recv.at[piece, side, hop],
            at.sides[side], at.mp,
        )

    def serve(piece, hop):
        for side in range(2):
            if piece_goes(piece, side, hop):
                if hop > 0:
                    piece_came(piece, side, hop - 1).wait_recv()
                piece_hop(piece, side, hop).start()

    def finish(piece):
        for side in range(2):
            last = half - 1 if piece_goes(piece, side, half - 1) else half - 2
            piece_came(piece, side, last).wait_recv()

    def block(array, number):
        return array.at[pl.ds(number * rows, rows)]

    def line_copy(array, ref, number):
        source, target, partner = ((0, 1, across), (0, 2, beside), (1, 3, beside))[number]
        return remote(
            block(ref, source), block(ref, target), r.line_send.at[array, number],
            r.line_recv.at[array, number], at.dp, partner,
        )

    shifts = [0] + [shift for hop in range(1, half) for shift in (-hop, hop)] + [half]

    def slab_copy(number, way):
        matrix = across if way == 2 else at.mp
        view = r.heads.at[matrix, slab_rows(at.owner(shifts[number]))]
        source = r.mine if number == 0 and way < 2 else view
        return remote(
            source, view, r.slab_send.at[number, way], r.slab_recv.at[number, way],
            at.dp, across if way == 0 else beside,
        )

    def slab_came(number, way):
        matrix = (across, beside, at.mp ^ 3)[way]
        view = r.heads.at[matrix, slab_rows(at.owner(shifts[number]))]
        return remote(
            view, view, r.slab_send.at[number, way], r.slab_recv.at[number, way],
            at.dp, across if way == 0 else beside,
        )

    def gain_copy(step):
        return remote(
            r.gains, r.gain_slots.at[at.dp], r.gain_send.at[step], r.gain_recv.at[step],
            lax.rem(at.dp + step, size), at.mp,
        )

    for step in range(1, size):
        gain_copy(step).start()
    for side in range(2):
        head_hop(side, 0).start()
    for way in range(2):
        slab_copy(0, way).start()
    serve(0, 0)
    r.gain_slots[at.dp] = r.gains[...]
    own = slab_rows(at.dp)
    r.heads[at.mp, own, :] = r.mine[...]
    r.gate_up[0, own, :] = r.wide_in[0]
    r.gate_up[1, own, :] = r.wide_in[1]
    r.down[own, :] = r.wide_out[...]
    positions = first_row + lax.broadcasted_iota(jnp.int32, (rows, 1), 0)
    used = positions < r.lens[0, 0] + r.lens[0, 1]
    block(r.upstream, 0)[...] = jnp.where(used, r.cotangent[...].astype(f32), 0.0).astype(bf16)
    for step in range(1, size):
        gain_copy(step).wait()
    r.full_gains[...] = jnp.concatenate(
        [r.gain_slots[2 * pair] + r.gain_slots[2 * pair + 1] for pair in range(half)], axis=1
    )
    block(r.normed, 0)[...] = rms_scale(
        r.tokens[...].astype(f32), r.full_gains[0:1, :], depth
    ).astype(bf16)
    for number in range(2):
        line_copy(0, r.normed, number).start()

    fillers = [[(1, 0)], [(2, 0)], [(3, 0), (0, 1)], [(1, 1)]]
    for hop in range(half):
        for side in range(2):
            head_came(side, hop).wait_recv()
            if hop + 1 < half:
                head_hop(side, hop + 1).start()
        for piece, piece_at in fillers[min(hop, 3)]:
            serve(piece, piece_at)
        done = (2 * hop + 1, 2 * hop + 2) if hop + 1 < half else (2 * hop + 1,)
        for number in done:
            for way in range(2):
                slab_copy(number, way).start()
    line_copy(0, r.normed, 0).wait_recv()
    line_copy(0, r.normed, 2).start()
    for number in range(2):
        line_copy(1, r.upstream, number).start()
    serve(2, 1)
    for number in range(size):
        slab_came(number, 0).wait_recv()
        slab_copy(number, 2).start()
    serve(3, 1)
    for number in range(size):
        slab_came(number, 1).wait_recv()
    for number in range(size):
        slab_came(number, 2).wait_recv()

    r.query[...] = matmul(block(r.normed, 0)[...], r.heads[0]).astype(bf16)
    for number, bit in ((0, 0), (2, 1), (1, 2), (3, 3)):
        if number == 2:
            line_copy(0, r.normed, 1).wait_recv()
        if number == 3:
            line_copy(0, r.normed, 2).wait_recv()
        place = pl.ds(pl.multiple_of((at.mp ^ bit) * rows, rows), rows)
        data = block(r.normed, number)[...]
        r.key[place, :] = matmul(data, r.heads[1]).astype(bf16)
        r.value[place, :] = matmul(data, r.heads[2]).astype(bf16)
    serve(0, 2)
    store(r.full_gains, r.normed, r.query, r.key, r.value)

    values = offset_values(r.table, first_row, rows, span)
    allowed = allowed_pairs(r.lens, first_row, rows, keys)
    lane = lax.broadcasted_iota(jnp.int32, (1, LANES), 1)
    logs = jnp.zeros((rows, LANES), f32)
    for pair in range(PAIRS):
        logs = attend_pair(
            pair, r.query, r.key, r.value, r.mixed, logs, values, allowed, lane, span
        )
        serve(1 + pair, 2)
    r.logs[...] = logs
    residual = r.tokens[...].astype(f32) + contract_cols(r.mixed[...], r.heads[3])
    r.residual[...] = residual
    block(r.normed_two, 0)[...] = rms_scale(residual, r.full_gains[1:2, :], depth).astype(bf16)
    store(r.heads, r.mixed, r.logs, r.residual)
    for number in range(2):
        line_copy(2, r.normed_two, number).start()
    for piece in range(4):
        serve(piece, 3)
    serve(4, 0)
    serve(5, 0)
    line_copy(2, r.normed_two, 0).wait_recv()
    line_copy(2, r.normed_two, 2).start()
    for piece in range(4):
        finish(piece)

    def expand(number):
        place = pl.ds(number * rows, rows)
        data = r.normed_two[place, :]
        gate = matmul(data, r.gate_up[0])
        up = matmul(data, r.gate_up[1])
        value, slope = gelu_parts(gate)
        r.gelu[place, :] = value
        r.slope[place, :] = slope * up
        r.hidden[place, :] = (value * up).astype(bf16)

    expand(0)
    serve(4, 1)
    line_copy(2, r.normed_two, 1).wait_recv()
    expand(2)
    serve(5, 1)
    expand(1)
    serve(4, 2)
    line_copy(2, r.normed_two, 2).wait_recv()
    expand(3)
    serve(5, 2)
    store(r.gelu, r.slope, r.hidden, r.gate_up, r.normed_two)
    line_copy(1, r.upstream, 0).wait_recv()
    line_copy(1, r.upstream, 2).start()
    line_copy(1, r.upstream, 1).wait_recv()
    line_copy(1, r.upstream, 2).wait_recv()
    store(r.upstream)
    tiles = 4
    tile = wide // tiles
    for number in range(tiles):
        lanes = slice(number * tile, (number + 1) * tile)
        r.hidden_grad_out[lanes, :] = contract_rows(
            r.upstream[:, lanes], r.hidden[...]
        ).astype(bf16)
        if number == 0:
            serve(4, 3)
            serve(5, 3)
    store(r.hidden_grad_out)
    for piece in (4, 5):
        finish(piece)
    store(r.down)

    for side in range(2):
        for hop in range(half):
            head_hop(side, hop).wait_send()
            for piece in range(6):
                if piece_goes(piece, side, hop):
                    piece_hop(piece, side, hop).wait_send()
    for number in range(size):
        for way in range(3):
            slab_copy(number, way).wait_send()
    for array, ref in enumerate((r.normed, r.upstream, r.normed_two)):
        for number in range(3):
            line_copy(array, ref, number).wait_send()
    for number in range(count):
        store_copy(number).wait()


def ring_forward(size, line, depth, slot, width, span, operands):
    rows = operands[1].shape[0]
    shapes = forward_shapes(rows, line, size, slot, width, span)
    wide, keys = size * slot, rows * line
    dma = pltpu.SemaphoreType.DMA
    half = size // 2
    specs = [pl.BlockSpec(memory_space=pltpu.VMEM)] * len(operands)
    specs[0] = pl.BlockSpec(memory_space=pltpu.SMEM)
    flops = 2 * keys * wide * (3 * width + 2 * INNER) + 4 * rows * wide * INNER
    results = pl.pallas_call(
        partial(ring_forward_kernel, size, depth, span),
        out_shape=[jax.ShapeDtypeStruct(*shape) for shape in shapes],
        in_specs=specs,
        out_specs=[pl.BlockSpec(memory_space=pl.ANY)] * len(shapes),
        scratch_shapes=[pltpu.VMEM(*shape) for shape in shapes]
        + [
            pltpu.VMEM((size, 8, 2 * slot), f32),
            dma((size,)),
            dma((size,)),
            dma((2, half)),
            dma((2, half)),
            dma((6, 2, half)),
            dma((6, 2, half)),
            dma((3, 3)),
            dma((3, 3)),
            dma((size, 3)),
            dma((size, 3)),
            dma((len(shapes),)),
        ],
        compiler_params=pltpu.CompilerParams(
            collective_id=4, has_side_effects=True, vmem_limit_bytes=60 * 2**20
        ),
        cost_estimate=pl.CostEstimate(flops=flops, bytes_accessed=40 * 2**20, transcendentals=0),
        name="ring_forward",
    )(*operands)
    return ForwardOut(*results)


class BackwardOut(NamedTuple):
    layer_out: object
    tokens_grad: object
    down_grad: object
    gate_up_grad: object
    heads_grad: object
    gains_grad: object
    table_grad: object


class BackwardRefs(NamedTuple):
    lens: object
    table: object
    tokens: object
    layer_out: object
    tokens_grad: object
    down_grad: object
    gate_up_grad: object
    heads_grad: object
    gains_grad: object
    table_grad: object
    hidden_grad_out: object
    upstream: object
    down: object
    gelu: object
    slope: object
    gate_up: object
    normed_two: object
    hidden: object
    residual: object
    full_gains: object
    heads: object
    query: object
    key: object
    value: object
    logs: object
    mixed: object
    load_sems: object
    both_grads: object
    wide_came: object
    down_came: object
    far_send: object
    far_came: object
    across_send: object
    across_came: object
    feed_send: object
    feed_far_came: object
    feed_across_send: object
    feed_across_came: object
    pair_send: object
    pair_came: object
    pair_across_send: object
    pair_across_came: object
    offered: object
    right: object
    mine_grad: object
    mine_came: object
    mine_sums: object
    small: object
    small_line: object
    small_gains: object
    small_table: object
    wide_sems: object
    line_sems: object
    attended_sems: object
    right_sems: object
    mine_sems: object
    sums_sems: object
    small_sems: object


def back_loads(values):
    return (
        values.hidden_grad_out,
        values.upstream,
        values.down,
        values.gelu,
        values.slope,
        values.gate_up,
        values.normed_two,
        values.hidden,
        values.residual,
        values.full_gains,
        values.heads,
        values.query,
        values.key,
        values.value,
        values.logs,
        values.mixed,
    )


def ring_backward_kernel(size, depth, span, *refs):
    loaded, outs = 16, len(BackwardOut._fields)
    sources = refs[3 : 3 + loaded]
    normed_source = refs[3 + loaded]
    r = BackwardRefs(*refs[:3], *refs[4 + loaded :])
    held = back_loads(r)

    def load_copy(number):
        return pltpu.make_async_copy(sources[number], held[number], r.load_sems.at[number])

    def arrive(*which):
        for number in range(loaded):
            if any(held[number] is ref for ref in which):
                load_copy(number).wait()

    for number in range(loaded):
        load_copy(number).start()
    at = Places(size)
    half = at.half
    rows = r.query.shape[0]
    keys = r.key.shape[0]
    wide = r.residual.shape[1]
    slot = wide // size
    width = r.down.shape[1]
    line = keys // rows
    cut, head_cut = cut_of(width), cut_of(INNER)
    first_row = at.mp * rows
    across, beside, corner = at.mp ^ 2, at.mp ^ 1, at.mp ^ 3
    part_wide = wide // 2

    barrier = pltpu.get_barrier_semaphore()
    for step in range(1, size):
        pl.semaphore_signal(
            barrier, 1, device_id=(lax.rem(at.dp + step, size), at.mp), device_id_type=MESH
        )
    for partner in (across, beside, corner):
        pl.semaphore_signal(barrier, 1, device_id=(at.dp, partner), device_id_type=MESH)
    pl.semaphore_wait(barrier, size + 2)

    def slab_rows(owner):
        return pl.ds(pl.multiple_of(owner * slot, slot), slot)

    def block_rows(number):
        return pl.ds(number * rows, rows)

    def piece_lanes(piece):
        return pl.ds(0, cut) if piece % 2 == 0 else pl.ds(cut, width - cut)

    def piece_term(piece, owner):
        if piece < 4:
            return r.gate_up.at[piece // 2, slab_rows(owner), piece_lanes(piece)]
        return r.hidden_grad_out.at[slab_rows(owner), piece_lanes(piece)]

    def piece_buffer(piece, side, hop):
        if piece < 4:
            return r.wide_came.at[side, hop, piece // 2, :, piece_lanes(piece)]
        return r.down_came.at[side, hop, :, piece_lanes(piece)]

    def piece_starts(piece, side):
        return piece in ((0, 3, 4), (1, 2, 5))[side]

    def piece_target(side, hop):
        return at.owner(half - hop if side == 0 else hop - half)

    def piece_has(piece, side, hop):
        return hop > 0 or piece_starts(piece, side)

    def piece_copy(piece, side, hop):
        fresh = hop == 0 or (hop == 1 and not piece_starts(piece, side))
        source = (
            piece_term(piece, piece_target(side, hop))
            if fresh
            else piece_buffer(piece, side, hop - 1)
        )
        return remote(
            source, piece_buffer(piece, side, hop), r.wide_sems.at[0, piece, side, hop],
            r.wide_sems.at[1, piece, side, hop], at.sides[side], at.mp,
        )

    def serve(piece, hop, sides=(0, 1)):
        for side in sides:
            if not piece_has(piece, side, hop):
                continue
            if hop > 0 and piece_has(piece, side, hop - 1):
                piece_copy(piece, side, hop - 1).wait_recv()
                came = piece_buffer(piece, side, hop - 1)
                term = piece_term(piece, piece_target(side, hop))
                came[...] = (came[...].astype(f32) + term[...].astype(f32)).astype(bf16)
            piece_copy(piece, side, hop).start()

    def finish(piece):
        for side in range(2):
            piece_copy(piece, side, half - 1).wait_recv()
        term = piece_term(piece, at.dp)
        total = (
            term[...].astype(f32)
            + piece_buffer(piece, 0, half - 1)[...].astype(f32)
            + piece_buffer(piece, 1, half - 1)[...].astype(f32)
        )
        if piece < 4:
            r.gate_up_grad[piece // 2, :, piece_lanes(piece)] = total
        else:
            r.down_grad[:, piece_lanes(piece)] = total

    def mine_lanes(side, hop):
        if hop > 0:
            return pl.ds(0, INNER)
        return pl.ds(0, head_cut) if side == 0 else pl.ds(head_cut, INNER - head_cut)

    def mine_copy(side, hop):
        lanes = mine_lanes(side, hop)
        source = (
            r.mine_grad.at[slab_rows(piece_target(side, hop)), lanes]
            if hop == 0
            else r.mine_came.at[side, hop - 1, :, lanes]
        )
        return remote(
            source, r.mine_came.at[side, hop, :, lanes], r.mine_sems.at[0, side, hop],
            r.mine_sems.at[1, side, hop], at.sides[side], at.mp,
        )

    def mine_serve(hop):
        for side in range(2):
            if hop > 0:
                mine_copy(side, hop - 1).wait_recv()
                came = r.mine_came.at[side, hop - 1]
                term = r.mine_grad.at[slab_rows(piece_target(side, hop))]
                lanes = mine_lanes(side, hop - 1)
                if hop == 1:
                    keep = pl.ds(head_cut, INNER - head_cut) if side == 0 else pl.ds(0, head_cut)
                    came[:, keep] = term[:, keep]
                came[:, lanes] = (
                    came[:, lanes].astype(f32) + term[:, lanes].astype(f32)
                ).astype(bf16)
            mine_copy(side, hop).start()

    def far_copy(number, send, came):
        return remote(
            send, came, r.line_sems.at[0, number], r.line_sems.at[1, number],
            at.dp, beside if number % 2 == 0 else across,
        )

    def attended_copy(number):
        source, target, partner = ((0, 1, across), (0, 2, beside), (1, 3, beside))[number]
        return remote(
            r.upstream.at[block_rows(source)], r.upstream.at[block_rows(target)],
            r.attended_sems.at[0, number], r.attended_sems.at[1, number], at.dp, partner,
        )

    def near_write(array, tile, values):
        array[tile * 2 * rows : (tile + 1) * 2 * rows, :part_wide] = values

    def near_read(array, number):
        return jnp.concatenate(
            [
                array[2 * rows * tile + number * rows : 2 * rows * tile + (number + 1) * rows, :part_wide]
                for tile in range(2)
            ],
            axis=1,
        )

    arrive(r.hidden_grad_out)
    for piece in (4, 5):
        serve(piece, 0)
    serve(4, 1, (1,))
    serve(5, 1, (0,))
    arrive(r.upstream, r.down, r.gelu, r.slope)
    order = (2, 3, 0, 1)
    for number in order:
        place = block_rows(number)
        hidden_grad = matmul(r.upstream[place, :], r.down[...])
        r.both_grads[0, place, :] = (hidden_grad * r.slope[place, :]).astype(bf16)
        r.both_grads[1, place, :] = (hidden_grad * r.gelu[place, :]).astype(bf16)
        if number == 3:
            serve(4, 1, (0,))
            serve(5, 1, (1,))
    arrive(r.gate_up)

    def normed_tile(first, tile):
        place = pl.ds(first, 2 * rows)
        part = slice(tile * part_wide, (tile + 1) * part_wide)
        return contract_cols(r.both_grads[0, place, :], r.gate_up[0, part, :]) + contract_cols(
            r.both_grads[1, place, :], r.gate_up[1, part, :]
        )

    for tile in range(2):
        r.far_send[:, tile * part_wide : (tile + 1) * part_wide] = normed_tile(
            2 * rows, tile
        ).astype(bf16)
    far_copy(0, r.far_send, r.far_came).start()
    for tile in range(2):
        near_write(r.slope, tile, normed_tile(0, tile))
    serve(4, 2)
    serve(5, 2)
    far_copy(0, r.far_send, r.far_came).wait_recv()
    r.across_send[...] = (
        near_read(r.slope, 1) + r.far_came[rows:, :].astype(f32)
    ).astype(bf16)
    far_copy(1, r.across_send, r.across_came).start()

    arrive(r.normed_two)
    tiles = 4
    tile_wide = wide // tiles
    for matrix in range(2):
        for tile in range(tiles):
            lanes = slice(tile * tile_wide, (tile + 1) * tile_wide)
            r.gate_up[matrix, lanes, :] = contract_rows(
                r.normed_two[:, lanes], r.both_grads[matrix]
            ).astype(bf16)
        for piece in (2 * matrix, 2 * matrix + 1):
            serve(piece, 0)
        serve(2 * matrix, 1, (1 - matrix,))
        serve(2 * matrix + 1, 1, (matrix,))
        if matrix == 0:
            serve(4, 3)
            serve(5, 3)
    arrive(r.hidden)

    normed_load = pltpu.make_async_copy(
        normed_source, r.normed_two, r.load_sems.at[loaded]
    )
    normed_load.start()

    def feed_tile(first, tile):
        part = slice(tile * part_wide, (tile + 1) * part_wide)
        return contract_cols(r.hidden[pl.ds(first, 2 * rows), :], r.down[part, :])

    for tile in range(2):
        r.feed_send[:, tile * part_wide : (tile + 1) * part_wide] = feed_tile(
            2 * rows, tile
        ).astype(bf16)
    far_copy(2, r.feed_send, r.feed_far_came).start()
    for tile in range(2):
        near_write(r.gelu, tile, feed_tile(0, tile))
    finish(4)
    finish(5)
    arrive(r.residual, r.full_gains, r.heads, r.query, r.key, r.value, r.logs, r.mixed)

    far_copy(1, r.across_send, r.across_came).wait_recv()
    grad = (
        near_read(r.slope, 0)
        + r.far_came[:rows, :].astype(f32)
        + r.across_came[...].astype(f32)
    )
    through, gain_two_grad = norm_backward(r.residual[...], r.full_gains[1:2, :], grad, depth)
    residual_grad = r.upstream[:rows, :].astype(f32) + through
    r.tokens_grad[...] = residual_grad
    attended = residual_grad.astype(bf16)
    r.upstream[:rows, :] = attended
    for number in range(2):
        attended_copy(number).start()
    mixed_grad_all = matmul(attended, r.heads[3]).astype(bf16)
    serve(0, 1, (0,))
    serve(1, 1, (1,))

    far_copy(2, r.feed_send, r.feed_far_came).wait_recv()
    r.feed_across_send[...] = (
        near_read(r.gelu, 1) + r.feed_far_came[rows:, :].astype(f32)
    ).astype(bf16)
    far_copy(3, r.feed_across_send, r.feed_across_came).start()
    serve(2, 1, (1,))
    serve(3, 1, (0,))

    values = offset_values(r.table, first_row, rows, span)
    allowed = allowed_pairs(r.lens, first_row, rows, keys)
    offsets = []
    for pair in range(PAIRS):
        part = slice(pair * LANES, (pair + 1) * LANES)
        query_grad, key_grad, value_grad, pair_offsets = attend_pair_backward(
            pair, r.query, r.key, r.value, r.logs, mixed_grad_all[:, part], values,
            allowed, span,
        )
        r.offered[0, :, part] = query_grad.astype(bf16)
        r.slope[:, part] = key_grad
        r.slope[:, INNER + pair * LANES : INNER + (pair + 1) * LANES] = value_grad
        offsets = offsets + pair_offsets
        if pair == 0:
            serve(0, 2)
            serve(1, 2)
        if pair == 1:
            serve(2, 2)
            serve(3, 2)
    pair_wide = 2 * INNER
    for number, bit in ((0, 1), (1, 3)):
        place = pl.ds(pl.multiple_of((at.mp ^ bit) * rows, rows), rows)
        r.pair_send[number * rows : (number + 1) * rows, :] = r.slope[place, :pair_wide].astype(
            bf16
        )
    far_copy(4, r.pair_send, r.pair_came).start()
    r.offered[3] = r.mixed[...]

    offset_grad = jnp.concatenate(offsets + [jnp.zeros((8 - HEADS, span), f32)], axis=0)
    reach = lax.broadcasted_iota(jnp.int32, (8, span), 1) - (rows - 1) - first_row
    reach = bucket_ids(reach)
    lane = lax.broadcasted_iota(jnp.int32, (8, LANES), 1)
    table_grad = jnp.zeros((8, LANES), f32)
    for number in range(r.table.shape[1]):
        mass = jnp.sum(jnp.where(reach == number, offset_grad, 0.0), axis=1, keepdims=True)
        table_grad = jnp.where(lane == number, mass, table_grad)

    attended_copy(0).wait_recv()
    attended_copy(2).start()
    far_copy(4, r.pair_send, r.pair_came).wait_recv()
    place = pl.ds(pl.multiple_of(across * rows, rows), rows)
    r.pair_across_send[...] = (
        r.slope[place, :pair_wide] + r.pair_came[rows:, :].astype(f32)
    ).astype(bf16)
    far_copy(5, r.pair_across_send, r.pair_across_came).start()
    far_copy(3, r.feed_across_send, r.feed_across_came).wait_recv()
    r.layer_out[...] = (
        r.residual[...]
        + (
            near_read(r.gelu, 0)
            + r.feed_far_came[:rows, :].astype(f32)
            + r.feed_across_came[...].astype(f32)
        )
    ).astype(bf16)
    serve(0, 3)
    serve(1, 3)
    far_copy(5, r.pair_across_send, r.pair_across_came).wait_recv()
    place = pl.ds(pl.multiple_of(at.mp * rows, rows), rows)
    both = (
        r.slope[place, :pair_wide]
        + r.pair_came[:rows, :].astype(f32)
        + r.pair_across_came[...].astype(f32)
    ).astype(bf16)
    r.offered[1] = both[:, :INNER]
    r.offered[2] = both[:, INNER:]

    def right_copy(number):
        partner = (across, beside, corner)[number - 1]
        return remote(
            r.offered.at[partner], r.right.at[block_rows(number)],
            r.right_sems.at[0, number], r.right_sems.at[1, number], at.dp, partner,
        )

    for number in range(1, line):
        right_copy(number).start()
    r.right[block_rows(0), :] = r.offered[at.mp]
    serve(2, 3)
    serve(3, 3)
    grad = (
        contract_cols(r.offered[0], r.heads[0])
        + contract_cols(r.offered[1], r.heads[1])
        + contract_cols(r.offered[2], r.heads[2])
    )
    through, gain_one_grad = norm_backward(
        r.tokens[...].astype(f32), r.full_gains[0:1, :], grad, depth
    )
    r.tokens_grad[...] = r.tokens_grad[...] + through

    normed_load.wait()
    for number in range(1, 3):
        attended_copy(number).wait_recv()
    for number in range(1, line):
        right_copy(number).wait_recv()
    last = at.mp == line - 1
    for tile in range(tiles):
        lanes = slice(tile * tile_wide, (tile + 1) * tile_wide)
        left = jnp.where(last, r.upstream[:, lanes], r.normed_two[:, lanes])
        r.mine_grad[lanes, :] = contract_rows(left, r.right[...]).astype(bf16)
    mine_serve(0)

    r.small[0, :, wide:] = table_grad
    r.small[0, 0:1, :wide] = gain_one_grad
    r.small[0, 1:2, :wide] = gain_two_grad
    r.small[0, 2:, :wide] = jnp.zeros((6, wide), f32)

    def small_line_copy(step):
        return remote(
            r.small.at[0], r.small_line.at[at.mp], r.small_sems.at[0, step],
            r.small_sems.at[1, step], at.dp, lax.rem(at.mp + step, line),
        )

    for step in range(1, line):
        small_line_copy(step).start()
    r.small_line[at.mp] = r.small[0]
    mine_serve(1)
    for step in range(1, line):
        small_line_copy(step).wait()
    total = r.small_line[0]
    for number in range(1, line):
        total = total + r.small_line[number]
    r.small[1] = total
    pair_slot = 2 * slot

    def small_copies(step):
        target = lax.rem(at.dp + step, size)
        lanes = pl.ds(pl.multiple_of(target // 2 * pair_slot, pair_slot), pair_slot)
        return (
            remote(
                r.small.at[1, :, lanes], r.small_gains.at[at.dp], r.small_sems.at[2, step],
                r.small_sems.at[3, step], target, at.mp,
            ),
            remote(
                r.small.at[1, :, pl.ds(wide, LANES)], r.small_table.at[at.dp],
                r.small_sems.at[4, step], r.small_sems.at[5, step], target, at.mp,
            ),
        )

    for step in range(1, size):
        for copy in small_copies(step):
            copy.start()
    lanes = pl.ds(pl.multiple_of(at.dp // 2 * pair_slot, pair_slot), pair_slot)
    r.small_gains[at.dp] = r.small[1, :, lanes]
    r.small_table[at.dp] = r.small[1, :, wide:]
    mine_serve(2)
    for step in range(1, size):
        for copy in small_copies(step):
            copy.wait()
    gains_total, table_total = r.small_gains[0], r.small_table[0]
    for number in range(1, size):
        gains_total = gains_total + r.small_gains[number]
        table_total = table_total + r.small_table[number]
    r.gains_grad[...] = gains_total
    r.table_grad[...] = table_total
    for piece in range(4):
        finish(piece)
    mine_serve(3)
    for side in range(2):
        mine_copy(side, half - 1).wait_recv()
    r.mine_sums[at.mp] = (
        r.mine_grad[slab_rows(at.dp), :].astype(f32)
        + r.mine_came[0, half - 1].astype(f32)
        + r.mine_came[1, half - 1].astype(f32)
    ).astype(bf16)

    def sums_copy(number):
        partner = (across, beside, corner)[number - 1]
        return remote(
            r.mine_sums.at[at.mp], r.mine_sums.at[at.mp],
            r.sums_sems.at[0, number], r.sums_sems.at[1, number], at.dp, partner,
        )

    for number in range(1, line):
        sums_copy(number).start()
    for side in range(2):
        for hop in range(half):
            mine_copy(side, hop).wait_send()
            for piece in range(6):
                if piece_has(piece, side, hop):
                    piece_copy(piece, side, hop).wait_send()
    sends = (r.far_send, r.across_send, r.feed_send, r.feed_across_send)
    cames = (r.far_came, r.across_came, r.feed_far_came, r.feed_across_came)
    sends = sends + (r.pair_send, r.pair_across_send)
    cames = cames + (r.pair_came, r.pair_across_came)
    for number in range(6):
        far_copy(number, sends[number], cames[number]).wait_send()
    for number in range(3):
        attended_copy(number).wait_send()
    for number in range(1, line):
        right_copy(number).wait_send()
    for number in range(1, line):
        sums_copy(number).wait()
    r.heads_grad[...] = r.mine_sums[...]


def ring_backward(size, line, depth, slot, width, span, lens, table, tokens, got):
    rows = tokens.shape[0]
    wide, keys, half = size * slot, rows * line, size // 2
    shapes = forward_shapes(rows, line, size, slot, width, span)
    dma = pltpu.SemaphoreType.DMA
    operands = [lens, table, tokens] + list(back_loads(got)) + [got.normed]
    specs = [
        pl.BlockSpec(memory_space=pltpu.SMEM),
        pl.BlockSpec(memory_space=pltpu.VMEM),
        pl.BlockSpec(memory_space=pltpu.VMEM),
    ] + [pl.BlockSpec(memory_space=pl.ANY)] * len(operands[3:])
    outs = [
        ((rows, wide), bf16),
        ((rows, wide), f32),
        ((slot, width), f32),
        ((2, slot, width), f32),
        ((line, slot, INNER), bf16),
        ((8, 2 * slot), f32),
        ((8, LANES), f32),
    ]
    half_send = pltpu.VMEM((2 * rows, wide), bf16)
    block_send = pltpu.VMEM((rows, wide), bf16)
    scratch = [pltpu.VMEM(*shape) for shape in back_loads(shapes)] + [
        dma((len(operands) - 3,)),
        pltpu.VMEM((2, keys, width), bf16),
        pltpu.VMEM((2, half, 2, slot, width), bf16),
        pltpu.VMEM((2, half, slot, width), bf16),
        half_send,
        half_send,
        block_send,
        block_send,
        half_send,
        half_send,
        block_send,
        block_send,
        pltpu.VMEM((2 * rows, 2 * INNER), bf16),
        pltpu.VMEM((2 * rows, 2 * INNER), bf16),
        pltpu.VMEM((rows, 2 * INNER), bf16),
        pltpu.VMEM((rows, 2 * INNER), bf16),
        pltpu.VMEM((line, rows, INNER), bf16),
        pltpu.VMEM((keys, INNER), bf16),
        pltpu.VMEM((wide, INNER), bf16),
        pltpu.VMEM((2, half, slot, INNER), bf16),
        pltpu.VMEM((line, slot, INNER), bf16),
        pltpu.VMEM((2, 8, wide + LANES), f32),
        pltpu.VMEM((line, 8, wide + LANES), f32),
        pltpu.VMEM((size, 8, 2 * slot), f32),
        pltpu.VMEM((size, 8, LANES), f32),
        dma((2, 6, 2, half)),
        dma((2, 6)),
        dma((2, 3)),
        dma((2, line)),
        dma((2, 2, half)),
        dma((2, line)),
        dma((6, size)),
    ]
    flops = 2 * keys * wide * (6 * width + INNER) + 16 * rows * wide * INNER
    results = pl.pallas_call(
        partial(ring_backward_kernel, size, depth, span),
        out_shape=[jax.ShapeDtypeStruct(*out) for out in outs],
        in_specs=specs,
        out_specs=[pl.BlockSpec(memory_space=pltpu.VMEM)] * len(outs),
        scratch_shapes=scratch,
        compiler_params=pltpu.CompilerParams(
            collective_id=5, has_side_effects=True, vmem_limit_bytes=62 * 2**20
        ),
        cost_estimate=pl.CostEstimate(flops=flops, bytes_accessed=40 * 2**20, transcendentals=0),
        name="ring_backward",
    )(*operands)
    return BackwardOut(*results)


def plain_gradients(
    tokens,
    cotangent,
    lengths,
    heads_in,
    heads_out,
    expand_in,
    expand_out,
    norm_gains,
    bias_table,
):
    rows, depth = tokens.shape
    mp_size = lax.axis_size("mp")
    mp_spot = lax.axis_index("mp")
    keys = rows * mp_size
    span = -(-(keys + rows - 1) // LANES) * LANES
    first_row = mp_spot * rows
    shard_width = norm_gains.shape[1]
    buckets = bias_table.shape[0]

    four = jnp.concatenate([heads_in, heads_out.T[None]], axis=0).astype(bf16)
    mine = lax.dynamic_slice_in_dim(four, mp_spot, 1, axis=0)
    mine_all = gather_dp(mine)
    full_gains = gather_gains(norm_gains.astype(bf16).astype(f32))
    gain_one, gain_two = full_gains[0:1], full_gains[1:2]
    inputs = tokens.astype(f32)
    normed = rms_scale(inputs, gain_one, depth).astype(bf16)
    normed_parts = gather_mp(normed)
    used = first_row + jnp.arange(rows, dtype=jnp.int32) < lengths[0, 0] + lengths[0, 1]
    upstream = jnp.where(used[:, None], cotangent, jnp.zeros_like(cotangent))
    upstream_parts = gather_mp(upstream)

    mine_parts = gather_mp(mine_all)
    by_bit = jnp.concatenate([mine_parts[0], mine_parts[2], mine_parts[1], mine_parts[3]], axis=0)
    full_heads = jnp.concatenate(
        [lax.dynamic_slice_in_dim(by_bit, mp_spot ^ number, 1, axis=0) for number in range(mp_size)],
        axis=0,
    )
    wide_in = gather_dp(expand_in.astype(bf16))
    wide_out = gather_dp(expand_out.T.astype(bf16)[None])[0]

    table = jnp.pad(bias_table.T, ((0, 8 - HEADS), (0, 0)))
    attention_flops = rows * keys * LANES * HEADS
    mixed, query, key, value, logs, residual, normed_two = vmem_call(
        partial(forward_kernel, span, depth),
        [
            ((rows, INNER), bf16),
            ((rows, INNER), bf16),
            ((keys, INNER), bf16),
            ((keys, INNER), bf16),
            ((rows, LANES), f32),
            ((rows, depth), f32),
            ((rows, depth), bf16),
        ],
        (
            2 * depth * INNER * (2 * keys + 2 * rows) + 4 * attention_flops,
            2 * (4 * depth * INNER + 2 * keys * depth),
            rows * keys * HEADS,
        ),
        name="attention_forward",
        smem_first=True,
    )(lengths, *normed_parts, full_heads, table, tokens, gain_two)

    normed_all = jnp.concatenate(gather_mp(normed_two), axis=0)
    upstream_all = jnp.concatenate(upstream_parts, axis=0)
    gate_pre = matmul(normed_all, wide_in[0])
    up_pre = matmul(normed_all, wide_in[1])
    gelu_gate, gelu_pull = jax.vjp(partial(jax.nn.gelu, approximate=True), gate_pre)
    hidden = (gelu_gate * up_pre).astype(bf16)
    expand_out_grad = scatter_dp(contract_rows(upstream_all, hidden).astype(bf16)[None])[0].T
    feed_part = contract_cols(hidden, wide_out).astype(bf16)
    feed_near = feed_part[: 2 * rows].astype(f32) + swap(feed_part[2 * rows :], 1).astype(f32)
    feed_out = feed_near[:rows] + swap(feed_near[rows:].astype(bf16), 2).astype(f32)
    layer_out = (residual + feed_out).astype(bf16)

    hidden_grad = matmul(upstream_all, wide_out)
    up_grad = (hidden_grad * gelu_gate).astype(bf16)
    gate_grad = gelu_pull(hidden_grad * up_pre)[0].astype(bf16)
    normed_part = contract_cols(gate_grad, wide_in[0]) + contract_cols(up_grad, wide_in[1])
    normed_near = normed_part[: 2 * rows] + swap(normed_part[2 * rows :].astype(bf16), 1).astype(f32)
    normed_across = swap(normed_near[rows:].astype(bf16), 2)
    expand_in_grad = scatter_dp(
        jnp.stack(
            [
                contract_rows(normed_all, gate_grad).astype(bf16),
                contract_rows(normed_all, up_grad).astype(bf16),
            ]
        )
    )

    residual_grad, attended_grad, query_grad, near, far, offset_grad, gain_two_grad = vmem_call(
        partial(backward_kernel, span, depth),
        [
            ((rows, depth), f32),
            ((rows, depth), bf16),
            ((rows, INNER), bf16),
            ((2 * rows, 2 * INNER), f32),
            ((2 * rows, 2 * INNER), bf16),
            ((8, span), f32),
            ((1, depth), f32),
        ],
        (
            2 * depth * INNER * rows + 10 * attention_flops,
            rows * depth * 16 + 2 * (4 * depth * INNER + 2 * keys * INNER),
            rows * keys * HEADS,
        ),
        scratch=[pltpu.VMEM((keys, 2 * INNER), f32)],
        name="attention_backward",
        smem_first=True,
    )(
        lengths,
        normed_near[:rows],
        normed_across,
        residual,
        upstream,
        gain_two,
        full_heads,
        query,
        key,
        value,
        logs,
        table,
    )
    attended_parts = gather_mp(attended_grad)
    beside = swap(far, 1)
    across = swap((near[rows:] + beside[rows:].astype(f32)).astype(bf16), 2)
    tokens_grad, both, gain_one_grad = vmem_call(
        partial(input_kernel, depth),
        [((rows, depth), f32), ((rows, 2 * INNER), bf16), ((1, depth), f32)],
        (6 * rows * depth * INNER, rows * depth * 14 + 8 * depth * INNER, 0),
        name="input_backward",
    )(near, beside, across, query_grad, full_heads, tokens, gain_one, residual_grad)

    offered = jnp.stack([query_grad, both[:, :INNER], both[:, INNER:], mixed])

    def for_bit(bit):
        return lax.dynamic_slice_in_dim(offered, mp_spot ^ bit, 1, axis=0)

    from_beside = swap(jnp.concatenate([for_bit(1), for_bit(3)], axis=0), 1)
    from_across = swap(jnp.concatenate([for_bit(2), from_beside[1:]], axis=0), 2)
    right = jnp.concatenate(
        [for_bit(0)[0], from_across[0], from_beside[0], from_across[1]], axis=0
    )
    left = jnp.where(
        mp_spot == mp_size - 1,
        jnp.concatenate(attended_parts, axis=0),
        jnp.concatenate(normed_parts, axis=0),
    )
    mine_grad = scatter_dp(contract_rows(left, right).astype(bf16)[None]).astype(bf16)
    grad_parts = gather_mp(mine_grad)
    grads_by_bit = jnp.concatenate(
        [grad_parts[0], grad_parts[2], grad_parts[1], grad_parts[3]], axis=0
    )
    heads_grad = [
        lax.dynamic_slice_in_dim(grads_by_bit, mp_spot ^ number, 1, axis=0)
        for number in range(mp_size)
    ]
    head_in_grad = jnp.concatenate(heads_grad[:3], axis=0).astype(f32)
    head_out_grad = heads_grad[3][0].T.astype(f32)

    reach = jnp.arange(span, dtype=jnp.int32) - (rows - 1) - first_row
    onehot = (bucket_ids(reach)[:, None] == jnp.arange(buckets, dtype=jnp.int32)[None, :]).astype(f32)
    table_part = jnp.dot(offset_grad, onehot, precision=highest)[:HEADS].T
    gain_parts = jnp.concatenate([gain_one_grad, gain_two_grad], axis=0)
    small = total_all(pack_rows([gain_parts, table_part]), 1).reshape(-1)
    gains_total = small[: 2 * depth].reshape(2, depth)
    table_grad = small[2 * depth : 2 * depth + buckets * HEADS].reshape(buckets, HEADS)
    gains_grad = lax.dynamic_slice_in_dim(
        gains_total, lax.axis_index("dp") * shard_width, shard_width, 1
    )

    return layer_out, tokens_grad, (
        head_in_grad,
        head_out_grad,
        expand_in_grad,
        expand_out_grad,
        gains_grad,
        table_grad,
    )


def ring_gradients(
    tokens, cotangent, lengths, heads_in, heads_out, expand_in, expand_out, norm_gains, bias_table
):
    rows, depth = tokens.shape
    size, mp_size = lax.axis_size("dp"), lax.axis_size("mp")
    mp_spot = lax.axis_index("mp")
    keys = rows * mp_size
    span = -(-(keys + rows - 1) // LANES) * LANES
    shard_width = norm_gains.shape[1]
    width = expand_in.shape[2]
    buckets = bias_table.shape[0]
    slot = -(-shard_width // 16) * 16
    spare = slot - shard_width
    source = jnp.arange(depth, dtype=jnp.int32)
    spread = (
        (source // shard_width * slot + lax.rem(source, shard_width))[:, None]
        == jnp.arange(size * slot, dtype=jnp.int32)[None, :]
    ).astype(bf16)

    mine = lax.dynamic_slice_in_dim(
        jnp.concatenate([heads_in, heads_out.T[None]], axis=0), mp_spot, 1, axis=0
    )[0]
    mine = jnp.pad(mine.astype(bf16), ((0, spare), (0, 0)))
    part_in = jnp.pad(expand_in.astype(bf16), ((0, 0), (0, spare), (0, 0)))
    part_out = jnp.pad(expand_out.T.astype(bf16), ((0, spare), (0, 0)))
    wide_tokens = matmul(tokens, spread).astype(bf16)
    wide_cotangent = matmul(cotangent, spread).astype(bf16)
    gains = jnp.pad(norm_gains.astype(bf16).astype(f32), ((0, 8 - 2), (0, spare)))
    odd = lax.rem(lax.axis_index("dp"), 2) == 1
    gains = jnp.concatenate(
        [jnp.where(odd, 0.0, gains), jnp.where(odd, gains, 0.0)], axis=1
    )
    table = jnp.pad(bias_table.T, ((0, 8 - HEADS), (0, 0)))
    got = ring_forward(
        size, mp_size, depth, slot, width, span,
        (lengths, wide_tokens, wide_cotangent, gains, table, mine, part_in, part_out),
    )
    back = ring_backward(
        size, mp_size, depth, slot, width, span, lengths, table, wide_tokens, got
    )
    layer_out = contract_cols(back.layer_out, spread).astype(bf16)
    coarse = back.tokens_grad.astype(bf16)
    fine = (back.tokens_grad - coarse.astype(f32)).astype(bf16)
    tokens_grad = contract_cols(coarse, spread) + contract_cols(fine, spread)
    heads_grad = back.heads_grad[:, :shard_width].astype(f32)
    head_in_grad, head_out_grad = heads_grad[:3], heads_grad[3].T
    expand_in_grad = back.gate_up_grad[:, :shard_width]
    expand_out_grad = back.down_grad[:shard_width].T
    gains = back.gains_grad[:2]
    gains_grad = jnp.where(odd, gains[:, slot : slot + shard_width], gains[:, :shard_width])
    table_grad = back.table_grad[:HEADS, :buckets].T
    return layer_out, tokens_grad, (
        head_in_grad,
        head_out_grad,
        expand_in_grad,
        expand_out_grad,
        gains_grad,
        table_grad,
    )


def shards(
    tokens,
    cotangent,
    lengths,
    heads_in,
    heads_out,
    expand_in,
    expand_out,
    norm_gains,
    bias_table,
    heads_in_first,
    heads_out_first,
    expand_in_first,
    expand_out_first,
    gains_first,
    table_first,
    heads_in_second,
    heads_out_second,
    expand_in_second,
    expand_out_second,
    gains_second,
    table_second,
):
    mp_size = lax.axis_size("mp")
    gradients = ring_gradients if lax.axis_size("dp") <= RING_LIMIT else plain_gradients
    layer_out, tokens_grad, grad_list = gradients(
        tokens, cotangent, lengths, heads_in, heads_out, expand_in, expand_out, norm_gains, bias_table
    )
    weight_list = (heads_in, heads_out, expand_in, expand_out, norm_gains, bias_table)
    first_list = (
        heads_in_first,
        heads_out_first,
        expand_in_first,
        expand_out_first,
        gains_first,
        table_first,
    )
    second_list = (
        heads_in_second,
        heads_out_second,
        expand_in_second,
        expand_out_second,
        gains_second,
        table_second,
    )
    decay_list = (weight_decay, weight_decay, weight_decay, weight_decay, 0.0, 0.0)
    sub_list = (3, 1, 2, 1, 2, 1)
    results = [
        lamb_parts(
            weight_list[number],
            grad_list[number],
            first_list[number],
            second_list[number],
            decay_list[number],
        )
        for number in range(6)
    ]
    shared_scale = 1.0 / mp_size
    share_list = (shared_scale, shared_scale, 1.0, 1.0, shared_scale)
    weight_sq = [sub_squares(weight_list[number], sub_list[number]) for number in range(6)]
    step_sq = [sub_squares(results[number][2], sub_list[number]) for number in range(6)]
    sums = total_all(
        pack_rows(
            [weight_sq[number] * share_list[number] for number in range(5)]
            + [step_sq[number] * share_list[number] for number in range(5)]
        ),
        2,
    )[0]
    count = sum(sub_list[:5])
    weight_norm = jnp.sqrt(jnp.concatenate([sums[:count], weight_sq[5]]))
    step_norm = jnp.sqrt(jnp.concatenate([sums[count : 2 * count], step_sq[5]]))
    ratios = weight_norm / step_norm
    starts = (0, 3, 4, 6, 7, 9)
    outputs = [layer_out, tokens_grad]
    for number in range(6):
        weight = weight_list[number]
        sub_count = sub_list[number]
        ratio_part = ratios[starts[number] : starts[number] + sub_count]
        shape = (sub_count,) + (1,) * (weight.ndim - 1) if sub_count > 1 else (1,) * weight.ndim
        new_weight = weight - learn_rate * ratio_part.reshape(shape) * results[number][2]
        outputs = outputs + [
            results[number][0],
            results[number][1],
            new_weight,
            new_weight.astype(bf16),
        ]
    outputs = outputs + [jnp.stack([weight_norm, step_norm])]
    return tuple(outputs)


def solution(mesh):
    return jax.shard_map(
        shards,
        mesh=mesh,
        in_specs=(
            P(("dp", "mp"), None),
            P(("dp", "mp"), None),
            P("dp", None),
            P(None, "dp", None),
            P(None, "dp"),
            P(None, "dp", "mp"),
            P("mp", "dp"),
            P(None, "dp"),
            P(),
            P(None, "dp", None),
            P(None, "dp"),
            P(None, "dp", "mp"),
            P("mp", "dp"),
            P(None, "dp"),
            P(),
            P(None, "dp", None),
            P(None, "dp"),
            P(None, "dp", "mp"),
            P("mp", "dp"),
            P(None, "dp"),
            P(),
        ),
        out_specs=(
            P(("dp", "mp"), None),
            P(("dp", "mp"), None),
            P(None, "dp", None),
            P(None, "dp", None),
            P(None, "dp", None),
            P(None, "dp", None),
            P(None, "dp"),
            P(None, "dp"),
            P(None, "dp"),
            P(None, "dp"),
            P(None, "dp", "mp"),
            P(None, "dp", "mp"),
            P(None, "dp", "mp"),
            P(None, "dp", "mp"),
            P("mp", "dp"),
            P("mp", "dp"),
            P("mp", "dp"),
            P("mp", "dp"),
            P(None, "dp"),
            P(None, "dp"),
            P(None, "dp"),
            P(None, "dp"),
            P(),
            P(),
            P(),
            P(),
            P(),
        ),
        check_vma=False,
    )
```

```python
from functools import partial
from typing import NamedTuple

import jax
import jax.numpy as jnp
from jax import lax
from jax.experimental import pallas as pl
from jax.experimental.pallas import tpu as pltpu
from jax.sharding import PartitionSpec as P

HEADS = 6
HEAD_DIM = 64
STEP = 10
INNER = 384
LANES = 128
PAIRS = INNER // LANES
MESH = pl.DeviceIdType.MESH
VMEM_BYTES = 56 * 2**20
BACKWARD_BYTES = 63 * 2**20
RING_LIMIT = 8


norm_eps = 1e-06
beta_first = 0.9
beta_second = 0.999
adam_eps = 1e-06
weight_decay = 0.01
learn_rate = 0.4
masked_fill = -1000000000.0
bucket_edges = (12, 16, 23, 32, 46, 64, 91)
highest = lax.Precision.HIGHEST
f32 = jnp.float32
bf16 = jnp.bfloat16


def bucket_ids(offsets):
    distance = jnp.abs(offsets)
    coarse = jnp.full_like(distance, 8)
    for edge_value in bucket_edges:
        coarse = coarse + (distance >= edge_value).astype(jnp.int32)
    nearby = jnp.where(distance < 8, distance, coarse)
    return nearby + 16 * (offsets > 0).astype(jnp.int32)


def row_mean(values, depth):
    return jnp.sum(values, axis=-1, keepdims=True) * (1.0 / depth)


def rms_scale(hidden_rows, gain_vector, depth):
    return (
        hidden_rows
        * lax.rsqrt(row_mean(hidden_rows * hidden_rows, depth) + norm_eps)
        * gain_vector
    )


def contract_rows(left_side, right_side):
    return lax.dot_general(
        left_side, right_side, (((0,), (0,)), ((), ())), preferred_element_type=f32
    )


def contract_cols(left_side, right_side):
    return lax.dot_general(
        left_side, right_side, (((1,), (1,)), ((), ())), preferred_element_type=f32
    )


def matmul(left_side, right_side):
    return jnp.dot(left_side, right_side, preferred_element_type=f32)


def ring_order(size):
    return list(range(0, size, 2)) + list(range(size - 1, 0, -2))


def ring_pairs(size):
    order = ring_order(size)
    forward = [(order[spot], order[(spot + 1) % size]) for spot in range(size)]
    return forward, [(target, source) for source, target in forward]


def ring_owner(spot, size):
    late = (spot >= size // 2).astype(jnp.int32)
    return 2 * spot + late * (2 * size - 1 - 4 * spot)


def ring_spot(index, size):
    return index // 2 + lax.rem(index, 2) * (size - 1 - 2 * (index // 2))


def cut_of(width):
    return ((width // LANES + 1) // 2) * LANES


def assemble_kernel(size, cut, *refs):
    slabs, (left, right, out, sems) = refs[:-4], refs[-4:]
    spot = ring_spot(lax.axis_index("dp"), size)
    copies = []
    for number, slab in enumerate(slabs):
        shift = number if number < size // 2 else number + 1
        owner = ring_owner(lax.rem(spot + shift, size), size)
        copies.append(pltpu.make_async_copy(slab, out.at[:, owner], sems.at[number]))
    owner = ring_owner(lax.rem(spot + size // 2, size), size)
    width = out.shape[-1]
    copies.append(
        pltpu.make_async_copy(left, out.at[:, owner, :, pl.ds(0, cut)], sems.at[size - 1])
    )
    copies.append(
        pltpu.make_async_copy(right, out.at[:, owner, :, pl.ds(cut, width - cut)], sems.at[size])
    )
    for copy in copies:
        copy.start()
    for copy in copies:
        copy.wait()


def gather_dp(part):
    size = lax.axis_size("dp")
    if size > RING_LIMIT:
        return lax.all_gather(part, "dp", axis=1, tiled=True)
    forward, backward = ring_pairs(size)
    count, rows, width = part.shape
    cut = cut_of(width)
    slabs = [None] * size
    slabs[0] = ahead = behind = part
    for hop in range(1, size // 2):
        ahead = lax.ppermute(ahead, "dp", forward)
        behind = lax.ppermute(behind, "dp", backward)
        slabs[size - hop] = ahead
        slabs[hop] = behind
    left = lax.ppermute(ahead[..., :cut], "dp", forward)
    right = lax.ppermute(behind[..., cut:], "dp", backward)
    operands = [slab for slab in slabs if slab is not None] + [left, right]
    total = count * size * rows * width * part.dtype.itemsize
    whole = pl.pallas_call(
        partial(assemble_kernel, size, cut),
        out_shape=jax.ShapeDtypeStruct((count, size, rows, width), part.dtype),
        in_specs=[pl.BlockSpec(memory_space=pl.ANY)] * len(operands),
        out_specs=pl.BlockSpec(memory_space=pltpu.VMEM),
        scratch_shapes=[pltpu.SemaphoreType.DMA((size + 1,))],
        compiler_params=pltpu.CompilerParams(vmem_limit_bytes=VMEM_BYTES),
        cost_estimate=pl.CostEstimate(flops=0, bytes_accessed=2 * total, transcendentals=0),
        name="assemble",
    )(*operands)
    return whole.reshape(count, size * rows, width)


def scatter_dp(whole):
    size = lax.axis_size("dp")
    if size > RING_LIMIT:
        return lax.psum_scatter(whole.astype(f32), "dp", scatter_dimension=1, tiled=True)
    forward, backward = ring_pairs(size)
    count, depth, width = whole.shape
    rows = depth // size
    cut = cut_of(width)
    spot = ring_spot(lax.axis_index("dp"), size)

    def term(shift):
        owner = ring_owner(lax.rem(spot + size + shift, size), size)
        return lax.dynamic_slice_in_dim(whole, owner * rows, rows, axis=1)

    far = term(size // 2)
    ahead = lax.ppermute(far[..., :cut], "dp", forward)
    behind = lax.ppermute(far[..., cut:], "dp", backward)
    for hop in range(size // 2 - 1, 0, -1):
        mine = term(hop).astype(f32)
        other = term(-hop).astype(f32)
        if hop == size // 2 - 1:
            ahead = jnp.concatenate([mine[..., :cut] + ahead.astype(f32), mine[..., cut:]], -1)
            behind = jnp.concatenate([other[..., :cut], other[..., cut:] + behind.astype(f32)], -1)
        else:
            ahead = mine + ahead.astype(f32)
            behind = other + behind.astype(f32)
        ahead = lax.ppermute(ahead.astype(bf16), "dp", forward)
        behind = lax.ppermute(behind.astype(bf16), "dp", backward)
    return term(0).astype(f32) + ahead.astype(f32) + behind.astype(f32)


def swap(part, bit):
    size = lax.axis_size("mp")
    return lax.ppermute(part, "mp", [(index, index ^ bit) for index in range(size)])


def gather_mp(part):
    across = swap(part, 2)
    beside = swap(part, 1)
    return part, across, beside, swap(across, 1)


def offset_values(table, first_row, rows, span):
    offsets = lax.broadcasted_iota(jnp.int32, (8, span), 1) - (rows - 1) - first_row
    buckets = bucket_ids(offsets)
    values = jnp.zeros((8, span), f32)
    for number in range(table.shape[1]):
        values = jnp.where(buckets == number, table[:, number : number + 1], values)
    return values


def segments_at(positions, first_len, second_len):
    return (positions >= first_len).astype(jnp.int32) + (
        positions >= first_len + second_len
    ).astype(jnp.int32)


def allowed_pairs(lens_ref, first_row, rows, keys):
    query = segments_at(
        first_row + lax.broadcasted_iota(jnp.int32, (rows, 1), 0), lens_ref[0, 0], lens_ref[0, 1]
    )
    key = segments_at(
        lax.broadcasted_iota(jnp.int32, (1, keys), 1), lens_ref[0, 0], lens_ref[0, 1]
    )
    return query == key


def skewed_bias(values, head, rows, keys, span):
    wide = jnp.broadcast_to(values[head : head + 1, :], (rows, span))
    return pltpu.roll(wide, span - (rows - 1), 1, stride=1, stride_axis=0)[:, :keys]


def attend_pair(pair, query_ref, key_ref, value_ref, mixed_ref, logs, values, allowed, lane, span):
    rows, keys = query_ref.shape[0], key_ref.shape[0]
    part = slice(pair * LANES, (pair + 1) * LANES)
    query, key, value = query_ref[:, part], key_ref[:, part], value_ref[:, part]
    mixed = jnp.zeros((rows, LANES), f32)
    for half in range(2):
        head = 2 * pair + half
        mask = (lane // HEAD_DIM) == half
        scores = contract_cols(jnp.where(mask, query, jnp.zeros_like(query)), key)
        scores = jnp.where(
            allowed, scores + skewed_bias(values, head, rows, keys, span), masked_fill
        )
        top = jnp.max(scores, axis=-1, keepdims=True)
        powers = jnp.exp(scores - top)
        total = jnp.sum(powers, axis=-1, keepdims=True)
        soft = (powers * (1.0 / total)).astype(bf16)
        mixed = jnp.where(mask, matmul(soft, value), mixed)
        logs = jnp.where(lane == head, top + jnp.log(total), logs)
    mixed_ref[:, part] = mixed.astype(bf16)
    return logs


def forward_kernel(
    span,
    depth,
    lens_ref,
    own_ref,
    across_ref,
    beside_ref,
    corner_ref,
    heads_ref,
    table_ref,
    tokens_ref,
    gain_ref,
    mixed_ref,
    query_ref,
    key_ref,
    value_ref,
    log_ref,
    residual_ref,
    normed_ref,
):
    rows = own_ref.shape[0]
    keys = key_ref.shape[0]
    spot = lax.axis_index("mp")
    first_row = spot * rows
    for block_ref, bit in ((own_ref, 0), (across_ref, 2), (beside_ref, 1), (corner_ref, 3)):
        place = pl.ds(pl.multiple_of((spot ^ bit) * rows, rows), rows)
        block = block_ref[...]
        key_ref[place, :] = matmul(block, heads_ref[1]).astype(bf16)
        value_ref[place, :] = matmul(block, heads_ref[2]).astype(bf16)
    query_ref[...] = matmul(own_ref[...], heads_ref[0]).astype(bf16)
    values = offset_values(table_ref[...], first_row, rows, span)
    allowed = allowed_pairs(lens_ref, first_row, rows, keys)
    lane = lax.broadcasted_iota(jnp.int32, (1, LANES), 1)
    logs = jnp.zeros((rows, LANES), f32)
    for pair in range(PAIRS):
        logs = attend_pair(
            pair, query_ref, key_ref, value_ref, mixed_ref, logs, values, allowed, lane, span
        )
    log_ref[...] = logs
    residual = tokens_ref[...].astype(f32) + contract_cols(mixed_ref[...], heads_ref[3])
    residual_ref[...] = residual
    normed_ref[...] = rms_scale(residual, gain_ref[...], depth).astype(bf16)


def norm_backward(rows_in, gain, grad, depth):
    scale = lax.rsqrt(row_mean(rows_in * rows_in, depth) + norm_eps)
    unit = rows_in * scale
    inner = grad * gain
    out = scale * (inner - unit * row_mean(inner * unit, depth))
    return out, jnp.sum(grad * unit, axis=0, keepdims=True)


def attend_pair_backward(
    pair, query_ref, key_ref, value_ref, log_ref, mixed_grad, values, allowed, span
):
    rows, keys = query_ref.shape[0], key_ref.shape[0]
    lane = lax.broadcasted_iota(jnp.int32, (1, LANES), 1)
    flip = (
        lax.broadcasted_iota(jnp.int32, (rows, rows), 0)
        + lax.broadcasted_iota(jnp.int32, (rows, rows), 1)
        == rows - 1
    ).astype(bf16)
    part = slice(pair * LANES, (pair + 1) * LANES)
    query, key, value = query_ref[:, part], key_ref[:, part], value_ref[:, part]
    query_grad = jnp.zeros((rows, LANES), f32)
    key_grad = jnp.zeros((keys, LANES), f32)
    value_grad = jnp.zeros((keys, LANES), f32)
    offsets = []
    for half in range(2):
        head = 2 * pair + half
        mask = (lane // HEAD_DIM) == half
        query_own = jnp.where(mask, query, jnp.zeros_like(query))
        mixed_own = jnp.where(mask, mixed_grad, jnp.zeros_like(mixed_grad))
        scores = contract_cols(query_own, key)
        scores = jnp.where(
            allowed, scores + skewed_bias(values, head, rows, keys, span), masked_fill
        )
        soft = jnp.exp(scores - log_ref[:, head : head + 1])
        soft_grad = contract_cols(mixed_own, value)
        corr = jnp.sum(soft * soft_grad, axis=-1, keepdims=True)
        scores_grad = (soft * (soft_grad - corr)).astype(bf16)
        query_grad = jnp.where(mask, matmul(scores_grad, key), query_grad)
        key_grad = key_grad + contract_rows(scores_grad, query_own)
        value_grad = value_grad + contract_rows(soft.astype(bf16), mixed_own)
        flipped = matmul(flip, scores_grad)
        flipped = jnp.concatenate([flipped, jnp.zeros((rows, span - keys), f32)], axis=1)
        skewed = pltpu.roll(flipped, 0, 1, stride=1, stride_axis=0)
        offsets.append(jnp.sum(skewed, axis=0, keepdims=True))
    return query_grad, key_grad, value_grad, offsets


def backward_kernel(
    span,
    depth,
    lens_ref,
    part_ref,
    across_ref,
    residual_ref,
    upstream_ref,
    gain_ref,
    heads_ref,
    query_ref,
    key_ref,
    value_ref,
    log_ref,
    table_ref,
    residual_grad_ref,
    attended_ref,
    query_grad_ref,
    near_ref,
    far_ref,
    offset_ref,
    gain_grad_ref,
    whole_ref,
):
    rows = query_ref.shape[0]
    keys = key_ref.shape[0]
    spot = lax.axis_index("mp")
    first_row = spot * rows
    grad = part_ref[...].astype(f32) + across_ref[...].astype(f32)
    through, gain_grad = norm_backward(residual_ref[...], gain_ref[...], grad, depth)
    gain_grad_ref[...] = gain_grad
    residual_grad = upstream_ref[...].astype(f32) + through
    residual_grad_ref[...] = residual_grad
    attended = residual_grad.astype(bf16)
    attended_ref[...] = attended
    mixed_grad_all = matmul(attended, heads_ref[3]).astype(bf16)
    values = offset_values(table_ref[...], first_row, rows, span)
    allowed = allowed_pairs(lens_ref, first_row, rows, keys)
    for pair in range(PAIRS):
        part = slice(pair * LANES, (pair + 1) * LANES)
        query_grad, key_grad, value_grad, offsets = attend_pair_backward(
            pair, query_ref, key_ref, value_ref, log_ref, mixed_grad_all[:, part], values, allowed,
            span,
        )
        for half in range(2):
            offset_ref[2 * pair + half : 2 * pair + half + 1, :] = offsets[half]
        query_grad_ref[:, part] = query_grad.astype(bf16)
        whole_ref[:, part] = key_grad
        whole_ref[:, INNER + pair * LANES : INNER + (pair + 1) * LANES] = value_grad
    offset_ref[HEADS:, :] = jnp.zeros((8 - HEADS, span), f32)
    for number, bit in enumerate((0, 2)):
        place = pl.ds(pl.multiple_of((spot ^ bit) * rows, rows), rows)
        near_ref[number * rows : (number + 1) * rows, :] = whole_ref[place, :]
    for number, bit in enumerate((1, 3)):
        place = pl.ds(pl.multiple_of((spot ^ bit) * rows, rows), rows)
        far_ref[number * rows : (number + 1) * rows, :] = whole_ref[place, :].astype(bf16)


def input_kernel(
    depth,
    own_ref,
    beside_ref,
    across_ref,
    query_grad_ref,
    heads_ref,
    tokens_ref,
    gain_ref,
    residual_grad_ref,
    tokens_grad_ref,
    both_ref,
    gain_grad_ref,
):
    rows = query_grad_ref.shape[0]
    both = (
        own_ref[:rows, :]
        + beside_ref[:rows, :].astype(f32)
        + across_ref[...].astype(f32)
    ).astype(bf16)
    both_ref[...] = both
    grad = (
        contract_cols(query_grad_ref[...], heads_ref[0])
        + contract_cols(both[:, :INNER], heads_ref[1])
        + contract_cols(both[:, INNER:], heads_ref[2])
    )
    through, gain_grad = norm_backward(tokens_ref[...].astype(f32), gain_ref[...], grad, depth)
    gain_grad_ref[...] = gain_grad
    tokens_grad_ref[...] = residual_grad_ref[...] + through


def vmem_call(body, outs, cost, scratch=(), name=None, smem_first=False):
    def run(*operands):
        specs = [pl.BlockSpec(memory_space=pltpu.VMEM)] * len(operands)
        if smem_first:
            specs[0] = pl.BlockSpec(memory_space=pltpu.SMEM)
        return pl.pallas_call(
            body,
            out_shape=[jax.ShapeDtypeStruct(shape, kind) for shape, kind in outs],
            in_specs=specs,
            out_specs=[pl.BlockSpec(memory_space=pltpu.VMEM)] * len(outs),
            scratch_shapes=list(scratch),
            compiler_params=pltpu.CompilerParams(vmem_limit_bytes=VMEM_BYTES),
            cost_estimate=pl.CostEstimate(
                flops=cost[0], bytes_accessed=cost[1], transcendentals=cost[2]
            ),
            name=name,
        )(*operands)

    return run


def total_kernel(sizes, part_ref, out_ref, line_ref, plane_ref, line_send, line_recv, plane_send, plane_recv):
    plane, line = sizes
    dp_spot, mp_spot = lax.axis_index("dp"), lax.axis_index("mp")
    barrier = pltpu.get_barrier_semaphore()
    for step in range(1, line):
        pl.semaphore_signal(
            barrier, 1, device_id=(dp_spot, lax.rem(mp_spot + step, line)), device_id_type=MESH
        )
    for step in range(1, plane):
        pl.semaphore_signal(
            barrier, 1, device_id=(lax.rem(dp_spot + step, plane), mp_spot), device_id_type=MESH
        )
    pl.semaphore_wait(barrier, line + plane - 2)

    def exchange(source, slots, size, spot, send, recv, target):
        slots[spot] = source[...]
        copies = [
            pltpu.make_async_remote_copy(
                src_ref=source,
                dst_ref=slots.at[spot],
                send_sem=send.at[step],
                recv_sem=recv.at[step],
                device_id=target(lax.rem(spot + step, size)),
                device_id_type=MESH,
            )
            for step in range(1, size)
        ]
        for copy in copies:
            copy.start()
        for copy in copies:
            copy.wait()
        total = slots[0]
        for index in range(1, size):
            total = total + slots[index]
        out_ref[...] = total

    exchange(part_ref, line_ref, line, mp_spot, line_send, line_recv, lambda to: (dp_spot, to))
    exchange(out_ref, plane_ref, plane, dp_spot, plane_send, plane_recv, lambda to: (to, mp_spot))


def total_all(part, number):
    plane, line = lax.axis_size("dp"), lax.axis_size("mp")
    if plane > RING_LIMIT:
        return lax.psum(part, ("dp", "mp"))
    return pl.pallas_call(
        partial(total_kernel, (plane, line)),
        out_shape=jax.ShapeDtypeStruct(part.shape, part.dtype),
        in_specs=[pl.BlockSpec(memory_space=pltpu.VMEM)],
        out_specs=pl.BlockSpec(memory_space=pltpu.VMEM),
        scratch_shapes=[
            pltpu.VMEM((line,) + part.shape, f32),
            pltpu.VMEM((plane,) + part.shape, f32),
            pltpu.SemaphoreType.DMA((line,)),
            pltpu.SemaphoreType.DMA((line,)),
            pltpu.SemaphoreType.DMA((plane,)),
            pltpu.SemaphoreType.DMA((plane,)),
        ],
        compiler_params=pltpu.CompilerParams(collective_id=number, has_side_effects=True),
        name="total",
    )(part)


def small_gather_kernel(size, part_ref, out_ref, send, recv):
    dp_spot, mp_spot = lax.axis_index("dp"), lax.axis_index("mp")
    barrier = pltpu.get_barrier_semaphore()
    for step in range(1, size):
        pl.semaphore_signal(
            barrier, 1, device_id=(lax.rem(dp_spot + step, size), mp_spot), device_id_type=MESH
        )
    pl.semaphore_wait(barrier, size - 1)
    out_ref[dp_spot] = part_ref[...]
    copies = [
        pltpu.make_async_remote_copy(
            src_ref=part_ref,
            dst_ref=out_ref.at[dp_spot],
            send_sem=send.at[step],
            recv_sem=recv.at[step],
            device_id=(lax.rem(dp_spot + step, size), mp_spot),
            device_id_type=MESH,
        )
        for step in range(1, size)
    ]
    for copy in copies:
        copy.start()
    for copy in copies:
        copy.wait()


def gather_gains(gains):
    size = lax.axis_size("dp")
    if size > RING_LIMIT:
        return lax.all_gather(gains, "dp", axis=1, tiled=True)
    count, width = gains.shape
    wide = -(-width // LANES) * LANES
    part = jnp.pad(gains, ((0, 8 - count), (0, wide - width)))
    whole = pl.pallas_call(
        partial(small_gather_kernel, size),
        out_shape=jax.ShapeDtypeStruct((size,) + part.shape, part.dtype),
        in_specs=[pl.BlockSpec(memory_space=pltpu.VMEM)],
        out_specs=pl.BlockSpec(memory_space=pltpu.VMEM),
        scratch_shapes=[pltpu.SemaphoreType.DMA((size,)), pltpu.SemaphoreType.DMA((size,))],
        compiler_params=pltpu.CompilerParams(collective_id=3, has_side_effects=True),
        name="gather_gains",
    )(part)
    return jnp.concatenate([whole[index, :count, :width] for index in range(size)], axis=1)


def pack_rows(parts):
    flat = jnp.concatenate([part.reshape(-1) for part in parts])
    count = -(-flat.shape[0] // (8 * LANES)) * 8
    return jnp.pad(flat, (0, count * LANES - flat.shape[0])).reshape(count, LANES)


def lamb_parts(weight, gradient, first_moment, second, decay_rate):
    new_first = beta_first * first_moment + (1.0 - beta_first) * gradient
    new_second = beta_second * second + (1.0 - beta_second) * gradient * gradient
    first_fix = 1.0 - beta_first**STEP
    second_fix = 1.0 - beta_second**STEP
    step_dir = (
        new_first / first_fix / (jnp.sqrt(new_second / second_fix) + adam_eps) + decay_rate * weight
    )
    return (new_first, new_second, step_dir)


def sub_squares(values, sub_count):
    flat_values = values.reshape(sub_count, -1)
    return jnp.sum(flat_values * flat_values, axis=1)


def gelu_parts(gate):
    root = (2.0 / 3.141592653589793) ** 0.5
    square = gate * gate
    curve = jnp.tanh(root * (gate + 0.044715 * gate * square))
    value = 0.5 * gate * (1.0 + curve)
    slope = 0.5 * (1.0 + curve) + 0.5 * gate * (1.0 - curve * curve) * root * (
        1.0 + 3.0 * 0.044715 * square
    )
    return value, slope


def spread_pair(values, pair, shard, slot):
    depth = values.shape[1]
    first = 2 * pair * shard
    low = first // LANES * LANES
    high = min(depth, -(-(first + 2 * shard) // LANES) * LANES)
    shape = (high - low, 2 * slot)
    source = low + lax.broadcasted_iota(jnp.int32, shape, 0)
    place = lax.broadcasted_iota(jnp.int32, shape, 1)
    late = (place >= slot).astype(jnp.int32)
    offset = place - late * slot
    chosen = (source == first + late * shard + offset) & (offset < shard)
    return matmul(values[:, low:high], chosen.astype(bf16))


def gathered_tile(coarse, fine, low, high, shard, slot):
    def place_of(lane):
        return lane // shard * slot + lane % shard

    first = place_of(low) // LANES * LANES
    last = -(-(place_of(high - 1) + 1) // LANES) * LANES
    shape = (last - first, high - low)
    source = first + lax.broadcasted_iota(jnp.int32, shape, 0)
    lane = low + lax.broadcasted_iota(jnp.int32, shape, 1)
    chosen = jnp.zeros(shape, jnp.bool_)
    for number in range(low // shard, (high - 1) // shard + 1):
        inside = (lane >= number * shard) & (lane < (number + 1) * shard)
        chosen = chosen | (inside & (source == lane + number * (slot - shard)))
    chosen = chosen.astype(bf16)
    total = matmul(coarse[:, first:last], chosen)
    if fine is not None:
        total = total + matmul(fine[:, first:last], chosen)
    return total


def head_table(table_ref):
    table = table_ref[...]
    return jnp.concatenate([table, jnp.zeros((8 - HEADS, table.shape[1]), f32)], axis=0)


class Places:
    def __init__(self, size):
        self.size, self.half = size, size // 2
        self.dp, self.mp = lax.axis_index("dp"), lax.axis_index("mp")
        self.spot = ring_spot(self.dp, size)
        self.sides = (
            ring_owner(lax.rem(self.spot + 1, size), size),
            ring_owner(lax.rem(self.spot + size - 1, size), size),
        )

    def owner(self, shift):
        return ring_owner(lax.rem(self.spot + self.size + shift, self.size), self.size)

    def sent(self, side, hop):
        return self.owner(-hop if side == 0 else hop)

    def came(self, side, hop):
        return self.sent(side, hop + 1)


def remote(source, target, send, recv, dp, mp):
    return pltpu.make_async_remote_copy(
        src_ref=source,
        dst_ref=target,
        send_sem=send,
        recv_sem=recv,
        device_id=(dp, mp),
        device_id_type=MESH,
    )


class ForwardOut(NamedTuple):
    heads: object
    gate_up: object
    down: object
    normed: object
    upstream: object
    normed_two: object
    gelu: object
    slope: object
    hidden: object
    hidden_grad_out: object
    query: object
    key: object
    value: object
    mixed: object
    logs: object
    residual: object
    full_gains: object
    wide_tokens: object


class ForwardRefs(NamedTuple):
    lens: object
    tokens: object
    cotangent: object
    norm_gains: object
    table: object
    heads_in: object
    heads_out: object
    expand_in: object
    expand_out: object
    heads: object
    gate_up: object
    down: object
    normed: object
    upstream: object
    normed_two: object
    gelu: object
    slope: object
    hidden: object
    hidden_grad_out: object
    query: object
    key: object
    value: object
    mixed: object
    logs: object
    residual: object
    full_gains: object
    wide_tokens: object
    gains: object
    mine: object
    wide_in: object
    wide_out: object
    gain_slots: object
    gain_send: object
    gain_recv: object
    head_send: object
    head_recv: object
    wide_send: object
    wide_recv: object
    line_send: object
    line_recv: object
    slab_send: object
    slab_recv: object
    store_sems: object


def forward_shapes(rows, line, size, slot, width, span):
    wide, keys = size * slot, rows * line
    return ForwardOut(
        heads=((4, wide, INNER), bf16),
        gate_up=((2, wide, width), bf16),
        down=((wide, width), bf16),
        normed=((keys, wide), bf16),
        upstream=((keys, wide), bf16),
        normed_two=((keys, wide), bf16),
        gelu=((keys, width), f32),
        slope=((keys, width), f32),
        hidden=((keys, width), bf16),
        hidden_grad_out=((wide, width), bf16),
        query=((rows, INNER), bf16),
        key=((keys, INNER), bf16),
        value=((keys, INNER), bf16),
        mixed=((rows, INNER), bf16),
        logs=((rows, LANES), f32),
        residual=((rows, wide), f32),
        full_gains=((8, wide), f32),
        wide_tokens=((rows, wide), bf16),
    )


def ring_forward_kernel(size, depth, span, *refs):
    count = len(ForwardOut._fields)
    inputs = 9
    stores = refs[inputs : inputs + count]
    r = ForwardRefs(*refs[:inputs], *refs[inputs + count :])
    kept = refs[inputs + count : inputs + 2 * count]

    def store_copy(number):
        return pltpu.make_async_copy(kept[number], stores[number], r.store_sems.at[number])

    def store(*which):
        for number in range(count):
            if any(kept[number] is ref for ref in which):
                store_copy(number).start()

    at = Places(size)
    half = at.half
    rows = r.tokens.shape[0]
    wide = r.residual.shape[1]
    keys = r.key.shape[0]
    slot = wide // size
    shard = r.norm_gains.shape[1]
    width = r.down.shape[1]
    line = keys // rows
    cut, head_cut = cut_of(width), cut_of(INNER)
    first_row = at.mp * rows
    across, beside = at.mp ^ 2, at.mp ^ 1

    barrier = pltpu.get_barrier_semaphore()
    for step in range(1, size):
        pl.semaphore_signal(
            barrier, 1, device_id=(lax.rem(at.dp + step, size), at.mp), device_id_type=MESH
        )
    for partner in (across, beside):
        pl.semaphore_signal(barrier, 1, device_id=(at.dp, partner), device_id_type=MESH)

    def filled(values):
        spare = jnp.zeros((slot - shard, values.shape[1]), f32)
        return jnp.concatenate([values, spare], axis=0).astype(bf16)

    last = at.mp == line - 1
    mine = r.heads_in[jnp.minimum(at.mp, line - 2)]
    r.mine[...] = filled(jnp.where(last, r.heads_out[...], mine))
    r.wide_in[0] = filled(r.expand_in[0])
    rounded = r.norm_gains[...].astype(bf16).astype(f32)
    rounded = jnp.concatenate([rounded, jnp.zeros((2, 2 * slot - shard), f32)], axis=1)
    rounded = jnp.concatenate([rounded, jnp.zeros((6, 2 * slot), f32)], axis=0)
    r.gains[...] = jnp.where(lax.rem(at.dp, 2) == 1, pltpu.roll(rounded, slot, 1), rounded)
    pl.semaphore_wait(barrier, size + 1)

    def slab_rows(owner):
        return pl.ds(pl.multiple_of(owner * slot, slot), slot)

    def head_lanes(side, hop):
        if hop < half - 1:
            return pl.ds(0, INNER)
        return pl.ds(0, head_cut) if side == 0 else pl.ds(head_cut, INNER - head_cut)

    def head_hop(side, hop):
        lanes = head_lanes(side, hop)
        target = r.heads.at[at.mp, slab_rows(at.sent(side, hop)), lanes]
        source = r.mine.at[:, lanes] if hop == 0 else target
        return remote(
            source, target, r.head_send.at[side, hop], r.head_recv.at[side, hop],
            at.sides[side], at.mp,
        )

    def head_came(side, hop):
        target = r.heads.at[at.mp, slab_rows(at.came(side, hop)), head_lanes(side, hop)]
        return remote(
            target, target, r.head_send.at[side, hop], r.head_recv.at[side, hop],
            at.sides[side], at.mp,
        )

    def piece_view(piece, owner):
        lanes = pl.ds(0, cut) if piece % 2 == 0 else pl.ds(cut, width - cut)
        if piece < 4:
            return r.gate_up.at[piece // 2, slab_rows(owner), lanes]
        return r.down.at[slab_rows(owner), lanes]

    def piece_source(piece):
        lanes = pl.ds(0, cut) if piece % 2 == 0 else pl.ds(cut, width - cut)
        if piece < 4:
            return r.wide_in.at[piece // 2, :, lanes]
        return r.wide_out.at[:, lanes]

    def piece_goes(piece, side, hop):
        return hop < half - 1 or piece in ((0, 3, 4), (1, 2, 5))[side]

    def piece_hop(piece, side, hop):
        target = piece_view(piece, at.sent(side, hop))
        source = piece_source(piece) if hop == 0 else target
        return remote(
            source, target, r.wide_send.at[piece, side, hop], r.wide_recv.at[piece, side, hop],
            at.sides[side], at.mp,
        )

    def piece_came(piece, side, hop):
        target = piece_view(piece, at.came(side, hop))
        return remote(
            target, target, r.wide_send.at[piece, side, hop], r.wide_recv.at[piece, side, hop],
            at.sides[side], at.mp,
        )

    def serve(piece, hop):
        for side in range(2):
            if piece_goes(piece, side, hop):
                if hop > 0:
                    piece_came(piece, side, hop - 1).wait_recv()
                piece_hop(piece, side, hop).start()

    def finish(piece):
        for side in range(2):
            last = half - 1 if piece_goes(piece, side, half - 1) else half - 2
            piece_came(piece, side, last).wait_recv()

    def block(array, number):
        return array.at[pl.ds(number * rows, rows)]

    def line_copy(array, ref, number):
        source, target, partner = ((0, 1, across), (0, 2, beside), (1, 3, beside))[number]
        return remote(
            block(ref, source), block(ref, target), r.line_send.at[array, number],
            r.line_recv.at[array, number], at.dp, partner,
        )

    shifts = [0] + [shift for hop in range(1, half) for shift in (-hop, hop)] + [half]

    def slab_copy(number, way):
        matrix = across if way == 2 else at.mp
        view = r.heads.at[matrix, slab_rows(at.owner(shifts[number]))]
        source = r.mine if number == 0 and way < 2 else view
        return remote(
            source, view, r.slab_send.at[number, way], r.slab_recv.at[number, way],
            at.dp, across if way == 0 else beside,
        )

    def slab_came(number, way):
        matrix = (across, beside, at.mp ^ 3)[way]
        view = r.heads.at[matrix, slab_rows(at.owner(shifts[number]))]
        return remote(
            view, view, r.slab_send.at[number, way], r.slab_recv.at[number, way],
            at.dp, across if way == 0 else beside,
        )

    def gain_copy(step):
        return remote(
            r.gains, r.gain_slots.at[at.dp], r.gain_send.at[step], r.gain_recv.at[step],
            lax.rem(at.dp + step, size), at.mp,
        )

    for step in range(1, size):
        gain_copy(step).start()
    for side in range(2):
        head_hop(side, 0).start()
    for way in range(2):
        slab_copy(0, way).start()
    serve(0, 0)
    r.wide_in[1] = filled(r.expand_in[1])
    r.wide_out[...] = filled(r.expand_out[...])
    for pair in range(half):
        lanes = slice(2 * pair * slot, 2 * (pair + 1) * slot)
        r.wide_tokens[:, lanes] = spread_pair(r.tokens[...], pair, shard, slot).astype(bf16)
    r.gain_slots[at.dp] = r.gains[...]
    own = slab_rows(at.dp)
    r.heads[at.mp, own, :] = r.mine[...]
    r.gate_up[0, own, :] = r.wide_in[0]
    r.gate_up[1, own, :] = r.wide_in[1]
    r.down[own, :] = r.wide_out[...]
    for step in range(1, size):
        gain_copy(step).wait()
    r.full_gains[...] = jnp.concatenate(
        [r.gain_slots[2 * pair] + r.gain_slots[2 * pair + 1] for pair in range(half)], axis=1
    )
    block(r.normed, 0)[...] = rms_scale(
        r.wide_tokens[...].astype(f32), r.full_gains[0:1, :], depth
    ).astype(bf16)
    for number in range(2):
        line_copy(0, r.normed, number).start()
    positions = first_row + lax.broadcasted_iota(jnp.int32, (rows, 1), 0)
    used = positions < r.lens[0, 0] + r.lens[0, 1]
    upstream = jnp.where(used, r.cotangent[...].astype(f32), 0.0).astype(bf16)
    for pair in range(half):
        lanes = slice(2 * pair * slot, 2 * (pair + 1) * slot)
        r.upstream[:rows, lanes] = spread_pair(upstream, pair, shard, slot).astype(bf16)

    fillers = [[(1, 0)], [(2, 0)], [(3, 0), (0, 1)], [(1, 1)]]
    for hop in range(half):
        for side in range(2):
            head_came(side, hop).wait_recv()
            if hop + 1 < half:
                head_hop(side, hop + 1).start()
        for piece, piece_at in fillers[min(hop, 3)]:
            serve(piece, piece_at)
        done = (2 * hop + 1, 2 * hop + 2) if hop + 1 < half else (2 * hop + 1,)
        for number in done:
            for way in range(2):
                slab_copy(number, way).start()
    line_copy(0, r.normed, 0).wait_recv()
    line_copy(0, r.normed, 2).start()
    for number in range(2):
        line_copy(1, r.upstream, number).start()
    serve(2, 1)
    for number in range(size):
        slab_came(number, 0).wait_recv()
        slab_copy(number, 2).start()
    serve(3, 1)
    for number in range(size):
        slab_came(number, 1).wait_recv()
    for number in range(size):
        slab_came(number, 2).wait_recv()

    r.query[...] = matmul(block(r.normed, 0)[...], r.heads[0]).astype(bf16)
    for number, bit in ((0, 0), (2, 1), (1, 2), (3, 3)):
        if number == 2:
            line_copy(0, r.normed, 1).wait_recv()
        if number == 3:
            line_copy(0, r.normed, 2).wait_recv()
        place = pl.ds(pl.multiple_of((at.mp ^ bit) * rows, rows), rows)
        data = block(r.normed, number)[...]
        r.key[place, :] = matmul(data, r.heads[1]).astype(bf16)
        r.value[place, :] = matmul(data, r.heads[2]).astype(bf16)
    serve(0, 2)
    store(r.full_gains, r.wide_tokens, r.normed, r.query, r.key, r.value)

    values = offset_values(head_table(r.table), first_row, rows, span)
    allowed = allowed_pairs(r.lens, first_row, rows, keys)
    lane = lax.broadcasted_iota(jnp.int32, (1, LANES), 1)
    logs = jnp.zeros((rows, LANES), f32)
    for pair in range(PAIRS):
        logs = attend_pair(
            pair, r.query, r.key, r.value, r.mixed, logs, values, allowed, lane, span
        )
        serve(1 + pair, 2)
    r.logs[...] = logs
    residual = r.wide_tokens[...].astype(f32) + contract_cols(r.mixed[...], r.heads[3])
    r.residual[...] = residual
    block(r.normed_two, 0)[...] = rms_scale(residual, r.full_gains[1:2, :], depth).astype(bf16)
    store(r.heads, r.mixed, r.logs, r.residual)
    for number in range(2):
        line_copy(2, r.normed_two, number).start()
    for piece in range(4):
        serve(piece, 3)
    serve(4, 0)
    serve(5, 0)
    line_copy(2, r.normed_two, 0).wait_recv()
    line_copy(2, r.normed_two, 2).start()
    for piece in range(4):
        finish(piece)

    def expand(number):
        place = pl.ds(number * rows, rows)
        data = r.normed_two[place, :]
        gate = matmul(data, r.gate_up[0])
        up = matmul(data, r.gate_up[1])
        value, slope = gelu_parts(gate)
        r.gelu[place, :] = value
        r.slope[place, :] = slope * up
        r.hidden[place, :] = (value * up).astype(bf16)

    expand(0)
    serve(4, 1)
    line_copy(2, r.normed_two, 1).wait_recv()
    expand(2)
    serve(5, 1)
    expand(1)
    serve(4, 2)
    line_copy(2, r.normed_two, 2).wait_recv()
    expand(3)
    serve(5, 2)
    store(r.gelu, r.slope, r.hidden, r.gate_up, r.normed_two)
    line_copy(1, r.upstream, 0).wait_recv()
    line_copy(1, r.upstream, 2).start()
    line_copy(1, r.upstream, 1).wait_recv()
    line_copy(1, r.upstream, 2).wait_recv()
    store(r.upstream)
    tiles = 4
    tile = wide // tiles
    for number in range(tiles):
        lanes = slice(number * tile, (number + 1) * tile)
        r.hidden_grad_out[lanes, :] = contract_rows(
            r.upstream[:, lanes], r.hidden[...]
        ).astype(bf16)
        if number == 0:
            serve(4, 3)
            serve(5, 3)
    store(r.hidden_grad_out)
    for piece in (4, 5):
        finish(piece)
    store(r.down)

    for side in range(2):
        for hop in range(half):
            head_hop(side, hop).wait_send()
            for piece in range(6):
                if piece_goes(piece, side, hop):
                    piece_hop(piece, side, hop).wait_send()
    for number in range(size):
        for way in range(3):
            slab_copy(number, way).wait_send()
    for array, ref in enumerate((r.normed, r.upstream, r.normed_two)):
        for number in range(3):
            line_copy(array, ref, number).wait_send()
    for number in range(count):
        store_copy(number).wait()


def ring_forward(size, line, depth, slot, width, span, operands):
    rows = operands[1].shape[0]
    shapes = forward_shapes(rows, line, size, slot, width, span)
    wide, keys = size * slot, rows * line
    dma = pltpu.SemaphoreType.DMA
    half = size // 2
    specs = [pl.BlockSpec(memory_space=pltpu.VMEM)] * len(operands)
    specs[0] = pl.BlockSpec(memory_space=pltpu.SMEM)
    flops = 2 * keys * wide * (3 * width + 2 * INNER) + 4 * rows * wide * INNER
    results = pl.pallas_call(
        partial(ring_forward_kernel, size, depth, span),
        out_shape=[jax.ShapeDtypeStruct(*shape) for shape in shapes],
        in_specs=specs,
        out_specs=[pl.BlockSpec(memory_space=pl.ANY)] * len(shapes),
        scratch_shapes=[pltpu.VMEM(*shape) for shape in shapes]
        + [
            pltpu.VMEM((8, 2 * slot), f32),
            pltpu.VMEM((slot, INNER), bf16),
            pltpu.VMEM((2, slot, width), bf16),
            pltpu.VMEM((slot, width), bf16),
            pltpu.VMEM((size, 8, 2 * slot), f32),
            dma((size,)),
            dma((size,)),
            dma((2, half)),
            dma((2, half)),
            dma((6, 2, half)),
            dma((6, 2, half)),
            dma((3, 3)),
            dma((3, 3)),
            dma((size, 3)),
            dma((size, 3)),
            dma((len(shapes),)),
        ],
        compiler_params=pltpu.CompilerParams(
            collective_id=4, has_side_effects=True, vmem_limit_bytes=60 * 2**20
        ),
        cost_estimate=pl.CostEstimate(flops=flops, bytes_accessed=40 * 2**20, transcendentals=0),
        name="ring_forward",
    )(*operands)
    return ForwardOut(*results)


class BackwardOut(NamedTuple):
    layer_out: object
    tokens_grad: object
    heads_in_grad: object
    heads_out_grad: object
    gate_up_grad: object
    down_grad: object
    gains_grad: object
    table_grad: object
    norms: object


class BackwardLoads(NamedTuple):
    hidden_grad_out: object
    upstream: object
    down: object
    gelu: object
    slope: object
    gate_up: object
    normed_two: object
    hidden: object
    residual: object
    full_gains: object
    heads: object
    query: object
    key: object
    value: object
    logs: object
    mixed: object
    wide_tokens: object


class Moments(NamedTuple):
    heads_in: object
    heads_out: object
    expand_in: object
    expand_out: object
    norm_gains: object
    bias_table: object


class BackwardScratch(NamedTuple):
    load_sems: object
    residual_grad: object
    both_grads: object
    wide_came: object
    down_came: object
    far_send: object
    far_came: object
    across_send: object
    across_came: object
    pair_send: object
    pair_came: object
    pair_across_send: object
    pair_across_came: object
    offered: object
    right: object
    mine_grad: object
    mine_came: object
    mine_sums: object
    small: object
    small_line: object
    small_gains: object
    small_table: object
    norm_part: object
    norm_line: object
    norm_plane: object
    down_stage: object
    mine_stage: object
    out_stage: object
    gains_stage: object
    table_stage: object
    wide_sems: object
    line_sems: object
    attended_sems: object
    right_sems: object
    mine_sems: object
    sums_sems: object
    small_sems: object
    norm_sems: object
    stage_sems: object


def back_loads(values):
    return BackwardLoads(*[getattr(values, name) for name in BackwardLoads._fields])


def ring_backward_kernel(size, depth, span, *refs):
    lens_ref, table_ref = refs[:2]
    refs = refs[2:]
    loaded = len(BackwardLoads._fields)
    sources, normed_source, refs = refs[:loaded], refs[loaded], refs[loaded + 1 :]
    states = [Moments(*refs[6 * number : 6 * number + 6]) for number in range(3)]
    refs = refs[18:]
    outs = len(BackwardOut._fields)
    out, refs = BackwardOut(*refs[:outs]), refs[outs:]
    r, s = BackwardLoads(*refs[:loaded]), BackwardScratch(*refs[loaded:])

    def load_copy(number):
        return pltpu.make_async_copy(sources[number], r[number], s.load_sems.at[number])

    def arrive(*which):
        for number in range(loaded):
            if any(r[number] is ref for ref in which):
                load_copy(number).wait()

    for number in range(loaded):
        load_copy(number).start()
    at = Places(size)
    half = at.half
    rows = r.query.shape[0]
    keys = r.key.shape[0]
    wide = r.residual.shape[1]
    slot = wide // size
    shard = depth // size
    width = r.down.shape[1]
    line = keys // rows
    cut, head_cut = cut_of(width), cut_of(INNER)
    first_row = at.mp * rows
    across, beside, corner = at.mp ^ 2, at.mp ^ 1, at.mp ^ 3
    part_wide = wide // 2

    barrier = pltpu.get_barrier_semaphore()
    for step in range(1, size):
        pl.semaphore_signal(
            barrier, 1, device_id=(lax.rem(at.dp + step, size), at.mp), device_id_type=MESH
        )
    for partner in (across, beside, corner):
        pl.semaphore_signal(barrier, 1, device_id=(at.dp, partner), device_id_type=MESH)
    pl.semaphore_wait(barrier, size + 2)

    def stage_copy(number):
        kind, state = number // 3, states[number % 3]
        index = number % 3
        if kind == 0:
            source, target = state.expand_out, s.down_stage.at[index]
        elif kind == 1:
            source, target = state.heads_in.at[jnp.minimum(at.mp, line - 2)], s.mine_stage.at[index]
        elif kind == 2:
            source, target = state.heads_out, s.out_stage.at[index]
        elif kind == 3:
            source, target = state.expand_in.at[0], r.gelu.at[pl.ds(index * shard, shard)]
        elif kind == 4:
            source, target = state.expand_in.at[1], r.slope.at[pl.ds(index * shard, shard)]
        elif kind == 5:
            source, target = state.norm_gains, s.gains_stage.at[index]
        else:
            source, target = state.bias_table, s.table_stage.at[index]
        return pltpu.make_async_copy(source, target, s.stage_sems.at[number])

    def stage(kind):
        for index in range(3):
            stage_copy(3 * kind + index).start()

    def staged(kind):
        for index in range(3):
            stage_copy(3 * kind + index).wait()

    norm_lane = lax.broadcasted_iota(jnp.int32, (8, LANES), 1)

    def square_sum(values):
        return jnp.sum(jnp.sum(values * values, axis=0, keepdims=True), axis=1, keepdims=True)

    def add_norms(number, weight, gradient, first, second, decay, scale=1.0):
        step_dir = lamb_parts(weight, gradient, first, second, decay)[2]
        mass = square_sum(weight) * scale
        push = square_sum(step_dir) * scale
        s.norm_part[...] = s.norm_part[...] + (
            jnp.where(norm_lane == number, mass, 0.0) + jnp.where(norm_lane == number + 10, push, 0.0)
        )

    s.norm_part[...] = jnp.zeros((8, LANES), f32)
    for kind in (0, 1, 2, 5, 6):
        stage(kind)

    def slab_rows(owner):
        return pl.ds(pl.multiple_of(owner * slot, slot), slot)

    def block_rows(number):
        return pl.ds(number * rows, rows)

    def piece_lanes(piece):
        return pl.ds(0, cut) if piece % 2 == 0 else pl.ds(cut, width - cut)

    def piece_slice(piece):
        return slice(0, cut) if piece % 2 == 0 else slice(cut, width)

    def piece_term(piece, owner):
        if piece < 4:
            return r.gate_up.at[piece // 2, slab_rows(owner), piece_lanes(piece)]
        return r.hidden_grad_out.at[slab_rows(owner), piece_lanes(piece)]

    def piece_buffer(piece, side, hop):
        if piece < 4:
            return s.wide_came.at[side, hop, piece // 2, :, piece_lanes(piece)]
        return s.down_came.at[side, hop, :, piece_lanes(piece)]

    def piece_starts(piece, side):
        return piece in ((0, 3, 4), (1, 2, 5))[side]

    def piece_target(side, hop):
        return at.owner(half - hop if side == 0 else hop - half)

    def piece_has(piece, side, hop):
        return hop > 0 or piece_starts(piece, side)

    def piece_copy(piece, side, hop):
        fresh = hop == 0 or (hop == 1 and not piece_starts(piece, side))
        source = (
            piece_term(piece, piece_target(side, hop))
            if fresh
            else piece_buffer(piece, side, hop - 1)
        )
        return remote(
            source, piece_buffer(piece, side, hop), s.wide_sems.at[0, piece, side, hop],
            s.wide_sems.at[1, piece, side, hop], at.sides[side], at.mp,
        )

    def serve(piece, hop, sides=(0, 1)):
        for side in sides:
            if not piece_has(piece, side, hop):
                continue
            if hop > 0 and piece_has(piece, side, hop - 1):
                piece_copy(piece, side, hop - 1).wait_recv()
                came = piece_buffer(piece, side, hop - 1)
                term = piece_term(piece, piece_target(side, hop))
                came[...] = (came[...].astype(f32) + term[...].astype(f32)).astype(bf16)
            piece_copy(piece, side, hop).start()

    def finish(piece):
        for side in range(2):
            piece_copy(piece, side, half - 1).wait_recv()
        term = piece_term(piece, at.dp)
        return (
            term[...].astype(f32)
            + piece_buffer(piece, 0, half - 1)[...].astype(f32)
            + piece_buffer(piece, 1, half - 1)[...].astype(f32)
        )

    def mine_lanes(side, hop):
        if hop > 0:
            return pl.ds(0, INNER)
        return pl.ds(0, head_cut) if side == 0 else pl.ds(head_cut, INNER - head_cut)

    def mine_copy(side, hop):
        lanes = mine_lanes(side, hop)
        source = (
            s.mine_grad.at[slab_rows(piece_target(side, hop)), lanes]
            if hop == 0
            else s.mine_came.at[side, hop - 1, :, lanes]
        )
        return remote(
            source, s.mine_came.at[side, hop, :, lanes], s.mine_sems.at[0, side, hop],
            s.mine_sems.at[1, side, hop], at.sides[side], at.mp,
        )

    def mine_serve(hop):
        for side in range(2):
            if hop > 0:
                mine_copy(side, hop - 1).wait_recv()
                came = s.mine_came.at[side, hop - 1]
                term = s.mine_grad.at[slab_rows(piece_target(side, hop))]
                lanes = mine_lanes(side, hop - 1)
                if hop == 1:
                    keep = pl.ds(head_cut, INNER - head_cut) if side == 0 else pl.ds(0, head_cut)
                    came[:, keep] = term[:, keep]
                came[:, lanes] = (
                    came[:, lanes].astype(f32) + term[:, lanes].astype(f32)
                ).astype(bf16)
            mine_copy(side, hop).start()

    def far_copy(number):
        send = (s.far_send, s.across_send, s.far_send, s.across_send, s.pair_send, s.pair_across_send)
        came = (s.far_came, s.across_came, s.far_came, s.across_came)
        came = came + (s.pair_came, s.pair_across_came)
        return remote(
            send[number], came[number], s.line_sems.at[0, number], s.line_sems.at[1, number],
            at.dp, beside if number % 2 == 0 else across,
        )

    def attended_copy(number):
        source, target, partner = ((0, 1, across), (0, 2, beside), (1, 3, beside))[number]
        return remote(
            r.upstream.at[block_rows(source)], r.upstream.at[block_rows(target)],
            s.attended_sems.at[0, number], s.attended_sems.at[1, number], at.dp, partner,
        )

    def near_write(array, tile, values):
        array[tile * 2 * rows : (tile + 1) * 2 * rows, :part_wide] = values

    def near_read(array, number):
        return jnp.concatenate(
            [
                array[2 * rows * tile + number * rows : 2 * rows * tile + (number + 1) * rows, :part_wide]
                for tile in range(2)
            ],
            axis=1,
        )

    def part_of(tile):
        return slice(tile * part_wide, (tile + 1) * part_wide)

    arrive(r.hidden_grad_out)
    for piece in (4, 5):
        serve(piece, 0)
    serve(4, 1, (1,))
    serve(5, 1, (0,))
    arrive(r.upstream, r.down, r.gelu, r.slope)
    for number in (2, 3, 0, 1):
        place = block_rows(number)
        hidden_grad = matmul(r.upstream[place, :], r.down[...])
        s.both_grads[0, place, :] = (hidden_grad * r.slope[place, :]).astype(bf16)
        s.both_grads[1, place, :] = (hidden_grad * r.gelu[place, :]).astype(bf16)
        if number == 3:
            serve(4, 1, (0,))
            serve(5, 1, (1,))
    arrive(r.gate_up)

    def normed_tile(first, tile):
        place = pl.ds(first, 2 * rows)
        return contract_cols(
            s.both_grads[0, place, :], r.gate_up[0, part_of(tile), :]
        ) + contract_cols(s.both_grads[1, place, :], r.gate_up[1, part_of(tile), :])

    for tile in range(2):
        s.far_send[:, part_of(tile)] = normed_tile(2 * rows, tile).astype(bf16)
    far_copy(0).start()
    serve(4, 2)
    for tile in range(2):
        near_write(r.slope, tile, normed_tile(0, tile))
    serve(5, 2)
    far_copy(0).wait()
    s.across_send[...] = (near_read(r.slope, 1) + s.far_came[rows:, :].astype(f32)).astype(bf16)
    far_copy(1).start()

    arrive(r.normed_two)
    tiles = 4
    tile_wide = wide // tiles
    for matrix in range(2):
        for tile in range(tiles):
            lanes = slice(tile * tile_wide, (tile + 1) * tile_wide)
            r.gate_up[matrix, lanes, :] = contract_rows(
                r.normed_two[:, lanes], s.both_grads[matrix]
            ).astype(bf16)
        if matrix == 1:
            serve(5, 3)
        serve(2 * matrix, 0)
        serve(2 * matrix + 1, 0)
        serve(2 * matrix, 1, (1 - matrix,))
        serve(2 * matrix + 1, 1, (matrix,))
        if matrix == 0:
            serve(4, 3)

    normed_load = pltpu.make_async_copy(
        normed_source, r.normed_two, s.load_sems.at[loaded]
    )
    normed_load.start()
    arrive(r.residual, r.full_gains, r.heads, r.query, r.key, r.value, r.logs, r.mixed)

    far_copy(1).wait()
    grad = (
        near_read(r.slope, 0) + s.far_came[:rows, :].astype(f32) + s.across_came[...].astype(f32)
    )
    through, gain_two_grad = norm_backward(r.residual[...], r.full_gains[1:2, :], grad, depth)
    residual_grad = r.upstream[:rows, :].astype(f32) + through
    s.residual_grad[...] = residual_grad
    attended = residual_grad.astype(bf16)
    r.upstream[:rows, :] = attended
    for number in range(2):
        attended_copy(number).start()
    mixed_grad_all = matmul(attended, r.heads[3]).astype(bf16)

    values = offset_values(head_table(table_ref), first_row, rows, span)
    allowed = allowed_pairs(lens_ref, first_row, rows, keys)
    offsets = []
    for pair in range(PAIRS):
        part = slice(pair * LANES, (pair + 1) * LANES)
        query_grad, key_grad, value_grad, pair_offsets = attend_pair_backward(
            pair, r.query, r.key, r.value, r.logs, mixed_grad_all[:, part], values, allowed, span,
        )
        s.offered[0, :, part] = query_grad.astype(bf16)
        r.slope[:, part] = key_grad
        r.slope[:, INNER + pair * LANES : INNER + (pair + 1) * LANES] = value_grad
        offsets = offsets + pair_offsets
        if pair == 0:
            serve(0, 1, (0,))
            serve(1, 1, (1,))
        if pair == 1:
            serve(2, 1, (1,))
            serve(3, 1, (0,))
    pair_wide = 2 * INNER
    for number, bit in ((0, 1), (1, 3)):
        place = pl.ds(pl.multiple_of((at.mp ^ bit) * rows, rows), rows)
        s.pair_send[number * rows : (number + 1) * rows, :] = r.slope[place, :pair_wide].astype(bf16)
    far_copy(4).start()
    s.offered[3] = r.mixed[...]
    far_copy(4).wait_recv()
    place = pl.ds(pl.multiple_of(across * rows, rows), rows)
    s.pair_across_send[...] = (
        r.slope[place, :pair_wide] + s.pair_came[rows:, :].astype(f32)
    ).astype(bf16)
    far_copy(5).start()
    attended_copy(0).wait_recv()
    attended_copy(2).start()

    arrive(r.hidden)

    def feed_tile(first, tile):
        return contract_cols(r.hidden[pl.ds(first, 2 * rows), :], r.down[part_of(tile), :])

    for tile in range(2):
        s.far_send[:, part_of(tile)] = feed_tile(2 * rows, tile).astype(bf16)
    far_copy(2).start()
    for tile in range(2):
        near_write(r.gelu, tile, feed_tile(0, tile))
    serve(0, 2)
    serve(1, 2)
    far_copy(5).wait_recv()
    place = pl.ds(pl.multiple_of(at.mp * rows, rows), rows)
    both = (
        r.slope[place, :pair_wide]
        + s.pair_came[:rows, :].astype(f32)
        + s.pair_across_came[...].astype(f32)
    ).astype(bf16)
    s.offered[1] = both[:, :INNER]
    s.offered[2] = both[:, INNER:]
    stage(4)

    def right_copy(number):
        partner = (across, beside, corner)[number - 1]
        return remote(
            s.offered.at[partner], s.right.at[block_rows(number)],
            s.right_sems.at[0, number], s.right_sems.at[1, number], at.dp, partner,
        )

    for number in range(1, line):
        right_copy(number).start()
    s.right[block_rows(0), :] = s.offered[at.mp]
    grad = (
        contract_cols(s.offered[0], r.heads[0])
        + contract_cols(s.offered[1], r.heads[1])
        + contract_cols(s.offered[2], r.heads[2])
    )
    arrive(r.wide_tokens)
    through, gain_one_grad = norm_backward(
        r.wide_tokens[...].astype(f32), r.full_gains[0:1, :], grad, depth
    )
    s.residual_grad[...] = s.residual_grad[...] + through

    offset_grad = jnp.concatenate(offsets + [jnp.zeros((8 - HEADS, span), f32)], axis=0)
    reach = lax.broadcasted_iota(jnp.int32, (8, span), 1) - (rows - 1) - first_row
    reach = bucket_ids(reach)
    table_grad = jnp.zeros((8, LANES), f32)
    buckets = table_ref.shape[1]
    for number in range(buckets):
        mass = jnp.sum(jnp.where(reach == number, offset_grad, 0.0), axis=1, keepdims=True)
        table_grad = jnp.where(norm_lane == number, mass, table_grad)
    s.small[0, :, wide:] = table_grad
    s.small[0, 0:1, :wide] = gain_one_grad
    s.small[0, 1:2, :wide] = gain_two_grad
    s.small[0, 2:, :wide] = jnp.zeros((6, wide), f32)

    def line_spread(source, slots, sems, first):
        copies = [
            remote(
                source, slots.at[at.mp], sems.at[first, step], sems.at[first + 1, step],
                at.dp, lax.rem(at.mp + step, line),
            )
            for step in range(1, line)
        ]
        for copy in copies:
            copy.start()
        slots[at.mp] = source[...]
        return copies

    def slot_total(slots, count):
        total = slots[0]
        for number in range(1, count):
            total = total + slots[number]
        return total

    small_copies = line_spread(s.small.at[0], s.small_line, s.small_sems, 0)
    serve(2, 2)
    far_copy(2).wait_recv()
    s.across_send[...] = (
        near_read(r.gelu, 1) + s.far_came[rows:, :].astype(f32)
    ).astype(bf16)
    far_copy(3).start()
    serve(3, 2)

    normed_load.wait()
    for number in range(1, 3):
        attended_copy(number).wait_recv()
    for number in range(1, line):
        right_copy(number).wait_recv()
    last = at.mp == line - 1
    for tile in range(tiles):
        lanes = slice(tile * tile_wide, (tile + 1) * tile_wide)
        left = jnp.where(last, r.upstream[:, lanes], r.normed_two[:, lanes])
        s.mine_grad[lanes, :] = contract_rows(left, s.right[...]).astype(bf16)
    mine_serve(0)

    for copy in small_copies:
        copy.wait()
    s.small[1] = slot_total(s.small_line, line)
    pair_slot = 2 * slot
    plane_copies = []
    for step in range(1, size):
        target = lax.rem(at.dp + step, size)
        lanes = pl.ds(pl.multiple_of(target // 2 * pair_slot, pair_slot), pair_slot)
        plane_copies.append(
            remote(
                s.small.at[1, :, lanes], s.small_gains.at[at.dp], s.small_sems.at[2, step],
                s.small_sems.at[3, step], target, at.mp,
            )
        )
        plane_copies.append(
            remote(
                s.small.at[1, :, pl.ds(wide, LANES)], s.small_table.at[at.dp],
                s.small_sems.at[4, step], s.small_sems.at[5, step], target, at.mp,
            )
        )
    for copy in plane_copies:
        copy.start()
    lanes = pl.ds(pl.multiple_of(at.dp // 2 * pair_slot, pair_slot), pair_slot)
    s.small_gains[at.dp] = s.small[1, :, lanes]
    s.small_table[at.dp] = s.small[1, :, wide:]

    serve(0, 3)
    mine_serve(1)
    serve(1, 3)
    down_total = jnp.concatenate([finish(4), finish(5)], axis=1)
    down_total = down_total[:shard]
    out.down_grad[...] = down_total
    staged(0)
    add_norms(
        6, s.down_stage[0], down_total, s.down_stage[1], s.down_stage[2], weight_decay
    )
    mine_serve(2)
    serve(2, 3)
    for copy in plane_copies:
        copy.wait()
    gains_total = slot_total(s.small_gains, size)
    odd = lax.rem(at.dp, 2) == 1
    gains_total = jnp.where(odd, pltpu.roll(gains_total, slot, 1), gains_total)[:2, :shard]
    out.gains_grad[...] = gains_total
    staged(5)
    for number in range(2):
        row = slice(number, number + 1)
        add_norms(
            7 + number, s.gains_stage[0, row], gains_total[row], s.gains_stage[1, row],
            s.gains_stage[2, row], 0.0, 1.0 / line,
        )
    table_total = slot_total(s.small_table, size)[:HEADS, :buckets]
    out.table_grad[...] = table_total
    staged(6)
    add_norms(
        9, s.table_stage[0], table_total, s.table_stage[1], s.table_stage[2], 0.0,
        1.0 / (line * size),
    )
    far_copy(3).wait_recv()
    layer_out = (
        r.residual[...]
        + (
            near_read(r.gelu, 0)
            + s.far_came[:rows, :].astype(f32)
            + s.across_came[...].astype(f32)
        )
    ).astype(bf16)
    stage(3)
    mine_serve(3)
    serve(3, 3)
    coarse = s.residual_grad[...].astype(bf16)
    fine = (s.residual_grad[...] - coarse.astype(f32)).astype(bf16)
    tile = 3 * LANES
    for low in range(0, depth, tile):
        high = min(low + tile, depth)
        out.layer_out[:, low:high] = gathered_tile(
            layer_out, None, low, high, shard, slot
        ).astype(bf16)
        out.tokens_grad[:, low:high] = gathered_tile(coarse, fine, low, high, shard, slot)

    for side in range(2):
        mine_copy(side, half - 1).wait_recv()
    mine_total = (
        s.mine_grad[slab_rows(at.dp), :].astype(f32)
        + s.mine_came[0, half - 1].astype(f32)
        + s.mine_came[1, half - 1].astype(f32)
    ).astype(bf16)
    s.mine_sums[at.mp] = mine_total

    def sums_copy(number):
        partner = (across, beside, corner)[number - 1]
        return remote(
            s.mine_sums.at[at.mp], s.mine_sums.at[at.mp],
            s.sums_sems.at[0, number], s.sums_sems.at[1, number], at.dp, partner,
        )

    for number in range(1, line):
        sums_copy(number).start()
    staged(1)
    staged(2)

    def mine_state(index):
        return jnp.where(last, s.out_stage[index], s.mine_stage[index])

    add_norms(
        at.mp, mine_state(0), mine_total.astype(f32)[:shard], mine_state(1), mine_state(2),
        weight_decay,
    )

    def grad_copy(matrix):
        held = (r.gelu, r.slope)[matrix]
        return pltpu.make_async_copy(
            held.at[pl.ds(3 * shard, shard)], out.gate_up_grad.at[matrix], s.stage_sems.at[21 + matrix]
        )

    staged(3)
    staged(4)
    for piece in range(4):
        total = finish(piece)[:shard]
        lanes = piece_slice(piece)
        held = (r.gelu, r.slope)[piece // 2]
        held[3 * shard : 4 * shard, lanes] = total
        if piece % 2 == 1:
            grad_copy(piece // 2).start()
        add_norms(
            4 + piece // 2, held[:shard, lanes], total, held[shard : 2 * shard, lanes],
            held[2 * shard : 3 * shard, lanes], weight_decay,
        )

    norm_copies = line_spread(s.norm_part, s.norm_line, s.norm_sems, 0)
    for copy in norm_copies:
        copy.wait()
    s.norm_part[...] = slot_total(s.norm_line, line)
    norm_copies = [
        remote(
            s.norm_part, s.norm_plane.at[at.dp], s.norm_sems.at[2, step], s.norm_sems.at[3, step],
            lax.rem(at.dp + step, size), at.mp,
        )
        for step in range(1, size)
    ]
    for copy in norm_copies:
        copy.start()
    s.norm_plane[at.dp] = s.norm_part[...]

    for side in range(2):
        for hop in range(half):
            mine_copy(side, hop).wait_send()
            for piece in range(6):
                if piece_has(piece, side, hop):
                    piece_copy(piece, side, hop).wait_send()
    for number in range(2, 6):
        far_copy(number).wait_send()
    for number in range(3):
        attended_copy(number).wait_send()
    for number in range(1, line):
        right_copy(number).wait_send()
    for number in range(1, line):
        sums_copy(number).wait()
    for number in range(line - 1):
        out.heads_in_grad[number] = s.mine_sums[number].astype(f32)[:shard]
    out.heads_out_grad[...] = s.mine_sums[line - 1].astype(f32)[:shard]
    for copy in norm_copies:
        copy.wait()
    out.norms[...] = slot_total(s.norm_plane, size)
    for matrix in range(2):
        grad_copy(matrix).wait()


def ring_backward(size, line, depth, slot, width, span, lens, table, got, states):
    rows = got.query.shape[0]
    wide, keys, half = size * slot, rows * line, size // 2
    shard, buckets = depth // size, table.shape[1]
    shapes = forward_shapes(rows, line, size, slot, width, span)
    dma = pltpu.SemaphoreType.DMA
    far = list(back_loads(got)) + [got.normed] + [array for state in states for array in state]
    operands = [lens, table] + far
    specs = [
        pl.BlockSpec(memory_space=pltpu.SMEM),
        pl.BlockSpec(memory_space=pltpu.VMEM),
    ] + [pl.BlockSpec(memory_space=pl.ANY)] * len(far)
    outs = BackwardOut(
        layer_out=((rows, depth), bf16),
        tokens_grad=((rows, depth), f32),
        heads_in_grad=((line - 1, shard, INNER), f32),
        heads_out_grad=((shard, INNER), f32),
        gate_up_grad=((2, shard, width), f32),
        down_grad=((shard, width), f32),
        gains_grad=((2, shard), f32),
        table_grad=((HEADS, buckets), f32),
        norms=((8, LANES), f32),
    )
    half_rows = pltpu.VMEM((2 * rows, wide), bf16)
    block = pltpu.VMEM((rows, wide), bf16)
    loads = back_loads(shapes)
    scratch = BackwardScratch(
        load_sems=dma((len(loads) + 1,)),
        residual_grad=pltpu.VMEM((rows, wide), f32),
        both_grads=pltpu.VMEM((2, keys, width), bf16),
        wide_came=pltpu.VMEM((2, half, 2, slot, width), bf16),
        down_came=pltpu.VMEM((2, half, slot, width), bf16),
        far_send=half_rows,
        far_came=half_rows,
        across_send=block,
        across_came=block,
        pair_send=pltpu.VMEM((2 * rows, 2 * INNER), bf16),
        pair_came=pltpu.VMEM((2 * rows, 2 * INNER), bf16),
        pair_across_send=pltpu.VMEM((rows, 2 * INNER), bf16),
        pair_across_came=pltpu.VMEM((rows, 2 * INNER), bf16),
        offered=pltpu.VMEM((line, rows, INNER), bf16),
        right=pltpu.VMEM((keys, INNER), bf16),
        mine_grad=pltpu.VMEM((wide, INNER), bf16),
        mine_came=pltpu.VMEM((2, half, slot, INNER), bf16),
        mine_sums=pltpu.VMEM((line, slot, INNER), bf16),
        small=pltpu.VMEM((2, 8, wide + LANES), f32),
        small_line=pltpu.VMEM((line, 8, wide + LANES), f32),
        small_gains=pltpu.VMEM((size, 8, 2 * slot), f32),
        small_table=pltpu.VMEM((size, 8, LANES), f32),
        norm_part=pltpu.VMEM((8, LANES), f32),
        norm_line=pltpu.VMEM((line, 8, LANES), f32),
        norm_plane=pltpu.VMEM((size, 8, LANES), f32),
        down_stage=pltpu.VMEM((3, shard, width), f32),
        mine_stage=pltpu.VMEM((3, shard, INNER), f32),
        out_stage=pltpu.VMEM((3, shard, INNER), f32),
        gains_stage=pltpu.VMEM((3, 2, shard), f32),
        table_stage=pltpu.VMEM((3, HEADS, buckets), f32),
        wide_sems=dma((2, 6, 2, half)),
        line_sems=dma((2, 6)),
        attended_sems=dma((2, 3)),
        right_sems=dma((2, line)),
        mine_sems=dma((2, 2, half)),
        sums_sems=dma((2, line)),
        small_sems=dma((6, size)),
        norm_sems=dma((4, size)),
        stage_sems=dma((23,)),
    )
    flops = 2 * keys * wide * (6 * width + INNER) + 16 * rows * wide * INNER
    results = pl.pallas_call(
        partial(ring_backward_kernel, size, depth, span),
        out_shape=[jax.ShapeDtypeStruct(*shape) for shape in outs],
        in_specs=specs,
        out_specs=[
            pl.BlockSpec(memory_space=pl.ANY if shape is outs.gate_up_grad else pltpu.VMEM)
            for shape in outs
        ],
        scratch_shapes=[pltpu.VMEM(*shape) for shape in loads] + list(scratch),
        compiler_params=pltpu.CompilerParams(
            collective_id=5, has_side_effects=True, vmem_limit_bytes=BACKWARD_BYTES
        ),
        cost_estimate=pl.CostEstimate(flops=flops, bytes_accessed=50 * 2**20, transcendentals=0),
        name="ring_backward",
    )(*operands)
    return BackwardOut(*results)


def plain_gradients(
    tokens,
    cotangent,
    lengths,
    heads_in,
    heads_out,
    expand_in,
    expand_out,
    norm_gains,
    bias_table,
):
    rows, depth = tokens.shape
    mp_size = lax.axis_size("mp")
    mp_spot = lax.axis_index("mp")
    keys = rows * mp_size
    span = -(-(keys + rows - 1) // LANES) * LANES
    first_row = mp_spot * rows
    shard_width = norm_gains.shape[1]
    buckets = bias_table.shape[0]

    four = jnp.concatenate([heads_in, heads_out.T[None]], axis=0).astype(bf16)
    mine = lax.dynamic_slice_in_dim(four, mp_spot, 1, axis=0)
    mine_all = gather_dp(mine)
    full_gains = gather_gains(norm_gains.astype(bf16).astype(f32))
    gain_one, gain_two = full_gains[0:1], full_gains[1:2]
    inputs = tokens.astype(f32)
    normed = rms_scale(inputs, gain_one, depth).astype(bf16)
    normed_parts = gather_mp(normed)
    used = first_row + jnp.arange(rows, dtype=jnp.int32) < lengths[0, 0] + lengths[0, 1]
    upstream = jnp.where(used[:, None], cotangent, jnp.zeros_like(cotangent))
    upstream_parts = gather_mp(upstream)

    mine_parts = gather_mp(mine_all)
    by_bit = jnp.concatenate([mine_parts[0], mine_parts[2], mine_parts[1], mine_parts[3]], axis=0)
    full_heads = jnp.concatenate(
        [lax.dynamic_slice_in_dim(by_bit, mp_spot ^ number, 1, axis=0) for number in range(mp_size)],
        axis=0,
    )
    wide_in = gather_dp(expand_in.astype(bf16))
    wide_out = gather_dp(expand_out.T.astype(bf16)[None])[0]

    table = jnp.pad(bias_table.T, ((0, 8 - HEADS), (0, 0)))
    attention_flops = rows * keys * LANES * HEADS
    mixed, query, key, value, logs, residual, normed_two = vmem_call(
        partial(forward_kernel, span, depth),
        [
            ((rows, INNER), bf16),
            ((rows, INNER), bf16),
            ((keys, INNER), bf16),
            ((keys, INNER), bf16),
            ((rows, LANES), f32),
            ((rows, depth), f32),
            ((rows, depth), bf16),
        ],
        (
            2 * depth * INNER * (2 * keys + 2 * rows) + 4 * attention_flops,
            2 * (4 * depth * INNER + 2 * keys * depth),
            rows * keys * HEADS,
        ),
        name="attention_forward",
        smem_first=True,
    )(lengths, *normed_parts, full_heads, table, tokens, gain_two)

    normed_all = jnp.concatenate(gather_mp(normed_two), axis=0)
    upstream_all = jnp.concatenate(upstream_parts, axis=0)
    gate_pre = matmul(normed_all, wide_in[0])
    up_pre = matmul(normed_all, wide_in[1])
    gelu_gate, gelu_pull = jax.vjp(partial(jax.nn.gelu, approximate=True), gate_pre)
    hidden = (gelu_gate * up_pre).astype(bf16)
    expand_out_grad = scatter_dp(contract_rows(upstream_all, hidden).astype(bf16)[None])[0].T
    feed_part = contract_cols(hidden, wide_out).astype(bf16)
    feed_near = feed_part[: 2 * rows].astype(f32) + swap(feed_part[2 * rows :], 1).astype(f32)
    feed_out = feed_near[:rows] + swap(feed_near[rows:].astype(bf16), 2).astype(f32)
    layer_out = (residual + feed_out).astype(bf16)

    hidden_grad = matmul(upstream_all, wide_out)
    up_grad = (hidden_grad * gelu_gate).astype(bf16)
    gate_grad = gelu_pull(hidden_grad * up_pre)[0].astype(bf16)
    normed_part = contract_cols(gate_grad, wide_in[0]) + contract_cols(up_grad, wide_in[1])
    normed_near = normed_part[: 2 * rows] + swap(normed_part[2 * rows :].astype(bf16), 1).astype(f32)
    normed_across = swap(normed_near[rows:].astype(bf16), 2)
    expand_in_grad = scatter_dp(
        jnp.stack(
            [
                contract_rows(normed_all, gate_grad).astype(bf16),
                contract_rows(normed_all, up_grad).astype(bf16),
            ]
        )
    )

    residual_grad, attended_grad, query_grad, near, far, offset_grad, gain_two_grad = vmem_call(
        partial(backward_kernel, span, depth),
        [
            ((rows, depth), f32),
            ((rows, depth), bf16),
            ((rows, INNER), bf16),
            ((2 * rows, 2 * INNER), f32),
            ((2 * rows, 2 * INNER), bf16),
            ((8, span), f32),
            ((1, depth), f32),
        ],
        (
            2 * depth * INNER * rows + 10 * attention_flops,
            rows * depth * 16 + 2 * (4 * depth * INNER + 2 * keys * INNER),
            rows * keys * HEADS,
        ),
        scratch=[pltpu.VMEM((keys, 2 * INNER), f32)],
        name="attention_backward",
        smem_first=True,
    )(
        lengths,
        normed_near[:rows],
        normed_across,
        residual,
        upstream,
        gain_two,
        full_heads,
        query,
        key,
        value,
        logs,
        table,
    )
    attended_parts = gather_mp(attended_grad)
    beside = swap(far, 1)
    across = swap((near[rows:] + beside[rows:].astype(f32)).astype(bf16), 2)
    tokens_grad, both, gain_one_grad = vmem_call(
        partial(input_kernel, depth),
        [((rows, depth), f32), ((rows, 2 * INNER), bf16), ((1, depth), f32)],
        (6 * rows * depth * INNER, rows * depth * 14 + 8 * depth * INNER, 0),
        name="input_backward",
    )(near, beside, across, query_grad, full_heads, tokens, gain_one, residual_grad)

    offered = jnp.stack([query_grad, both[:, :INNER], both[:, INNER:], mixed])

    def for_bit(bit):
        return lax.dynamic_slice_in_dim(offered, mp_spot ^ bit, 1, axis=0)

    from_beside = swap(jnp.concatenate([for_bit(1), for_bit(3)], axis=0), 1)
    from_across = swap(jnp.concatenate([for_bit(2), from_beside[1:]], axis=0), 2)
    right = jnp.concatenate(
        [for_bit(0)[0], from_across[0], from_beside[0], from_across[1]], axis=0
    )
    left = jnp.where(
        mp_spot == mp_size - 1,
        jnp.concatenate(attended_parts, axis=0),
        jnp.concatenate(normed_parts, axis=0),
    )
    mine_grad = scatter_dp(contract_rows(left, right).astype(bf16)[None]).astype(bf16)
    grad_parts = gather_mp(mine_grad)
    grads_by_bit = jnp.concatenate(
        [grad_parts[0], grad_parts[2], grad_parts[1], grad_parts[3]], axis=0
    )
    heads_grad = [
        lax.dynamic_slice_in_dim(grads_by_bit, mp_spot ^ number, 1, axis=0)
        for number in range(mp_size)
    ]
    head_in_grad = jnp.concatenate(heads_grad[:3], axis=0).astype(f32)
    head_out_grad = heads_grad[3][0].T.astype(f32)

    reach = jnp.arange(span, dtype=jnp.int32) - (rows - 1) - first_row
    onehot = (bucket_ids(reach)[:, None] == jnp.arange(buckets, dtype=jnp.int32)[None, :]).astype(f32)
    table_part = jnp.dot(offset_grad, onehot, precision=highest)[:HEADS].T
    gain_parts = jnp.concatenate([gain_one_grad, gain_two_grad], axis=0)
    small = total_all(pack_rows([gain_parts, table_part]), 1).reshape(-1)
    gains_total = small[: 2 * depth].reshape(2, depth)
    table_grad = small[2 * depth : 2 * depth + buckets * HEADS].reshape(buckets, HEADS)
    gains_grad = lax.dynamic_slice_in_dim(
        gains_total, lax.axis_index("dp") * shard_width, shard_width, 1
    )

    return layer_out, tokens_grad, (
        head_in_grad,
        head_out_grad,
        expand_in_grad,
        expand_out_grad,
        gains_grad,
        table_grad,
    )


def ring_gradients(
    tokens, cotangent, lengths, heads_in, heads_out, expand_in, expand_out, norm_gains, bias_table, firsts, seconds
):
    rows, depth = tokens.shape
    size, line = lax.axis_size("dp"), lax.axis_size("mp")
    span = -(-(rows * line + rows - 1) // LANES) * LANES
    width = expand_in.shape[2]
    slot = -(-norm_gains.shape[1] // 16) * 16
    weights = Moments(heads_in, heads_out, expand_in, expand_out, norm_gains, bias_table)
    weights, firsts, seconds = [
        Moments(state[0], state[1].T, state[2], state[3].T, state[4], state[5].T)
        for state in (weights, firsts, seconds)
    ]
    got = ring_forward(
        size, line, depth, slot, width, span,
        (lengths, tokens, cotangent, norm_gains, weights.bias_table) + tuple(weights[:4]),
    )
    back = ring_backward(
        size, line, depth, slot, width, span, lengths, weights.bias_table, got,
        (weights, firsts, seconds),
    )
    grads = (
        back.heads_in_grad,
        back.heads_out_grad.T,
        back.gate_up_grad,
        back.down_grad.T,
        back.gains_grad,
        back.table_grad.T,
    )
    return back.layer_out, back.tokens_grad, grads, back.norms[0]


def shards(
    tokens,
    cotangent,
    lengths,
    heads_in,
    heads_out,
    expand_in,
    expand_out,
    norm_gains,
    bias_table,
    heads_in_first,
    heads_out_first,
    expand_in_first,
    expand_out_first,
    gains_first,
    table_first,
    heads_in_second,
    heads_out_second,
    expand_in_second,
    expand_out_second,
    gains_second,
    table_second,
):
    given = (
        tokens, cotangent, lengths, heads_in, heads_out, expand_in, expand_out, norm_gains, bias_table
    )
    weight_list = (heads_in, heads_out, expand_in, expand_out, norm_gains, bias_table)
    first_list = (
        heads_in_first,
        heads_out_first,
        expand_in_first,
        expand_out_first,
        gains_first,
        table_first,
    )
    second_list = (
        heads_in_second,
        heads_out_second,
        expand_in_second,
        expand_out_second,
        gains_second,
        table_second,
    )
    decay_list = (weight_decay, weight_decay, weight_decay, weight_decay, 0.0, 0.0)
    sub_list = (3, 1, 2, 1, 2, 1)
    sums = None
    if lax.axis_size("dp") <= RING_LIMIT:
        layer_out, tokens_grad, grad_list, sums = ring_gradients(*given, first_list, second_list)
    else:
        layer_out, tokens_grad, grad_list = plain_gradients(*given)
    results = [
        lamb_parts(
            weight_list[number],
            grad_list[number],
            first_list[number],
            second_list[number],
            decay_list[number],
        )
        for number in range(6)
    ]
    count = sum(sub_list)
    if sums is None:
        shared = 1.0 / lax.axis_size("mp")
        share_list = (shared, shared, 1.0, 1.0, shared, shared / lax.axis_size("dp"))
        parts = [weight_list, [result[2] for result in results]]
        sums = lax.psum(
            jnp.concatenate(
                [
                    sub_squares(part[number], sub_list[number]) * share_list[number]
                    for part in parts
                    for number in range(6)
                ]
            ),
            ("dp", "mp"),
        )
    weight_norm = jnp.sqrt(sums[:count])
    step_norm = jnp.sqrt(sums[count : 2 * count])
    ratios = weight_norm / step_norm
    starts = (0, 3, 4, 6, 7, 9)
    outputs = [layer_out, tokens_grad]
    for number in range(6):
        weight = weight_list[number]
        sub_count = sub_list[number]
        ratio_part = ratios[starts[number] : starts[number] + sub_count]
        shape = (sub_count,) + (1,) * (weight.ndim - 1) if sub_count > 1 else (1,) * weight.ndim
        new_weight = weight - learn_rate * ratio_part.reshape(shape) * results[number][2]
        outputs = outputs + [
            results[number][0],
            results[number][1],
            new_weight,
            new_weight.astype(bf16),
        ]
    outputs = outputs + [jnp.stack([weight_norm, step_norm])]
    return tuple(outputs)


def solution(mesh):
    return jax.shard_map(
        shards,
        mesh=mesh,
        in_specs=(
            P(("dp", "mp"), None),
            P(("dp", "mp"), None),
            P("dp", None),
            P(None, "dp", None),
            P(None, "dp"),
            P(None, "dp", "mp"),
            P("mp", "dp"),
            P(None, "dp"),
            P(),
            P(None, "dp", None),
            P(None, "dp"),
            P(None, "dp", "mp"),
            P("mp", "dp"),
            P(None, "dp"),
            P(),
            P(None, "dp", None),
            P(None, "dp"),
            P(None, "dp", "mp"),
            P("mp", "dp"),
            P(None, "dp"),
            P(),
        ),
        out_specs=(
            P(("dp", "mp"), None),
            P(("dp", "mp"), None),
            P(None, "dp", None),
            P(None, "dp", None),
            P(None, "dp", None),
            P(None, "dp", None),
            P(None, "dp"),
            P(None, "dp"),
            P(None, "dp"),
            P(None, "dp"),
            P(None, "dp", "mp"),
            P(None, "dp", "mp"),
            P(None, "dp", "mp"),
            P(None, "dp", "mp"),
            P("mp", "dp"),
            P("mp", "dp"),
            P("mp", "dp"),
            P("mp", "dp"),
            P(None, "dp"),
            P(None, "dp"),
            P(None, "dp"),
            P(None, "dp"),
            P(),
            P(),
            P(),
            P(),
            P(),
        ),
        check_vma=False,
    )
```

```python
from functools import partial
from typing import NamedTuple

import jax
import jax.numpy as jnp
from jax import lax
from jax.experimental import pallas as pl
from jax.experimental.pallas import tpu as pltpu
from jax.sharding import PartitionSpec as P

HEADS = 6
HEAD_DIM = 64
STEP = 10
INNER = 384
LANES = 128
PAIRS = INNER // LANES
MESH = pl.DeviceIdType.MESH
VMEM_BYTES = 56 * 2**20
BACKWARD_BYTES = 63 * 2**20
RING_LIMIT = 8


norm_eps = 1e-06
beta_first = 0.9
beta_second = 0.999
adam_eps = 1e-06
weight_decay = 0.01
learn_rate = 0.4
masked_fill = -1000000000.0
bucket_edges = (12, 16, 23, 32, 46, 64, 91)
highest = lax.Precision.HIGHEST
f32 = jnp.float32
bf16 = jnp.bfloat16


def bucket_ids(offsets):
    distance = jnp.abs(offsets)
    coarse = jnp.full_like(distance, 8)
    for edge_value in bucket_edges:
        coarse = coarse + (distance >= edge_value).astype(jnp.int32)
    nearby = jnp.where(distance < 8, distance, coarse)
    return nearby + 16 * (offsets > 0).astype(jnp.int32)


def row_mean(values, depth):
    return jnp.sum(values, axis=-1, keepdims=True) * (1.0 / depth)


def rms_scale(hidden_rows, gain_vector, depth):
    return (
        hidden_rows
        * lax.rsqrt(row_mean(hidden_rows * hidden_rows, depth) + norm_eps)
        * gain_vector
    )


def contract_rows(left_side, right_side):
    return lax.dot_general(
        left_side, right_side, (((0,), (0,)), ((), ())), preferred_element_type=f32
    )


def contract_cols(left_side, right_side):
    return lax.dot_general(
        left_side, right_side, (((1,), (1,)), ((), ())), preferred_element_type=f32
    )


def matmul(left_side, right_side):
    return jnp.dot(left_side, right_side, preferred_element_type=f32)


def ring_order(size):
    return list(range(0, size, 2)) + list(range(size - 1, 0, -2))


def ring_pairs(size):
    order = ring_order(size)
    forward = [(order[spot], order[(spot + 1) % size]) for spot in range(size)]
    return forward, [(target, source) for source, target in forward]


def ring_owner(spot, size):
    late = (spot >= size // 2).astype(jnp.int32)
    return 2 * spot + late * (2 * size - 1 - 4 * spot)


def ring_spot(index, size):
    return index // 2 + lax.rem(index, 2) * (size - 1 - 2 * (index // 2))


def cut_of(width):
    return ((width // LANES + 1) // 2) * LANES


def assemble_kernel(size, cut, *refs):
    slabs, (left, right, out, sems) = refs[:-4], refs[-4:]
    spot = ring_spot(lax.axis_index("dp"), size)
    copies = []
    for number, slab in enumerate(slabs):
        shift = number if number < size // 2 else number + 1
        owner = ring_owner(lax.rem(spot + shift, size), size)
        copies.append(pltpu.make_async_copy(slab, out.at[:, owner], sems.at[number]))
    owner = ring_owner(lax.rem(spot + size // 2, size), size)
    width = out.shape[-1]
    copies.append(
        pltpu.make_async_copy(left, out.at[:, owner, :, pl.ds(0, cut)], sems.at[size - 1])
    )
    copies.append(
        pltpu.make_async_copy(right, out.at[:, owner, :, pl.ds(cut, width - cut)], sems.at[size])
    )
    for copy in copies:
        copy.start()
    for copy in copies:
        copy.wait()


def gather_dp(part):
    size = lax.axis_size("dp")
    if size > RING_LIMIT:
        return lax.all_gather(part, "dp", axis=1, tiled=True)
    forward, backward = ring_pairs(size)
    count, rows, width = part.shape
    cut = cut_of(width)
    slabs = [None] * size
    slabs[0] = ahead = behind = part
    for hop in range(1, size // 2):
        ahead = lax.ppermute(ahead, "dp", forward)
        behind = lax.ppermute(behind, "dp", backward)
        slabs[size - hop] = ahead
        slabs[hop] = behind
    left = lax.ppermute(ahead[..., :cut], "dp", forward)
    right = lax.ppermute(behind[..., cut:], "dp", backward)
    operands = [slab for slab in slabs if slab is not None] + [left, right]
    total = count * size * rows * width * part.dtype.itemsize
    whole = pl.pallas_call(
        partial(assemble_kernel, size, cut),
        out_shape=jax.ShapeDtypeStruct((count, size, rows, width), part.dtype),
        in_specs=[pl.BlockSpec(memory_space=pl.ANY)] * len(operands),
        out_specs=pl.BlockSpec(memory_space=pltpu.VMEM),
        scratch_shapes=[pltpu.SemaphoreType.DMA((size + 1,))],
        compiler_params=pltpu.CompilerParams(vmem_limit_bytes=VMEM_BYTES),
        cost_estimate=pl.CostEstimate(flops=0, bytes_accessed=2 * total, transcendentals=0),
        name="assemble",
    )(*operands)
    return whole.reshape(count, size * rows, width)


def scatter_dp(whole):
    size = lax.axis_size("dp")
    if size > RING_LIMIT:
        return lax.psum_scatter(whole.astype(f32), "dp", scatter_dimension=1, tiled=True)
    forward, backward = ring_pairs(size)
    count, depth, width = whole.shape
    rows = depth // size
    cut = cut_of(width)
    spot = ring_spot(lax.axis_index("dp"), size)

    def term(shift):
        owner = ring_owner(lax.rem(spot + size + shift, size), size)
        return lax.dynamic_slice_in_dim(whole, owner * rows, rows, axis=1)

    far = term(size // 2)
    ahead = lax.ppermute(far[..., :cut], "dp", forward)
    behind = lax.ppermute(far[..., cut:], "dp", backward)
    for hop in range(size // 2 - 1, 0, -1):
        mine = term(hop).astype(f32)
        other = term(-hop).astype(f32)
        if hop == size // 2 - 1:
            ahead = jnp.concatenate([mine[..., :cut] + ahead.astype(f32), mine[..., cut:]], -1)
            behind = jnp.concatenate([other[..., :cut], other[..., cut:] + behind.astype(f32)], -1)
        else:
            ahead = mine + ahead.astype(f32)
            behind = other + behind.astype(f32)
        ahead = lax.ppermute(ahead.astype(bf16), "dp", forward)
        behind = lax.ppermute(behind.astype(bf16), "dp", backward)
    return term(0).astype(f32) + ahead.astype(f32) + behind.astype(f32)


def swap(part, bit):
    size = lax.axis_size("mp")
    return lax.ppermute(part, "mp", [(index, index ^ bit) for index in range(size)])


def gather_mp(part):
    across = swap(part, 2)
    beside = swap(part, 1)
    return part, across, beside, swap(across, 1)


def offset_values(table, first_row, rows, span):
    offsets = lax.broadcasted_iota(jnp.int32, (8, span), 1) - (rows - 1) - first_row
    buckets = bucket_ids(offsets)
    values = jnp.zeros((8, span), f32)
    for number in range(table.shape[1]):
        values = jnp.where(buckets == number, table[:, number : number + 1], values)
    return values


def segments_at(positions, first_len, second_len):
    return (positions >= first_len).astype(jnp.int32) + (
        positions >= first_len + second_len
    ).astype(jnp.int32)


def allowed_pairs(lens_ref, first_row, rows, keys):
    query = segments_at(
        first_row + lax.broadcasted_iota(jnp.int32, (rows, 1), 0), lens_ref[0, 0], lens_ref[0, 1]
    )
    key = segments_at(
        lax.broadcasted_iota(jnp.int32, (1, keys), 1), lens_ref[0, 0], lens_ref[0, 1]
    )
    return query == key


def skewed_bias(values, head, rows, keys, span):
    wide = jnp.broadcast_to(values[head : head + 1, :], (rows, span))
    return pltpu.roll(wide, span - (rows - 1), 1, stride=1, stride_axis=0)[:, :keys]


def attend_pair(pair, query_ref, key_ref, value_ref, mixed_ref, logs, values, allowed, lane, span):
    rows, keys = query_ref.shape[0], key_ref.shape[0]
    part = slice(pair * LANES, (pair + 1) * LANES)
    query, key, value = query_ref[:, part], key_ref[:, part], value_ref[:, part]
    mixed = jnp.zeros((rows, LANES), f32)
    for half in range(2):
        head = 2 * pair + half
        mask = (lane // HEAD_DIM) == half
        scores = contract_cols(jnp.where(mask, query, jnp.zeros_like(query)), key)
        scores = jnp.where(
            allowed, scores + skewed_bias(values, head, rows, keys, span), masked_fill
        )
        top = jnp.max(scores, axis=-1, keepdims=True)
        powers = jnp.exp(scores - top)
        total = jnp.sum(powers, axis=-1, keepdims=True)
        soft = (powers * (1.0 / total)).astype(bf16)
        mixed = jnp.where(mask, matmul(soft, value), mixed)
        logs = jnp.where(lane == head, top + jnp.log(total), logs)
    mixed_ref[:, part] = mixed.astype(bf16)
    return logs


def forward_kernel(
    span,
    depth,
    lens_ref,
    own_ref,
    across_ref,
    beside_ref,
    corner_ref,
    heads_ref,
    table_ref,
    tokens_ref,
    gain_ref,
    mixed_ref,
    query_ref,
    key_ref,
    value_ref,
    log_ref,
    residual_ref,
    normed_ref,
):
    rows = own_ref.shape[0]
    keys = key_ref.shape[0]
    spot = lax.axis_index("mp")
    first_row = spot * rows
    for block_ref, bit in ((own_ref, 0), (across_ref, 2), (beside_ref, 1), (corner_ref, 3)):
        place = pl.ds(pl.multiple_of((spot ^ bit) * rows, rows), rows)
        block = block_ref[...]
        key_ref[place, :] = matmul(block, heads_ref[1]).astype(bf16)
        value_ref[place, :] = matmul(block, heads_ref[2]).astype(bf16)
    query_ref[...] = matmul(own_ref[...], heads_ref[0]).astype(bf16)
    values = offset_values(table_ref[...], first_row, rows, span)
    allowed = allowed_pairs(lens_ref, first_row, rows, keys)
    lane = lax.broadcasted_iota(jnp.int32, (1, LANES), 1)
    logs = jnp.zeros((rows, LANES), f32)
    for pair in range(PAIRS):
        logs = attend_pair(
            pair, query_ref, key_ref, value_ref, mixed_ref, logs, values, allowed, lane, span
        )
    log_ref[...] = logs
    residual = tokens_ref[...].astype(f32) + contract_cols(mixed_ref[...], heads_ref[3])
    residual_ref[...] = residual
    normed_ref[...] = rms_scale(residual, gain_ref[...], depth).astype(bf16)


def norm_backward(rows_in, gain, grad, depth):
    scale = lax.rsqrt(row_mean(rows_in * rows_in, depth) + norm_eps)
    unit = rows_in * scale
    inner = grad * gain
    out = scale * (inner - unit * row_mean(inner * unit, depth))
    return out, jnp.sum(grad * unit, axis=0, keepdims=True)


def attend_pair_backward(
    pair, query_ref, key_ref, value_ref, log_ref, mixed_grad, values, allowed, span
):
    rows, keys = query_ref.shape[0], key_ref.shape[0]
    lane = lax.broadcasted_iota(jnp.int32, (1, LANES), 1)
    flip = (
        lax.broadcasted_iota(jnp.int32, (rows, rows), 0)
        + lax.broadcasted_iota(jnp.int32, (rows, rows), 1)
        == rows - 1
    ).astype(bf16)
    part = slice(pair * LANES, (pair + 1) * LANES)
    query, key, value = query_ref[:, part], key_ref[:, part], value_ref[:, part]
    query_grad = jnp.zeros((rows, LANES), f32)
    key_grad = jnp.zeros((keys, LANES), f32)
    value_grad = jnp.zeros((keys, LANES), f32)
    offsets = []
    for half in range(2):
        head = 2 * pair + half
        mask = (lane // HEAD_DIM) == half
        query_own = jnp.where(mask, query, jnp.zeros_like(query))
        mixed_own = jnp.where(mask, mixed_grad, jnp.zeros_like(mixed_grad))
        scores = contract_cols(query_own, key)
        scores = jnp.where(
            allowed, scores + skewed_bias(values, head, rows, keys, span), masked_fill
        )
        soft = jnp.exp(scores - log_ref[:, head : head + 1])
        soft_grad = contract_cols(mixed_own, value)
        corr = jnp.sum(soft * soft_grad, axis=-1, keepdims=True)
        scores_grad = (soft * (soft_grad - corr)).astype(bf16)
        query_grad = jnp.where(mask, matmul(scores_grad, key), query_grad)
        key_grad = key_grad + contract_rows(scores_grad, query_own)
        value_grad = value_grad + contract_rows(soft.astype(bf16), mixed_own)
        flipped = matmul(flip, scores_grad)
        flipped = jnp.concatenate([flipped, jnp.zeros((rows, span - keys), f32)], axis=1)
        skewed = pltpu.roll(flipped, 0, 1, stride=1, stride_axis=0)
        offsets.append(jnp.sum(skewed, axis=0, keepdims=True))
    return query_grad, key_grad, value_grad, offsets


def backward_kernel(
    span,
    depth,
    lens_ref,
    part_ref,
    across_ref,
    residual_ref,
    upstream_ref,
    gain_ref,
    heads_ref,
    query_ref,
    key_ref,
    value_ref,
    log_ref,
    table_ref,
    residual_grad_ref,
    attended_ref,
    query_grad_ref,
    near_ref,
    far_ref,
    offset_ref,
    gain_grad_ref,
    whole_ref,
):
    rows = query_ref.shape[0]
    keys = key_ref.shape[0]
    spot = lax.axis_index("mp")
    first_row = spot * rows
    grad = part_ref[...].astype(f32) + across_ref[...].astype(f32)
    through, gain_grad = norm_backward(residual_ref[...], gain_ref[...], grad, depth)
    gain_grad_ref[...] = gain_grad
    residual_grad = upstream_ref[...].astype(f32) + through
    residual_grad_ref[...] = residual_grad
    attended = residual_grad.astype(bf16)
    attended_ref[...] = attended
    mixed_grad_all = matmul(attended, heads_ref[3]).astype(bf16)
    values = offset_values(table_ref[...], first_row, rows, span)
    allowed = allowed_pairs(lens_ref, first_row, rows, keys)
    for pair in range(PAIRS):
        part = slice(pair * LANES, (pair + 1) * LANES)
        query_grad, key_grad, value_grad, offsets = attend_pair_backward(
            pair, query_ref, key_ref, value_ref, log_ref, mixed_grad_all[:, part], values, allowed,
            span,
        )
        for half in range(2):
            offset_ref[2 * pair + half : 2 * pair + half + 1, :] = offsets[half]
        query_grad_ref[:, part] = query_grad.astype(bf16)
        whole_ref[:, part] = key_grad
        whole_ref[:, INNER + pair * LANES : INNER + (pair + 1) * LANES] = value_grad
    offset_ref[HEADS:, :] = jnp.zeros((8 - HEADS, span), f32)
    for number, bit in enumerate((0, 2)):
        place = pl.ds(pl.multiple_of((spot ^ bit) * rows, rows), rows)
        near_ref[number * rows : (number + 1) * rows, :] = whole_ref[place, :]
    for number, bit in enumerate((1, 3)):
        place = pl.ds(pl.multiple_of((spot ^ bit) * rows, rows), rows)
        far_ref[number * rows : (number + 1) * rows, :] = whole_ref[place, :].astype(bf16)


def input_kernel(
    depth,
    own_ref,
    beside_ref,
    across_ref,
    query_grad_ref,
    heads_ref,
    tokens_ref,
    gain_ref,
    residual_grad_ref,
    tokens_grad_ref,
    both_ref,
    gain_grad_ref,
):
    rows = query_grad_ref.shape[0]
    both = (
        own_ref[:rows, :]
        + beside_ref[:rows, :].astype(f32)
        + across_ref[...].astype(f32)
    ).astype(bf16)
    both_ref[...] = both
    grad = (
        contract_cols(query_grad_ref[...], heads_ref[0])
        + contract_cols(both[:, :INNER], heads_ref[1])
        + contract_cols(both[:, INNER:], heads_ref[2])
    )
    through, gain_grad = norm_backward(tokens_ref[...].astype(f32), gain_ref[...], grad, depth)
    gain_grad_ref[...] = gain_grad
    tokens_grad_ref[...] = residual_grad_ref[...] + through


def vmem_call(body, outs, cost, scratch=(), name=None, smem_first=False):
    def run(*operands):
        specs = [pl.BlockSpec(memory_space=pltpu.VMEM)] * len(operands)
        if smem_first:
            specs[0] = pl.BlockSpec(memory_space=pltpu.SMEM)
        return pl.pallas_call(
            body,
            out_shape=[jax.ShapeDtypeStruct(shape, kind) for shape, kind in outs],
            in_specs=specs,
            out_specs=[pl.BlockSpec(memory_space=pltpu.VMEM)] * len(outs),
            scratch_shapes=list(scratch),
            compiler_params=pltpu.CompilerParams(vmem_limit_bytes=VMEM_BYTES),
            cost_estimate=pl.CostEstimate(
                flops=cost[0], bytes_accessed=cost[1], transcendentals=cost[2]
            ),
            name=name,
        )(*operands)

    return run


def total_kernel(sizes, part_ref, out_ref, line_ref, plane_ref, line_send, line_recv, plane_send, plane_recv):
    plane, line = sizes
    dp_spot, mp_spot = lax.axis_index("dp"), lax.axis_index("mp")
    barrier = pltpu.get_barrier_semaphore()
    for step in range(1, line):
        pl.semaphore_signal(
            barrier, 1, device_id=(dp_spot, lax.rem(mp_spot + step, line)), device_id_type=MESH
        )
    for step in range(1, plane):
        pl.semaphore_signal(
            barrier, 1, device_id=(lax.rem(dp_spot + step, plane), mp_spot), device_id_type=MESH
        )
    pl.semaphore_wait(barrier, line + plane - 2)

    def exchange(source, slots, size, spot, send, recv, target):
        slots[spot] = source[...]
        copies = [
            pltpu.make_async_remote_copy(
                src_ref=source,
                dst_ref=slots.at[spot],
                send_sem=send.at[step],
                recv_sem=recv.at[step],
                device_id=target(lax.rem(spot + step, size)),
                device_id_type=MESH,
            )
            for step in range(1, size)
        ]
        for copy in copies:
            copy.start()
        for copy in copies:
            copy.wait()
        total = slots[0]
        for index in range(1, size):
            total = total + slots[index]
        out_ref[...] = total

    exchange(part_ref, line_ref, line, mp_spot, line_send, line_recv, lambda to: (dp_spot, to))
    exchange(out_ref, plane_ref, plane, dp_spot, plane_send, plane_recv, lambda to: (to, mp_spot))


def total_all(part, number):
    plane, line = lax.axis_size("dp"), lax.axis_size("mp")
    if plane > RING_LIMIT:
        return lax.psum(part, ("dp", "mp"))
    return pl.pallas_call(
        partial(total_kernel, (plane, line)),
        out_shape=jax.ShapeDtypeStruct(part.shape, part.dtype),
        in_specs=[pl.BlockSpec(memory_space=pltpu.VMEM)],
        out_specs=pl.BlockSpec(memory_space=pltpu.VMEM),
        scratch_shapes=[
            pltpu.VMEM((line,) + part.shape, f32),
            pltpu.VMEM((plane,) + part.shape, f32),
            pltpu.SemaphoreType.DMA((line,)),
            pltpu.SemaphoreType.DMA((line,)),
            pltpu.SemaphoreType.DMA((plane,)),
            pltpu.SemaphoreType.DMA((plane,)),
        ],
        compiler_params=pltpu.CompilerParams(collective_id=number, has_side_effects=True),
        name="total",
    )(part)


def small_gather_kernel(size, part_ref, out_ref, send, recv):
    dp_spot, mp_spot = lax.axis_index("dp"), lax.axis_index("mp")
    barrier = pltpu.get_barrier_semaphore()
    for step in range(1, size):
        pl.semaphore_signal(
            barrier, 1, device_id=(lax.rem(dp_spot + step, size), mp_spot), device_id_type=MESH
        )
    pl.semaphore_wait(barrier, size - 1)
    out_ref[dp_spot] = part_ref[...]
    copies = [
        pltpu.make_async_remote_copy(
            src_ref=part_ref,
            dst_ref=out_ref.at[dp_spot],
            send_sem=send.at[step],
            recv_sem=recv.at[step],
            device_id=(lax.rem(dp_spot + step, size), mp_spot),
            device_id_type=MESH,
        )
        for step in range(1, size)
    ]
    for copy in copies:
        copy.start()
    for copy in copies:
        copy.wait()


def gather_gains(gains):
    size = lax.axis_size("dp")
    if size > RING_LIMIT:
        return lax.all_gather(gains, "dp", axis=1, tiled=True)
    count, width = gains.shape
    wide = -(-width // LANES) * LANES
    part = jnp.pad(gains, ((0, 8 - count), (0, wide - width)))
    whole = pl.pallas_call(
        partial(small_gather_kernel, size),
        out_shape=jax.ShapeDtypeStruct((size,) + part.shape, part.dtype),
        in_specs=[pl.BlockSpec(memory_space=pltpu.VMEM)],
        out_specs=pl.BlockSpec(memory_space=pltpu.VMEM),
        scratch_shapes=[pltpu.SemaphoreType.DMA((size,)), pltpu.SemaphoreType.DMA((size,))],
        compiler_params=pltpu.CompilerParams(collective_id=3, has_side_effects=True),
        name="gather_gains",
    )(part)
    return jnp.concatenate([whole[index, :count, :width] for index in range(size)], axis=1)


def pack_rows(parts):
    flat = jnp.concatenate([part.reshape(-1) for part in parts])
    count = -(-flat.shape[0] // (8 * LANES)) * 8
    return jnp.pad(flat, (0, count * LANES - flat.shape[0])).reshape(count, LANES)


def lamb_parts(weight, gradient, first_moment, second, decay_rate):
    new_first = beta_first * first_moment + (1.0 - beta_first) * gradient
    new_second = beta_second * second + (1.0 - beta_second) * gradient * gradient
    first_fix = 1.0 - beta_first**STEP
    second_fix = 1.0 - beta_second**STEP
    step_dir = (new_first * (1.0 / first_fix)) / (
        jnp.sqrt(new_second * (1.0 / second_fix)) + adam_eps
    ) + decay_rate * weight
    return (new_first, new_second, step_dir)


def sub_squares(values, sub_count):
    flat_values = values.reshape(sub_count, -1)
    return jnp.sum(flat_values * flat_values, axis=1)


def gelu_parts(gate):
    root = (2.0 / 3.141592653589793) ** 0.5
    square = gate * gate
    curve = jnp.tanh(root * (gate + 0.044715 * gate * square))
    value = 0.5 * gate * (1.0 + curve)
    slope = 0.5 * (1.0 + curve) + 0.5 * gate * (1.0 - curve * curve) * root * (
        1.0 + 3.0 * 0.044715 * square
    )
    return value, slope


def spread_pair(values, pair, shard, slot):
    depth = values.shape[1]
    first = 2 * pair * shard
    low = first // LANES * LANES
    high = min(depth, -(-(first + 2 * shard) // LANES) * LANES)
    shape = (high - low, 2 * slot)
    source = low + lax.broadcasted_iota(jnp.int32, shape, 0)
    place = lax.broadcasted_iota(jnp.int32, shape, 1)
    late = (place >= slot).astype(jnp.int32)
    offset = place - late * slot
    chosen = (source == first + late * shard + offset) & (offset < shard)
    return matmul(values[:, low:high], chosen.astype(bf16))


def gathered_tile(coarse, fine, low, high, shard, slot):
    def place_of(lane):
        return lane // shard * slot + lane % shard

    first = place_of(low) // LANES * LANES
    last = -(-(place_of(high - 1) + 1) // LANES) * LANES
    shape = (last - first, high - low)
    source = first + lax.broadcasted_iota(jnp.int32, shape, 0)
    lane = low + lax.broadcasted_iota(jnp.int32, shape, 1)
    chosen = jnp.zeros(shape, jnp.bool_)
    for number in range(low // shard, (high - 1) // shard + 1):
        inside = (lane >= number * shard) & (lane < (number + 1) * shard)
        chosen = chosen | (inside & (source == lane + number * (slot - shard)))
    chosen = chosen.astype(bf16)
    total = matmul(coarse[:, first:last], chosen)
    if fine is not None:
        total = total + matmul(fine[:, first:last], chosen)
    return total


def head_table(table_ref):
    table = table_ref[...]
    return jnp.concatenate([table, jnp.zeros((8 - HEADS, table.shape[1]), f32)], axis=0)


class Places:
    def __init__(self, size):
        self.size, self.half = size, size // 2
        self.dp, self.mp = lax.axis_index("dp"), lax.axis_index("mp")
        self.spot = ring_spot(self.dp, size)
        self.sides = (
            ring_owner(lax.rem(self.spot + 1, size), size),
            ring_owner(lax.rem(self.spot + size - 1, size), size),
        )

    def owner(self, shift):
        return ring_owner(lax.rem(self.spot + self.size + shift, self.size), self.size)

    def sent(self, side, hop):
        return self.owner(-hop if side == 0 else hop)

    def came(self, side, hop):
        return self.sent(side, hop + 1)


def remote(source, target, send, recv, dp, mp):
    return pltpu.make_async_remote_copy(
        src_ref=source,
        dst_ref=target,
        send_sem=send,
        recv_sem=recv,
        device_id=(dp, mp),
        device_id_type=MESH,
    )


class ForwardOut(NamedTuple):
    heads: object
    gate_up: object
    down: object
    normed: object
    upstream: object
    normed_two: object
    gelu: object
    slope: object
    hidden: object
    hidden_grad_out: object
    query: object
    key: object
    value: object
    mixed: object
    logs: object
    residual: object
    full_gains: object
    wide_tokens: object


class ForwardRefs(NamedTuple):
    lens: object
    tokens: object
    cotangent: object
    norm_gains: object
    table: object
    heads_in: object
    heads_out: object
    expand_in: object
    expand_out: object
    heads: object
    gate_up: object
    down: object
    normed: object
    upstream: object
    normed_two: object
    gelu: object
    slope: object
    hidden: object
    hidden_grad_out: object
    query: object
    key: object
    value: object
    mixed: object
    logs: object
    residual: object
    full_gains: object
    wide_tokens: object
    tokens_in: object
    cotangent_in: object
    mine_in: object
    out_in: object
    gate_in: object
    down_in: object
    bring_sems: object
    gains: object
    mine: object
    wide_in: object
    wide_out: object
    gain_slots: object
    gain_send: object
    gain_recv: object
    head_send: object
    head_recv: object
    wide_send: object
    wide_recv: object
    line_send: object
    line_recv: object
    slab_send: object
    slab_recv: object
    store_sems: object


def forward_shapes(rows, line, size, slot, width, span):
    wide, keys = size * slot, rows * line
    return ForwardOut(
        heads=((4, wide, INNER), bf16),
        gate_up=((2, wide, width), bf16),
        down=((wide, width), bf16),
        normed=((keys, wide), bf16),
        upstream=((keys, wide), bf16),
        normed_two=((keys, wide), bf16),
        gelu=((keys, width), f32),
        slope=((keys, width), f32),
        hidden=((keys, width), bf16),
        hidden_grad_out=((wide, width), bf16),
        query=((rows, INNER), bf16),
        key=((keys, INNER), bf16),
        value=((keys, INNER), bf16),
        mixed=((rows, INNER), bf16),
        logs=((rows, LANES), f32),
        residual=((rows, wide), f32),
        full_gains=((8, wide), f32),
        wide_tokens=((rows, wide), bf16),
    )


def ring_forward_kernel(size, depth, span, *refs):
    count = len(ForwardOut._fields)
    inputs = 9
    stores = refs[inputs : inputs + count]
    r = ForwardRefs(*refs[:inputs], *refs[inputs + count :])
    places = (None, r.tokens_in, r.cotangent_in, None, None, r.mine_in, r.out_in, r.gate_in, r.down_in)

    def bring(number, index=None):
        source = refs[number] if index is None else refs[number].at[index]
        return pltpu.make_async_copy(source, places[number], r.bring_sems.at[number])
    kept = refs[inputs + count : inputs + 2 * count]

    def store_copy(number):
        return pltpu.make_async_copy(kept[number], stores[number], r.store_sems.at[number])

    def store(*which):
        for number in range(count):
            if any(kept[number] is ref for ref in which):
                store_copy(number).start()

    at = Places(size)
    half = at.half
    rows = r.tokens_in.shape[0]
    wide = r.residual.shape[1]
    keys = r.key.shape[0]
    slot = wide // size
    shard = r.norm_gains.shape[1]
    width = r.down.shape[1]
    line = keys // rows
    cut, head_cut = cut_of(width), cut_of(INNER)
    first_row = at.mp * rows
    across, beside = at.mp ^ 2, at.mp ^ 1

    brought = (bring(5, jnp.minimum(at.mp, line - 2)), bring(6), bring(7), bring(1), bring(8), bring(2))
    for copy in brought:
        copy.start()
    barrier = pltpu.get_barrier_semaphore()
    for step in range(1, size):
        pl.semaphore_signal(
            barrier, 1, device_id=(lax.rem(at.dp + step, size), at.mp), device_id_type=MESH
        )
    for partner in (across, beside):
        pl.semaphore_signal(barrier, 1, device_id=(at.dp, partner), device_id_type=MESH)

    def filled(values):
        spare = jnp.zeros((slot - shard, values.shape[1]), f32)
        return jnp.concatenate([values, spare], axis=0).astype(bf16)

    last = at.mp == line - 1
    brought[0].wait()
    brought[1].wait()
    r.mine[...] = filled(jnp.where(last, r.out_in[...], r.mine_in[...]))
    brought[2].wait()
    r.wide_in[0] = filled(r.gate_in[0])
    rounded = r.norm_gains[...].astype(bf16).astype(f32)
    rounded = jnp.concatenate([rounded, jnp.zeros((2, 2 * slot - shard), f32)], axis=1)
    rounded = jnp.concatenate([rounded, jnp.zeros((6, 2 * slot), f32)], axis=0)
    r.gains[...] = jnp.where(lax.rem(at.dp, 2) == 1, pltpu.roll(rounded, slot, 1), rounded)
    pl.semaphore_wait(barrier, size + 1)

    def slab_rows(owner):
        return pl.ds(pl.multiple_of(owner * slot, slot), slot)

    def head_lanes(side, hop):
        if hop < half - 1:
            return pl.ds(0, INNER)
        return pl.ds(0, head_cut) if side == 0 else pl.ds(head_cut, INNER - head_cut)

    def head_hop(side, hop):
        lanes = head_lanes(side, hop)
        target = r.heads.at[at.mp, slab_rows(at.sent(side, hop)), lanes]
        source = r.mine.at[:, lanes] if hop == 0 else target
        return remote(
            source, target, r.head_send.at[side, hop], r.head_recv.at[side, hop],
            at.sides[side], at.mp,
        )

    def head_came(side, hop):
        target = r.heads.at[at.mp, slab_rows(at.came(side, hop)), head_lanes(side, hop)]
        return remote(
            target, target, r.head_send.at[side, hop], r.head_recv.at[side, hop],
            at.sides[side], at.mp,
        )

    def piece_view(piece, owner):
        lanes = pl.ds(0, cut) if piece % 2 == 0 else pl.ds(cut, width - cut)
        if piece < 4:
            return r.gate_up.at[piece // 2, slab_rows(owner), lanes]
        return r.down.at[slab_rows(owner), lanes]

    def piece_source(piece):
        lanes = pl.ds(0, cut) if piece % 2 == 0 else pl.ds(cut, width - cut)
        if piece < 4:
            return r.wide_in.at[piece // 2, :, lanes]
        return r.wide_out.at[:, lanes]

    def piece_goes(piece, side, hop):
        return hop < half - 1 or piece in ((0, 3, 4), (1, 2, 5))[side]

    def piece_hop(piece, side, hop):
        target = piece_view(piece, at.sent(side, hop))
        source = piece_source(piece) if hop == 0 else target
        return remote(
            source, target, r.wide_send.at[piece, side, hop], r.wide_recv.at[piece, side, hop],
            at.sides[side], at.mp,
        )

    def piece_came(piece, side, hop):
        target = piece_view(piece, at.came(side, hop))
        return remote(
            target, target, r.wide_send.at[piece, side, hop], r.wide_recv.at[piece, side, hop],
            at.sides[side], at.mp,
        )

    def serve(piece, hop):
        for side in range(2):
            if piece_goes(piece, side, hop):
                if hop > 0:
                    piece_came(piece, side, hop - 1).wait_recv()
                piece_hop(piece, side, hop).start()

    def finish(piece):
        for side in range(2):
            last = half - 1 if piece_goes(piece, side, half - 1) else half - 2
            piece_came(piece, side, last).wait_recv()

    def block(array, number):
        return array.at[pl.ds(number * rows, rows)]

    def line_copy(array, ref, number):
        source, target, partner = ((0, 1, across), (0, 2, beside), (1, 3, beside))[number]
        return remote(
            block(ref, source), block(ref, target), r.line_send.at[array, number],
            r.line_recv.at[array, number], at.dp, partner,
        )

    shifts = [0] + [shift for hop in range(1, half) for shift in (-hop, hop)] + [half]

    def slab_copy(number, way):
        matrix = across if way == 2 else at.mp
        view = r.heads.at[matrix, slab_rows(at.owner(shifts[number]))]
        source = r.mine if number == 0 and way < 2 else view
        return remote(
            source, view, r.slab_send.at[number, way], r.slab_recv.at[number, way],
            at.dp, across if way == 0 else beside,
        )

    def slab_came(number, way):
        matrix = (across, beside, at.mp ^ 3)[way]
        view = r.heads.at[matrix, slab_rows(at.owner(shifts[number]))]
        return remote(
            view, view, r.slab_send.at[number, way], r.slab_recv.at[number, way],
            at.dp, across if way == 0 else beside,
        )

    def gain_copy(step):
        return remote(
            r.gains, r.gain_slots.at[at.dp], r.gain_send.at[step], r.gain_recv.at[step],
            lax.rem(at.dp + step, size), at.mp,
        )

    for step in range(1, size):
        gain_copy(step).start()
    for side in range(2):
        head_hop(side, 0).start()
    for way in range(2):
        slab_copy(0, way).start()
    serve(0, 0)
    r.wide_in[1] = filled(r.gate_in[1])
    brought[3].wait()
    for pair in range(half):
        lanes = slice(2 * pair * slot, 2 * (pair + 1) * slot)
        r.wide_tokens[:, lanes] = spread_pair(r.tokens_in[...], pair, shard, slot).astype(bf16)
    r.gain_slots[at.dp] = r.gains[...]
    own = slab_rows(at.dp)
    r.heads[at.mp, own, :] = r.mine[...]
    r.gate_up[0, own, :] = r.wide_in[0]
    r.gate_up[1, own, :] = r.wide_in[1]
    for step in range(1, size):
        gain_copy(step).wait()
    r.full_gains[...] = jnp.concatenate(
        [r.gain_slots[2 * pair] + r.gain_slots[2 * pair + 1] for pair in range(half)], axis=1
    )
    block(r.normed, 0)[...] = rms_scale(
        r.wide_tokens[...].astype(f32), r.full_gains[0:1, :], depth
    ).astype(bf16)
    for number in range(2):
        line_copy(0, r.normed, number).start()
    brought[4].wait()
    r.wide_out[...] = filled(r.down_in[...])
    r.down[own, :] = r.wide_out[...]
    brought[5].wait()
    positions = first_row + lax.broadcasted_iota(jnp.int32, (rows, 1), 0)
    used = positions < r.lens[0, 0] + r.lens[0, 1]
    upstream = jnp.where(used, r.cotangent_in[...].astype(f32), 0.0).astype(bf16)
    for pair in range(half):
        lanes = slice(2 * pair * slot, 2 * (pair + 1) * slot)
        r.upstream[:rows, lanes] = spread_pair(upstream, pair, shard, slot).astype(bf16)

    fillers = [[(1, 0)], [(2, 0)], [(3, 0), (0, 1)], [(1, 1)]]
    for hop in range(half):
        for side in range(2):
            head_came(side, hop).wait_recv()
            if hop + 1 < half:
                head_hop(side, hop + 1).start()
        for piece, piece_at in fillers[min(hop, 3)]:
            serve(piece, piece_at)
        done = (2 * hop + 1, 2 * hop + 2) if hop + 1 < half else (2 * hop + 1,)
        for number in done:
            for way in range(2):
                slab_copy(number, way).start()
    line_copy(0, r.normed, 0).wait_recv()
    line_copy(0, r.normed, 2).start()
    for number in range(2):
        line_copy(1, r.upstream, number).start()
    serve(2, 1)
    serve(3, 1)
    for number in range(size):
        slab_came(number, 0).wait_recv()
        slab_copy(number, 2).start()
        if number == size // 2:
            serve(0, 2)
    for number in range(size):
        slab_came(number, 1).wait_recv()
    for number in range(size):
        slab_came(number, 2).wait_recv()

    r.query[...] = matmul(block(r.normed, 0)[...], r.heads[0]).astype(bf16)
    for number, bit in ((0, 0), (2, 1), (1, 2), (3, 3)):
        if number == 2:
            line_copy(0, r.normed, 1).wait_recv()
        if number == 3:
            line_copy(0, r.normed, 2).wait_recv()
        place = pl.ds(pl.multiple_of((at.mp ^ bit) * rows, rows), rows)
        data = block(r.normed, number)[...]
        r.key[place, :] = matmul(data, r.heads[1]).astype(bf16)
        r.value[place, :] = matmul(data, r.heads[2]).astype(bf16)
    serve(1, 2)
    store(r.full_gains, r.wide_tokens, r.normed, r.query, r.key, r.value)

    values = offset_values(head_table(r.table), first_row, rows, span)
    allowed = allowed_pairs(r.lens, first_row, rows, keys)
    lane = lax.broadcasted_iota(jnp.int32, (1, LANES), 1)
    logs = jnp.zeros((rows, LANES), f32)
    for pair in range(PAIRS):
        logs = attend_pair(
            pair, r.query, r.key, r.value, r.mixed, logs, values, allowed, lane, span
        )
        if pair < 2:
            serve(2 + pair, 2)
    r.logs[...] = logs
    residual = r.wide_tokens[...].astype(f32) + contract_cols(r.mixed[...], r.heads[3])
    r.residual[...] = residual
    block(r.normed_two, 0)[...] = rms_scale(residual, r.full_gains[1:2, :], depth).astype(bf16)
    store(r.heads, r.mixed, r.logs, r.residual)
    for number in range(2):
        line_copy(2, r.normed_two, number).start()
    for piece in range(4):
        serve(piece, 3)
    serve(4, 0)
    serve(5, 0)
    line_copy(2, r.normed_two, 0).wait_recv()
    line_copy(2, r.normed_two, 2).start()
    for piece in range(4):
        finish(piece)

    def expand(number):
        place = pl.ds(number * rows, rows)
        data = r.normed_two[place, :]
        gate = matmul(data, r.gate_up[0])
        up = matmul(data, r.gate_up[1])
        value, slope = gelu_parts(gate)
        r.gelu[place, :] = value
        r.slope[place, :] = slope * up
        r.hidden[place, :] = (value * up).astype(bf16)

    expand(0)
    serve(4, 1)
    line_copy(2, r.normed_two, 1).wait_recv()
    expand(2)
    serve(5, 1)
    expand(1)
    serve(4, 2)
    line_copy(2, r.normed_two, 2).wait_recv()
    expand(3)
    serve(5, 2)
    store(r.gelu, r.slope, r.hidden, r.gate_up, r.normed_two)
    line_copy(1, r.upstream, 0).wait_recv()
    line_copy(1, r.upstream, 2).start()
    line_copy(1, r.upstream, 1).wait_recv()
    line_copy(1, r.upstream, 2).wait_recv()
    store(r.upstream)
    tiles = 4
    tile = wide // tiles
    for number in range(tiles):
        lanes = slice(number * tile, (number + 1) * tile)
        r.hidden_grad_out[lanes, :] = contract_rows(
            r.upstream[:, lanes], r.hidden[...]
        ).astype(bf16)
        if number == 0:
            serve(4, 3)
            serve(5, 3)
    store(r.hidden_grad_out)
    for piece in (4, 5):
        finish(piece)
    store(r.down)

    for side in range(2):
        for hop in range(half):
            head_hop(side, hop).wait_send()
            for piece in range(6):
                if piece_goes(piece, side, hop):
                    piece_hop(piece, side, hop).wait_send()
    for number in range(size):
        for way in range(3):
            slab_copy(number, way).wait_send()
    for array, ref in enumerate((r.normed, r.upstream, r.normed_two)):
        for number in range(3):
            line_copy(array, ref, number).wait_send()
    for number in range(count):
        store_copy(number).wait()


def ring_forward(size, line, depth, slot, width, span, operands):
    rows, shard = operands[1].shape[0], depth // size
    shapes = forward_shapes(rows, line, size, slot, width, span)
    wide, keys = size * slot, rows * line
    dma = pltpu.SemaphoreType.DMA
    half = size // 2
    specs = [pl.BlockSpec(memory_space=pl.ANY)] * len(operands)
    specs[0] = pl.BlockSpec(memory_space=pltpu.SMEM)
    specs[3] = specs[4] = pl.BlockSpec(memory_space=pltpu.VMEM)
    flops = 2 * keys * wide * (3 * width + 2 * INNER) + 4 * rows * wide * INNER
    results = pl.pallas_call(
        partial(ring_forward_kernel, size, depth, span),
        out_shape=[jax.ShapeDtypeStruct(*shape) for shape in shapes],
        in_specs=specs,
        out_specs=[pl.BlockSpec(memory_space=pl.ANY)] * len(shapes),
        scratch_shapes=[pltpu.VMEM(*shape) for shape in shapes]
        + [
            pltpu.VMEM((rows, depth), bf16),
            pltpu.VMEM((rows, depth), bf16),
            pltpu.VMEM((shard, INNER), f32),
            pltpu.VMEM((shard, INNER), f32),
            pltpu.VMEM((2, shard, width), f32),
            pltpu.VMEM((shard, width), f32),
            dma((len(operands),)),
            pltpu.VMEM((8, 2 * slot), f32),
            pltpu.VMEM((slot, INNER), bf16),
            pltpu.VMEM((2, slot, width), bf16),
            pltpu.VMEM((slot, width), bf16),
            pltpu.VMEM((size, 8, 2 * slot), f32),
            dma((size,)),
            dma((size,)),
            dma((2, half)),
            dma((2, half)),
            dma((6, 2, half)),
            dma((6, 2, half)),
            dma((3, 3)),
            dma((3, 3)),
            dma((size, 3)),
            dma((size, 3)),
            dma((len(shapes),)),
        ],
        compiler_params=pltpu.CompilerParams(
            collective_id=4, has_side_effects=True, vmem_limit_bytes=60 * 2**20
        ),
        cost_estimate=pl.CostEstimate(flops=flops, bytes_accessed=40 * 2**20, transcendentals=0),
        name="ring_forward",
    )(*operands)
    return ForwardOut(*results)


class BackwardOut(NamedTuple):
    layer_out: object
    tokens_grad: object
    heads_in_grad: object
    heads_out_grad: object
    gate_up_grad: object
    down_grad: object
    gains_grad: object
    table_grad: object
    norms: object


class BackwardLoads(NamedTuple):
    hidden_grad_out: object
    upstream: object
    down: object
    gelu: object
    slope: object
    gate_up: object
    normed_two: object
    hidden: object
    residual: object
    full_gains: object
    heads: object
    query: object
    key: object
    value: object
    logs: object
    mixed: object
    wide_tokens: object


class Moments(NamedTuple):
    heads_in: object
    heads_out: object
    expand_in: object
    expand_out: object
    norm_gains: object
    bias_table: object


class BackwardScratch(NamedTuple):
    load_sems: object
    residual_grad: object
    both_grads: object
    wide_came: object
    down_came: object
    far_send: object
    far_came: object
    across_send: object
    across_came: object
    pair_send: object
    pair_came: object
    pair_across_send: object
    pair_across_came: object
    offered: object
    right: object
    mine_grad: object
    mine_came: object
    mine_sums: object
    small: object
    small_line: object
    small_gains: object
    small_table: object
    norm_part: object
    norm_line: object
    norm_plane: object
    down_stage: object
    mine_stage: object
    out_stage: object
    gains_stage: object
    table_stage: object
    wide_sems: object
    line_sems: object
    attended_sems: object
    right_sems: object
    mine_sems: object
    sums_sems: object
    small_sems: object
    norm_sems: object
    stage_sems: object


def back_loads(values):
    return BackwardLoads(*[getattr(values, name) for name in BackwardLoads._fields])


def ring_backward_kernel(size, depth, span, *refs):
    lens_ref, table_ref = refs[:2]
    refs = refs[2:]
    loaded = len(BackwardLoads._fields)
    sources, normed_source, refs = refs[:loaded], refs[loaded], refs[loaded + 1 :]
    states = [Moments(*refs[6 * number : 6 * number + 6]) for number in range(3)]
    refs = refs[18:]
    outs = len(BackwardOut._fields)
    out, refs = BackwardOut(*refs[:outs]), refs[outs:]
    hand_sems, refs = refs[-1], refs[:-1]
    layer_held, tokens_held, down_held = refs[-3:]
    refs = refs[:-3]
    hands = [
        pltpu.make_async_copy(layer_held, out.layer_out, hand_sems.at[0]),
        pltpu.make_async_copy(tokens_held, out.tokens_grad, hand_sems.at[1]),
        pltpu.make_async_copy(down_held, out.down_grad, hand_sems.at[2]),
    ]
    r, s = BackwardLoads(*refs[:loaded]), BackwardScratch(*refs[loaded:])

    def load_copy(number):
        return pltpu.make_async_copy(sources[number], r[number], s.load_sems.at[number])

    def arrive(*which):
        for number in range(loaded):
            if any(r[number] is ref for ref in which):
                load_copy(number).wait()

    for number in range(loaded):
        load_copy(number).start()
    at = Places(size)
    half = at.half
    rows = r.query.shape[0]
    keys = r.key.shape[0]
    wide = r.residual.shape[1]
    slot = wide // size
    shard = depth // size
    width = r.down.shape[1]
    line = keys // rows
    cut, head_cut = cut_of(width), cut_of(INNER)
    first_row = at.mp * rows
    across, beside, corner = at.mp ^ 2, at.mp ^ 1, at.mp ^ 3
    part_wide = wide // 2

    barrier = pltpu.get_barrier_semaphore()
    for step in range(1, size):
        pl.semaphore_signal(
            barrier, 1, device_id=(lax.rem(at.dp + step, size), at.mp), device_id_type=MESH
        )
    for partner in (across, beside, corner):
        pl.semaphore_signal(barrier, 1, device_id=(at.dp, partner), device_id_type=MESH)
    pl.semaphore_wait(barrier, size + 2)

    def stage_copy(number):
        kind, state = number // 3, states[number % 3]
        index = number % 3
        if kind == 0:
            source, target = state.expand_out, s.down_stage.at[index]
        elif kind == 1:
            source, target = state.heads_in.at[jnp.minimum(at.mp, line - 2)], s.mine_stage.at[index]
        elif kind == 2:
            source, target = state.heads_out, s.out_stage.at[index]
        elif kind == 3:
            source, target = state.expand_in.at[0], r.gelu.at[pl.ds(index * shard, shard)]
        elif kind == 4:
            source, target = state.expand_in.at[1], r.slope.at[pl.ds(index * shard, shard)]
        elif kind == 5:
            source, target = state.norm_gains, s.gains_stage.at[index]
        else:
            source, target = state.bias_table, s.table_stage.at[index]
        return pltpu.make_async_copy(source, target, s.stage_sems.at[number])

    def stage(kind):
        for index in range(3):
            stage_copy(3 * kind + index).start()

    def staged(kind):
        for index in range(3):
            stage_copy(3 * kind + index).wait()

    norm_lane = lax.broadcasted_iota(jnp.int32, (8, LANES), 1)

    def square_sum(values):
        return jnp.sum(jnp.sum(values * values, axis=0, keepdims=True), axis=1, keepdims=True)

    def add_norms(number, weight, gradient, first, second, decay, scale=1.0):
        step_dir = lamb_parts(weight, gradient, first, second, decay)[2]
        mass = square_sum(weight) * scale
        push = square_sum(step_dir) * scale
        s.norm_part[...] = s.norm_part[...] + (
            jnp.where(norm_lane == number, mass, 0.0) + jnp.where(norm_lane == number + 10, push, 0.0)
        )

    s.norm_part[...] = jnp.zeros((8, LANES), f32)

    def slab_rows(owner):
        return pl.ds(pl.multiple_of(owner * slot, slot), slot)

    def block_rows(number):
        return pl.ds(number * rows, rows)

    def piece_lanes(piece):
        return pl.ds(0, cut) if piece % 2 == 0 else pl.ds(cut, width - cut)

    def piece_slice(piece):
        return slice(0, cut) if piece % 2 == 0 else slice(cut, width)

    def piece_term(piece, owner):
        if piece < 4:
            return r.gate_up.at[piece // 2, slab_rows(owner), piece_lanes(piece)]
        return r.hidden_grad_out.at[slab_rows(owner), piece_lanes(piece)]

    def piece_buffer(piece, side, hop):
        if piece < 4:
            return s.wide_came.at[side, hop, piece // 2, :, piece_lanes(piece)]
        return s.down_came.at[side, hop, :, piece_lanes(piece)]

    def piece_starts(piece, side):
        return piece in ((0, 3, 4), (1, 2, 5))[side]

    def piece_target(side, hop):
        return at.owner(half - hop if side == 0 else hop - half)

    def piece_has(piece, side, hop):
        return hop > 0 or piece_starts(piece, side)

    def piece_copy(piece, side, hop):
        fresh = hop == 0 or (hop == 1 and not piece_starts(piece, side))
        source = (
            piece_term(piece, piece_target(side, hop))
            if fresh
            else piece_buffer(piece, side, hop - 1)
        )
        if fresh and piece > 3:
            source = sources[0].at[slab_rows(piece_target(side, hop)), piece_lanes(piece)]
        return remote(
            source, piece_buffer(piece, side, hop), s.wide_sems.at[0, piece, side, hop],
            s.wide_sems.at[1, piece, side, hop], at.sides[side], at.mp,
        )

    def serve(piece, hop, sides=(0, 1)):
        for side in sides:
            if not piece_has(piece, side, hop):
                continue
            if hop > 0 and piece_has(piece, side, hop - 1):
                piece_copy(piece, side, hop - 1).wait_recv()
                came = piece_buffer(piece, side, hop - 1)
                term = piece_term(piece, piece_target(side, hop))
                came[...] = (came[...].astype(f32) + term[...].astype(f32)).astype(bf16)
            piece_copy(piece, side, hop).start()

    def finish(piece):
        for side in range(2):
            piece_copy(piece, side, half - 1).wait_recv()
        term = piece_term(piece, at.dp)
        return (
            term[...].astype(f32)
            + piece_buffer(piece, 0, half - 1)[...].astype(f32)
            + piece_buffer(piece, 1, half - 1)[...].astype(f32)
        )

    def mine_lanes(side, hop):
        if hop > 0:
            return pl.ds(0, INNER)
        return pl.ds(0, head_cut) if side == 0 else pl.ds(head_cut, INNER - head_cut)

    def mine_copy(side, hop):
        lanes = mine_lanes(side, hop)
        source = (
            s.mine_grad.at[slab_rows(piece_target(side, hop)), lanes]
            if hop == 0
            else s.mine_came.at[side, hop - 1, :, lanes]
        )
        return remote(
            source, s.mine_came.at[side, hop, :, lanes], s.mine_sems.at[0, side, hop],
            s.mine_sems.at[1, side, hop], at.sides[side], at.mp,
        )

    def mine_serve(hop):
        for side in range(2):
            if hop > 0:
                mine_copy(side, hop - 1).wait_recv()
                came = s.mine_came.at[side, hop - 1]
                term = s.mine_grad.at[slab_rows(piece_target(side, hop))]
                lanes = mine_lanes(side, hop - 1)
                if hop == 1:
                    keep = pl.ds(head_cut, INNER - head_cut) if side == 0 else pl.ds(0, head_cut)
                    came[:, keep] = term[:, keep]
                came[:, lanes] = (
                    came[:, lanes].astype(f32) + term[:, lanes].astype(f32)
                ).astype(bf16)
            mine_copy(side, hop).start()

    def far_copy(number):
        send = (s.far_send, s.across_send, s.far_send, s.across_send, s.pair_send, s.pair_across_send)
        came = (s.far_came, s.across_came, s.far_came, s.across_came)
        came = came + (s.pair_came, s.pair_across_came)
        return remote(
            send[number], came[number], s.line_sems.at[0, number], s.line_sems.at[1, number],
            at.dp, beside if number % 2 == 0 else across,
        )

    def attended_copy(number):
        source, target, partner = ((0, 1, across), (0, 2, beside), (1, 3, beside))[number]
        return remote(
            r.upstream.at[block_rows(source)], r.upstream.at[block_rows(target)],
            s.attended_sems.at[0, number], s.attended_sems.at[1, number], at.dp, partner,
        )

    def near_write(array, tile, values):
        array[tile * 2 * rows : (tile + 1) * 2 * rows, :part_wide] = values

    def near_read(array, number):
        return jnp.concatenate(
            [
                array[2 * rows * tile + number * rows : 2 * rows * tile + (number + 1) * rows, :part_wide]
                for tile in range(2)
            ],
            axis=1,
        )

    def part_of(tile):
        return slice(tile * part_wide, (tile + 1) * part_wide)

    for piece in (4, 5):
        serve(piece, 0)
    serve(4, 1, (1,))
    serve(5, 1, (0,))
    arrive(r.upstream, r.down, r.gelu, r.slope, r.hidden_grad_out)
    for number in (2, 3, 0, 1):
        place = block_rows(number)
        hidden_grad = matmul(r.upstream[place, :], r.down[...])
        s.both_grads[0, place, :] = (hidden_grad * r.slope[place, :]).astype(bf16)
        s.both_grads[1, place, :] = (hidden_grad * r.gelu[place, :]).astype(bf16)
        if number == 3:
            serve(4, 1, (0,))
            serve(5, 1, (1,))
    arrive(r.gate_up)
    for kind in (0, 1, 2, 5, 6):
        stage(kind)

    def normed_tile(first, tile):
        place = pl.ds(first, 2 * rows)
        return contract_cols(
            s.both_grads[0, place, :], r.gate_up[0, part_of(tile), :]
        ) + contract_cols(s.both_grads[1, place, :], r.gate_up[1, part_of(tile), :])

    for tile in range(2):
        s.far_send[:, part_of(tile)] = normed_tile(2 * rows, tile).astype(bf16)
    far_copy(0).start()
    serve(4, 2)
    for tile in range(2):
        near_write(r.slope, tile, normed_tile(0, tile))
    serve(5, 2)
    far_copy(0).wait()
    s.across_send[...] = (near_read(r.slope, 1) + s.far_came[rows:, :].astype(f32)).astype(bf16)
    far_copy(1).start()

    arrive(r.normed_two)
    tiles = 4
    tile_wide = wide // tiles
    for matrix in range(2):
        for tile in range(tiles):
            lanes = slice(tile * tile_wide, (tile + 1) * tile_wide)
            r.gate_up[matrix, lanes, :] = contract_rows(
                r.normed_two[:, lanes], s.both_grads[matrix]
            ).astype(bf16)
        if matrix == 1:
            serve(5, 3)
        serve(2 * matrix, 0)
        serve(2 * matrix + 1, 0)
        serve(2 * matrix, 1, (1 - matrix,))
        serve(2 * matrix + 1, 1, (matrix,))
        if matrix == 0:
            serve(4, 3)

    normed_load = pltpu.make_async_copy(
        normed_source, r.normed_two, s.load_sems.at[loaded]
    )
    normed_load.start()
    arrive(r.residual, r.full_gains, r.heads, r.query, r.key, r.value, r.logs, r.mixed)

    far_copy(1).wait()
    grad = (
        near_read(r.slope, 0) + s.far_came[:rows, :].astype(f32) + s.across_came[...].astype(f32)
    )
    through, gain_two_grad = norm_backward(r.residual[...], r.full_gains[1:2, :], grad, depth)
    residual_grad = r.upstream[:rows, :].astype(f32) + through
    s.residual_grad[...] = residual_grad
    attended = residual_grad.astype(bf16)
    r.upstream[:rows, :] = attended
    for number in range(2):
        attended_copy(number).start()
    mixed_grad_all = matmul(attended, r.heads[3]).astype(bf16)

    values = offset_values(head_table(table_ref), first_row, rows, span)
    allowed = allowed_pairs(lens_ref, first_row, rows, keys)
    offsets = []
    for pair in range(PAIRS):
        part = slice(pair * LANES, (pair + 1) * LANES)
        query_grad, key_grad, value_grad, pair_offsets = attend_pair_backward(
            pair, r.query, r.key, r.value, r.logs, mixed_grad_all[:, part], values, allowed, span,
        )
        s.offered[0, :, part] = query_grad.astype(bf16)
        r.slope[:, part] = key_grad
        r.slope[:, INNER + pair * LANES : INNER + (pair + 1) * LANES] = value_grad
        offsets = offsets + pair_offsets
        if pair == 0:
            serve(0, 1, (0,))
            serve(1, 1, (1,))
        if pair == 1:
            serve(2, 1, (1,))
            serve(3, 1, (0,))
    pair_wide = 2 * INNER
    for number, bit in ((0, 1), (1, 3)):
        place = pl.ds(pl.multiple_of((at.mp ^ bit) * rows, rows), rows)
        s.pair_send[number * rows : (number + 1) * rows, :] = r.slope[place, :pair_wide].astype(bf16)
    far_copy(4).start()
    s.offered[3] = r.mixed[...]
    far_copy(4).wait_recv()
    place = pl.ds(pl.multiple_of(across * rows, rows), rows)
    s.pair_across_send[...] = (
        r.slope[place, :pair_wide] + s.pair_came[rows:, :].astype(f32)
    ).astype(bf16)
    far_copy(5).start()
    attended_copy(0).wait_recv()
    attended_copy(2).start()

    arrive(r.hidden)

    def feed_tile(first, tile):
        return contract_cols(r.hidden[pl.ds(first, 2 * rows), :], r.down[part_of(tile), :])

    for tile in range(2):
        s.far_send[:, part_of(tile)] = feed_tile(2 * rows, tile).astype(bf16)
    far_copy(2).start()
    for tile in range(2):
        near_write(r.gelu, tile, feed_tile(0, tile))
    serve(0, 2)
    serve(1, 2)
    far_copy(5).wait_recv()
    place = pl.ds(pl.multiple_of(at.mp * rows, rows), rows)
    both = (
        r.slope[place, :pair_wide]
        + s.pair_came[:rows, :].astype(f32)
        + s.pair_across_came[...].astype(f32)
    ).astype(bf16)
    s.offered[1] = both[:, :INNER]
    s.offered[2] = both[:, INNER:]
    stage(4)

    def right_copy(number):
        partner = (across, beside, corner)[number - 1]
        return remote(
            s.offered.at[partner], s.right.at[block_rows(number)],
            s.right_sems.at[0, number], s.right_sems.at[1, number], at.dp, partner,
        )

    for number in range(1, line):
        right_copy(number).start()
    s.right[block_rows(0), :] = s.offered[at.mp]
    grad = (
        contract_cols(s.offered[0], r.heads[0])
        + contract_cols(s.offered[1], r.heads[1])
        + contract_cols(s.offered[2], r.heads[2])
    )
    arrive(r.wide_tokens)
    through, gain_one_grad = norm_backward(
        r.wide_tokens[...].astype(f32), r.full_gains[0:1, :], grad, depth
    )
    s.residual_grad[...] = s.residual_grad[...] + through

    offset_grad = jnp.concatenate(offsets + [jnp.zeros((8 - HEADS, span), f32)], axis=0)
    reach = lax.broadcasted_iota(jnp.int32, (8, span), 1) - (rows - 1) - first_row
    reach = bucket_ids(reach)
    table_grad = jnp.zeros((8, LANES), f32)
    buckets = table_ref.shape[1]
    for number in range(buckets):
        mass = jnp.sum(jnp.where(reach == number, offset_grad, 0.0), axis=1, keepdims=True)
        table_grad = jnp.where(norm_lane == number, mass, table_grad)
    s.small[0, :, wide:] = table_grad
    s.small[0, 0:1, :wide] = gain_one_grad
    s.small[0, 1:2, :wide] = gain_two_grad
    s.small[0, 2:, :wide] = jnp.zeros((6, wide), f32)

    def line_spread(source, slots, sems, first):
        copies = [
            remote(
                source, slots.at[at.mp], sems.at[first, step], sems.at[first + 1, step],
                at.dp, lax.rem(at.mp + step, line),
            )
            for step in range(1, line)
        ]
        for copy in copies:
            copy.start()
        slots[at.mp] = source[...]
        return copies

    def slot_total(slots, count):
        total = slots[0]
        for number in range(1, count):
            total = total + slots[number]
        return total

    small_copies = line_spread(s.small.at[0], s.small_line, s.small_sems, 0)
    serve(2, 2)
    far_copy(2).wait_recv()
    s.across_send[...] = (
        near_read(r.gelu, 1) + s.far_came[rows:, :].astype(f32)
    ).astype(bf16)
    far_copy(3).start()
    serve(3, 2)

    normed_load.wait()
    for number in range(1, 3):
        attended_copy(number).wait_recv()
    for number in range(1, line):
        right_copy(number).wait_recv()
    last = at.mp == line - 1
    for tile in range(tiles):
        lanes = slice(tile * tile_wide, (tile + 1) * tile_wide)
        left = jnp.where(last, r.upstream[:, lanes], r.normed_two[:, lanes])
        s.mine_grad[lanes, :] = contract_rows(left, s.right[...]).astype(bf16)
    mine_serve(0)

    for copy in small_copies:
        copy.wait()
    s.small[1] = slot_total(s.small_line, line)
    pair_slot = 2 * slot
    plane_copies = []
    for step in range(1, size):
        target = lax.rem(at.dp + step, size)
        lanes = pl.ds(pl.multiple_of(target // 2 * pair_slot, pair_slot), pair_slot)
        plane_copies.append(
            remote(
                s.small.at[1, :, lanes], s.small_gains.at[at.dp], s.small_sems.at[2, step],
                s.small_sems.at[3, step], target, at.mp,
            )
        )
        plane_copies.append(
            remote(
                s.small.at[1, :, pl.ds(wide, LANES)], s.small_table.at[at.dp],
                s.small_sems.at[4, step], s.small_sems.at[5, step], target, at.mp,
            )
        )
    for copy in plane_copies:
        copy.start()
    lanes = pl.ds(pl.multiple_of(at.dp // 2 * pair_slot, pair_slot), pair_slot)
    s.small_gains[at.dp] = s.small[1, :, lanes]
    s.small_table[at.dp] = s.small[1, :, wide:]

    serve(0, 3)
    mine_serve(1)
    serve(1, 3)
    down_total = jnp.concatenate([finish(4), finish(5)], axis=1)
    down_total = down_total[:shard]
    down_held[...] = down_total
    hands[2].start()
    staged(0)
    add_norms(
        6, s.down_stage[0], down_total, s.down_stage[1], s.down_stage[2], weight_decay
    )
    mine_serve(2)
    serve(2, 3)
    for copy in plane_copies:
        copy.wait()
    gains_total = slot_total(s.small_gains, size)
    odd = lax.rem(at.dp, 2) == 1
    gains_total = jnp.where(odd, pltpu.roll(gains_total, slot, 1), gains_total)[:2, :shard]
    out.gains_grad[...] = gains_total
    staged(5)
    for number in range(2):
        row = slice(number, number + 1)
        add_norms(
            7 + number, s.gains_stage[0, row], gains_total[row], s.gains_stage[1, row],
            s.gains_stage[2, row], 0.0, 1.0 / line,
        )
    table_total = slot_total(s.small_table, size)[:HEADS, :buckets]
    out.table_grad[...] = table_total
    staged(6)
    add_norms(
        9, s.table_stage[0], table_total, s.table_stage[1], s.table_stage[2], 0.0,
        1.0 / (line * size),
    )
    far_copy(3).wait_recv()
    layer_out = (
        r.residual[...]
        + (
            near_read(r.gelu, 0)
            + s.far_came[:rows, :].astype(f32)
            + s.across_came[...].astype(f32)
        )
    ).astype(bf16)
    stage(3)
    def grad_copy(matrix):
        held = (r.gelu, r.slope)[matrix]
        return pltpu.make_async_copy(
            held.at[pl.ds(3 * shard, shard)], out.gate_up_grad.at[matrix], s.stage_sems.at[21 + matrix]
        )

    def close(piece):
        total = finish(piece)[:shard]
        lanes = piece_slice(piece)
        held = (r.gelu, r.slope)[piece // 2]
        held[3 * shard : 4 * shard, lanes] = total
        if piece % 2 == 1:
            grad_copy(piece // 2).start()
        add_norms(
            4 + piece // 2, held[:shard, lanes], total, held[shard : 2 * shard, lanes],
            held[2 * shard : 3 * shard, lanes], weight_decay,
        )

    mine_serve(3)
    serve(3, 3)
    staged(3)
    close(0)
    close(1)
    coarse = s.residual_grad[...].astype(bf16)
    fine = (s.residual_grad[...] - coarse.astype(f32)).astype(bf16)
    tile = 3 * LANES
    for low in range(0, depth, tile):
        high = min(low + tile, depth)
        layer_held[:, low:high] = gathered_tile(
            layer_out, None, low, high, shard, slot
        ).astype(bf16)
        tokens_held[:, low:high] = gathered_tile(coarse, fine, low, high, shard, slot)
    hands[0].start()
    hands[1].start()

    staged(4)
    close(2)

    for side in range(2):
        mine_copy(side, half - 1).wait_recv()
    mine_total = (
        s.mine_grad[slab_rows(at.dp), :].astype(f32)
        + s.mine_came[0, half - 1].astype(f32)
        + s.mine_came[1, half - 1].astype(f32)
    ).astype(bf16)
    s.mine_sums[at.mp] = mine_total

    def sums_copy(number):
        partner = (across, beside, corner)[number - 1]
        return remote(
            s.mine_sums.at[at.mp], s.mine_sums.at[at.mp],
            s.sums_sems.at[0, number], s.sums_sems.at[1, number], at.dp, partner,
        )

    for number in range(1, line):
        sums_copy(number).start()
    staged(1)
    staged(2)

    def mine_state(index):
        return jnp.where(last, s.out_stage[index], s.mine_stage[index])

    add_norms(
        at.mp, mine_state(0), mine_total.astype(f32)[:shard], mine_state(1), mine_state(2),
        weight_decay,
    )

    close(3)

    norm_copies = line_spread(s.norm_part, s.norm_line, s.norm_sems, 0)
    for copy in norm_copies:
        copy.wait()
    s.norm_part[...] = slot_total(s.norm_line, line)
    norm_copies = [
        remote(
            s.norm_part, s.norm_plane.at[at.dp], s.norm_sems.at[2, step], s.norm_sems.at[3, step],
            lax.rem(at.dp + step, size), at.mp,
        )
        for step in range(1, size)
    ]
    for copy in norm_copies:
        copy.start()
    s.norm_plane[at.dp] = s.norm_part[...]

    for side in range(2):
        for hop in range(half):
            mine_copy(side, hop).wait_send()
            for piece in range(6):
                if piece_has(piece, side, hop):
                    piece_copy(piece, side, hop).wait_send()
    for number in range(2, 6):
        far_copy(number).wait_send()
    for number in range(3):
        attended_copy(number).wait_send()
    for number in range(1, line):
        right_copy(number).wait_send()
    for number in range(1, line):
        sums_copy(number).wait()
    for number in range(line - 1):
        out.heads_in_grad[number] = s.mine_sums[number].astype(f32)[:shard]
    out.heads_out_grad[...] = s.mine_sums[line - 1].astype(f32)[:shard]
    for copy in norm_copies:
        copy.wait()
    out.norms[...] = slot_total(s.norm_plane, size)
    for matrix in range(2):
        grad_copy(matrix).wait()
    for hand in hands:
        hand.wait()


def ring_backward(size, line, depth, slot, width, span, lens, table, got, states):
    rows = got.query.shape[0]
    wide, keys, half = size * slot, rows * line, size // 2
    shard, buckets = depth // size, table.shape[1]
    shapes = forward_shapes(rows, line, size, slot, width, span)
    dma = pltpu.SemaphoreType.DMA
    far = list(back_loads(got)) + [got.normed] + [array for state in states for array in state]
    operands = [lens, table] + far
    specs = [
        pl.BlockSpec(memory_space=pltpu.SMEM),
        pl.BlockSpec(memory_space=pltpu.VMEM),
    ] + [pl.BlockSpec(memory_space=pl.ANY)] * len(far)
    outs = BackwardOut(
        layer_out=((rows, depth), bf16),
        tokens_grad=((rows, depth), f32),
        heads_in_grad=((line - 1, shard, INNER), f32),
        heads_out_grad=((shard, INNER), f32),
        gate_up_grad=((2, shard, width), f32),
        down_grad=((shard, width), f32),
        gains_grad=((2, shard), f32),
        table_grad=((HEADS, buckets), f32),
        norms=((8, LANES), f32),
    )
    handed = (outs.gate_up_grad, outs.layer_out, outs.tokens_grad, outs.down_grad)
    half_rows = pltpu.VMEM((2 * rows, wide), bf16)
    block = pltpu.VMEM((rows, wide), bf16)
    loads = back_loads(shapes)
    scratch = BackwardScratch(
        load_sems=dma((len(loads) + 1,)),
        residual_grad=pltpu.VMEM((rows, wide), f32),
        both_grads=pltpu.VMEM((2, keys, width), bf16),
        wide_came=pltpu.VMEM((2, half, 2, slot, width), bf16),
        down_came=pltpu.VMEM((2, half, slot, width), bf16),
        far_send=half_rows,
        far_came=half_rows,
        across_send=block,
        across_came=block,
        pair_send=pltpu.VMEM((2 * rows, 2 * INNER), bf16),
        pair_came=pltpu.VMEM((2 * rows, 2 * INNER), bf16),
        pair_across_send=pltpu.VMEM((rows, 2 * INNER), bf16),
        pair_across_came=pltpu.VMEM((rows, 2 * INNER), bf16),
        offered=pltpu.VMEM((line, rows, INNER), bf16),
        right=pltpu.VMEM((keys, INNER), bf16),
        mine_grad=pltpu.VMEM((wide, INNER), bf16),
        mine_came=pltpu.VMEM((2, half, slot, INNER), bf16),
        mine_sums=pltpu.VMEM((line, slot, INNER), bf16),
        small=pltpu.VMEM((2, 8, wide + LANES), f32),
        small_line=pltpu.VMEM((line, 8, wide + LANES), f32),
        small_gains=pltpu.VMEM((size, 8, 2 * slot), f32),
        small_table=pltpu.VMEM((size, 8, LANES), f32),
        norm_part=pltpu.VMEM((8, LANES), f32),
        norm_line=pltpu.VMEM((line, 8, LANES), f32),
        norm_plane=pltpu.VMEM((size, 8, LANES), f32),
        down_stage=pltpu.VMEM((3, shard, width), f32),
        mine_stage=pltpu.VMEM((3, shard, INNER), f32),
        out_stage=pltpu.VMEM((3, shard, INNER), f32),
        gains_stage=pltpu.VMEM((3, 2, shard), f32),
        table_stage=pltpu.VMEM((3, HEADS, buckets), f32),
        wide_sems=dma((2, 6, 2, half)),
        line_sems=dma((2, 6)),
        attended_sems=dma((2, 3)),
        right_sems=dma((2, line)),
        mine_sems=dma((2, 2, half)),
        sums_sems=dma((2, line)),
        small_sems=dma((6, size)),
        norm_sems=dma((4, size)),
        stage_sems=dma((23,)),
    )
    flops = 2 * keys * wide * (6 * width + INNER) + 16 * rows * wide * INNER
    results = pl.pallas_call(
        partial(ring_backward_kernel, size, depth, span),
        out_shape=[jax.ShapeDtypeStruct(*shape) for shape in outs],
        in_specs=specs,
        out_specs=[
            pl.BlockSpec(memory_space=pl.ANY if any(shape is one for one in handed) else pltpu.VMEM)
            for shape in outs
        ],
        scratch_shapes=[pltpu.VMEM(*shape) for shape in loads]
        + list(scratch)
        + [pltpu.VMEM(*shape) for shape in handed[1:]]
        + [dma((3,))],
        compiler_params=pltpu.CompilerParams(
            collective_id=5, has_side_effects=True, vmem_limit_bytes=BACKWARD_BYTES
        ),
        cost_estimate=pl.CostEstimate(flops=flops, bytes_accessed=50 * 2**20, transcendentals=0),
        name="ring_backward",
    )(*operands)
    return BackwardOut(*results)


class UpdateOut(NamedTuple):
    layer_out: object
    tokens_grad: object
    first: object
    second: object
    new: object
    copy: object
    norms: object


def update_kernel(*refs):
    norms_ref, layer_source, tokens_source = refs[:3]
    sources = [refs[3 + 6 * kind : 9 + 6 * kind] for kind in range(4)]
    refs = refs[27:]
    layer_target, tokens_target = refs[:2]
    targets = [refs[2 + 6 * kind : 8 + 6 * kind] for kind in range(4)]
    norms_out = refs[26]
    refs = refs[27:]
    held = [refs[6 * kind : 6 * kind + 6] for kind in range(5)]
    layer_held, tokens_held, load_sems, store_sems = refs[30:]
    parts = [(number, None) for number in (5, 4, 1)]
    parts = parts + [(0, index) for index in range(held[0][0].shape[0])]
    parts = parts + [(2, 0), (2, 1), (3, None)]

    def view(ref, index):
        return ref if index is None else ref.at[index]

    def load_copy(spot, kind):
        number, index = parts[spot]
        return pltpu.make_async_copy(
            view(sources[kind][number], index), view(held[kind][number], index),
            load_sems.at[spot, kind],
        )

    def store_copy(spot, kind):
        number, index = parts[spot]
        return pltpu.make_async_copy(
            view(held[kind + 1][number], index), view(targets[kind][number], index),
            store_sems.at[spot, kind],
        )

    passed = [
        pltpu.make_async_copy(layer_source, layer_held, load_sems.at[len(parts), 0]),
        pltpu.make_async_copy(tokens_source, tokens_held, load_sems.at[len(parts), 1]),
    ]
    handed = [
        pltpu.make_async_copy(layer_held, layer_target, store_sems.at[len(parts), 0]),
        pltpu.make_async_copy(tokens_held, tokens_target, store_sems.at[len(parts), 1]),
    ]
    for spot in range(len(parts)):
        for kind in range(4):
            load_copy(spot, kind).start()
    for copy in passed:
        copy.start()
    roots = jnp.sqrt(norms_ref[...])
    count = norms_out.shape[1]
    steps = pltpu.roll(roots, LANES - count, 1)
    norms_out[...] = jnp.concatenate([roots[:1], steps[:1]], axis=0)[:, :count]
    lane = lax.broadcasted_iota(jnp.int32, roots.shape, 1)
    rates = learn_rate * roots / jnp.where(lane < count, steps, 1.0)
    starts = (0, 3, 4, 6, 7, 9)
    for spot, (number, index) in enumerate(parts):
        for kind in range(4):
            load_copy(spot, kind).wait()
        gradient, first, second, weight, copy = [view(held[kind][number], index) for kind in range(5)]
        decay = 0.0 if number > 3 else weight_decay
        rate = rates[:1, starts[number] + (index or 0) : starts[number] + (index or 0) + 1]
        if number == 4:
            rate = jnp.concatenate([rate, rates[:1, starts[number] + 1 : starts[number] + 2]], axis=0)
        old = weight[...]
        new_first, new_second, step_dir = lamb_parts(
            old, gradient[...], first[...], second[...], decay
        )
        new = old - rate * step_dir
        first[...] = new_first
        second[...] = new_second
        weight[...] = new
        copy[...] = new.astype(bf16)
        for kind in range(4):
            store_copy(spot, kind).start()
    for number in range(2):
        passed[number].wait()
        handed[number].start()
    for copy in handed:
        copy.wait()
    for spot in range(len(parts)):
        for kind in range(4):
            store_copy(spot, kind).wait()


def update_all(norms, layer_out, tokens_grad, grads, firsts, seconds, weights, count):
    far = [layer_out, tokens_grad] + list(grads) + list(firsts) + list(seconds) + list(weights)
    shapes = [array.shape for array in grads]
    outs = [(layer_out.shape, bf16), (tokens_grad.shape, f32)]
    for kind in (f32, f32, f32, bf16):
        outs = outs + [(shape, kind) for shape in shapes]
    outs = outs + [((2, count), f32)]
    held = []
    for kind in (f32, f32, f32, f32, bf16):
        held = held + [pltpu.VMEM(shape, kind) for shape in shapes]
    held = held + [pltpu.VMEM(layer_out.shape, bf16), pltpu.VMEM(tokens_grad.shape, f32)]
    spots = 6 + shapes[0][0] + 1
    size = sum(array.size * 4 for array in far)
    any_spec = pl.BlockSpec(memory_space=pl.ANY)
    vmem_spec = pl.BlockSpec(memory_space=pltpu.VMEM)
    results = pl.pallas_call(
        update_kernel,
        out_shape=[jax.ShapeDtypeStruct(*out) for out in outs],
        in_specs=[vmem_spec] + [any_spec] * len(far),
        out_specs=[any_spec] * (len(outs) - 1) + [vmem_spec],
        scratch_shapes=held
        + [pltpu.SemaphoreType.DMA((spots, 4)), pltpu.SemaphoreType.DMA((spots, 4))],
        compiler_params=pltpu.CompilerParams(vmem_limit_bytes=VMEM_BYTES),
        cost_estimate=pl.CostEstimate(flops=size * 4, bytes_accessed=2 * size, transcendentals=size),
        name="update",
    )(norms, *far)
    kinds = [results[2 + 6 * kind : 8 + 6 * kind] for kind in range(4)]
    return UpdateOut(results[0], results[1], *kinds, results[26])


def plain_gradients(
    tokens,
    cotangent,
    lengths,
    heads_in,
    heads_out,
    expand_in,
    expand_out,
    norm_gains,
    bias_table,
):
    rows, depth = tokens.shape
    mp_size = lax.axis_size("mp")
    mp_spot = lax.axis_index("mp")
    keys = rows * mp_size
    span = -(-(keys + rows - 1) // LANES) * LANES
    first_row = mp_spot * rows
    shard_width = norm_gains.shape[1]
    buckets = bias_table.shape[0]

    four = jnp.concatenate([heads_in, heads_out.T[None]], axis=0).astype(bf16)
    mine = lax.dynamic_slice_in_dim(four, mp_spot, 1, axis=0)
    mine_all = gather_dp(mine)
    full_gains = gather_gains(norm_gains.astype(bf16).astype(f32))
    gain_one, gain_two = full_gains[0:1], full_gains[1:2]
    inputs = tokens.astype(f32)
    normed = rms_scale(inputs, gain_one, depth).astype(bf16)
    normed_parts = gather_mp(normed)
    used = first_row + jnp.arange(rows, dtype=jnp.int32) < lengths[0, 0] + lengths[0, 1]
    upstream = jnp.where(used[:, None], cotangent, jnp.zeros_like(cotangent))
    upstream_parts = gather_mp(upstream)

    mine_parts = gather_mp(mine_all)
    by_bit = jnp.concatenate([mine_parts[0], mine_parts[2], mine_parts[1], mine_parts[3]], axis=0)
    full_heads = jnp.concatenate(
        [lax.dynamic_slice_in_dim(by_bit, mp_spot ^ number, 1, axis=0) for number in range(mp_size)],
        axis=0,
    )
    wide_in = gather_dp(expand_in.astype(bf16))
    wide_out = gather_dp(expand_out.T.astype(bf16)[None])[0]

    table = jnp.pad(bias_table.T, ((0, 8 - HEADS), (0, 0)))
    attention_flops = rows * keys * LANES * HEADS
    mixed, query, key, value, logs, residual, normed_two = vmem_call(
        partial(forward_kernel, span, depth),
        [
            ((rows, INNER), bf16),
            ((rows, INNER), bf16),
            ((keys, INNER), bf16),
            ((keys, INNER), bf16),
            ((rows, LANES), f32),
            ((rows, depth), f32),
            ((rows, depth), bf16),
        ],
        (
            2 * depth * INNER * (2 * keys + 2 * rows) + 4 * attention_flops,
            2 * (4 * depth * INNER + 2 * keys * depth),
            rows * keys * HEADS,
        ),
        name="attention_forward",
        smem_first=True,
    )(lengths, *normed_parts, full_heads, table, tokens, gain_two)

    normed_all = jnp.concatenate(gather_mp(normed_two), axis=0)
    upstream_all = jnp.concatenate(upstream_parts, axis=0)
    gate_pre = matmul(normed_all, wide_in[0])
    up_pre = matmul(normed_all, wide_in[1])
    gelu_gate, gelu_pull = jax.vjp(partial(jax.nn.gelu, approximate=True), gate_pre)
    hidden = (gelu_gate * up_pre).astype(bf16)
    expand_out_grad = scatter_dp(contract_rows(upstream_all, hidden).astype(bf16)[None])[0].T
    feed_part = contract_cols(hidden, wide_out).astype(bf16)
    feed_near = feed_part[: 2 * rows].astype(f32) + swap(feed_part[2 * rows :], 1).astype(f32)
    feed_out = feed_near[:rows] + swap(feed_near[rows:].astype(bf16), 2).astype(f32)
    layer_out = (residual + feed_out).astype(bf16)

    hidden_grad = matmul(upstream_all, wide_out)
    up_grad = (hidden_grad * gelu_gate).astype(bf16)
    gate_grad = gelu_pull(hidden_grad * up_pre)[0].astype(bf16)
    normed_part = contract_cols(gate_grad, wide_in[0]) + contract_cols(up_grad, wide_in[1])
    normed_near = normed_part[: 2 * rows] + swap(normed_part[2 * rows :].astype(bf16), 1).astype(f32)
    normed_across = swap(normed_near[rows:].astype(bf16), 2)
    expand_in_grad = scatter_dp(
        jnp.stack(
            [
                contract_rows(normed_all, gate_grad).astype(bf16),
                contract_rows(normed_all, up_grad).astype(bf16),
            ]
        )
    )

    residual_grad, attended_grad, query_grad, near, far, offset_grad, gain_two_grad = vmem_call(
        partial(backward_kernel, span, depth),
        [
            ((rows, depth), f32),
            ((rows, depth), bf16),
            ((rows, INNER), bf16),
            ((2 * rows, 2 * INNER), f32),
            ((2 * rows, 2 * INNER), bf16),
            ((8, span), f32),
            ((1, depth), f32),
        ],
        (
            2 * depth * INNER * rows + 10 * attention_flops,
            rows * depth * 16 + 2 * (4 * depth * INNER + 2 * keys * INNER),
            rows * keys * HEADS,
        ),
        scratch=[pltpu.VMEM((keys, 2 * INNER), f32)],
        name="attention_backward",
        smem_first=True,
    )(
        lengths,
        normed_near[:rows],
        normed_across,
        residual,
        upstream,
        gain_two,
        full_heads,
        query,
        key,
        value,
        logs,
        table,
    )
    attended_parts = gather_mp(attended_grad)
    beside = swap(far, 1)
    across = swap((near[rows:] + beside[rows:].astype(f32)).astype(bf16), 2)
    tokens_grad, both, gain_one_grad = vmem_call(
        partial(input_kernel, depth),
        [((rows, depth), f32), ((rows, 2 * INNER), bf16), ((1, depth), f32)],
        (6 * rows * depth * INNER, rows * depth * 14 + 8 * depth * INNER, 0),
        name="input_backward",
    )(near, beside, across, query_grad, full_heads, tokens, gain_one, residual_grad)

    offered = jnp.stack([query_grad, both[:, :INNER], both[:, INNER:], mixed])

    def for_bit(bit):
        return lax.dynamic_slice_in_dim(offered, mp_spot ^ bit, 1, axis=0)

    from_beside = swap(jnp.concatenate([for_bit(1), for_bit(3)], axis=0), 1)
    from_across = swap(jnp.concatenate([for_bit(2), from_beside[1:]], axis=0), 2)
    right = jnp.concatenate(
        [for_bit(0)[0], from_across[0], from_beside[0], from_across[1]], axis=0
    )
    left = jnp.where(
        mp_spot == mp_size - 1,
        jnp.concatenate(attended_parts, axis=0),
        jnp.concatenate(normed_parts, axis=0),
    )
    mine_grad = scatter_dp(contract_rows(left, right).astype(bf16)[None]).astype(bf16)
    grad_parts = gather_mp(mine_grad)
    grads_by_bit = jnp.concatenate(
        [grad_parts[0], grad_parts[2], grad_parts[1], grad_parts[3]], axis=0
    )
    heads_grad = [
        lax.dynamic_slice_in_dim(grads_by_bit, mp_spot ^ number, 1, axis=0)
        for number in range(mp_size)
    ]
    head_in_grad = jnp.concatenate(heads_grad[:3], axis=0).astype(f32)
    head_out_grad = heads_grad[3][0].T.astype(f32)

    reach = jnp.arange(span, dtype=jnp.int32) - (rows - 1) - first_row
    onehot = (bucket_ids(reach)[:, None] == jnp.arange(buckets, dtype=jnp.int32)[None, :]).astype(f32)
    table_part = jnp.dot(offset_grad, onehot, precision=highest)[:HEADS].T
    gain_parts = jnp.concatenate([gain_one_grad, gain_two_grad], axis=0)
    small = total_all(pack_rows([gain_parts, table_part]), 1).reshape(-1)
    gains_total = small[: 2 * depth].reshape(2, depth)
    table_grad = small[2 * depth : 2 * depth + buckets * HEADS].reshape(buckets, HEADS)
    gains_grad = lax.dynamic_slice_in_dim(
        gains_total, lax.axis_index("dp") * shard_width, shard_width, 1
    )

    return layer_out, tokens_grad, (
        head_in_grad,
        head_out_grad,
        expand_in_grad,
        expand_out_grad,
        gains_grad,
        table_grad,
    )


def ring_step(
    tokens, cotangent, lengths, heads_in, heads_out, expand_in, expand_out, norm_gains, bias_table, firsts, seconds
):
    rows, depth = tokens.shape
    size, line = lax.axis_size("dp"), lax.axis_size("mp")
    span = -(-(rows * line + rows - 1) // LANES) * LANES
    width = expand_in.shape[2]
    slot = -(-norm_gains.shape[1] // 16) * 16
    weights = Moments(heads_in, heads_out, expand_in, expand_out, norm_gains, bias_table)
    weights, firsts, seconds = [
        Moments(state[0], state[1].T, state[2], state[3].T, state[4], state[5].T)
        for state in (weights, firsts, seconds)
    ]
    got = ring_forward(
        size, line, depth, slot, width, span,
        (lengths, tokens, cotangent, norm_gains, weights.bias_table) + tuple(weights[:4]),
    )
    back = ring_backward(
        size, line, depth, slot, width, span, lengths, weights.bias_table, got,
        (weights, firsts, seconds),
    )
    grads = Moments(
        back.heads_in_grad,
        back.heads_out_grad,
        back.gate_up_grad,
        back.down_grad,
        back.gains_grad,
        back.table_grad,
    )
    update = update_all(
        back.norms, back.layer_out, back.tokens_grad, grads, firsts, seconds, weights, 10
    )
    outputs = [update.layer_out, update.tokens_grad]
    for number in range(6):
        for kind in (update.first, update.second, update.new, update.copy):
            outputs.append(kind[number].T if number in (1, 3, 5) else kind[number])
    return tuple(outputs + [update.norms])


def shards(
    tokens,
    cotangent,
    lengths,
    heads_in,
    heads_out,
    expand_in,
    expand_out,
    norm_gains,
    bias_table,
    heads_in_first,
    heads_out_first,
    expand_in_first,
    expand_out_first,
    gains_first,
    table_first,
    heads_in_second,
    heads_out_second,
    expand_in_second,
    expand_out_second,
    gains_second,
    table_second,
):
    given = (
        tokens, cotangent, lengths, heads_in, heads_out, expand_in, expand_out, norm_gains, bias_table
    )
    weight_list = (heads_in, heads_out, expand_in, expand_out, norm_gains, bias_table)
    first_list = (
        heads_in_first,
        heads_out_first,
        expand_in_first,
        expand_out_first,
        gains_first,
        table_first,
    )
    second_list = (
        heads_in_second,
        heads_out_second,
        expand_in_second,
        expand_out_second,
        gains_second,
        table_second,
    )
    decay_list = (weight_decay, weight_decay, weight_decay, weight_decay, 0.0, 0.0)
    sub_list = (3, 1, 2, 1, 2, 1)
    if lax.axis_size("dp") <= RING_LIMIT:
        return ring_step(*given, first_list, second_list)
    layer_out, tokens_grad, grad_list = plain_gradients(*given)
    results = [
        lamb_parts(
            weight_list[number],
            grad_list[number],
            first_list[number],
            second_list[number],
            decay_list[number],
        )
        for number in range(6)
    ]
    count = sum(sub_list)
    shared = 1.0 / lax.axis_size("mp")
    share_list = (shared, shared, 1.0, 1.0, shared, shared / lax.axis_size("dp"))
    parts = [weight_list, [result[2] for result in results]]
    sums = lax.psum(
        jnp.concatenate(
            [
                sub_squares(part[number], sub_list[number]) * share_list[number]
                for part in parts
                for number in range(6)
            ]
        ),
        ("dp", "mp"),
    )
    weight_norm = jnp.sqrt(sums[:count])
    step_norm = jnp.sqrt(sums[count : 2 * count])
    ratios = weight_norm / step_norm
    starts = (0, 3, 4, 6, 7, 9)
    outputs = [layer_out, tokens_grad]
    for number in range(6):
        weight = weight_list[number]
        sub_count = sub_list[number]
        ratio_part = ratios[starts[number] : starts[number] + sub_count]
        shape = (sub_count,) + (1,) * (weight.ndim - 1) if sub_count > 1 else (1,) * weight.ndim
        new_weight = weight - learn_rate * ratio_part.reshape(shape) * results[number][2]
        outputs = outputs + [
            results[number][0],
            results[number][1],
            new_weight,
            new_weight.astype(bf16),
        ]
    outputs = outputs + [jnp.stack([weight_norm, step_norm])]
    return tuple(outputs)


def solution(mesh):
    return jax.shard_map(
        shards,
        mesh=mesh,
        in_specs=(
            P(("dp", "mp"), None),
            P(("dp", "mp"), None),
            P("dp", None),
            P(None, "dp", None),
            P(None, "dp"),
            P(None, "dp", "mp"),
            P("mp", "dp"),
            P(None, "dp"),
            P(),
            P(None, "dp", None),
            P(None, "dp"),
            P(None, "dp", "mp"),
            P("mp", "dp"),
            P(None, "dp"),
            P(),
            P(None, "dp", None),
            P(None, "dp"),
            P(None, "dp", "mp"),
            P("mp", "dp"),
            P(None, "dp"),
            P(),
        ),
        out_specs=(
            P(("dp", "mp"), None),
            P(("dp", "mp"), None),
            P(None, "dp", None),
            P(None, "dp", None),
            P(None, "dp", None),
            P(None, "dp", None),
            P(None, "dp"),
            P(None, "dp"),
            P(None, "dp"),
            P(None, "dp"),
            P(None, "dp", "mp"),
            P(None, "dp", "mp"),
            P(None, "dp", "mp"),
            P(None, "dp", "mp"),
            P("mp", "dp"),
            P("mp", "dp"),
            P("mp", "dp"),
            P("mp", "dp"),
            P(None, "dp"),
            P(None, "dp"),
            P(None, "dp"),
            P(None, "dp"),
            P(),
            P(),
            P(),
            P(),
            P(),
        ),
        check_vma=False,
    )
```

```python
from functools import partial
from typing import NamedTuple

import jax
import jax.numpy as jnp
from jax import lax
from jax.experimental import pallas as pl
from jax.experimental.pallas import tpu as pltpu
from jax.sharding import PartitionSpec as P

HEADS = 6
HEAD_DIM = 64
STEP = 10
INNER = 384
LANES = 128
PAIRS = INNER // LANES
MESH = pl.DeviceIdType.MESH
VMEM_BYTES = 56 * 2**20
BACKWARD_BYTES = 63 * 2**20
RING_LIMIT = 8


norm_eps = 1e-06
beta_first = 0.9
beta_second = 0.999
adam_eps = 1e-06
weight_decay = 0.01
learn_rate = 0.4
masked_fill = -1000000000.0
bucket_edges = (12, 16, 23, 32, 46, 64, 91)
highest = lax.Precision.HIGHEST
f32 = jnp.float32
bf16 = jnp.bfloat16


def bucket_ids(offsets):
    distance = jnp.abs(offsets)
    coarse = jnp.full_like(distance, 8)
    for edge_value in bucket_edges:
        coarse = coarse + (distance >= edge_value).astype(jnp.int32)
    nearby = jnp.where(distance < 8, distance, coarse)
    return nearby + 16 * (offsets > 0).astype(jnp.int32)


def row_mean(values, depth):
    return jnp.sum(values, axis=-1, keepdims=True) * (1.0 / depth)


def rms_scale(hidden_rows, gain_vector, depth):
    return (
        hidden_rows
        * lax.rsqrt(row_mean(hidden_rows * hidden_rows, depth) + norm_eps)
        * gain_vector
    )


def contract_rows(left_side, right_side):
    return lax.dot_general(
        left_side, right_side, (((0,), (0,)), ((), ())), preferred_element_type=f32
    )


def contract_cols(left_side, right_side):
    return lax.dot_general(
        left_side, right_side, (((1,), (1,)), ((), ())), preferred_element_type=f32
    )


def matmul(left_side, right_side):
    return jnp.dot(left_side, right_side, preferred_element_type=f32)


def ring_order(size):
    return list(range(0, size, 2)) + list(range(size - 1, 0, -2))


def ring_pairs(size):
    order = ring_order(size)
    forward = [(order[spot], order[(spot + 1) % size]) for spot in range(size)]
    return forward, [(target, source) for source, target in forward]


def ring_owner(spot, size):
    late = (spot >= size // 2).astype(jnp.int32)
    return 2 * spot + late * (2 * size - 1 - 4 * spot)


def ring_spot(index, size):
    return index // 2 + lax.rem(index, 2) * (size - 1 - 2 * (index // 2))


def cut_of(width):
    return ((width // LANES + 1) // 2) * LANES


def assemble_kernel(size, cut, *refs):
    slabs, (left, right, out, sems) = refs[:-4], refs[-4:]
    spot = ring_spot(lax.axis_index("dp"), size)
    copies = []
    for number, slab in enumerate(slabs):
        shift = number if number < size // 2 else number + 1
        owner = ring_owner(lax.rem(spot + shift, size), size)
        copies.append(pltpu.make_async_copy(slab, out.at[:, owner], sems.at[number]))
    owner = ring_owner(lax.rem(spot + size // 2, size), size)
    width = out.shape[-1]
    copies.append(
        pltpu.make_async_copy(left, out.at[:, owner, :, pl.ds(0, cut)], sems.at[size - 1])
    )
    copies.append(
        pltpu.make_async_copy(right, out.at[:, owner, :, pl.ds(cut, width - cut)], sems.at[size])
    )
    for copy in copies:
        copy.start()
    for copy in copies:
        copy.wait()


def gather_dp(part):
    size = lax.axis_size("dp")
    if size > RING_LIMIT:
        return lax.all_gather(part, "dp", axis=1, tiled=True)
    forward, backward = ring_pairs(size)
    count, rows, width = part.shape
    cut = cut_of(width)
    slabs = [None] * size
    slabs[0] = ahead = behind = part
    for hop in range(1, size // 2):
        ahead = lax.ppermute(ahead, "dp", forward)
        behind = lax.ppermute(behind, "dp", backward)
        slabs[size - hop] = ahead
        slabs[hop] = behind
    left = lax.ppermute(ahead[..., :cut], "dp", forward)
    right = lax.ppermute(behind[..., cut:], "dp", backward)
    operands = [slab for slab in slabs if slab is not None] + [left, right]
    total = count * size * rows * width * part.dtype.itemsize
    whole = pl.pallas_call(
        partial(assemble_kernel, size, cut),
        out_shape=jax.ShapeDtypeStruct((count, size, rows, width), part.dtype),
        in_specs=[pl.BlockSpec(memory_space=pl.ANY)] * len(operands),
        out_specs=pl.BlockSpec(memory_space=pltpu.VMEM),
        scratch_shapes=[pltpu.SemaphoreType.DMA((size + 1,))],
        compiler_params=pltpu.CompilerParams(vmem_limit_bytes=VMEM_BYTES),
        cost_estimate=pl.CostEstimate(flops=0, bytes_accessed=2 * total, transcendentals=0),
        name="assemble",
    )(*operands)
    return whole.reshape(count, size * rows, width)


def scatter_dp(whole):
    size = lax.axis_size("dp")
    if size > RING_LIMIT:
        return lax.psum_scatter(whole.astype(f32), "dp", scatter_dimension=1, tiled=True)
    forward, backward = ring_pairs(size)
    count, depth, width = whole.shape
    rows = depth // size
    cut = cut_of(width)
    spot = ring_spot(lax.axis_index("dp"), size)

    def term(shift):
        owner = ring_owner(lax.rem(spot + size + shift, size), size)
        return lax.dynamic_slice_in_dim(whole, owner * rows, rows, axis=1)

    far = term(size // 2)
    ahead = lax.ppermute(far[..., :cut], "dp", forward)
    behind = lax.ppermute(far[..., cut:], "dp", backward)
    for hop in range(size // 2 - 1, 0, -1):
        mine = term(hop).astype(f32)
        other = term(-hop).astype(f32)
        if hop == size // 2 - 1:
            ahead = jnp.concatenate([mine[..., :cut] + ahead.astype(f32), mine[..., cut:]], -1)
            behind = jnp.concatenate([other[..., :cut], other[..., cut:] + behind.astype(f32)], -1)
        else:
            ahead = mine + ahead.astype(f32)
            behind = other + behind.astype(f32)
        ahead = lax.ppermute(ahead.astype(bf16), "dp", forward)
        behind = lax.ppermute(behind.astype(bf16), "dp", backward)
    return term(0).astype(f32) + ahead.astype(f32) + behind.astype(f32)


def swap(part, bit):
    size = lax.axis_size("mp")
    return lax.ppermute(part, "mp", [(index, index ^ bit) for index in range(size)])


def gather_mp(part):
    across = swap(part, 2)
    beside = swap(part, 1)
    return part, across, beside, swap(across, 1)


def offset_values(table, first_row, rows, span):
    offsets = lax.broadcasted_iota(jnp.int32, (8, span), 1) - (rows - 1) - first_row
    buckets = bucket_ids(offsets)
    values = jnp.zeros((8, span), f32)
    for number in range(table.shape[1]):
        values = jnp.where(buckets == number, table[:, number : number + 1], values)
    return values


def segments_at(positions, first_len, second_len):
    return (positions >= first_len).astype(jnp.int32) + (
        positions >= first_len + second_len
    ).astype(jnp.int32)


def allowed_pairs(lens_ref, first_row, rows, keys):
    query = segments_at(
        first_row + lax.broadcasted_iota(jnp.int32, (rows, 1), 0), lens_ref[0, 0], lens_ref[0, 1]
    )
    key = segments_at(
        lax.broadcasted_iota(jnp.int32, (1, keys), 1), lens_ref[0, 0], lens_ref[0, 1]
    )
    return query == key


def skewed_bias(values, head, rows, keys, span):
    wide = jnp.broadcast_to(values[head : head + 1, :], (rows, span))
    return pltpu.roll(wide, span - (rows - 1), 1, stride=1, stride_axis=0)[:, :keys]


def attend_pair(pair, query_ref, key_ref, value_ref, mixed_ref, logs, values, allowed, lane, span):
    rows, keys = query_ref.shape[0], key_ref.shape[0]
    part = slice(pair * LANES, (pair + 1) * LANES)
    query, key, value = query_ref[:, part], key_ref[:, part], value_ref[:, part]
    mixed = jnp.zeros((rows, LANES), f32)
    for half in range(2):
        head = 2 * pair + half
        mask = (lane // HEAD_DIM) == half
        scores = contract_cols(jnp.where(mask, query, jnp.zeros_like(query)), key)
        scores = jnp.where(
            allowed, scores + skewed_bias(values, head, rows, keys, span), masked_fill
        )
        top = jnp.max(scores, axis=-1, keepdims=True)
        powers = jnp.exp(scores - top)
        total = jnp.sum(powers, axis=-1, keepdims=True)
        soft = (powers * (1.0 / total)).astype(bf16)
        mixed = jnp.where(mask, matmul(soft, value), mixed)
        logs = jnp.where(lane == head, top + jnp.log(total), logs)
    mixed_ref[:, part] = mixed.astype(bf16)
    return logs


def forward_kernel(
    span,
    depth,
    lens_ref,
    own_ref,
    across_ref,
    beside_ref,
    corner_ref,
    heads_ref,
    table_ref,
    tokens_ref,
    gain_ref,
    mixed_ref,
    query_ref,
    key_ref,
    value_ref,
    log_ref,
    residual_ref,
    normed_ref,
):
    rows = own_ref.shape[0]
    keys = key_ref.shape[0]
    spot = lax.axis_index("mp")
    first_row = spot * rows
    for block_ref, bit in ((own_ref, 0), (across_ref, 2), (beside_ref, 1), (corner_ref, 3)):
        place = pl.ds(pl.multiple_of((spot ^ bit) * rows, rows), rows)
        block = block_ref[...]
        key_ref[place, :] = matmul(block, heads_ref[1]).astype(bf16)
        value_ref[place, :] = matmul(block, heads_ref[2]).astype(bf16)
    query_ref[...] = matmul(own_ref[...], heads_ref[0]).astype(bf16)
    values = offset_values(table_ref[...], first_row, rows, span)
    allowed = allowed_pairs(lens_ref, first_row, rows, keys)
    lane = lax.broadcasted_iota(jnp.int32, (1, LANES), 1)
    logs = jnp.zeros((rows, LANES), f32)
    for pair in range(PAIRS):
        logs = attend_pair(
            pair, query_ref, key_ref, value_ref, mixed_ref, logs, values, allowed, lane, span
        )
    log_ref[...] = logs
    residual = tokens_ref[...].astype(f32) + contract_cols(mixed_ref[...], heads_ref[3])
    residual_ref[...] = residual
    normed_ref[...] = rms_scale(residual, gain_ref[...], depth).astype(bf16)


def norm_backward(rows_in, gain, grad, depth):
    scale = lax.rsqrt(row_mean(rows_in * rows_in, depth) + norm_eps)
    unit = rows_in * scale
    inner = grad * gain
    out = scale * (inner - unit * row_mean(inner * unit, depth))
    return out, jnp.sum(grad * unit, axis=0, keepdims=True)


def attend_pair_backward(
    pair, query_ref, key_ref, value_ref, log_ref, mixed_grad, values, allowed, span
):
    rows, keys = query_ref.shape[0], key_ref.shape[0]
    lane = lax.broadcasted_iota(jnp.int32, (1, LANES), 1)
    flip = (
        lax.broadcasted_iota(jnp.int32, (rows, rows), 0)
        + lax.broadcasted_iota(jnp.int32, (rows, rows), 1)
        == rows - 1
    ).astype(bf16)
    part = slice(pair * LANES, (pair + 1) * LANES)
    query, key, value = query_ref[:, part], key_ref[:, part], value_ref[:, part]
    query_grad = jnp.zeros((rows, LANES), f32)
    key_grad = jnp.zeros((keys, LANES), f32)
    value_grad = jnp.zeros((keys, LANES), f32)
    offsets = []
    for half in range(2):
        head = 2 * pair + half
        mask = (lane // HEAD_DIM) == half
        query_own = jnp.where(mask, query, jnp.zeros_like(query))
        mixed_own = jnp.where(mask, mixed_grad, jnp.zeros_like(mixed_grad))
        scores = contract_cols(query_own, key)
        scores = jnp.where(
            allowed, scores + skewed_bias(values, head, rows, keys, span), masked_fill
        )
        soft = jnp.exp(scores - log_ref[:, head : head + 1])
        soft_grad = contract_cols(mixed_own, value)
        corr = jnp.sum(soft * soft_grad, axis=-1, keepdims=True)
        scores_grad = (soft * (soft_grad - corr)).astype(bf16)
        query_grad = jnp.where(mask, matmul(scores_grad, key), query_grad)
        key_grad = key_grad + contract_rows(scores_grad, query_own)
        value_grad = value_grad + contract_rows(soft.astype(bf16), mixed_own)
        flipped = matmul(flip, scores_grad)
        flipped = jnp.concatenate([flipped, jnp.zeros((rows, span - keys), f32)], axis=1)
        skewed = pltpu.roll(flipped, 0, 1, stride=1, stride_axis=0)
        offsets.append(jnp.sum(skewed, axis=0, keepdims=True))
    return query_grad, key_grad, value_grad, offsets


def backward_kernel(
    span,
    depth,
    lens_ref,
    part_ref,
    across_ref,
    residual_ref,
    upstream_ref,
    gain_ref,
    heads_ref,
    query_ref,
    key_ref,
    value_ref,
    log_ref,
    table_ref,
    residual_grad_ref,
    attended_ref,
    query_grad_ref,
    near_ref,
    far_ref,
    offset_ref,
    gain_grad_ref,
    whole_ref,
):
    rows = query_ref.shape[0]
    keys = key_ref.shape[0]
    spot = lax.axis_index("mp")
    first_row = spot * rows
    grad = part_ref[...].astype(f32) + across_ref[...].astype(f32)
    through, gain_grad = norm_backward(residual_ref[...], gain_ref[...], grad, depth)
    gain_grad_ref[...] = gain_grad
    residual_grad = upstream_ref[...].astype(f32) + through
    residual_grad_ref[...] = residual_grad
    attended = residual_grad.astype(bf16)
    attended_ref[...] = attended
    mixed_grad_all = matmul(attended, heads_ref[3]).astype(bf16)
    values = offset_values(table_ref[...], first_row, rows, span)
    allowed = allowed_pairs(lens_ref, first_row, rows, keys)
    for pair in range(PAIRS):
        part = slice(pair * LANES, (pair + 1) * LANES)
        query_grad, key_grad, value_grad, offsets = attend_pair_backward(
            pair, query_ref, key_ref, value_ref, log_ref, mixed_grad_all[:, part], values, allowed,
            span,
        )
        for half in range(2):
            offset_ref[2 * pair + half : 2 * pair + half + 1, :] = offsets[half]
        query_grad_ref[:, part] = query_grad.astype(bf16)
        whole_ref[:, part] = key_grad
        whole_ref[:, INNER + pair * LANES : INNER + (pair + 1) * LANES] = value_grad
    offset_ref[HEADS:, :] = jnp.zeros((8 - HEADS, span), f32)
    for number, bit in enumerate((0, 2)):
        place = pl.ds(pl.multiple_of((spot ^ bit) * rows, rows), rows)
        near_ref[number * rows : (number + 1) * rows, :] = whole_ref[place, :]
    for number, bit in enumerate((1, 3)):
        place = pl.ds(pl.multiple_of((spot ^ bit) * rows, rows), rows)
        far_ref[number * rows : (number + 1) * rows, :] = whole_ref[place, :].astype(bf16)


def input_kernel(
    depth,
    own_ref,
    beside_ref,
    across_ref,
    query_grad_ref,
    heads_ref,
    tokens_ref,
    gain_ref,
    residual_grad_ref,
    tokens_grad_ref,
    both_ref,
    gain_grad_ref,
):
    rows = query_grad_ref.shape[0]
    both = (
        own_ref[:rows, :]
        + beside_ref[:rows, :].astype(f32)
        + across_ref[...].astype(f32)
    ).astype(bf16)
    both_ref[...] = both
    grad = (
        contract_cols(query_grad_ref[...], heads_ref[0])
        + contract_cols(both[:, :INNER], heads_ref[1])
        + contract_cols(both[:, INNER:], heads_ref[2])
    )
    through, gain_grad = norm_backward(tokens_ref[...].astype(f32), gain_ref[...], grad, depth)
    gain_grad_ref[...] = gain_grad
    tokens_grad_ref[...] = residual_grad_ref[...] + through


def vmem_call(body, outs, cost, scratch=(), name=None, smem_first=False):
    def run(*operands):
        specs = [pl.BlockSpec(memory_space=pltpu.VMEM)] * len(operands)
        if smem_first:
            specs[0] = pl.BlockSpec(memory_space=pltpu.SMEM)
        return pl.pallas_call(
            body,
            out_shape=[jax.ShapeDtypeStruct(shape, kind) for shape, kind in outs],
            in_specs=specs,
            out_specs=[pl.BlockSpec(memory_space=pltpu.VMEM)] * len(outs),
            scratch_shapes=list(scratch),
            compiler_params=pltpu.CompilerParams(vmem_limit_bytes=VMEM_BYTES),
            cost_estimate=pl.CostEstimate(
                flops=cost[0], bytes_accessed=cost[1], transcendentals=cost[2]
            ),
            name=name,
        )(*operands)

    return run


def total_kernel(sizes, part_ref, out_ref, line_ref, plane_ref, line_send, line_recv, plane_send, plane_recv):
    plane, line = sizes
    dp_spot, mp_spot = lax.axis_index("dp"), lax.axis_index("mp")
    barrier = pltpu.get_barrier_semaphore()
    for step in range(1, line):
        pl.semaphore_signal(
            barrier, 1, device_id=(dp_spot, lax.rem(mp_spot + step, line)), device_id_type=MESH
        )
    for step in range(1, plane):
        pl.semaphore_signal(
            barrier, 1, device_id=(lax.rem(dp_spot + step, plane), mp_spot), device_id_type=MESH
        )
    pl.semaphore_wait(barrier, line + plane - 2)

    def exchange(source, slots, size, spot, send, recv, target):
        slots[spot] = source[...]
        copies = [
            pltpu.make_async_remote_copy(
                src_ref=source,
                dst_ref=slots.at[spot],
                send_sem=send.at[step],
                recv_sem=recv.at[step],
                device_id=target(lax.rem(spot + step, size)),
                device_id_type=MESH,
            )
            for step in range(1, size)
        ]
        for copy in copies:
            copy.start()
        for copy in copies:
            copy.wait()
        total = slots[0]
        for index in range(1, size):
            total = total + slots[index]
        out_ref[...] = total

    exchange(part_ref, line_ref, line, mp_spot, line_send, line_recv, lambda to: (dp_spot, to))
    exchange(out_ref, plane_ref, plane, dp_spot, plane_send, plane_recv, lambda to: (to, mp_spot))


def total_all(part, number):
    plane, line = lax.axis_size("dp"), lax.axis_size("mp")
    if plane > RING_LIMIT:
        return lax.psum(part, ("dp", "mp"))
    return pl.pallas_call(
        partial(total_kernel, (plane, line)),
        out_shape=jax.ShapeDtypeStruct(part.shape, part.dtype),
        in_specs=[pl.BlockSpec(memory_space=pltpu.VMEM)],
        out_specs=pl.BlockSpec(memory_space=pltpu.VMEM),
        scratch_shapes=[
            pltpu.VMEM((line,) + part.shape, f32),
            pltpu.VMEM((plane,) + part.shape, f32),
            pltpu.SemaphoreType.DMA((line,)),
            pltpu.SemaphoreType.DMA((line,)),
            pltpu.SemaphoreType.DMA((plane,)),
            pltpu.SemaphoreType.DMA((plane,)),
        ],
        compiler_params=pltpu.CompilerParams(collective_id=number, has_side_effects=True),
        name="total",
    )(part)


def small_gather_kernel(size, part_ref, out_ref, send, recv):
    dp_spot, mp_spot = lax.axis_index("dp"), lax.axis_index("mp")
    barrier = pltpu.get_barrier_semaphore()
    for step in range(1, size):
        pl.semaphore_signal(
            barrier, 1, device_id=(lax.rem(dp_spot + step, size), mp_spot), device_id_type=MESH
        )
    pl.semaphore_wait(barrier, size - 1)
    out_ref[dp_spot] = part_ref[...]
    copies = [
        pltpu.make_async_remote_copy(
            src_ref=part_ref,
            dst_ref=out_ref.at[dp_spot],
            send_sem=send.at[step],
            recv_sem=recv.at[step],
            device_id=(lax.rem(dp_spot + step, size), mp_spot),
            device_id_type=MESH,
        )
        for step in range(1, size)
    ]
    for copy in copies:
        copy.start()
    for copy in copies:
        copy.wait()


def gather_gains(gains):
    size = lax.axis_size("dp")
    if size > RING_LIMIT:
        return lax.all_gather(gains, "dp", axis=1, tiled=True)
    count, width = gains.shape
    wide = -(-width // LANES) * LANES
    part = jnp.pad(gains, ((0, 8 - count), (0, wide - width)))
    whole = pl.pallas_call(
        partial(small_gather_kernel, size),
        out_shape=jax.ShapeDtypeStruct((size,) + part.shape, part.dtype),
        in_specs=[pl.BlockSpec(memory_space=pltpu.VMEM)],
        out_specs=pl.BlockSpec(memory_space=pltpu.VMEM),
        scratch_shapes=[pltpu.SemaphoreType.DMA((size,)), pltpu.SemaphoreType.DMA((size,))],
        compiler_params=pltpu.CompilerParams(collective_id=3, has_side_effects=True),
        name="gather_gains",
    )(part)
    return jnp.concatenate([whole[index, :count, :width] for index in range(size)], axis=1)


def pack_rows(parts):
    flat = jnp.concatenate([part.reshape(-1) for part in parts])
    count = -(-flat.shape[0] // (8 * LANES)) * 8
    return jnp.pad(flat, (0, count * LANES - flat.shape[0])).reshape(count, LANES)


def lamb_parts(weight, gradient, first_moment, second, decay_rate):
    new_first = beta_first * first_moment + (1.0 - beta_first) * gradient
    new_second = beta_second * second + (1.0 - beta_second) * gradient * gradient
    first_fix = 1.0 - beta_first**STEP
    second_fix = 1.0 - beta_second**STEP
    step_dir = (new_first * (1.0 / first_fix)) / (
        jnp.sqrt(new_second * (1.0 / second_fix)) + adam_eps
    ) + decay_rate * weight
    return (new_first, new_second, step_dir)


def sub_squares(values, sub_count):
    flat_values = values.reshape(sub_count, -1)
    return jnp.sum(flat_values * flat_values, axis=1)


def gelu_parts(gate):
    root = (2.0 / 3.141592653589793) ** 0.5
    square = gate * gate
    curve = jnp.tanh(root * (gate + 0.044715 * gate * square))
    value = 0.5 * gate * (1.0 + curve)
    slope = 0.5 * (1.0 + curve) + 0.5 * gate * (1.0 - curve * curve) * root * (
        1.0 + 3.0 * 0.044715 * square
    )
    return value, slope


def spread_pair(values, pair, shard, slot):
    depth = values.shape[1]
    first = 2 * pair * shard
    low = first // LANES * LANES
    high = min(depth, -(-(first + 2 * shard) // LANES) * LANES)
    shape = (high - low, 2 * slot)
    source = low + lax.broadcasted_iota(jnp.int32, shape, 0)
    place = lax.broadcasted_iota(jnp.int32, shape, 1)
    late = (place >= slot).astype(jnp.int32)
    offset = place - late * slot
    chosen = (source == first + late * shard + offset) & (offset < shard)
    return matmul(values[:, low:high], chosen.astype(bf16))


def gathered_tile(coarse, fine, low, high, shard, slot):
    def place_of(lane):
        return lane // shard * slot + lane % shard

    first = place_of(low) // LANES * LANES
    last = -(-(place_of(high - 1) + 1) // LANES) * LANES
    shape = (last - first, high - low)
    source = first + lax.broadcasted_iota(jnp.int32, shape, 0)
    lane = low + lax.broadcasted_iota(jnp.int32, shape, 1)
    chosen = jnp.zeros(shape, jnp.bool_)
    for number in range(low // shard, (high - 1) // shard + 1):
        inside = (lane >= number * shard) & (lane < (number + 1) * shard)
        chosen = chosen | (inside & (source == lane + number * (slot - shard)))
    chosen = chosen.astype(bf16)
    total = matmul(coarse[:, first:last], chosen)
    if fine is not None:
        total = total + matmul(fine[:, first:last], chosen)
    return total


def head_table(table_ref):
    table = table_ref[...]
    return jnp.concatenate([table, jnp.zeros((8 - HEADS, table.shape[1]), f32)], axis=0)


class Places:
    def __init__(self, size):
        self.size, self.half = size, size // 2
        self.dp, self.mp = lax.axis_index("dp"), lax.axis_index("mp")
        self.spot = ring_spot(self.dp, size)
        self.sides = (
            ring_owner(lax.rem(self.spot + 1, size), size),
            ring_owner(lax.rem(self.spot + size - 1, size), size),
        )

    def owner(self, shift):
        return ring_owner(lax.rem(self.spot + self.size + shift, self.size), self.size)

    def sent(self, side, hop):
        return self.owner(-hop if side == 0 else hop)

    def came(self, side, hop):
        return self.sent(side, hop + 1)


def remote(source, target, send, recv, dp, mp):
    return pltpu.make_async_remote_copy(
        src_ref=source,
        dst_ref=target,
        send_sem=send,
        recv_sem=recv,
        device_id=(dp, mp),
        device_id_type=MESH,
    )


class ForwardOut(NamedTuple):
    heads: object
    gate_up: object
    down: object
    normed: object
    upstream: object
    normed_two: object
    gelu: object
    slope: object
    hidden: object
    hidden_grad_out: object
    query: object
    key: object
    value: object
    mixed: object
    logs: object
    residual: object
    full_gains: object
    wide_tokens: object


class ForwardRefs(NamedTuple):
    lens: object
    tokens: object
    cotangent: object
    norm_gains: object
    table: object
    heads_in: object
    heads_out: object
    expand_in: object
    expand_out: object
    heads: object
    gate_up: object
    down: object
    normed: object
    upstream: object
    normed_two: object
    gelu: object
    slope: object
    hidden: object
    hidden_grad_out: object
    query: object
    key: object
    value: object
    mixed: object
    logs: object
    residual: object
    full_gains: object
    wide_tokens: object
    tokens_in: object
    cotangent_in: object
    mine_in: object
    out_in: object
    gate_in: object
    down_in: object
    bring_sems: object
    stack: object
    gains: object
    mine: object
    wide_in: object
    wide_out: object
    gain_slots: object
    gain_send: object
    gain_recv: object
    head_send: object
    head_recv: object
    wide_send: object
    wide_recv: object
    line_send: object
    line_recv: object
    slab_send: object
    slab_recv: object
    store_sems: object
    down_sems: object


def forward_shapes(rows, line, size, slot, width, span):
    wide, keys = size * slot, rows * line
    return ForwardOut(
        heads=((4, wide, INNER), bf16),
        gate_up=((2, wide, width), bf16),
        down=((wide, width), bf16),
        normed=((keys, wide), bf16),
        upstream=((keys, wide), bf16),
        normed_two=((keys, wide), bf16),
        gelu=((keys, width), f32),
        slope=((keys, width), f32),
        hidden=((keys, width), bf16),
        hidden_grad_out=((wide, width), bf16),
        query=((rows, INNER), bf16),
        key=((keys, INNER), bf16),
        value=((keys, INNER), bf16),
        mixed=((rows, INNER), bf16),
        logs=((rows, LANES), f32),
        residual=((rows, wide), f32),
        full_gains=((8, wide), f32),
        wide_tokens=((rows, wide), bf16),
    )


def ring_forward_kernel(size, depth, span, *refs):
    count = len(ForwardOut._fields)
    inputs = 9
    stores = refs[inputs : inputs + count]
    r = ForwardRefs(*refs[:inputs], *refs[inputs + count :])
    places = (None, r.tokens_in, r.cotangent_in, None, None, r.mine_in, r.out_in, r.gate_in, r.down_in)

    def bring(number, index=None):
        source = refs[number] if index is None else refs[number].at[index]
        return pltpu.make_async_copy(source, places[number], r.bring_sems.at[number])
    kept = refs[inputs + count : inputs + 2 * count]

    def store_copy(number):
        return pltpu.make_async_copy(kept[number], stores[number], r.store_sems.at[number])

    def store(*which):
        for number in range(count):
            if any(kept[number] is ref for ref in which):
                store_copy(number).start()

    at = Places(size)
    half = at.half
    rows = r.tokens_in.shape[0]
    wide = r.residual.shape[1]
    keys = r.key.shape[0]
    slot = wide // size
    shard = r.norm_gains.shape[1]
    width = r.down.shape[1]
    line = keys // rows
    cut, head_cut = cut_of(width), cut_of(INNER)
    first_row = at.mp * rows
    across, beside = at.mp ^ 2, at.mp ^ 1

    brought = (bring(5, jnp.minimum(at.mp, line - 2)), bring(6), bring(7), bring(1), bring(8), bring(2))
    for copy in brought:
        copy.start()
    barrier = pltpu.get_barrier_semaphore()
    for step in range(1, size):
        pl.semaphore_signal(
            barrier, 1, device_id=(lax.rem(at.dp + step, size), at.mp), device_id_type=MESH
        )
    for partner in (across, beside):
        pl.semaphore_signal(barrier, 1, device_id=(at.dp, partner), device_id_type=MESH)

    def filled(values):
        spare = jnp.zeros((slot - shard, values.shape[1]), f32)
        return jnp.concatenate([values, spare], axis=0).astype(bf16)

    last = at.mp == line - 1
    brought[0].wait()
    brought[1].wait()
    r.mine[...] = filled(jnp.where(last, r.out_in[...], r.mine_in[...]))
    brought[2].wait()
    r.wide_in[...] = jnp.concatenate([r.gate_in[0], r.gate_in[1]], axis=0).astype(bf16)
    rounded = r.norm_gains[...].astype(bf16).astype(f32)
    rounded = jnp.concatenate([rounded, jnp.zeros((2, 2 * slot - shard), f32)], axis=1)
    rounded = jnp.concatenate([rounded, jnp.zeros((6, 2 * slot), f32)], axis=0)
    r.gains[...] = jnp.where(lax.rem(at.dp, 2) == 1, pltpu.roll(rounded, slot, 1), rounded)
    pl.semaphore_wait(barrier, size + 1)

    def slab_rows(owner):
        return pl.ds(pl.multiple_of(owner * slot, slot), slot)

    def head_lanes(side, hop):
        if hop < half - 1:
            return pl.ds(0, INNER)
        return pl.ds(0, head_cut) if side == 0 else pl.ds(head_cut, INNER - head_cut)

    def head_hop(side, hop):
        lanes = head_lanes(side, hop)
        target = r.heads.at[at.mp, slab_rows(at.sent(side, hop)), lanes]
        source = r.mine.at[:, lanes] if hop == 0 else target
        return remote(
            source, target, r.head_send.at[side, hop], r.head_recv.at[side, hop],
            at.sides[side], at.mp,
        )

    def head_came(side, hop):
        target = r.heads.at[at.mp, slab_rows(at.came(side, hop)), head_lanes(side, hop)]
        return remote(
            target, target, r.head_send.at[side, hop], r.head_recv.at[side, hop],
            at.sides[side], at.mp,
        )

    def piece_part(piece):
        lanes = pl.ds(0, cut) if piece % 2 == 0 else pl.ds(cut, width - cut)
        return (pl.ds(0, slot) if piece < 2 else pl.ds(slot, 2 * shard - slot)), lanes

    def piece_view(piece, owner):
        part, lanes = piece_part(piece)
        if piece < 4:
            return r.stack.at[owner, part, lanes]
        return r.down.at[slab_rows(owner), lanes]

    def piece_source(piece):
        part, lanes = piece_part(piece)
        if piece < 4:
            return r.wide_in.at[part, lanes]
        return r.wide_out.at[:, lanes]

    def down_copy(shift):
        view = slab_rows(at.owner(shift))
        return pltpu.make_async_copy(
            r.down.at[view], stores[ForwardOut._fields.index("down")].at[view],
            r.down_sems.at[shift % size],
        )

    def store_down(*which):
        for shift in which:
            down_copy(shift).start()

    def unstack(shift):
        owner = at.owner(shift)
        both = r.stack[owner].astype(f32)
        r.gate_up[0, slab_rows(owner), :] = filled(both[:shard])
        r.gate_up[1, slab_rows(owner), :] = filled(both[shard:])

    def piece_goes(piece, side, hop):
        return hop < half - 1 or piece in ((0, 3, 4), (1, 2, 5))[side]

    def piece_hop(piece, side, hop):
        target = piece_view(piece, at.sent(side, hop))
        source = piece_source(piece) if hop == 0 else target
        return remote(
            source, target, r.wide_send.at[piece, side, hop], r.wide_recv.at[piece, side, hop],
            at.sides[side], at.mp,
        )

    def piece_came(piece, side, hop):
        target = piece_view(piece, at.came(side, hop))
        return remote(
            target, target, r.wide_send.at[piece, side, hop], r.wide_recv.at[piece, side, hop],
            at.sides[side], at.mp,
        )

    def serve(piece, hop):
        for side in range(2):
            if piece_goes(piece, side, hop):
                if hop > 0:
                    piece_came(piece, side, hop - 1).wait_recv()
                piece_hop(piece, side, hop).start()

    def finish(piece):
        for side in range(2):
            last = half - 1 if piece_goes(piece, side, half - 1) else half - 2
            piece_came(piece, side, last).wait_recv()

    def block(array, number):
        return array.at[pl.ds(number * rows, rows)]

    def line_copy(array, ref, number):
        source, target, partner = ((0, 1, across), (0, 2, beside), (1, 3, beside))[number]
        return remote(
            block(ref, source), block(ref, target), r.line_send.at[array, number],
            r.line_recv.at[array, number], at.dp, partner,
        )

    shifts = [0] + [shift for hop in range(1, half) for shift in (-hop, hop)] + [half]

    def slab_copy(number, way):
        matrix = across if way == 2 else at.mp
        view = r.heads.at[matrix, slab_rows(at.owner(shifts[number]))]
        source = r.mine if number == 0 and way < 2 else view
        return remote(
            source, view, r.slab_send.at[number, way], r.slab_recv.at[number, way],
            at.dp, across if way == 0 else beside,
        )

    def slab_came(number, way):
        matrix = (across, beside, at.mp ^ 3)[way]
        view = r.heads.at[matrix, slab_rows(at.owner(shifts[number]))]
        return remote(
            view, view, r.slab_send.at[number, way], r.slab_recv.at[number, way],
            at.dp, across if way == 0 else beside,
        )

    def gain_copy(step):
        return remote(
            r.gains, r.gain_slots.at[at.dp], r.gain_send.at[step], r.gain_recv.at[step],
            lax.rem(at.dp + step, size), at.mp,
        )

    for step in range(1, size):
        gain_copy(step).start()
    for side in range(2):
        head_hop(side, 0).start()
    for way in range(2):
        slab_copy(0, way).start()
    serve(0, 0)
    brought[3].wait()
    for pair in range(half):
        lanes = slice(2 * pair * slot, 2 * (pair + 1) * slot)
        r.wide_tokens[:, lanes] = spread_pair(r.tokens_in[...], pair, shard, slot).astype(bf16)
    r.gain_slots[at.dp] = r.gains[...]
    own = slab_rows(at.dp)
    r.heads[at.mp, own, :] = r.mine[...]
    r.gate_up[0, own, :] = filled(r.gate_in[0])
    r.gate_up[1, own, :] = filled(r.gate_in[1])
    for step in range(1, size):
        gain_copy(step).wait()
    r.full_gains[...] = jnp.concatenate(
        [r.gain_slots[2 * pair] + r.gain_slots[2 * pair + 1] for pair in range(half)], axis=1
    )
    block(r.normed, 0)[...] = rms_scale(
        r.wide_tokens[...].astype(f32), r.full_gains[0:1, :], depth
    ).astype(bf16)
    for number in range(2):
        line_copy(0, r.normed, number).start()
    brought[4].wait()
    r.wide_out[...] = filled(r.down_in[...])
    r.down[own, :] = r.wide_out[...]
    brought[5].wait()
    positions = first_row + lax.broadcasted_iota(jnp.int32, (rows, 1), 0)
    used = positions < r.lens[0, 0] + r.lens[0, 1]
    upstream = jnp.where(used, r.cotangent_in[...].astype(f32), 0.0).astype(bf16)
    for pair in range(half):
        lanes = slice(2 * pair * slot, 2 * (pair + 1) * slot)
        r.upstream[:rows, lanes] = spread_pair(upstream, pair, shard, slot).astype(bf16)

    fillers = [[(1, 0)], [(2, 0)], [(3, 0), (0, 1)], [(1, 1)]]
    for hop in range(half):
        for side in range(2):
            head_came(side, hop).wait_recv()
            if hop + 1 < half:
                head_hop(side, hop + 1).start()
        for piece, piece_at in fillers[min(hop, 3)]:
            serve(piece, piece_at)
        done = (2 * hop + 1, 2 * hop + 2) if hop + 1 < half else (2 * hop + 1,)
        for number in done:
            for way in range(2):
                slab_copy(number, way).start()
    line_copy(0, r.normed, 0).wait_recv()
    line_copy(0, r.normed, 2).start()
    for number in range(2):
        line_copy(1, r.upstream, number).start()
    serve(2, 1)
    serve(3, 1)
    for number in range(size):
        slab_came(number, 0).wait_recv()
        slab_copy(number, 2).start()
        if number in (size // 2, size - 2):
            serve(int(number == size - 2), 2)
    for number in range(size):
        slab_came(number, 1).wait_recv()
    for number in range(size):
        slab_came(number, 2).wait_recv()

    serve(2, 2)
    serve(3, 2)

    r.query[...] = matmul(block(r.normed, 0)[...], r.heads[0]).astype(bf16)
    for number, bit in ((0, 0), (2, 1), (1, 2), (3, 3)):
        if number == 2:
            line_copy(0, r.normed, 1).wait_recv()
        if number == 3:
            line_copy(0, r.normed, 2).wait_recv()
        place = pl.ds(pl.multiple_of((at.mp ^ bit) * rows, rows), rows)
        data = block(r.normed, number)[...]
        r.key[place, :] = matmul(data, r.heads[1]).astype(bf16)
        r.value[place, :] = matmul(data, r.heads[2]).astype(bf16)
    store(r.full_gains, r.wide_tokens, r.normed, r.query, r.key, r.value)

    unstack(-1)
    unstack(1)

    values = offset_values(head_table(r.table), first_row, rows, span)
    allowed = allowed_pairs(r.lens, first_row, rows, keys)
    lane = lax.broadcasted_iota(jnp.int32, (1, LANES), 1)
    logs = jnp.zeros((rows, LANES), f32)
    for pair in range(PAIRS):
        logs = attend_pair(
            pair, r.query, r.key, r.value, r.mixed, logs, values, allowed, lane, span
        )
        if pair > 0:
            serve(2 * pair - 2, 3)
            serve(2 * pair - 1, 3)
    serve(4, 0)
    serve(5, 0)
    r.logs[...] = logs
    residual = r.wide_tokens[...].astype(f32) + contract_cols(r.mixed[...], r.heads[3])
    r.residual[...] = residual
    block(r.normed_two, 0)[...] = rms_scale(residual, r.full_gains[1:2, :], depth).astype(bf16)
    store(r.heads, r.mixed, r.logs, r.residual)
    for number in range(2):
        line_copy(2, r.normed_two, number).start()
    unstack(-2)
    unstack(2)
    for piece in range(4):
        finish(piece)
    for shift in (-3, 3, half):
        unstack(shift)

    def expand(number):
        place = pl.ds(number * rows, rows)
        data = r.normed_two[place, :]
        gate = matmul(data, r.gate_up[0])
        up = matmul(data, r.gate_up[1])
        value, slope = gelu_parts(gate)
        r.gelu[place, :] = value
        r.slope[place, :] = slope * up
        r.hidden[place, :] = (value * up).astype(bf16)

    expand(0)
    serve(4, 1)
    line_copy(2, r.normed_two, 0).wait_recv()
    line_copy(2, r.normed_two, 2).start()
    line_copy(2, r.normed_two, 1).wait_recv()
    serve(5, 1)
    expand(2)
    serve(4, 2)
    store_down(0, -1, 1)
    expand(1)
    serve(5, 2)
    line_copy(2, r.normed_two, 2).wait_recv()
    expand(3)
    store_down(-2, 2)
    store(r.gelu, r.slope, r.hidden, r.gate_up, r.normed_two)
    line_copy(1, r.upstream, 0).wait_recv()
    line_copy(1, r.upstream, 2).start()
    line_copy(1, r.upstream, 1).wait_recv()
    line_copy(1, r.upstream, 2).wait_recv()
    store(r.upstream)
    tiles = 4
    tile = wide // tiles
    for number in range(tiles):
        lanes = slice(number * tile, (number + 1) * tile)
        r.hidden_grad_out[lanes, :] = contract_rows(
            r.upstream[:, lanes], r.hidden[...]
        ).astype(bf16)
        if number == 0:
            serve(4, 3)
            serve(5, 3)
    store(r.hidden_grad_out)
    for piece in (4, 5):
        finish(piece)
    store_down(-3, 3, half)

    for side in range(2):
        for hop in range(half):
            head_hop(side, hop).wait_send()
            for piece in range(6):
                if piece_goes(piece, side, hop):
                    piece_hop(piece, side, hop).wait_send()
    for number in range(size):
        for way in range(3):
            slab_copy(number, way).wait_send()
    for array, ref in enumerate((r.normed, r.upstream, r.normed_two)):
        for number in range(3):
            line_copy(array, ref, number).wait_send()
    for number in range(count):
        if kept[number] is not r.down:
            store_copy(number).wait()
    for shift in range(size):
        down_copy(shift).wait()


def ring_forward(size, line, depth, slot, width, span, operands):
    rows, shard = operands[1].shape[0], depth // size
    shapes = forward_shapes(rows, line, size, slot, width, span)
    wide, keys = size * slot, rows * line
    dma = pltpu.SemaphoreType.DMA
    half = size // 2
    specs = [pl.BlockSpec(memory_space=pl.ANY)] * len(operands)
    specs[0] = pl.BlockSpec(memory_space=pltpu.SMEM)
    specs[3] = specs[4] = pl.BlockSpec(memory_space=pltpu.VMEM)
    flops = 2 * keys * wide * (3 * width + 2 * INNER) + 4 * rows * wide * INNER
    results = pl.pallas_call(
        partial(ring_forward_kernel, size, depth, span),
        out_shape=[jax.ShapeDtypeStruct(*shape) for shape in shapes],
        in_specs=specs,
        out_specs=[pl.BlockSpec(memory_space=pl.ANY)] * len(shapes),
        scratch_shapes=[pltpu.VMEM(*shape) for shape in shapes]
        + [
            pltpu.VMEM((rows, depth), bf16),
            pltpu.VMEM((rows, depth), bf16),
            pltpu.VMEM((shard, INNER), f32),
            pltpu.VMEM((shard, INNER), f32),
            pltpu.VMEM((2, shard, width), f32),
            pltpu.VMEM((shard, width), f32),
            dma((len(operands),)),
            pltpu.VMEM((size, 2 * shard, width), bf16),
            pltpu.VMEM((8, 2 * slot), f32),
            pltpu.VMEM((slot, INNER), bf16),
            pltpu.VMEM((2 * shard, width), bf16),
            pltpu.VMEM((slot, width), bf16),
            pltpu.VMEM((size, 8, 2 * slot), f32),
            dma((size,)),
            dma((size,)),
            dma((2, half)),
            dma((2, half)),
            dma((6, 2, half)),
            dma((6, 2, half)),
            dma((3, 3)),
            dma((3, 3)),
            dma((size, 3)),
            dma((size, 3)),
            dma((len(shapes),)),
            dma((size,)),
        ],
        compiler_params=pltpu.CompilerParams(
            collective_id=4, has_side_effects=True, vmem_limit_bytes=60 * 2**20
        ),
        cost_estimate=pl.CostEstimate(flops=flops, bytes_accessed=40 * 2**20, transcendentals=0),
        name="ring_forward",
    )(*operands)
    return ForwardOut(*results)


class BackwardOut(NamedTuple):
    layer_out: object
    tokens_grad: object
    heads_in_grad: object
    heads_out_grad: object
    gate_up_grad: object
    down_grad: object
    gains_grad: object
    table_grad: object
    norms: object


class BackwardLoads(NamedTuple):
    hidden_grad_out: object
    upstream: object
    down: object
    gelu: object
    slope: object
    gate_up: object
    normed_two: object
    hidden: object
    residual: object
    full_gains: object
    heads: object
    query: object
    key: object
    value: object
    logs: object
    mixed: object
    wide_tokens: object


class Moments(NamedTuple):
    heads_in: object
    heads_out: object
    expand_in: object
    expand_out: object
    norm_gains: object
    bias_table: object


class BackwardScratch(NamedTuple):
    load_sems: object
    residual_grad: object
    both_grads: object
    fresh: object
    wide_came: object
    down_came: object
    far_send: object
    far_came: object
    across_send: object
    across_came: object
    pair_send: object
    pair_came: object
    pair_across_send: object
    pair_across_came: object
    offered: object
    right: object
    mine_grad: object
    mine_came: object
    mine_sums: object
    small: object
    small_line: object
    small_gains: object
    small_table: object
    norm_part: object
    norm_line: object
    norm_plane: object
    down_stage: object
    mine_stage: object
    out_stage: object
    gains_stage: object
    table_stage: object
    wide_sems: object
    line_sems: object
    attended_sems: object
    right_sems: object
    mine_sems: object
    sums_sems: object
    small_sems: object
    norm_sems: object
    stage_sems: object


def back_loads(values):
    return BackwardLoads(*[getattr(values, name) for name in BackwardLoads._fields])


def ring_backward_kernel(size, depth, span, *refs):
    lens_ref, table_ref = refs[:2]
    refs = refs[2:]
    loaded = len(BackwardLoads._fields)
    sources, normed_source, refs = refs[:loaded], refs[loaded], refs[loaded + 1 :]
    states = [Moments(*refs[6 * number : 6 * number + 6]) for number in range(3)]
    refs = refs[18:]
    outs = len(BackwardOut._fields)
    out, refs = BackwardOut(*refs[:outs]), refs[outs:]
    hand_sems, refs = refs[-1], refs[:-1]
    layer_held, tokens_held, down_held = refs[-3:]
    refs = refs[:-3]
    hands = [
        pltpu.make_async_copy(layer_held, out.layer_out, hand_sems.at[0]),
        pltpu.make_async_copy(tokens_held, out.tokens_grad, hand_sems.at[1]),
        pltpu.make_async_copy(down_held, out.down_grad, hand_sems.at[2]),
    ]
    r, s = BackwardLoads(*refs[:loaded]), BackwardScratch(*refs[loaded:])

    def load_copy(number):
        return pltpu.make_async_copy(sources[number], r[number], s.load_sems.at[number])

    def arrive(*which):
        for number in range(loaded):
            if any(r[number] is ref for ref in which):
                load_copy(number).wait()

    for number in range(loaded):
        load_copy(number).start()
    at = Places(size)
    half = at.half
    rows = r.query.shape[0]
    keys = r.key.shape[0]
    wide = r.residual.shape[1]
    slot = wide // size
    shard = depth // size
    width = r.down.shape[1]
    line = keys // rows
    cut, head_cut = cut_of(width), cut_of(INNER)
    first_row = at.mp * rows
    across, beside, corner = at.mp ^ 2, at.mp ^ 1, at.mp ^ 3
    part_wide = wide // 2

    barrier = pltpu.get_barrier_semaphore()
    for step in range(1, size):
        pl.semaphore_signal(
            barrier, 1, device_id=(lax.rem(at.dp + step, size), at.mp), device_id_type=MESH
        )
    for partner in (across, beside, corner):
        pl.semaphore_signal(barrier, 1, device_id=(at.dp, partner), device_id_type=MESH)
    pl.semaphore_wait(barrier, size + 2)

    def stage_copy(number):
        kind, state = number // 3, states[number % 3]
        index = number % 3
        if kind == 0:
            source, target = state.expand_out, s.down_stage.at[index]
        elif kind == 1:
            source, target = state.heads_in.at[jnp.minimum(at.mp, line - 2)], s.mine_stage.at[index]
        elif kind == 2:
            source, target = state.heads_out, s.out_stage.at[index]
        elif kind == 3:
            source, target = state.expand_in.at[0], r.gelu.at[pl.ds(index * shard, shard)]
        elif kind == 4:
            source, target = state.expand_in.at[1], r.slope.at[pl.ds(index * shard, shard)]
        elif kind == 5:
            source, target = state.norm_gains, s.gains_stage.at[index]
        else:
            source, target = state.bias_table, s.table_stage.at[index]
        return pltpu.make_async_copy(source, target, s.stage_sems.at[number])

    def stage(kind):
        for index in range(3):
            stage_copy(3 * kind + index).start()

    def staged(kind):
        for index in range(3):
            stage_copy(3 * kind + index).wait()

    norm_lane = lax.broadcasted_iota(jnp.int32, (8, LANES), 1)

    def square_sum(values):
        return jnp.sum(jnp.sum(values * values, axis=0, keepdims=True), axis=1, keepdims=True)

    def add_norms(number, weight, gradient, first, second, decay, scale=1.0):
        step_dir = lamb_parts(weight, gradient, first, second, decay)[2]
        mass = square_sum(weight) * scale
        push = square_sum(step_dir) * scale
        s.norm_part[...] = s.norm_part[...] + (
            jnp.where(norm_lane == number, mass, 0.0) + jnp.where(norm_lane == number + 10, push, 0.0)
        )

    s.norm_part[...] = jnp.zeros((8, LANES), f32)

    def slab_rows(owner):
        return pl.ds(pl.multiple_of(owner * slot, slot), slot)

    def block_rows(number):
        return pl.ds(number * rows, rows)

    def piece_lanes(piece):
        return pl.ds(0, cut) if piece % 2 == 0 else pl.ds(cut, width - cut)

    def piece_slice(piece):
        return slice(0, cut) if piece % 2 == 0 else slice(cut, width)

    def piece_part(piece):
        return pl.ds(0, slot) if piece < 2 else pl.ds(slot, 2 * shard - slot)

    def piece_term(piece, owner):
        lanes = piece_lanes(piece)
        if piece > 3:
            return r.hidden_grad_out[slab_rows(owner), lanes].astype(f32)
        up = r.gate_up[1, slab_rows(owner), lanes].astype(f32)
        if piece > 1:
            return up[slot - shard : shard]
        gate = r.gate_up[0, slab_rows(owner), lanes].astype(f32)
        return jnp.concatenate([gate[:shard], up[: slot - shard]], axis=0)

    def piece_buffer(piece, side, hop):
        if piece < 4:
            return s.wide_came.at[side, hop, piece_part(piece), piece_lanes(piece)]
        return s.down_came.at[side, hop, :, piece_lanes(piece)]

    def piece_starts(piece, side):
        return piece in ((0, 3, 4), (1, 2, 5))[side]

    def piece_target(side, hop):
        return at.owner(half - hop if side == 0 else hop - half)

    def piece_has(piece, side, hop):
        return hop > 0 or piece_starts(piece, side)

    def piece_fresh(piece, side, hop):
        return hop == 0 or (hop == 1 and not piece_starts(piece, side))

    def piece_copy(piece, side, hop):
        if not piece_fresh(piece, side, hop):
            source = piece_buffer(piece, side, hop - 1)
        elif piece > 3:
            source = sources[0].at[slab_rows(piece_target(side, hop)), piece_lanes(piece)]
        else:
            source = s.fresh.at[side, piece_part(piece), piece_lanes(piece)]
        return remote(
            source, piece_buffer(piece, side, hop), s.wide_sems.at[0, piece, side, hop],
            s.wide_sems.at[1, piece, side, hop], at.sides[side], at.mp,
        )

    def serve(piece, hop, sides=(0, 1)):
        for side in sides:
            if not piece_has(piece, side, hop):
                continue
            if hop > 0 and piece_has(piece, side, hop - 1):
                piece_copy(piece, side, hop - 1).wait_recv()
                came = piece_buffer(piece, side, hop - 1)
                term = piece_term(piece, piece_target(side, hop))
                came[...] = (came[...].astype(f32) + term).astype(bf16)
            elif piece < 4:
                term = piece_term(piece, piece_target(side, hop))
                s.fresh[side, piece_part(piece), piece_lanes(piece)] = term.astype(bf16)
            piece_copy(piece, side, hop).start()

    def finish(piece):
        for side in range(2):
            piece_copy(piece, side, half - 1).wait_recv()
        return (
            piece_term(piece, at.dp)
            + piece_buffer(piece, 0, half - 1)[...].astype(f32)
            + piece_buffer(piece, 1, half - 1)[...].astype(f32)
        )

    def mine_lanes(side, hop):
        if hop > 0:
            return pl.ds(0, INNER)
        return pl.ds(0, head_cut) if side == 0 else pl.ds(head_cut, INNER - head_cut)

    def mine_copy(side, hop):
        lanes = mine_lanes(side, hop)
        source = (
            s.mine_grad.at[slab_rows(piece_target(side, hop)), lanes]
            if hop == 0
            else s.mine_came.at[side, hop - 1, :, lanes]
        )
        return remote(
            source, s.mine_came.at[side, hop, :, lanes], s.mine_sems.at[0, side, hop],
            s.mine_sems.at[1, side, hop], at.sides[side], at.mp,
        )

    def mine_serve(hop):
        for side in range(2):
            if hop > 0:
                mine_copy(side, hop - 1).wait_recv()
                came = s.mine_came.at[side, hop - 1]
                term = s.mine_grad.at[slab_rows(piece_target(side, hop))]
                lanes = mine_lanes(side, hop - 1)
                if hop == 1:
                    keep = pl.ds(head_cut, INNER - head_cut) if side == 0 else pl.ds(0, head_cut)
                    came[:, keep] = term[:, keep]
                came[:, lanes] = (
                    came[:, lanes].astype(f32) + term[:, lanes].astype(f32)
                ).astype(bf16)
            mine_copy(side, hop).start()

    def far_copy(number):
        send = (s.far_send, s.across_send, s.far_send, s.across_send, s.pair_send, s.pair_across_send)
        came = (s.far_came, s.across_came, s.far_came, s.across_came)
        came = came + (s.pair_came, s.pair_across_came)
        return remote(
            send[number], came[number], s.line_sems.at[0, number], s.line_sems.at[1, number],
            at.dp, beside if number % 2 == 0 else across,
        )

    def attended_copy(number):
        source, target, partner = ((0, 1, across), (0, 2, beside), (1, 3, beside))[number]
        return remote(
            r.upstream.at[block_rows(source)], r.upstream.at[block_rows(target)],
            s.attended_sems.at[0, number], s.attended_sems.at[1, number], at.dp, partner,
        )

    def near_write(array, tile, values):
        array[tile * 2 * rows : (tile + 1) * 2 * rows, :part_wide] = values

    def near_read(array, number):
        return jnp.concatenate(
            [
                array[2 * rows * tile + number * rows : 2 * rows * tile + (number + 1) * rows, :part_wide]
                for tile in range(2)
            ],
            axis=1,
        )

    def part_of(tile):
        return slice(tile * part_wide, (tile + 1) * part_wide)

    for piece in (4, 5):
        serve(piece, 0)
    serve(4, 1, (1,))
    serve(5, 1, (0,))
    arrive(r.upstream, r.down, r.gelu, r.slope, r.hidden_grad_out)
    for number in (2, 3, 0, 1):
        place = block_rows(number)
        hidden_grad = matmul(r.upstream[place, :], r.down[...])
        s.both_grads[0, place, :] = (hidden_grad * r.slope[place, :]).astype(bf16)
        s.both_grads[1, place, :] = (hidden_grad * r.gelu[place, :]).astype(bf16)
        if number == 3:
            serve(4, 1, (0,))
            serve(5, 1, (1,))
    arrive(r.gate_up)
    for kind in (0, 1, 2, 5, 6):
        stage(kind)

    def normed_tile(first, tile):
        place = pl.ds(first, 2 * rows)
        return contract_cols(
            s.both_grads[0, place, :], r.gate_up[0, part_of(tile), :]
        ) + contract_cols(s.both_grads[1, place, :], r.gate_up[1, part_of(tile), :])

    for tile in range(2):
        s.far_send[:, part_of(tile)] = normed_tile(2 * rows, tile).astype(bf16)
    far_copy(0).start()
    serve(4, 2)
    for tile in range(2):
        near_write(r.slope, tile, normed_tile(0, tile))
    serve(5, 2)
    far_copy(0).wait()
    s.across_send[...] = (near_read(r.slope, 1) + s.far_came[rows:, :].astype(f32)).astype(bf16)
    far_copy(1).start()

    arrive(r.normed_two)
    tiles = 4
    tile_wide = wide // tiles
    for matrix in range(2):
        for tile in range(tiles):
            lanes = slice(tile * tile_wide, (tile + 1) * tile_wide)
            r.gate_up[matrix, lanes, :] = contract_rows(
                r.normed_two[:, lanes], s.both_grads[matrix]
            ).astype(bf16)
        serve(4 + matrix, 3)
    for piece in range(4):
        serve(piece, 0)
    for piece in range(4):
        serve(piece, 1, (0 if piece in (1, 2) else 1,))

    normed_load = pltpu.make_async_copy(
        normed_source, r.normed_two, s.load_sems.at[loaded]
    )
    normed_load.start()
    arrive(r.residual, r.full_gains, r.heads, r.query, r.key, r.value, r.logs, r.mixed)

    far_copy(1).wait()
    grad = (
        near_read(r.slope, 0) + s.far_came[:rows, :].astype(f32) + s.across_came[...].astype(f32)
    )
    through, gain_two_grad = norm_backward(r.residual[...], r.full_gains[1:2, :], grad, depth)
    residual_grad = r.upstream[:rows, :].astype(f32) + through
    s.residual_grad[...] = residual_grad
    attended = residual_grad.astype(bf16)
    r.upstream[:rows, :] = attended
    for number in range(2):
        attended_copy(number).start()
    mixed_grad_all = matmul(attended, r.heads[3]).astype(bf16)

    values = offset_values(head_table(table_ref), first_row, rows, span)
    allowed = allowed_pairs(lens_ref, first_row, rows, keys)
    offsets = []
    for pair in range(PAIRS):
        part = slice(pair * LANES, (pair + 1) * LANES)
        query_grad, key_grad, value_grad, pair_offsets = attend_pair_backward(
            pair, r.query, r.key, r.value, r.logs, mixed_grad_all[:, part], values, allowed, span,
        )
        s.offered[0, :, part] = query_grad.astype(bf16)
        r.slope[:, part] = key_grad
        r.slope[:, INNER + pair * LANES : INNER + (pair + 1) * LANES] = value_grad
        offsets = offsets + pair_offsets
        if pair == 0:
            serve(0, 1, (0,))
            serve(1, 1, (1,))
        if pair == 1:
            serve(2, 1, (1,))
            serve(3, 1, (0,))
    pair_wide = 2 * INNER
    for number, bit in ((0, 1), (1, 3)):
        place = pl.ds(pl.multiple_of((at.mp ^ bit) * rows, rows), rows)
        s.pair_send[number * rows : (number + 1) * rows, :] = r.slope[place, :pair_wide].astype(bf16)
    far_copy(4).start()
    s.offered[3] = r.mixed[...]
    far_copy(4).wait_recv()
    place = pl.ds(pl.multiple_of(across * rows, rows), rows)
    s.pair_across_send[...] = (
        r.slope[place, :pair_wide] + s.pair_came[rows:, :].astype(f32)
    ).astype(bf16)
    far_copy(5).start()
    attended_copy(0).wait_recv()
    attended_copy(2).start()

    arrive(r.hidden)

    def feed_tile(first, tile):
        return contract_cols(r.hidden[pl.ds(first, 2 * rows), :], r.down[part_of(tile), :])

    for tile in range(2):
        s.far_send[:, part_of(tile)] = feed_tile(2 * rows, tile).astype(bf16)
    far_copy(2).start()
    for tile in range(2):
        near_write(r.gelu, tile, feed_tile(0, tile))
    serve(0, 2)
    serve(1, 2)
    far_copy(5).wait_recv()
    place = pl.ds(pl.multiple_of(at.mp * rows, rows), rows)
    both = (
        r.slope[place, :pair_wide]
        + s.pair_came[:rows, :].astype(f32)
        + s.pair_across_came[...].astype(f32)
    ).astype(bf16)
    s.offered[1] = both[:, :INNER]
    s.offered[2] = both[:, INNER:]
    stage(4)

    def right_copy(number):
        partner = (across, beside, corner)[number - 1]
        return remote(
            s.offered.at[partner], s.right.at[block_rows(number)],
            s.right_sems.at[0, number], s.right_sems.at[1, number], at.dp, partner,
        )

    for number in range(1, line):
        right_copy(number).start()
    s.right[block_rows(0), :] = s.offered[at.mp]
    grad = (
        contract_cols(s.offered[0], r.heads[0])
        + contract_cols(s.offered[1], r.heads[1])
        + contract_cols(s.offered[2], r.heads[2])
    )
    arrive(r.wide_tokens)
    through, gain_one_grad = norm_backward(
        r.wide_tokens[...].astype(f32), r.full_gains[0:1, :], grad, depth
    )
    s.residual_grad[...] = s.residual_grad[...] + through

    offset_grad = jnp.concatenate(offsets + [jnp.zeros((8 - HEADS, span), f32)], axis=0)
    reach = lax.broadcasted_iota(jnp.int32, (8, span), 1) - (rows - 1) - first_row
    reach = bucket_ids(reach)
    table_grad = jnp.zeros((8, LANES), f32)
    buckets = table_ref.shape[1]
    for number in range(buckets):
        mass = jnp.sum(jnp.where(reach == number, offset_grad, 0.0), axis=1, keepdims=True)
        table_grad = jnp.where(norm_lane == number, mass, table_grad)
    s.small[0, :, wide:] = table_grad
    s.small[0, 0:1, :wide] = gain_one_grad
    s.small[0, 1:2, :wide] = gain_two_grad
    s.small[0, 2:, :wide] = jnp.zeros((6, wide), f32)

    def line_spread(source, slots, sems, first):
        copies = [
            remote(
                source, slots.at[at.mp], sems.at[first, step], sems.at[first + 1, step],
                at.dp, lax.rem(at.mp + step, line),
            )
            for step in range(1, line)
        ]
        for copy in copies:
            copy.start()
        slots[at.mp] = source[...]
        return copies

    def slot_total(slots, count):
        total = slots[0]
        for number in range(1, count):
            total = total + slots[number]
        return total

    small_copies = line_spread(s.small.at[0], s.small_line, s.small_sems, 0)
    serve(2, 2)
    far_copy(2).wait_recv()
    s.across_send[...] = (
        near_read(r.gelu, 1) + s.far_came[rows:, :].astype(f32)
    ).astype(bf16)
    far_copy(3).start()
    serve(3, 2)

    normed_load.wait()
    for number in range(1, 3):
        attended_copy(number).wait_recv()
    for number in range(1, line):
        right_copy(number).wait_recv()
    last = at.mp == line - 1
    for tile in range(tiles):
        lanes = slice(tile * tile_wide, (tile + 1) * tile_wide)
        left = jnp.where(last, r.upstream[:, lanes], r.normed_two[:, lanes])
        s.mine_grad[lanes, :] = contract_rows(left, s.right[...]).astype(bf16)
    mine_serve(0)

    for copy in small_copies:
        copy.wait()
    s.small[1] = slot_total(s.small_line, line)
    pair_slot = 2 * slot
    plane_copies = []
    for step in range(1, size):
        target = lax.rem(at.dp + step, size)
        lanes = pl.ds(pl.multiple_of(target // 2 * pair_slot, pair_slot), pair_slot)
        plane_copies.append(
            remote(
                s.small.at[1, :, lanes], s.small_gains.at[at.dp], s.small_sems.at[2, step],
                s.small_sems.at[3, step], target, at.mp,
            )
        )
        plane_copies.append(
            remote(
                s.small.at[1, :, pl.ds(wide, LANES)], s.small_table.at[at.dp],
                s.small_sems.at[4, step], s.small_sems.at[5, step], target, at.mp,
            )
        )
    for copy in plane_copies:
        copy.start()
    lanes = pl.ds(pl.multiple_of(at.dp // 2 * pair_slot, pair_slot), pair_slot)
    s.small_gains[at.dp] = s.small[1, :, lanes]
    s.small_table[at.dp] = s.small[1, :, wide:]

    serve(0, 3)
    mine_serve(1)
    serve(1, 3)
    down_total = jnp.concatenate([finish(4), finish(5)], axis=1)
    down_total = down_total[:shard]
    down_held[...] = down_total
    hands[2].start()
    staged(0)
    add_norms(
        6, s.down_stage[0], down_total, s.down_stage[1], s.down_stage[2], weight_decay
    )
    mine_serve(2)
    serve(2, 3)
    for copy in plane_copies:
        copy.wait()
    gains_total = slot_total(s.small_gains, size)
    odd = lax.rem(at.dp, 2) == 1
    gains_total = jnp.where(odd, pltpu.roll(gains_total, slot, 1), gains_total)[:2, :shard]
    out.gains_grad[...] = gains_total
    staged(5)
    for number in range(2):
        row = slice(number, number + 1)
        add_norms(
            7 + number, s.gains_stage[0, row], gains_total[row], s.gains_stage[1, row],
            s.gains_stage[2, row], 0.0, 1.0 / line,
        )
    table_total = slot_total(s.small_table, size)[:HEADS, :buckets]
    out.table_grad[...] = table_total
    staged(6)
    add_norms(
        9, s.table_stage[0], table_total, s.table_stage[1], s.table_stage[2], 0.0,
        1.0 / (line * size),
    )
    far_copy(3).wait_recv()
    layer_out = (
        r.residual[...]
        + (
            near_read(r.gelu, 0)
            + s.far_came[:rows, :].astype(f32)
            + s.across_came[...].astype(f32)
        )
    ).astype(bf16)
    stage(3)
    def grad_copy(matrix):
        held = (r.gelu, r.slope)[matrix]
        return pltpu.make_async_copy(
            held.at[pl.ds(3 * shard, shard)], out.gate_up_grad.at[matrix], s.stage_sems.at[21 + matrix]
        )

    def close(piece):
        total = finish(piece)
        lanes = piece_slice(piece)
        early = slot - shard
        shares = [(0, total[:shard], 0), (1, total[shard:], 0)] if piece < 2 else [(1, total, early)]
        for matrix, gradient, first in shares:
            held = (r.gelu, r.slope)[matrix]
            last_row = first + gradient.shape[0]
            rows_of = [slice(place * shard + first, place * shard + last_row) for place in range(4)]
            held[rows_of[3], lanes] = gradient
            add_norms(
                4 + matrix, held[rows_of[0], lanes], gradient, held[rows_of[1], lanes],
                held[rows_of[2], lanes], weight_decay,
            )
        if piece % 2 == 1:
            grad_copy(piece // 2).start()

    mine_serve(3)
    serve(3, 3)
    staged(3)
    staged(4)
    close(0)
    close(1)
    coarse = s.residual_grad[...].astype(bf16)
    fine = (s.residual_grad[...] - coarse.astype(f32)).astype(bf16)
    tile = 3 * LANES
    for low in range(0, depth, tile):
        high = min(low + tile, depth)
        layer_held[:, low:high] = gathered_tile(
            layer_out, None, low, high, shard, slot
        ).astype(bf16)
        tokens_held[:, low:high] = gathered_tile(coarse, fine, low, high, shard, slot)
    hands[0].start()
    hands[1].start()

    close(2)

    for side in range(2):
        mine_copy(side, half - 1).wait_recv()
    mine_total = (
        s.mine_grad[slab_rows(at.dp), :].astype(f32)
        + s.mine_came[0, half - 1].astype(f32)
        + s.mine_came[1, half - 1].astype(f32)
    ).astype(bf16)
    s.mine_sums[at.mp] = mine_total

    def sums_copy(number):
        partner = (across, beside, corner)[number - 1]
        return remote(
            s.mine_sums.at[at.mp], s.mine_sums.at[at.mp],
            s.sums_sems.at[0, number], s.sums_sems.at[1, number], at.dp, partner,
        )

    for number in range(1, line):
        sums_copy(number).start()
    staged(1)
    staged(2)

    def mine_state(index):
        return jnp.where(last, s.out_stage[index], s.mine_stage[index])

    add_norms(
        at.mp, mine_state(0), mine_total.astype(f32)[:shard], mine_state(1), mine_state(2),
        weight_decay,
    )

    close(3)

    norm_copies = line_spread(s.norm_part, s.norm_line, s.norm_sems, 0)
    for copy in norm_copies:
        copy.wait()
    s.norm_part[...] = slot_total(s.norm_line, line)
    norm_copies = [
        remote(
            s.norm_part, s.norm_plane.at[at.dp], s.norm_sems.at[2, step], s.norm_sems.at[3, step],
            lax.rem(at.dp + step, size), at.mp,
        )
        for step in range(1, size)
    ]
    for copy in norm_copies:
        copy.start()
    s.norm_plane[at.dp] = s.norm_part[...]

    for side in range(2):
        for hop in range(half):
            mine_copy(side, hop).wait_send()
            for piece in range(6):
                if piece_has(piece, side, hop):
                    piece_copy(piece, side, hop).wait_send()
    for number in range(2, 6):
        far_copy(number).wait_send()
    for number in range(3):
        attended_copy(number).wait_send()
    for number in range(1, line):
        right_copy(number).wait_send()
    for number in range(1, line):
        sums_copy(number).wait()
    for number in range(line - 1):
        out.heads_in_grad[number] = s.mine_sums[number].astype(f32)[:shard]
    out.heads_out_grad[...] = s.mine_sums[line - 1].astype(f32)[:shard]
    for copy in norm_copies:
        copy.wait()
    out.norms[...] = slot_total(s.norm_plane, size)
    for matrix in range(2):
        grad_copy(matrix).wait()
    for hand in hands:
        hand.wait()


def ring_backward(size, line, depth, slot, width, span, lens, table, got, states):
    rows = got.query.shape[0]
    wide, keys, half = size * slot, rows * line, size // 2
    shard, buckets = depth // size, table.shape[1]
    shapes = forward_shapes(rows, line, size, slot, width, span)
    dma = pltpu.SemaphoreType.DMA
    far = list(back_loads(got)) + [got.normed] + [array for state in states for array in state]
    operands = [lens, table] + far
    specs = [
        pl.BlockSpec(memory_space=pltpu.SMEM),
        pl.BlockSpec(memory_space=pltpu.VMEM),
    ] + [pl.BlockSpec(memory_space=pl.ANY)] * len(far)
    outs = BackwardOut(
        layer_out=((rows, depth), bf16),
        tokens_grad=((rows, depth), f32),
        heads_in_grad=((line - 1, shard, INNER), f32),
        heads_out_grad=((shard, INNER), f32),
        gate_up_grad=((2, shard, width), f32),
        down_grad=((shard, width), f32),
        gains_grad=((2, shard), f32),
        table_grad=((HEADS, buckets), f32),
        norms=((8, LANES), f32),
    )
    handed = (outs.gate_up_grad, outs.layer_out, outs.tokens_grad, outs.down_grad)
    half_rows = pltpu.VMEM((2 * rows, wide), bf16)
    block = pltpu.VMEM((rows, wide), bf16)
    loads = back_loads(shapes)
    scratch = BackwardScratch(
        load_sems=dma((len(loads) + 1,)),
        residual_grad=pltpu.VMEM((rows, wide), f32),
        both_grads=pltpu.VMEM((2, keys, width), bf16),
        fresh=pltpu.VMEM((2, 2 * shard, width), bf16),
        wide_came=pltpu.VMEM((2, half, 2 * shard, width), bf16),
        down_came=pltpu.VMEM((2, half, slot, width), bf16),
        far_send=half_rows,
        far_came=half_rows,
        across_send=block,
        across_came=block,
        pair_send=pltpu.VMEM((2 * rows, 2 * INNER), bf16),
        pair_came=pltpu.VMEM((2 * rows, 2 * INNER), bf16),
        pair_across_send=pltpu.VMEM((rows, 2 * INNER), bf16),
        pair_across_came=pltpu.VMEM((rows, 2 * INNER), bf16),
        offered=pltpu.VMEM((line, rows, INNER), bf16),
        right=pltpu.VMEM((keys, INNER), bf16),
        mine_grad=pltpu.VMEM((wide, INNER), bf16),
        mine_came=pltpu.VMEM((2, half, slot, INNER), bf16),
        mine_sums=pltpu.VMEM((line, slot, INNER), bf16),
        small=pltpu.VMEM((2, 8, wide + LANES), f32),
        small_line=pltpu.VMEM((line, 8, wide + LANES), f32),
        small_gains=pltpu.VMEM((size, 8, 2 * slot), f32),
        small_table=pltpu.VMEM((size, 8, LANES), f32),
        norm_part=pltpu.VMEM((8, LANES), f32),
        norm_line=pltpu.VMEM((line, 8, LANES), f32),
        norm_plane=pltpu.VMEM((size, 8, LANES), f32),
        down_stage=pltpu.VMEM((3, shard, width), f32),
        mine_stage=pltpu.VMEM((3, shard, INNER), f32),
        out_stage=pltpu.VMEM((3, shard, INNER), f32),
        gains_stage=pltpu.VMEM((3, 2, shard), f32),
        table_stage=pltpu.VMEM((3, HEADS, buckets), f32),
        wide_sems=dma((2, 6, 2, half)),
        line_sems=dma((2, 6)),
        attended_sems=dma((2, 3)),
        right_sems=dma((2, line)),
        mine_sems=dma((2, 2, half)),
        sums_sems=dma((2, line)),
        small_sems=dma((6, size)),
        norm_sems=dma((4, size)),
        stage_sems=dma((23,)),
    )
    flops = 2 * keys * wide * (6 * width + INNER) + 16 * rows * wide * INNER
    results = pl.pallas_call(
        partial(ring_backward_kernel, size, depth, span),
        out_shape=[jax.ShapeDtypeStruct(*shape) for shape in outs],
        in_specs=specs,
        out_specs=[
            pl.BlockSpec(memory_space=pl.ANY if any(shape is one for one in handed) else pltpu.VMEM)
            for shape in outs
        ],
        scratch_shapes=[pltpu.VMEM(*shape) for shape in loads]
        + list(scratch)
        + [pltpu.VMEM(*shape) for shape in handed[1:]]
        + [dma((3,))],
        compiler_params=pltpu.CompilerParams(
            collective_id=5, has_side_effects=True, vmem_limit_bytes=BACKWARD_BYTES
        ),
        cost_estimate=pl.CostEstimate(flops=flops, bytes_accessed=50 * 2**20, transcendentals=0),
        name="ring_backward",
    )(*operands)
    return BackwardOut(*results)


class UpdateOut(NamedTuple):
    layer_out: object
    tokens_grad: object
    first: object
    second: object
    new: object
    copy: object
    norms: object


def update_kernel(*refs):
    norms_ref, layer_source, tokens_source = refs[:3]
    sources = [refs[3 + 6 * kind : 9 + 6 * kind] for kind in range(4)]
    refs = refs[27:]
    layer_target, tokens_target = refs[:2]
    targets = [refs[2 + 6 * kind : 8 + 6 * kind] for kind in range(4)]
    norms_out = refs[26]
    refs = refs[27:]
    held = [refs[6 * kind : 6 * kind + 6] for kind in range(5)]
    layer_held, tokens_held, load_sems, store_sems = refs[30:]
    parts = [(number, None) for number in (5, 4, 1)]
    parts = parts + [(0, index) for index in range(held[0][0].shape[0])]
    parts = parts + [(2, 0), (2, 1), (3, None)]

    def view(ref, index):
        return ref if index is None else ref.at[index]

    def load_copy(spot, kind):
        number, index = parts[spot]
        return pltpu.make_async_copy(
            view(sources[kind][number], index), view(held[kind][number], index),
            load_sems.at[spot, kind],
        )

    def store_copy(spot, kind):
        number, index = parts[spot]
        return pltpu.make_async_copy(
            view(held[kind + 1][number], index), view(targets[kind][number], index),
            store_sems.at[spot, kind],
        )

    passed = [
        pltpu.make_async_copy(layer_source, layer_held, load_sems.at[len(parts), 0]),
        pltpu.make_async_copy(tokens_source, tokens_held, load_sems.at[len(parts), 1]),
    ]
    handed = [
        pltpu.make_async_copy(layer_held, layer_target, store_sems.at[len(parts), 0]),
        pltpu.make_async_copy(tokens_held, tokens_target, store_sems.at[len(parts), 1]),
    ]
    for spot in range(len(parts)):
        for kind in range(4):
            load_copy(spot, kind).start()
    for copy in passed:
        copy.start()
    roots = jnp.sqrt(norms_ref[...])
    count = norms_out.shape[1]
    steps = pltpu.roll(roots, LANES - count, 1)
    norms_out[...] = jnp.concatenate([roots[:1], steps[:1]], axis=0)[:, :count]
    lane = lax.broadcasted_iota(jnp.int32, roots.shape, 1)
    rates = learn_rate * roots / jnp.where(lane < count, steps, 1.0)
    starts = (0, 3, 4, 6, 7, 9)
    for spot, (number, index) in enumerate(parts):
        for kind in range(4):
            load_copy(spot, kind).wait()
        gradient, first, second, weight, copy = [view(held[kind][number], index) for kind in range(5)]
        decay = 0.0 if number > 3 else weight_decay
        rate = rates[:1, starts[number] + (index or 0) : starts[number] + (index or 0) + 1]
        if number == 4:
            rate = jnp.concatenate([rate, rates[:1, starts[number] + 1 : starts[number] + 2]], axis=0)
        old = weight[...]
        new_first, new_second, step_dir = lamb_parts(
            old, gradient[...], first[...], second[...], decay
        )
        new = old - rate * step_dir
        first[...] = new_first
        second[...] = new_second
        weight[...] = new
        copy[...] = new.astype(bf16)
        for kind in range(4):
            store_copy(spot, kind).start()
    for number in range(2):
        passed[number].wait()
        handed[number].start()
    for copy in handed:
        copy.wait()
    for spot in range(len(parts)):
        for kind in range(4):
            store_copy(spot, kind).wait()


def update_all(norms, layer_out, tokens_grad, grads, firsts, seconds, weights, count):
    far = [layer_out, tokens_grad] + list(grads) + list(firsts) + list(seconds) + list(weights)
    shapes = [array.shape for array in grads]
    outs = [(layer_out.shape, bf16), (tokens_grad.shape, f32)]
    for kind in (f32, f32, f32, bf16):
        outs = outs + [(shape, kind) for shape in shapes]
    outs = outs + [((2, count), f32)]
    held = []
    for kind in (f32, f32, f32, f32, bf16):
        held = held + [pltpu.VMEM(shape, kind) for shape in shapes]
    held = held + [pltpu.VMEM(layer_out.shape, bf16), pltpu.VMEM(tokens_grad.shape, f32)]
    spots = 6 + shapes[0][0] + 1
    size = sum(array.size * 4 for array in far)
    any_spec = pl.BlockSpec(memory_space=pl.ANY)
    vmem_spec = pl.BlockSpec(memory_space=pltpu.VMEM)
    results = pl.pallas_call(
        update_kernel,
        out_shape=[jax.ShapeDtypeStruct(*out) for out in outs],
        in_specs=[vmem_spec] + [any_spec] * len(far),
        out_specs=[any_spec] * (len(outs) - 1) + [vmem_spec],
        scratch_shapes=held
        + [pltpu.SemaphoreType.DMA((spots, 4)), pltpu.SemaphoreType.DMA((spots, 4))],
        compiler_params=pltpu.CompilerParams(vmem_limit_bytes=VMEM_BYTES),
        cost_estimate=pl.CostEstimate(flops=size * 4, bytes_accessed=2 * size, transcendentals=size),
        name="update",
    )(norms, *far)
    kinds = [results[2 + 6 * kind : 8 + 6 * kind] for kind in range(4)]
    return UpdateOut(results[0], results[1], *kinds, results[26])


def plain_gradients(
    tokens,
    cotangent,
    lengths,
    heads_in,
    heads_out,
    expand_in,
    expand_out,
    norm_gains,
    bias_table,
):
    rows, depth = tokens.shape
    mp_size = lax.axis_size("mp")
    mp_spot = lax.axis_index("mp")
    keys = rows * mp_size
    span = -(-(keys + rows - 1) // LANES) * LANES
    first_row = mp_spot * rows
    shard_width = norm_gains.shape[1]
    buckets = bias_table.shape[0]

    four = jnp.concatenate([heads_in, heads_out.T[None]], axis=0).astype(bf16)
    mine = lax.dynamic_slice_in_dim(four, mp_spot, 1, axis=0)
    mine_all = gather_dp(mine)
    full_gains = gather_gains(norm_gains.astype(bf16).astype(f32))
    gain_one, gain_two = full_gains[0:1], full_gains[1:2]
    inputs = tokens.astype(f32)
    normed = rms_scale(inputs, gain_one, depth).astype(bf16)
    normed_parts = gather_mp(normed)
    used = first_row + jnp.arange(rows, dtype=jnp.int32) < lengths[0, 0] + lengths[0, 1]
    upstream = jnp.where(used[:, None], cotangent, jnp.zeros_like(cotangent))
    upstream_parts = gather_mp(upstream)

    mine_parts = gather_mp(mine_all)
    by_bit = jnp.concatenate([mine_parts[0], mine_parts[2], mine_parts[1], mine_parts[3]], axis=0)
    full_heads = jnp.concatenate(
        [lax.dynamic_slice_in_dim(by_bit, mp_spot ^ number, 1, axis=0) for number in range(mp_size)],
        axis=0,
    )
    wide_in = gather_dp(expand_in.astype(bf16))
    wide_out = gather_dp(expand_out.T.astype(bf16)[None])[0]

    table = jnp.pad(bias_table.T, ((0, 8 - HEADS), (0, 0)))
    attention_flops = rows * keys * LANES * HEADS
    mixed, query, key, value, logs, residual, normed_two = vmem_call(
        partial(forward_kernel, span, depth),
        [
            ((rows, INNER), bf16),
            ((rows, INNER), bf16),
            ((keys, INNER), bf16),
            ((keys, INNER), bf16),
            ((rows, LANES), f32),
            ((rows, depth), f32),
            ((rows, depth), bf16),
        ],
        (
            2 * depth * INNER * (2 * keys + 2 * rows) + 4 * attention_flops,
            2 * (4 * depth * INNER + 2 * keys * depth),
            rows * keys * HEADS,
        ),
        name="attention_forward",
        smem_first=True,
    )(lengths, *normed_parts, full_heads, table, tokens, gain_two)

    normed_all = jnp.concatenate(gather_mp(normed_two), axis=0)
    upstream_all = jnp.concatenate(upstream_parts, axis=0)
    gate_pre = matmul(normed_all, wide_in[0])
    up_pre = matmul(normed_all, wide_in[1])
    gelu_gate, gelu_pull = jax.vjp(partial(jax.nn.gelu, approximate=True), gate_pre)
    hidden = (gelu_gate * up_pre).astype(bf16)
    expand_out_grad = scatter_dp(contract_rows(upstream_all, hidden).astype(bf16)[None])[0].T
    feed_part = contract_cols(hidden, wide_out).astype(bf16)
    feed_near = feed_part[: 2 * rows].astype(f32) + swap(feed_part[2 * rows :], 1).astype(f32)
    feed_out = feed_near[:rows] + swap(feed_near[rows:].astype(bf16), 2).astype(f32)
    layer_out = (residual + feed_out).astype(bf16)

    hidden_grad = matmul(upstream_all, wide_out)
    up_grad = (hidden_grad * gelu_gate).astype(bf16)
    gate_grad = gelu_pull(hidden_grad * up_pre)[0].astype(bf16)
    normed_part = contract_cols(gate_grad, wide_in[0]) + contract_cols(up_grad, wide_in[1])
    normed_near = normed_part[: 2 * rows] + swap(normed_part[2 * rows :].astype(bf16), 1).astype(f32)
    normed_across = swap(normed_near[rows:].astype(bf16), 2)
    expand_in_grad = scatter_dp(
        jnp.stack(
            [
                contract_rows(normed_all, gate_grad).astype(bf16),
                contract_rows(normed_all, up_grad).astype(bf16),
            ]
        )
    )

    residual_grad, attended_grad, query_grad, near, far, offset_grad, gain_two_grad = vmem_call(
        partial(backward_kernel, span, depth),
        [
            ((rows, depth), f32),
            ((rows, depth), bf16),
            ((rows, INNER), bf16),
            ((2 * rows, 2 * INNER), f32),
            ((2 * rows, 2 * INNER), bf16),
            ((8, span), f32),
            ((1, depth), f32),
        ],
        (
            2 * depth * INNER * rows + 10 * attention_flops,
            rows * depth * 16 + 2 * (4 * depth * INNER + 2 * keys * INNER),
            rows * keys * HEADS,
        ),
        scratch=[pltpu.VMEM((keys, 2 * INNER), f32)],
        name="attention_backward",
        smem_first=True,
    )(
        lengths,
        normed_near[:rows],
        normed_across,
        residual,
        upstream,
        gain_two,
        full_heads,
        query,
        key,
        value,
        logs,
        table,
    )
    attended_parts = gather_mp(attended_grad)
    beside = swap(far, 1)
    across = swap((near[rows:] + beside[rows:].astype(f32)).astype(bf16), 2)
    tokens_grad, both, gain_one_grad = vmem_call(
        partial(input_kernel, depth),
        [((rows, depth), f32), ((rows, 2 * INNER), bf16), ((1, depth), f32)],
        (6 * rows * depth * INNER, rows * depth * 14 + 8 * depth * INNER, 0),
        name="input_backward",
    )(near, beside, across, query_grad, full_heads, tokens, gain_one, residual_grad)

    offered = jnp.stack([query_grad, both[:, :INNER], both[:, INNER:], mixed])

    def for_bit(bit):
        return lax.dynamic_slice_in_dim(offered, mp_spot ^ bit, 1, axis=0)

    from_beside = swap(jnp.concatenate([for_bit(1), for_bit(3)], axis=0), 1)
    from_across = swap(jnp.concatenate([for_bit(2), from_beside[1:]], axis=0), 2)
    right = jnp.concatenate(
        [for_bit(0)[0], from_across[0], from_beside[0], from_across[1]], axis=0
    )
    left = jnp.where(
        mp_spot == mp_size - 1,
        jnp.concatenate(attended_parts, axis=0),
        jnp.concatenate(normed_parts, axis=0),
    )
    mine_grad = scatter_dp(contract_rows(left, right).astype(bf16)[None]).astype(bf16)
    grad_parts = gather_mp(mine_grad)
    grads_by_bit = jnp.concatenate(
        [grad_parts[0], grad_parts[2], grad_parts[1], grad_parts[3]], axis=0
    )
    heads_grad = [
        lax.dynamic_slice_in_dim(grads_by_bit, mp_spot ^ number, 1, axis=0)
        for number in range(mp_size)
    ]
    head_in_grad = jnp.concatenate(heads_grad[:3], axis=0).astype(f32)
    head_out_grad = heads_grad[3][0].T.astype(f32)

    reach = jnp.arange(span, dtype=jnp.int32) - (rows - 1) - first_row
    onehot = (bucket_ids(reach)[:, None] == jnp.arange(buckets, dtype=jnp.int32)[None, :]).astype(f32)
    table_part = jnp.dot(offset_grad, onehot, precision=highest)[:HEADS].T
    gain_parts = jnp.concatenate([gain_one_grad, gain_two_grad], axis=0)
    small = total_all(pack_rows([gain_parts, table_part]), 1).reshape(-1)
    gains_total = small[: 2 * depth].reshape(2, depth)
    table_grad = small[2 * depth : 2 * depth + buckets * HEADS].reshape(buckets, HEADS)
    gains_grad = lax.dynamic_slice_in_dim(
        gains_total, lax.axis_index("dp") * shard_width, shard_width, 1
    )

    return layer_out, tokens_grad, (
        head_in_grad,
        head_out_grad,
        expand_in_grad,
        expand_out_grad,
        gains_grad,
        table_grad,
    )


def ring_step(
    tokens, cotangent, lengths, heads_in, heads_out, expand_in, expand_out, norm_gains, bias_table, firsts, seconds
):
    rows, depth = tokens.shape
    size, line = lax.axis_size("dp"), lax.axis_size("mp")
    span = -(-(rows * line + rows - 1) // LANES) * LANES
    width = expand_in.shape[2]
    slot = -(-norm_gains.shape[1] // 16) * 16
    weights = Moments(heads_in, heads_out, expand_in, expand_out, norm_gains, bias_table)
    weights, firsts, seconds = [
        Moments(state[0], state[1].T, state[2], state[3].T, state[4], state[5].T)
        for state in (weights, firsts, seconds)
    ]
    got = ring_forward(
        size, line, depth, slot, width, span,
        (lengths, tokens, cotangent, norm_gains, weights.bias_table) + tuple(weights[:4]),
    )
    back = ring_backward(
        size, line, depth, slot, width, span, lengths, weights.bias_table, got,
        (weights, firsts, seconds),
    )
    grads = Moments(
        back.heads_in_grad,
        back.heads_out_grad,
        back.gate_up_grad,
        back.down_grad,
        back.gains_grad,
        back.table_grad,
    )
    update = update_all(
        back.norms, back.layer_out, back.tokens_grad, grads, firsts, seconds, weights, 10
    )
    outputs = [update.layer_out, update.tokens_grad]
    for number in range(6):
        for kind in (update.first, update.second, update.new, update.copy):
            outputs.append(kind[number].T if number in (1, 3, 5) else kind[number])
    return tuple(outputs + [update.norms])


def shards(
    tokens,
    cotangent,
    lengths,
    heads_in,
    heads_out,
    expand_in,
    expand_out,
    norm_gains,
    bias_table,
    heads_in_first,
    heads_out_first,
    expand_in_first,
    expand_out_first,
    gains_first,
    table_first,
    heads_in_second,
    heads_out_second,
    expand_in_second,
    expand_out_second,
    gains_second,
    table_second,
):
    given = (
        tokens, cotangent, lengths, heads_in, heads_out, expand_in, expand_out, norm_gains, bias_table
    )
    weight_list = (heads_in, heads_out, expand_in, expand_out, norm_gains, bias_table)
    first_list = (
        heads_in_first,
        heads_out_first,
        expand_in_first,
        expand_out_first,
        gains_first,
        table_first,
    )
    second_list = (
        heads_in_second,
        heads_out_second,
        expand_in_second,
        expand_out_second,
        gains_second,
        table_second,
    )
    decay_list = (weight_decay, weight_decay, weight_decay, weight_decay, 0.0, 0.0)
    sub_list = (3, 1, 2, 1, 2, 1)
    if lax.axis_size("dp") <= RING_LIMIT:
        return ring_step(*given, first_list, second_list)
    layer_out, tokens_grad, grad_list = plain_gradients(*given)
    results = [
        lamb_parts(
            weight_list[number],
            grad_list[number],
            first_list[number],
            second_list[number],
            decay_list[number],
        )
        for number in range(6)
    ]
    count = sum(sub_list)
    shared = 1.0 / lax.axis_size("mp")
    share_list = (shared, shared, 1.0, 1.0, shared, shared / lax.axis_size("dp"))
    parts = [weight_list, [result[2] for result in results]]
    sums = lax.psum(
        jnp.concatenate(
            [
                sub_squares(part[number], sub_list[number]) * share_list[number]
                for part in parts
                for number in range(6)
            ]
        ),
        ("dp", "mp"),
    )
    weight_norm = jnp.sqrt(sums[:count])
    step_norm = jnp.sqrt(sums[count : 2 * count])
    ratios = weight_norm / step_norm
    starts = (0, 3, 4, 6, 7, 9)
    outputs = [layer_out, tokens_grad]
    for number in range(6):
        weight = weight_list[number]
        sub_count = sub_list[number]
        ratio_part = ratios[starts[number] : starts[number] + sub_count]
        shape = (sub_count,) + (1,) * (weight.ndim - 1) if sub_count > 1 else (1,) * weight.ndim
        new_weight = weight - learn_rate * ratio_part.reshape(shape) * results[number][2]
        outputs = outputs + [
            results[number][0],
            results[number][1],
            new_weight,
            new_weight.astype(bf16),
        ]
    outputs = outputs + [jnp.stack([weight_norm, step_norm])]
    return tuple(outputs)


def solution(mesh):
    return jax.shard_map(
        shards,
        mesh=mesh,
        in_specs=(
            P(("dp", "mp"), None),
            P(("dp", "mp"), None),
            P("dp", None),
            P(None, "dp", None),
            P(None, "dp"),
            P(None, "dp", "mp"),
            P("mp", "dp"),
            P(None, "dp"),
            P(),
            P(None, "dp", None),
            P(None, "dp"),
            P(None, "dp", "mp"),
            P("mp", "dp"),
            P(None, "dp"),
            P(),
            P(None, "dp", None),
            P(None, "dp"),
            P(None, "dp", "mp"),
            P("mp", "dp"),
            P(None, "dp"),
            P(),
        ),
        out_specs=(
            P(("dp", "mp"), None),
            P(("dp", "mp"), None),
            P(None, "dp", None),
            P(None, "dp", None),
            P(None, "dp", None),
            P(None, "dp", None),
            P(None, "dp"),
            P(None, "dp"),
            P(None, "dp"),
            P(None, "dp"),
            P(None, "dp", "mp"),
            P(None, "dp", "mp"),
            P(None, "dp", "mp"),
            P(None, "dp", "mp"),
            P("mp", "dp"),
            P("mp", "dp"),
            P("mp", "dp"),
            P("mp", "dp"),
            P(None, "dp"),
            P(None, "dp"),
            P(None, "dp"),
            P(None, "dp"),
            P(),
            P(),
            P(),
            P(),
            P(),
        ),
        check_vma=False,
    )
```

```python
from functools import partial
from typing import NamedTuple

import jax
import jax.numpy as jnp
from jax import lax
from jax.experimental import pallas as pl
from jax.experimental.pallas import tpu as pltpu
from jax.sharding import PartitionSpec as P

HEADS = 6
HEAD_DIM = 64
STEP = 10
INNER = 384
LANES = 128
PAIRS = INNER // LANES
MESH = pl.DeviceIdType.MESH
VMEM_BYTES = 56 * 2**20
BACKWARD_BYTES = 63 * 2**20
RING_LIMIT = 8


norm_eps = 1e-06
beta_first = 0.9
beta_second = 0.999
adam_eps = 1e-06
weight_decay = 0.01
learn_rate = 0.4
masked_fill = -1000000000.0
bucket_edges = (12, 16, 23, 32, 46, 64, 91)
highest = lax.Precision.HIGHEST
f32 = jnp.float32
bf16 = jnp.bfloat16


def bucket_ids(offsets):
    distance = jnp.abs(offsets)
    coarse = jnp.full_like(distance, 8)
    for edge_value in bucket_edges:
        coarse = coarse + (distance >= edge_value).astype(jnp.int32)
    nearby = jnp.where(distance < 8, distance, coarse)
    return nearby + 16 * (offsets > 0).astype(jnp.int32)


def row_mean(values, depth):
    return jnp.sum(values, axis=-1, keepdims=True) * (1.0 / depth)


def rms_scale(hidden_rows, gain_vector, depth):
    return (
        hidden_rows
        * lax.rsqrt(row_mean(hidden_rows * hidden_rows, depth) + norm_eps)
        * gain_vector
    )


def contract_rows(left_side, right_side):
    return lax.dot_general(
        left_side, right_side, (((0,), (0,)), ((), ())), preferred_element_type=f32
    )


def contract_cols(left_side, right_side):
    return lax.dot_general(
        left_side, right_side, (((1,), (1,)), ((), ())), preferred_element_type=f32
    )


def matmul(left_side, right_side):
    return jnp.dot(left_side, right_side, preferred_element_type=f32)


def ring_order(size):
    return list(range(0, size, 2)) + list(range(size - 1, 0, -2))


def ring_pairs(size):
    order = ring_order(size)
    forward = [(order[spot], order[(spot + 1) % size]) for spot in range(size)]
    return forward, [(target, source) for source, target in forward]


def ring_owner(spot, size):
    late = (spot >= size // 2).astype(jnp.int32)
    return 2 * spot + late * (2 * size - 1 - 4 * spot)


def ring_spot(index, size):
    return index // 2 + lax.rem(index, 2) * (size - 1 - 2 * (index // 2))


def cut_of(width):
    return ((width // LANES + 1) // 2) * LANES


def assemble_kernel(size, cut, *refs):
    slabs, (left, right, out, sems) = refs[:-4], refs[-4:]
    spot = ring_spot(lax.axis_index("dp"), size)
    copies = []
    for number, slab in enumerate(slabs):
        shift = number if number < size // 2 else number + 1
        owner = ring_owner(lax.rem(spot + shift, size), size)
        copies.append(pltpu.make_async_copy(slab, out.at[:, owner], sems.at[number]))
    owner = ring_owner(lax.rem(spot + size // 2, size), size)
    width = out.shape[-1]
    copies.append(
        pltpu.make_async_copy(left, out.at[:, owner, :, pl.ds(0, cut)], sems.at[size - 1])
    )
    copies.append(
        pltpu.make_async_copy(right, out.at[:, owner, :, pl.ds(cut, width - cut)], sems.at[size])
    )
    for copy in copies:
        copy.start()
    for copy in copies:
        copy.wait()


def gather_dp(part):
    size = lax.axis_size("dp")
    if size > RING_LIMIT:
        return lax.all_gather(part, "dp", axis=1, tiled=True)
    forward, backward = ring_pairs(size)
    count, rows, width = part.shape
    cut = cut_of(width)
    slabs = [None] * size
    slabs[0] = ahead = behind = part
    for hop in range(1, size // 2):
        ahead = lax.ppermute(ahead, "dp", forward)
        behind = lax.ppermute(behind, "dp", backward)
        slabs[size - hop] = ahead
        slabs[hop] = behind
    left = lax.ppermute(ahead[..., :cut], "dp", forward)
    right = lax.ppermute(behind[..., cut:], "dp", backward)
    operands = [slab for slab in slabs if slab is not None] + [left, right]
    total = count * size * rows * width * part.dtype.itemsize
    whole = pl.pallas_call(
        partial(assemble_kernel, size, cut),
        out_shape=jax.ShapeDtypeStruct((count, size, rows, width), part.dtype),
        in_specs=[pl.BlockSpec(memory_space=pl.ANY)] * len(operands),
        out_specs=pl.BlockSpec(memory_space=pltpu.VMEM),
        scratch_shapes=[pltpu.SemaphoreType.DMA((size + 1,))],
        compiler_params=pltpu.CompilerParams(vmem_limit_bytes=VMEM_BYTES),
        cost_estimate=pl.CostEstimate(flops=0, bytes_accessed=2 * total, transcendentals=0),
        name="assemble",
    )(*operands)
    return whole.reshape(count, size * rows, width)


def scatter_dp(whole):
    size = lax.axis_size("dp")
    if size > RING_LIMIT:
        return lax.psum_scatter(whole.astype(f32), "dp", scatter_dimension=1, tiled=True)
    forward, backward = ring_pairs(size)
    count, depth, width = whole.shape
    rows = depth // size
    cut = cut_of(width)
    spot = ring_spot(lax.axis_index("dp"), size)

    def term(shift):
        owner = ring_owner(lax.rem(spot + size + shift, size), size)
        return lax.dynamic_slice_in_dim(whole, owner * rows, rows, axis=1)

    far = term(size // 2)
    ahead = lax.ppermute(far[..., :cut], "dp", forward)
    behind = lax.ppermute(far[..., cut:], "dp", backward)
    for hop in range(size // 2 - 1, 0, -1):
        mine = term(hop).astype(f32)
        other = term(-hop).astype(f32)
        if hop == size // 2 - 1:
            ahead = jnp.concatenate([mine[..., :cut] + ahead.astype(f32), mine[..., cut:]], -1)
            behind = jnp.concatenate([other[..., :cut], other[..., cut:] + behind.astype(f32)], -1)
        else:
            ahead = mine + ahead.astype(f32)
            behind = other + behind.astype(f32)
        ahead = lax.ppermute(ahead.astype(bf16), "dp", forward)
        behind = lax.ppermute(behind.astype(bf16), "dp", backward)
    return term(0).astype(f32) + ahead.astype(f32) + behind.astype(f32)


def swap(part, bit):
    size = lax.axis_size("mp")
    return lax.ppermute(part, "mp", [(index, index ^ bit) for index in range(size)])


def gather_mp(part):
    across = swap(part, 2)
    beside = swap(part, 1)
    return part, across, beside, swap(across, 1)


def offset_values(table, first_row, rows, span):
    offsets = lax.broadcasted_iota(jnp.int32, (8, span), 1) - (rows - 1) - first_row
    buckets = bucket_ids(offsets)
    values = jnp.zeros((8, span), f32)
    for number in range(table.shape[1]):
        values = jnp.where(buckets == number, table[:, number : number + 1], values)
    return values


def segments_at(positions, first_len, second_len):
    return (positions >= first_len).astype(jnp.int32) + (
        positions >= first_len + second_len
    ).astype(jnp.int32)


def allowed_pairs(lens_ref, first_row, rows, keys):
    query = segments_at(
        first_row + lax.broadcasted_iota(jnp.int32, (rows, 1), 0), lens_ref[0, 0], lens_ref[0, 1]
    )
    key = segments_at(
        lax.broadcasted_iota(jnp.int32, (1, keys), 1), lens_ref[0, 0], lens_ref[0, 1]
    )
    return query == key


def skewed_bias(values, head, rows, keys, span):
    wide = jnp.broadcast_to(values[head : head + 1, :], (rows, span))
    return pltpu.roll(wide, span - (rows - 1), 1, stride=1, stride_axis=0)[:, :keys]


def attend_pair(pair, query_ref, key_ref, value_ref, mixed_ref, logs, values, allowed, lane, span):
    rows, keys = query_ref.shape[0], key_ref.shape[0]
    part = slice(pair * LANES, (pair + 1) * LANES)
    query, key, value = query_ref[:, part], key_ref[:, part], value_ref[:, part]
    mixed = jnp.zeros((rows, LANES), f32)
    for half in range(2):
        head = 2 * pair + half
        mask = (lane // HEAD_DIM) == half
        scores = contract_cols(jnp.where(mask, query, jnp.zeros_like(query)), key)
        scores = jnp.where(
            allowed, scores + skewed_bias(values, head, rows, keys, span), masked_fill
        )
        top = jnp.max(scores, axis=-1, keepdims=True)
        powers = jnp.exp(scores - top)
        total = jnp.sum(powers, axis=-1, keepdims=True)
        soft = (powers * (1.0 / total)).astype(bf16)
        mixed = jnp.where(mask, matmul(soft, value), mixed)
        logs = jnp.where(lane == head, top + jnp.log(total), logs)
    mixed_ref[:, part] = mixed.astype(bf16)
    return logs


def forward_kernel(
    span,
    depth,
    lens_ref,
    own_ref,
    across_ref,
    beside_ref,
    corner_ref,
    heads_ref,
    table_ref,
    tokens_ref,
    gain_ref,
    mixed_ref,
    query_ref,
    key_ref,
    value_ref,
    log_ref,
    residual_ref,
    normed_ref,
):
    rows = own_ref.shape[0]
    keys = key_ref.shape[0]
    spot = lax.axis_index("mp")
    first_row = spot * rows
    for block_ref, bit in ((own_ref, 0), (across_ref, 2), (beside_ref, 1), (corner_ref, 3)):
        place = pl.ds(pl.multiple_of((spot ^ bit) * rows, rows), rows)
        block = block_ref[...]
        key_ref[place, :] = matmul(block, heads_ref[1]).astype(bf16)
        value_ref[place, :] = matmul(block, heads_ref[2]).astype(bf16)
    query_ref[...] = matmul(own_ref[...], heads_ref[0]).astype(bf16)
    values = offset_values(table_ref[...], first_row, rows, span)
    allowed = allowed_pairs(lens_ref, first_row, rows, keys)
    lane = lax.broadcasted_iota(jnp.int32, (1, LANES), 1)
    logs = jnp.zeros((rows, LANES), f32)
    for pair in range(PAIRS):
        logs = attend_pair(
            pair, query_ref, key_ref, value_ref, mixed_ref, logs, values, allowed, lane, span
        )
    log_ref[...] = logs
    residual = tokens_ref[...].astype(f32) + contract_cols(mixed_ref[...], heads_ref[3])
    residual_ref[...] = residual
    normed_ref[...] = rms_scale(residual, gain_ref[...], depth).astype(bf16)


def norm_backward(rows_in, gain, grad, depth):
    scale = lax.rsqrt(row_mean(rows_in * rows_in, depth) + norm_eps)
    unit = rows_in * scale
    inner = grad * gain
    out = scale * (inner - unit * row_mean(inner * unit, depth))
    return out, jnp.sum(grad * unit, axis=0, keepdims=True)


def attend_pair_backward(
    pair, query_ref, key_ref, value_ref, log_ref, mixed_grad, values, allowed, span
):
    rows, keys = query_ref.shape[0], key_ref.shape[0]
    lane = lax.broadcasted_iota(jnp.int32, (1, LANES), 1)
    flip = (
        lax.broadcasted_iota(jnp.int32, (rows, rows), 0)
        + lax.broadcasted_iota(jnp.int32, (rows, rows), 1)
        == rows - 1
    ).astype(bf16)
    part = slice(pair * LANES, (pair + 1) * LANES)
    query, key, value = query_ref[:, part], key_ref[:, part], value_ref[:, part]
    query_grad = jnp.zeros((rows, LANES), f32)
    key_grad = jnp.zeros((keys, LANES), f32)
    value_grad = jnp.zeros((keys, LANES), f32)
    offsets = []
    for half in range(2):
        head = 2 * pair + half
        mask = (lane // HEAD_DIM) == half
        query_own = jnp.where(mask, query, jnp.zeros_like(query))
        mixed_own = jnp.where(mask, mixed_grad, jnp.zeros_like(mixed_grad))
        scores = contract_cols(query_own, key)
        scores = jnp.where(
            allowed, scores + skewed_bias(values, head, rows, keys, span), masked_fill
        )
        soft = jnp.exp(scores - log_ref[:, head : head + 1])
        soft_grad = contract_cols(mixed_own, value)
        corr = jnp.sum(soft * soft_grad, axis=-1, keepdims=True)
        scores_grad = (soft * (soft_grad - corr)).astype(bf16)
        query_grad = jnp.where(mask, matmul(scores_grad, key), query_grad)
        key_grad = key_grad + contract_rows(scores_grad, query_own)
        value_grad = value_grad + contract_rows(soft.astype(bf16), mixed_own)
        flipped = matmul(flip, scores_grad)
        flipped = jnp.concatenate([flipped, jnp.zeros((rows, span - keys), f32)], axis=1)
        skewed = pltpu.roll(flipped, 0, 1, stride=1, stride_axis=0)
        offsets.append(jnp.sum(skewed, axis=0, keepdims=True))
    return query_grad, key_grad, value_grad, offsets


def backward_kernel(
    span,
    depth,
    lens_ref,
    part_ref,
    across_ref,
    residual_ref,
    upstream_ref,
    gain_ref,
    heads_ref,
    query_ref,
    key_ref,
    value_ref,
    log_ref,
    table_ref,
    residual_grad_ref,
    attended_ref,
    query_grad_ref,
    near_ref,
    far_ref,
    offset_ref,
    gain_grad_ref,
    whole_ref,
):
    rows = query_ref.shape[0]
    keys = key_ref.shape[0]
    spot = lax.axis_index("mp")
    first_row = spot * rows
    grad = part_ref[...].astype(f32) + across_ref[...].astype(f32)
    through, gain_grad = norm_backward(residual_ref[...], gain_ref[...], grad, depth)
    gain_grad_ref[...] = gain_grad
    residual_grad = upstream_ref[...].astype(f32) + through
    residual_grad_ref[...] = residual_grad
    attended = residual_grad.astype(bf16)
    attended_ref[...] = attended
    mixed_grad_all = matmul(attended, heads_ref[3]).astype(bf16)
    values = offset_values(table_ref[...], first_row, rows, span)
    allowed = allowed_pairs(lens_ref, first_row, rows, keys)
    for pair in range(PAIRS):
        part = slice(pair * LANES, (pair + 1) * LANES)
        query_grad, key_grad, value_grad, offsets = attend_pair_backward(
            pair, query_ref, key_ref, value_ref, log_ref, mixed_grad_all[:, part], values, allowed,
            span,
        )
        for half in range(2):
            offset_ref[2 * pair + half : 2 * pair + half + 1, :] = offsets[half]
        query_grad_ref[:, part] = query_grad.astype(bf16)
        whole_ref[:, part] = key_grad
        whole_ref[:, INNER + pair * LANES : INNER + (pair + 1) * LANES] = value_grad
    offset_ref[HEADS:, :] = jnp.zeros((8 - HEADS, span), f32)
    for number, bit in enumerate((0, 2)):
        place = pl.ds(pl.multiple_of((spot ^ bit) * rows, rows), rows)
        near_ref[number * rows : (number + 1) * rows, :] = whole_ref[place, :]
    for number, bit in enumerate((1, 3)):
        place = pl.ds(pl.multiple_of((spot ^ bit) * rows, rows), rows)
        far_ref[number * rows : (number + 1) * rows, :] = whole_ref[place, :].astype(bf16)


def input_kernel(
    depth,
    own_ref,
    beside_ref,
    across_ref,
    query_grad_ref,
    heads_ref,
    tokens_ref,
    gain_ref,
    residual_grad_ref,
    tokens_grad_ref,
    both_ref,
    gain_grad_ref,
):
    rows = query_grad_ref.shape[0]
    both = (
        own_ref[:rows, :]
        + beside_ref[:rows, :].astype(f32)
        + across_ref[...].astype(f32)
    ).astype(bf16)
    both_ref[...] = both
    grad = (
        contract_cols(query_grad_ref[...], heads_ref[0])
        + contract_cols(both[:, :INNER], heads_ref[1])
        + contract_cols(both[:, INNER:], heads_ref[2])
    )
    through, gain_grad = norm_backward(tokens_ref[...].astype(f32), gain_ref[...], grad, depth)
    gain_grad_ref[...] = gain_grad
    tokens_grad_ref[...] = residual_grad_ref[...] + through


def vmem_call(body, outs, cost, scratch=(), name=None, smem_first=False):
    def run(*operands):
        specs = [pl.BlockSpec(memory_space=pltpu.VMEM)] * len(operands)
        if smem_first:
            specs[0] = pl.BlockSpec(memory_space=pltpu.SMEM)
        return pl.pallas_call(
            body,
            out_shape=[jax.ShapeDtypeStruct(shape, kind) for shape, kind in outs],
            in_specs=specs,
            out_specs=[pl.BlockSpec(memory_space=pltpu.VMEM)] * len(outs),
            scratch_shapes=list(scratch),
            compiler_params=pltpu.CompilerParams(vmem_limit_bytes=VMEM_BYTES),
            cost_estimate=pl.CostEstimate(
                flops=cost[0], bytes_accessed=cost[1], transcendentals=cost[2]
            ),
            name=name,
        )(*operands)

    return run


def total_kernel(sizes, part_ref, out_ref, line_ref, plane_ref, line_send, line_recv, plane_send, plane_recv):
    plane, line = sizes
    dp_spot, mp_spot = lax.axis_index("dp"), lax.axis_index("mp")
    barrier = pltpu.get_barrier_semaphore()
    for step in range(1, line):
        pl.semaphore_signal(
            barrier, 1, device_id=(dp_spot, lax.rem(mp_spot + step, line)), device_id_type=MESH
        )
    for step in range(1, plane):
        pl.semaphore_signal(
            barrier, 1, device_id=(lax.rem(dp_spot + step, plane), mp_spot), device_id_type=MESH
        )
    pl.semaphore_wait(barrier, line + plane - 2)

    def exchange(source, slots, size, spot, send, recv, target):
        slots[spot] = source[...]
        copies = [
            pltpu.make_async_remote_copy(
                src_ref=source,
                dst_ref=slots.at[spot],
                send_sem=send.at[step],
                recv_sem=recv.at[step],
                device_id=target(lax.rem(spot + step, size)),
                device_id_type=MESH,
            )
            for step in range(1, size)
        ]
        for copy in copies:
            copy.start()
        for copy in copies:
            copy.wait()
        total = slots[0]
        for index in range(1, size):
            total = total + slots[index]
        out_ref[...] = total

    exchange(part_ref, line_ref, line, mp_spot, line_send, line_recv, lambda to: (dp_spot, to))
    exchange(out_ref, plane_ref, plane, dp_spot, plane_send, plane_recv, lambda to: (to, mp_spot))


def total_all(part, number):
    plane, line = lax.axis_size("dp"), lax.axis_size("mp")
    if plane > RING_LIMIT:
        return lax.psum(part, ("dp", "mp"))
    return pl.pallas_call(
        partial(total_kernel, (plane, line)),
        out_shape=jax.ShapeDtypeStruct(part.shape, part.dtype),
        in_specs=[pl.BlockSpec(memory_space=pltpu.VMEM)],
        out_specs=pl.BlockSpec(memory_space=pltpu.VMEM),
        scratch_shapes=[
            pltpu.VMEM((line,) + part.shape, f32),
            pltpu.VMEM((plane,) + part.shape, f32),
            pltpu.SemaphoreType.DMA((line,)),
            pltpu.SemaphoreType.DMA((line,)),
            pltpu.SemaphoreType.DMA((plane,)),
            pltpu.SemaphoreType.DMA((plane,)),
        ],
        compiler_params=pltpu.CompilerParams(collective_id=number, has_side_effects=True),
        name="total",
    )(part)


def small_gather_kernel(size, part_ref, out_ref, send, recv):
    dp_spot, mp_spot = lax.axis_index("dp"), lax.axis_index("mp")
    barrier = pltpu.get_barrier_semaphore()
    for step in range(1, size):
        pl.semaphore_signal(
            barrier, 1, device_id=(lax.rem(dp_spot + step, size), mp_spot), device_id_type=MESH
        )
    pl.semaphore_wait(barrier, size - 1)
    out_ref[dp_spot] = part_ref[...]
    copies = [
        pltpu.make_async_remote_copy(
            src_ref=part_ref,
            dst_ref=out_ref.at[dp_spot],
            send_sem=send.at[step],
            recv_sem=recv.at[step],
            device_id=(lax.rem(dp_spot + step, size), mp_spot),
            device_id_type=MESH,
        )
        for step in range(1, size)
    ]
    for copy in copies:
        copy.start()
    for copy in copies:
        copy.wait()


def gather_gains(gains):
    size = lax.axis_size("dp")
    if size > RING_LIMIT:
        return lax.all_gather(gains, "dp", axis=1, tiled=True)
    count, width = gains.shape
    wide = -(-width // LANES) * LANES
    part = jnp.pad(gains, ((0, 8 - count), (0, wide - width)))
    whole = pl.pallas_call(
        partial(small_gather_kernel, size),
        out_shape=jax.ShapeDtypeStruct((size,) + part.shape, part.dtype),
        in_specs=[pl.BlockSpec(memory_space=pltpu.VMEM)],
        out_specs=pl.BlockSpec(memory_space=pltpu.VMEM),
        scratch_shapes=[pltpu.SemaphoreType.DMA((size,)), pltpu.SemaphoreType.DMA((size,))],
        compiler_params=pltpu.CompilerParams(collective_id=3, has_side_effects=True),
        name="gather_gains",
    )(part)
    return jnp.concatenate([whole[index, :count, :width] for index in range(size)], axis=1)


def pack_rows(parts):
    flat = jnp.concatenate([part.reshape(-1) for part in parts])
    count = -(-flat.shape[0] // (8 * LANES)) * 8
    return jnp.pad(flat, (0, count * LANES - flat.shape[0])).reshape(count, LANES)


def lamb_parts(weight, gradient, first_moment, second, decay_rate):
    new_first = beta_first * first_moment + (1.0 - beta_first) * gradient
    new_second = beta_second * second + (1.0 - beta_second) * gradient * gradient
    first_fix = 1.0 - beta_first**STEP
    second_fix = 1.0 - beta_second**STEP
    step_dir = (new_first * (1.0 / first_fix)) / (
        jnp.sqrt(new_second * (1.0 / second_fix)) + adam_eps
    ) + decay_rate * weight
    return (new_first, new_second, step_dir)


def sub_squares(values, sub_count):
    flat_values = values.reshape(sub_count, -1)
    return jnp.sum(flat_values * flat_values, axis=1)


def gelu_parts(gate):
    root = (2.0 / 3.141592653589793) ** 0.5
    square = gate * gate
    curve = jnp.tanh(root * (gate + 0.044715 * gate * square))
    value = 0.5 * gate * (1.0 + curve)
    slope = 0.5 * (1.0 + curve) + 0.5 * gate * (1.0 - curve * curve) * root * (
        1.0 + 3.0 * 0.044715 * square
    )
    return value, slope


def spread_pair(values, pair, shard, slot):
    depth = values.shape[1]
    first = 2 * pair * shard
    low = first // LANES * LANES
    high = min(depth, -(-(first + 2 * shard) // LANES) * LANES)
    shape = (high - low, 2 * slot)
    source = low + lax.broadcasted_iota(jnp.int32, shape, 0)
    place = lax.broadcasted_iota(jnp.int32, shape, 1)
    late = (place >= slot).astype(jnp.int32)
    offset = place - late * slot
    chosen = (source == first + late * shard + offset) & (offset < shard)
    return matmul(values[:, low:high], chosen.astype(bf16))


def gathered_tile(coarse, fine, low, high, shard, slot):
    def place_of(lane):
        return lane // shard * slot + lane % shard

    first = place_of(low) // LANES * LANES
    last = -(-(place_of(high - 1) + 1) // LANES) * LANES
    shape = (last - first, high - low)
    source = first + lax.broadcasted_iota(jnp.int32, shape, 0)
    lane = low + lax.broadcasted_iota(jnp.int32, shape, 1)
    chosen = jnp.zeros(shape, jnp.bool_)
    for number in range(low // shard, (high - 1) // shard + 1):
        inside = (lane >= number * shard) & (lane < (number + 1) * shard)
        chosen = chosen | (inside & (source == lane + number * (slot - shard)))
    chosen = chosen.astype(bf16)
    total = matmul(coarse[:, first:last], chosen)
    if fine is not None:
        total = total + matmul(fine[:, first:last], chosen)
    return total


def head_table(table_ref):
    table = table_ref[...]
    return jnp.concatenate([table, jnp.zeros((8 - HEADS, table.shape[1]), f32)], axis=0)


class Places:
    def __init__(self, size):
        self.size, self.half = size, size // 2
        self.dp, self.mp = lax.axis_index("dp"), lax.axis_index("mp")
        self.spot = ring_spot(self.dp, size)
        self.sides = (
            ring_owner(lax.rem(self.spot + 1, size), size),
            ring_owner(lax.rem(self.spot + size - 1, size), size),
        )

    def owner(self, shift):
        return ring_owner(lax.rem(self.spot + self.size + shift, self.size), self.size)

    def sent(self, side, hop):
        return self.owner(-hop if side == 0 else hop)

    def came(self, side, hop):
        return self.sent(side, hop + 1)


def remote(source, target, send, recv, dp, mp):
    return pltpu.make_async_remote_copy(
        src_ref=source,
        dst_ref=target,
        send_sem=send,
        recv_sem=recv,
        device_id=(dp, mp),
        device_id_type=MESH,
    )


class ForwardOut(NamedTuple):
    heads: object
    gate_up: object
    down: object
    normed: object
    upstream: object
    normed_two: object
    gelu: object
    slope: object
    hidden: object
    hidden_grad_out: object
    query: object
    key: object
    value: object
    mixed: object
    logs: object
    residual: object
    full_gains: object
    wide_tokens: object


class ForwardRefs(NamedTuple):
    lens: object
    tokens: object
    cotangent: object
    norm_gains: object
    table: object
    heads_in: object
    heads_out: object
    expand_in: object
    expand_out: object
    heads: object
    gate_up: object
    down: object
    normed: object
    upstream: object
    normed_two: object
    gelu: object
    slope: object
    hidden: object
    hidden_grad_out: object
    query: object
    key: object
    value: object
    mixed: object
    logs: object
    residual: object
    full_gains: object
    wide_tokens: object
    tokens_in: object
    cotangent_in: object
    mine_in: object
    out_in: object
    gate_in: object
    down_in: object
    bring_sems: object
    stack: object
    gains: object
    mine: object
    wide_in: object
    wide_out: object
    gain_slots: object
    gain_send: object
    gain_recv: object
    head_send: object
    head_recv: object
    wide_send: object
    wide_recv: object
    line_send: object
    line_recv: object
    slab_send: object
    slab_recv: object
    store_sems: object
    down_sems: object


def forward_shapes(rows, line, size, slot, width, span):
    wide, keys = size * slot, rows * line
    return ForwardOut(
        heads=((4, wide, INNER), bf16),
        gate_up=((2, wide, width), bf16),
        down=((wide, width), bf16),
        normed=((keys, wide), bf16),
        upstream=((keys, wide), bf16),
        normed_two=((keys, wide), bf16),
        gelu=((keys, width), f32),
        slope=((keys, width), f32),
        hidden=((keys, width), bf16),
        hidden_grad_out=((wide, width), bf16),
        query=((rows, INNER), bf16),
        key=((keys, INNER), bf16),
        value=((keys, INNER), bf16),
        mixed=((rows, INNER), bf16),
        logs=((rows, LANES), f32),
        residual=((rows, wide), f32),
        full_gains=((8, wide), f32),
        wide_tokens=((rows, wide), bf16),
    )


def ring_forward_kernel(size, depth, span, *refs):
    count = len(ForwardOut._fields)
    inputs = 9
    stores = refs[inputs : inputs + count]
    r = ForwardRefs(*refs[:inputs], *refs[inputs + count :])
    places = (None, r.tokens_in, r.cotangent_in, None, None, r.mine_in, r.out_in, r.gate_in, r.down_in)

    def bring(number, index=None):
        source = refs[number] if index is None else refs[number].at[index]
        return pltpu.make_async_copy(source, places[number], r.bring_sems.at[number])
    kept = refs[inputs + count : inputs + 2 * count]

    def store_copy(number):
        return pltpu.make_async_copy(kept[number], stores[number], r.store_sems.at[number])

    def store(*which):
        for number in range(count):
            if any(kept[number] is ref for ref in which):
                store_copy(number).start()

    at = Places(size)
    half = at.half
    rows = r.tokens_in.shape[0]
    wide = r.residual.shape[1]
    keys = r.key.shape[0]
    slot = wide // size
    shard = r.norm_gains.shape[1]
    width = r.down.shape[1]
    line = keys // rows
    cut, head_cut = cut_of(width), cut_of(INNER)
    first_row = at.mp * rows
    across, beside = at.mp ^ 2, at.mp ^ 1

    brought = (bring(5, jnp.minimum(at.mp, line - 2)), bring(6), bring(7), bring(1), bring(8), bring(2))
    for copy in brought:
        copy.start()
    barrier = pltpu.get_barrier_semaphore()
    for step in range(1, size):
        pl.semaphore_signal(
            barrier, 1, device_id=(lax.rem(at.dp + step, size), at.mp), device_id_type=MESH
        )
    for partner in (across, beside):
        pl.semaphore_signal(barrier, 1, device_id=(at.dp, partner), device_id_type=MESH)

    def filled(values):
        spare = jnp.zeros((slot - shard, values.shape[1]), f32)
        return jnp.concatenate([values, spare], axis=0).astype(bf16)

    last = at.mp == line - 1
    brought[0].wait()
    brought[1].wait()
    r.mine[...] = filled(jnp.where(last, r.out_in[...], r.mine_in[...]))
    brought[2].wait()
    r.wide_in[...] = jnp.concatenate([r.gate_in[0], r.gate_in[1]], axis=0).astype(bf16)
    rounded = r.norm_gains[...].astype(bf16).astype(f32)
    rounded = jnp.concatenate([rounded, jnp.zeros((2, 2 * slot - shard), f32)], axis=1)
    rounded = jnp.concatenate([rounded, jnp.zeros((6, 2 * slot), f32)], axis=0)
    r.gains[...] = jnp.where(lax.rem(at.dp, 2) == 1, pltpu.roll(rounded, slot, 1), rounded)
    pl.semaphore_wait(barrier, size + 1)

    def slab_rows(owner):
        return pl.ds(pl.multiple_of(owner * slot, slot), slot)

    def head_lanes(side, hop):
        if hop < half - 1:
            return pl.ds(0, INNER)
        return pl.ds(0, head_cut) if side == 0 else pl.ds(head_cut, INNER - head_cut)

    def head_hop(side, hop):
        lanes = head_lanes(side, hop)
        target = r.heads.at[at.mp, slab_rows(at.sent(side, hop)), lanes]
        source = r.mine.at[:, lanes] if hop == 0 else target
        return remote(
            source, target, r.head_send.at[side, hop], r.head_recv.at[side, hop],
            at.sides[side], at.mp,
        )

    def head_came(side, hop):
        target = r.heads.at[at.mp, slab_rows(at.came(side, hop)), head_lanes(side, hop)]
        return remote(
            target, target, r.head_send.at[side, hop], r.head_recv.at[side, hop],
            at.sides[side], at.mp,
        )

    def piece_part(piece):
        lanes = pl.ds(0, cut) if piece % 2 == 0 else pl.ds(cut, width - cut)
        return (pl.ds(0, slot) if piece < 2 else pl.ds(slot, 2 * shard - slot)), lanes

    def piece_view(piece, owner):
        part, lanes = piece_part(piece)
        if piece < 4:
            return r.stack.at[owner, part, lanes]
        return r.down.at[slab_rows(owner), lanes]

    def piece_source(piece):
        part, lanes = piece_part(piece)
        if piece < 4:
            return r.wide_in.at[part, lanes]
        return r.wide_out.at[:, lanes]

    def down_copy(shift):
        view = slab_rows(at.owner(shift))
        return pltpu.make_async_copy(
            r.down.at[view], stores[ForwardOut._fields.index("down")].at[view],
            r.down_sems.at[shift % size],
        )

    def store_down(*which):
        for shift in which:
            down_copy(shift).start()

    def unstack(shift):
        owner = at.owner(shift)
        both = r.stack[owner].astype(f32)
        r.gate_up[0, slab_rows(owner), :] = filled(both[:shard])
        r.gate_up[1, slab_rows(owner), :] = filled(both[shard:])

    def piece_goes(piece, side, hop):
        return hop < half - 1 or piece in ((0, 3, 4), (1, 2, 5))[side]

    def piece_hop(piece, side, hop):
        target = piece_view(piece, at.sent(side, hop))
        source = piece_source(piece) if hop == 0 else target
        return remote(
            source, target, r.wide_send.at[piece, side, hop], r.wide_recv.at[piece, side, hop],
            at.sides[side], at.mp,
        )

    def piece_came(piece, side, hop):
        target = piece_view(piece, at.came(side, hop))
        return remote(
            target, target, r.wide_send.at[piece, side, hop], r.wide_recv.at[piece, side, hop],
            at.sides[side], at.mp,
        )

    def serve(piece, hop):
        for side in range(2):
            if piece_goes(piece, side, hop):
                if hop > 0:
                    piece_came(piece, side, hop - 1).wait_recv()
                piece_hop(piece, side, hop).start()

    def finish(piece):
        for side in range(2):
            last = half - 1 if piece_goes(piece, side, half - 1) else half - 2
            piece_came(piece, side, last).wait_recv()

    def block(array, number):
        return array.at[pl.ds(number * rows, rows)]

    def line_copy(array, ref, number):
        source, target, partner = ((0, 1, across), (0, 2, beside), (1, 3, beside))[number]
        return remote(
            block(ref, source), block(ref, target), r.line_send.at[array, number],
            r.line_recv.at[array, number], at.dp, partner,
        )

    shifts = [0] + [shift for hop in range(1, half) for shift in (-hop, hop)] + [half]

    def slab_copy(number, way):
        matrix = across if way == 2 else at.mp
        view = r.heads.at[matrix, slab_rows(at.owner(shifts[number]))]
        source = r.mine if number == 0 and way < 2 else view
        return remote(
            source, view, r.slab_send.at[number, way], r.slab_recv.at[number, way],
            at.dp, across if way == 0 else beside,
        )

    def slab_came(number, way):
        matrix = (across, beside, at.mp ^ 3)[way]
        view = r.heads.at[matrix, slab_rows(at.owner(shifts[number]))]
        return remote(
            view, view, r.slab_send.at[number, way], r.slab_recv.at[number, way],
            at.dp, across if way == 0 else beside,
        )

    def gain_copy(step):
        return remote(
            r.gains, r.gain_slots.at[at.dp], r.gain_send.at[step], r.gain_recv.at[step],
            lax.rem(at.dp + step, size), at.mp,
        )

    for step in range(1, size):
        gain_copy(step).start()
    for side in range(2):
        head_hop(side, 0).start()
    for way in range(2):
        slab_copy(0, way).start()
    serve(0, 0)
    brought[3].wait()
    for pair in range(half):
        lanes = slice(2 * pair * slot, 2 * (pair + 1) * slot)
        r.wide_tokens[:, lanes] = spread_pair(r.tokens_in[...], pair, shard, slot).astype(bf16)
    r.gain_slots[at.dp] = r.gains[...]
    for step in range(1, size):
        gain_copy(step).wait()
    r.full_gains[...] = jnp.concatenate(
        [r.gain_slots[2 * pair] + r.gain_slots[2 * pair + 1] for pair in range(half)], axis=1
    )
    block(r.normed, 0)[...] = rms_scale(
        r.wide_tokens[...].astype(f32), r.full_gains[0:1, :], depth
    ).astype(bf16)
    for number in range(2):
        line_copy(0, r.normed, number).start()

    def fill_own():
        own = slab_rows(at.dp)
        r.heads[at.mp, own, :] = r.mine[...]
        r.gate_up[0, own, :] = filled(r.gate_in[0])
        r.gate_up[1, own, :] = filled(r.gate_in[1])
        brought[4].wait()
        r.wide_out[...] = filled(r.down_in[...])
        r.down[own, :] = r.wide_out[...]

    def fill_upstream():
        brought[5].wait()
        positions = first_row + lax.broadcasted_iota(jnp.int32, (rows, 1), 0)
        used = positions < r.lens[0, 0] + r.lens[0, 1]
        upstream = jnp.where(used, r.cotangent_in[...].astype(f32), 0.0).astype(bf16)
        for pair in range(half):
            lanes = slice(2 * pair * slot, 2 * (pair + 1) * slot)
            r.upstream[:rows, lanes] = spread_pair(upstream, pair, shard, slot).astype(bf16)

    fillers = [[(1, 0)], [(2, 0)], [(3, 0), (0, 1)], [(1, 1)]]
    for hop in range(half):
        for side in range(2):
            head_came(side, hop).wait_recv()
            if hop + 1 < half:
                head_hop(side, hop + 1).start()
        for piece, piece_at in fillers[min(hop, 3)]:
            serve(piece, piece_at)
        done = (2 * hop + 1, 2 * hop + 2) if hop + 1 < half else (2 * hop + 1,)
        for number in done:
            for way in range(2):
                slab_copy(number, way).start()
        if hop == 0:
            fill_own()
        if hop == 1:
            fill_upstream()
    line_copy(0, r.normed, 0).wait_recv()
    line_copy(0, r.normed, 2).start()
    for number in range(2):
        line_copy(1, r.upstream, number).start()
    serve(2, 1)
    serve(3, 1)
    for number in range(size):
        slab_came(number, 0).wait_recv()
        slab_copy(number, 2).start()
        if number in (size // 2, size - 2):
            serve(int(number == size - 2), 2)
    for number in range(size):
        slab_came(number, 1).wait_recv()
    for number in range(size):
        slab_came(number, 2).wait_recv()

    serve(2, 2)
    serve(3, 2)

    r.query[...] = matmul(block(r.normed, 0)[...], r.heads[0]).astype(bf16)
    for number, bit in ((0, 0), (2, 1), (1, 2), (3, 3)):
        if number == 2:
            line_copy(0, r.normed, 1).wait_recv()
        if number == 3:
            line_copy(0, r.normed, 2).wait_recv()
        place = pl.ds(pl.multiple_of((at.mp ^ bit) * rows, rows), rows)
        data = block(r.normed, number)[...]
        r.key[place, :] = matmul(data, r.heads[1]).astype(bf16)
        r.value[place, :] = matmul(data, r.heads[2]).astype(bf16)
    store(r.full_gains, r.wide_tokens, r.normed, r.query, r.key, r.value)

    unstack(-1)
    unstack(1)

    values = offset_values(head_table(r.table), first_row, rows, span)
    allowed = allowed_pairs(r.lens, first_row, rows, keys)
    lane = lax.broadcasted_iota(jnp.int32, (1, LANES), 1)
    logs = jnp.zeros((rows, LANES), f32)
    for pair in range(PAIRS):
        logs = attend_pair(
            pair, r.query, r.key, r.value, r.mixed, logs, values, allowed, lane, span
        )
        if pair > 0:
            serve(2 * pair - 2, 3)
            serve(2 * pair - 1, 3)
    serve(4, 0)
    serve(5, 0)
    r.logs[...] = logs
    residual = r.wide_tokens[...].astype(f32) + contract_cols(r.mixed[...], r.heads[3])
    r.residual[...] = residual
    block(r.normed_two, 0)[...] = rms_scale(residual, r.full_gains[1:2, :], depth).astype(bf16)
    store(r.heads, r.mixed, r.logs, r.residual)
    for number in range(2):
        line_copy(2, r.normed_two, number).start()
    unstack(-2)
    unstack(2)
    for piece in range(4):
        finish(piece)
    for shift in (-3, 3, half):
        unstack(shift)

    def expand(number):
        place = pl.ds(number * rows, rows)
        data = r.normed_two[place, :]
        gate = matmul(data, r.gate_up[0])
        up = matmul(data, r.gate_up[1])
        value, slope = gelu_parts(gate)
        r.gelu[place, :] = value
        r.slope[place, :] = slope * up
        r.hidden[place, :] = (value * up).astype(bf16)

    expand(0)
    serve(4, 1)
    line_copy(2, r.normed_two, 0).wait_recv()
    line_copy(2, r.normed_two, 2).start()
    line_copy(2, r.normed_two, 1).wait_recv()
    serve(5, 1)
    expand(2)
    serve(4, 2)
    store_down(0, -1, 1)
    expand(1)
    serve(5, 2)
    line_copy(2, r.normed_two, 2).wait_recv()
    expand(3)
    store_down(-2, 2)
    store(r.gelu, r.slope, r.hidden, r.gate_up, r.normed_two)
    line_copy(1, r.upstream, 0).wait_recv()
    line_copy(1, r.upstream, 2).start()
    line_copy(1, r.upstream, 1).wait_recv()
    line_copy(1, r.upstream, 2).wait_recv()
    store(r.upstream)
    tiles = 4
    tile = wide // tiles
    for number in range(tiles):
        lanes = slice(number * tile, (number + 1) * tile)
        r.hidden_grad_out[lanes, :] = contract_rows(
            r.upstream[:, lanes], r.hidden[...]
        ).astype(bf16)
        if number == 0:
            serve(4, 3)
            serve(5, 3)
    store(r.hidden_grad_out)
    for piece in (4, 5):
        finish(piece)
    store_down(-3, 3, half)

    for side in range(2):
        for hop in range(half):
            head_hop(side, hop).wait_send()
            for piece in range(6):
                if piece_goes(piece, side, hop):
                    piece_hop(piece, side, hop).wait_send()
    for number in range(size):
        for way in range(3):
            slab_copy(number, way).wait_send()
    for array, ref in enumerate((r.normed, r.upstream, r.normed_two)):
        for number in range(3):
            line_copy(array, ref, number).wait_send()
    for number in range(count):
        if kept[number] is not r.down:
            store_copy(number).wait()
    for shift in range(size):
        down_copy(shift).wait()


def ring_forward(size, line, depth, slot, width, span, operands):
    rows, shard = operands[1].shape[0], depth // size
    shapes = forward_shapes(rows, line, size, slot, width, span)
    wide, keys = size * slot, rows * line
    dma = pltpu.SemaphoreType.DMA
    half = size // 2
    specs = [pl.BlockSpec(memory_space=pl.ANY)] * len(operands)
    specs[0] = pl.BlockSpec(memory_space=pltpu.SMEM)
    specs[3] = specs[4] = pl.BlockSpec(memory_space=pltpu.VMEM)
    flops = 2 * keys * wide * (3 * width + 2 * INNER) + 4 * rows * wide * INNER
    results = pl.pallas_call(
        partial(ring_forward_kernel, size, depth, span),
        out_shape=[jax.ShapeDtypeStruct(*shape) for shape in shapes],
        in_specs=specs,
        out_specs=[pl.BlockSpec(memory_space=pl.ANY)] * len(shapes),
        scratch_shapes=[pltpu.VMEM(*shape) for shape in shapes]
        + [
            pltpu.VMEM((rows, depth), bf16),
            pltpu.VMEM((rows, depth), bf16),
            pltpu.VMEM((shard, INNER), f32),
            pltpu.VMEM((shard, INNER), f32),
            pltpu.VMEM((2, shard, width), f32),
            pltpu.VMEM((shard, width), f32),
            dma((len(operands),)),
            pltpu.VMEM((size, 2 * shard, width), bf16),
            pltpu.VMEM((8, 2 * slot), f32),
            pltpu.VMEM((slot, INNER), bf16),
            pltpu.VMEM((2 * shard, width), bf16),
            pltpu.VMEM((slot, width), bf16),
            pltpu.VMEM((size, 8, 2 * slot), f32),
            dma((size,)),
            dma((size,)),
            dma((2, half)),
            dma((2, half)),
            dma((6, 2, half)),
            dma((6, 2, half)),
            dma((3, 3)),
            dma((3, 3)),
            dma((size, 3)),
            dma((size, 3)),
            dma((len(shapes),)),
            dma((size,)),
        ],
        compiler_params=pltpu.CompilerParams(
            collective_id=4, has_side_effects=True, vmem_limit_bytes=60 * 2**20
        ),
        cost_estimate=pl.CostEstimate(flops=flops, bytes_accessed=40 * 2**20, transcendentals=0),
        name="ring_forward",
    )(*operands)
    return ForwardOut(*results)


class BackwardOut(NamedTuple):
    layer_out: object
    tokens_grad: object
    heads_grad: object
    gate_up_grad: object
    down_grad: object
    gains_grad: object
    table_grad: object
    norms: object


class BackwardLoads(NamedTuple):
    hidden_grad_out: object
    upstream: object
    down: object
    gelu: object
    slope: object
    gate_up: object
    normed_two: object
    hidden: object
    residual: object
    full_gains: object
    heads: object
    query: object
    key: object
    value: object
    logs: object
    mixed: object
    wide_tokens: object


class Moments(NamedTuple):
    heads_in: object
    heads_out: object
    expand_in: object
    expand_out: object
    norm_gains: object
    bias_table: object


class BackwardScratch(NamedTuple):
    load_sems: object
    residual_grad: object
    both_grads: object
    fresh: object
    wide_came: object
    down_came: object
    far_send: object
    far_came: object
    across_send: object
    across_came: object
    pair_send: object
    pair_came: object
    pair_across_send: object
    pair_across_came: object
    offered: object
    right: object
    mine_grad: object
    mine_came: object
    mine_sums: object
    small: object
    small_line: object
    small_gains: object
    small_table: object
    norm_part: object
    norm_line: object
    norm_plane: object
    down_stage: object
    mine_stage: object
    out_stage: object
    gains_stage: object
    table_stage: object
    wide_sems: object
    line_sems: object
    attended_sems: object
    right_sems: object
    mine_sems: object
    sums_sems: object
    small_sems: object
    norm_sems: object
    stage_sems: object


def back_loads(values):
    return BackwardLoads(*[getattr(values, name) for name in BackwardLoads._fields])


def ring_backward_kernel(size, depth, span, *refs):
    lens_ref, table_ref = refs[:2]
    refs = refs[2:]
    loaded = len(BackwardLoads._fields)
    sources, normed_source, refs = refs[:loaded], refs[loaded], refs[loaded + 1 :]
    states = [Moments(*refs[6 * number : 6 * number + 6]) for number in range(3)]
    refs = refs[18:]
    outs = len(BackwardOut._fields)
    out, refs = BackwardOut(*refs[:outs]), refs[outs:]
    hand_sems, refs = refs[-1], refs[:-1]
    layer_held, tokens_held, down_held = refs[-3:]
    refs = refs[:-3]
    hands = [
        pltpu.make_async_copy(layer_held, out.layer_out, hand_sems.at[0]),
        pltpu.make_async_copy(tokens_held, out.tokens_grad, hand_sems.at[1]),
        pltpu.make_async_copy(down_held, out.down_grad, hand_sems.at[2]),
    ]
    r, s = BackwardLoads(*refs[:loaded]), BackwardScratch(*refs[loaded:])

    def load_copy(number):
        return pltpu.make_async_copy(sources[number], r[number], s.load_sems.at[number])

    def arrive(*which):
        for number in range(loaded):
            if any(r[number] is ref for ref in which):
                load_copy(number).wait()

    for number in range(loaded):
        load_copy(number).start()
    at = Places(size)
    half = at.half
    rows = r.query.shape[0]
    keys = r.key.shape[0]
    wide = r.residual.shape[1]
    slot = wide // size
    shard = depth // size
    width = r.down.shape[1]
    line = keys // rows
    cut, head_cut = cut_of(width), cut_of(INNER)
    first_row = at.mp * rows
    across, beside, corner = at.mp ^ 2, at.mp ^ 1, at.mp ^ 3
    part_wide = wide // 2

    barrier = pltpu.get_barrier_semaphore()
    for step in range(1, size * line):
        target = lax.rem(at.dp * line + at.mp + step, size * line)
        pl.semaphore_signal(
            barrier, 1, device_id=(target // line, lax.rem(target, line)), device_id_type=MESH
        )
    pl.semaphore_wait(barrier, size * line - 1)

    def stage_copy(number):
        kind, state = number // 3, states[number % 3]
        index = number % 3
        if kind == 0:
            source, target = state.expand_out, s.down_stage.at[index]
        elif kind == 1:
            source, target = state.heads_in.at[jnp.minimum(at.mp, line - 2)], s.mine_stage.at[index]
        elif kind == 2:
            source, target = state.heads_out, s.out_stage.at[index]
        elif kind == 3:
            source, target = state.expand_in.at[0], r.gelu.at[pl.ds(index * shard, shard)]
        elif kind == 4:
            source, target = state.expand_in.at[1], r.slope.at[pl.ds(index * shard, shard)]
        elif kind == 5:
            source, target = state.norm_gains, s.gains_stage.at[index]
        else:
            source, target = state.bias_table, s.table_stage.at[index]
        return pltpu.make_async_copy(source, target, s.stage_sems.at[number])

    def stage(kind):
        for index in range(3):
            stage_copy(3 * kind + index).start()

    def staged(kind):
        for index in range(3):
            stage_copy(3 * kind + index).wait()

    norm_lane = lax.broadcasted_iota(jnp.int32, (8, LANES), 1)

    def square_sum(values):
        return jnp.sum(jnp.sum(values * values, axis=0, keepdims=True), axis=1, keepdims=True)

    def add_norms(number, weight, gradient, first, second, decay, scale=1.0):
        step_dir = lamb_parts(weight, gradient, first, second, decay)[2]
        mass = square_sum(weight) * scale
        push = square_sum(step_dir) * scale
        s.norm_part[...] = s.norm_part[...] + (
            jnp.where(norm_lane == number, mass, 0.0) + jnp.where(norm_lane == number + 10, push, 0.0)
        )

    s.norm_part[...] = jnp.zeros((8, LANES), f32)

    def slab_rows(owner):
        return pl.ds(pl.multiple_of(owner * slot, slot), slot)

    def block_rows(number):
        return pl.ds(number * rows, rows)

    def piece_lanes(piece):
        return pl.ds(0, cut) if piece % 2 == 0 else pl.ds(cut, width - cut)

    def piece_slice(piece):
        return slice(0, cut) if piece % 2 == 0 else slice(cut, width)

    def piece_part(piece):
        return pl.ds(0, slot) if piece < 2 else pl.ds(slot, 2 * shard - slot)

    def piece_term(piece, owner):
        lanes = piece_lanes(piece)
        if piece > 3:
            return r.hidden_grad_out[slab_rows(owner), lanes].astype(f32)
        up = r.gate_up[1, slab_rows(owner), lanes].astype(f32)
        if piece > 1:
            return up[slot - shard : shard]
        gate = r.gate_up[0, slab_rows(owner), lanes].astype(f32)
        return jnp.concatenate([gate[:shard], up[: slot - shard]], axis=0)

    def piece_buffer(piece, side, hop):
        if piece < 4:
            return s.wide_came.at[side, hop, piece_part(piece), piece_lanes(piece)]
        return s.down_came.at[side, hop, :, piece_lanes(piece)]

    def piece_starts(piece, side):
        return piece in ((0, 3, 4), (1, 2, 5))[side]

    def piece_target(side, hop):
        return at.owner(half - hop if side == 0 else hop - half)

    def piece_has(piece, side, hop):
        return hop > 0 or piece_starts(piece, side)

    def piece_fresh(piece, side, hop):
        return hop == 0 or (hop == 1 and not piece_starts(piece, side))

    def piece_copy(piece, side, hop):
        if not piece_fresh(piece, side, hop):
            source = piece_buffer(piece, side, hop - 1)
        elif piece > 3:
            source = sources[0].at[slab_rows(piece_target(side, hop)), piece_lanes(piece)]
        else:
            source = s.fresh.at[side, piece_part(piece), piece_lanes(piece)]
        return remote(
            source, piece_buffer(piece, side, hop), s.wide_sems.at[0, piece, side, hop],
            s.wide_sems.at[1, piece, side, hop], at.sides[side], at.mp,
        )

    def serve(piece, hop, sides=(0, 1)):
        for side in sides:
            if not piece_has(piece, side, hop):
                continue
            if hop > 0 and piece_has(piece, side, hop - 1):
                piece_copy(piece, side, hop - 1).wait_recv()
                came = piece_buffer(piece, side, hop - 1)
                term = piece_term(piece, piece_target(side, hop))
                came[...] = (came[...].astype(f32) + term).astype(bf16)
            elif piece < 4:
                term = piece_term(piece, piece_target(side, hop))
                s.fresh[side, piece_part(piece), piece_lanes(piece)] = term.astype(bf16)
            piece_copy(piece, side, hop).start()

    def finish(piece):
        for side in range(2):
            piece_copy(piece, side, half - 1).wait_recv()
        return (
            piece_term(piece, at.dp)
            + piece_buffer(piece, 0, half - 1)[...].astype(f32)
            + piece_buffer(piece, 1, half - 1)[...].astype(f32)
        )

    def mine_lanes(side, hop):
        if hop > 0:
            return pl.ds(0, INNER)
        return pl.ds(0, head_cut) if side == 0 else pl.ds(head_cut, INNER - head_cut)

    def mine_copy(side, hop):
        lanes = mine_lanes(side, hop)
        source = (
            s.mine_grad.at[slab_rows(piece_target(side, hop)), lanes]
            if hop == 0
            else s.mine_came.at[side, hop - 1, :, lanes]
        )
        return remote(
            source, s.mine_came.at[side, hop, :, lanes], s.mine_sems.at[0, side, hop],
            s.mine_sems.at[1, side, hop], at.sides[side], at.mp,
        )

    def mine_serve(hop):
        for side in range(2):
            if hop > 0:
                mine_copy(side, hop - 1).wait_recv()
                came = s.mine_came.at[side, hop - 1]
                term = s.mine_grad.at[slab_rows(piece_target(side, hop))]
                lanes = mine_lanes(side, hop - 1)
                if hop == 1:
                    keep = pl.ds(head_cut, INNER - head_cut) if side == 0 else pl.ds(0, head_cut)
                    came[:, keep] = term[:, keep]
                came[:, lanes] = (
                    came[:, lanes].astype(f32) + term[:, lanes].astype(f32)
                ).astype(bf16)
            mine_copy(side, hop).start()

    def far_copy(number):
        send = (s.far_send, s.across_send, s.far_send, s.across_send, s.pair_send, s.pair_across_send)
        came = (s.far_came, s.across_came, s.far_came, s.across_came)
        came = came + (s.pair_came, s.pair_across_came)
        return remote(
            send[number], came[number], s.line_sems.at[0, number], s.line_sems.at[1, number],
            at.dp, beside if number % 2 == 0 else across,
        )

    def attended_copy(number):
        source, target, partner = ((0, 1, across), (0, 2, beside), (1, 3, beside))[number]
        return remote(
            r.upstream.at[block_rows(source)], r.upstream.at[block_rows(target)],
            s.attended_sems.at[0, number], s.attended_sems.at[1, number], at.dp, partner,
        )

    def near_write(array, tile, values):
        array[tile * 2 * rows : (tile + 1) * 2 * rows, :part_wide] = values

    def near_read(array, number):
        return jnp.concatenate(
            [
                array[2 * rows * tile + number * rows : 2 * rows * tile + (number + 1) * rows, :part_wide]
                for tile in range(2)
            ],
            axis=1,
        )

    def part_of(tile):
        return slice(tile * part_wide, (tile + 1) * part_wide)

    for piece in (4, 5):
        serve(piece, 0)
    serve(4, 1, (1,))
    serve(5, 1, (0,))
    arrive(r.upstream, r.down, r.gelu, r.slope, r.hidden_grad_out)
    for number in (2, 3, 0, 1):
        place = block_rows(number)
        hidden_grad = matmul(r.upstream[place, :], r.down[...])
        s.both_grads[0, place, :] = (hidden_grad * r.slope[place, :]).astype(bf16)
        s.both_grads[1, place, :] = (hidden_grad * r.gelu[place, :]).astype(bf16)
        if number == 3:
            serve(4, 1, (0,))
            serve(5, 1, (1,))
    arrive(r.gate_up)
    for kind in (0, 1, 2, 5, 6):
        stage(kind)

    def normed_tile(first, tile):
        place = pl.ds(first, 2 * rows)
        return contract_cols(
            s.both_grads[0, place, :], r.gate_up[0, part_of(tile), :]
        ) + contract_cols(s.both_grads[1, place, :], r.gate_up[1, part_of(tile), :])

    for tile in range(2):
        s.far_send[:, part_of(tile)] = normed_tile(2 * rows, tile).astype(bf16)
    far_copy(0).start()
    serve(4, 2)
    for tile in range(2):
        near_write(r.slope, tile, normed_tile(0, tile))
    serve(5, 2)
    far_copy(0).wait()
    s.across_send[...] = (near_read(r.slope, 1) + s.far_came[rows:, :].astype(f32)).astype(bf16)
    far_copy(1).start()

    arrive(r.normed_two)
    tiles = 4
    tile_wide = wide // tiles
    for matrix in range(2):
        for tile in range(tiles):
            lanes = slice(tile * tile_wide, (tile + 1) * tile_wide)
            r.gate_up[matrix, lanes, :] = contract_rows(
                r.normed_two[:, lanes], s.both_grads[matrix]
            ).astype(bf16)
        serve(4 + matrix, 3)
    for piece in range(4):
        serve(piece, 0)
    for piece in range(4):
        serve(piece, 1, (0 if piece in (1, 2) else 1,))

    normed_load = pltpu.make_async_copy(
        normed_source, r.normed_two, s.load_sems.at[loaded]
    )
    normed_load.start()
    arrive(r.residual, r.full_gains, r.heads, r.query, r.key, r.value, r.logs, r.mixed)

    far_copy(1).wait()
    grad = (
        near_read(r.slope, 0) + s.far_came[:rows, :].astype(f32) + s.across_came[...].astype(f32)
    )
    through, gain_two_grad = norm_backward(r.residual[...], r.full_gains[1:2, :], grad, depth)
    residual_grad = r.upstream[:rows, :].astype(f32) + through
    s.residual_grad[...] = residual_grad
    attended = residual_grad.astype(bf16)
    r.upstream[:rows, :] = attended
    for number in range(2):
        attended_copy(number).start()
    mixed_grad_all = matmul(attended, r.heads[3]).astype(bf16)

    values = offset_values(head_table(table_ref), first_row, rows, span)
    allowed = allowed_pairs(lens_ref, first_row, rows, keys)
    offsets = []
    for pair in range(PAIRS):
        part = slice(pair * LANES, (pair + 1) * LANES)
        query_grad, key_grad, value_grad, pair_offsets = attend_pair_backward(
            pair, r.query, r.key, r.value, r.logs, mixed_grad_all[:, part], values, allowed, span,
        )
        s.offered[0, :, part] = query_grad.astype(bf16)
        r.slope[:, part] = key_grad
        r.slope[:, INNER + pair * LANES : INNER + (pair + 1) * LANES] = value_grad
        offsets = offsets + pair_offsets
        if pair == 0:
            serve(0, 1, (0,))
            serve(1, 1, (1,))
        if pair == 1:
            serve(2, 1, (1,))
            serve(3, 1, (0,))
    pair_wide = 2 * INNER
    for number, bit in ((0, 1), (1, 3)):
        place = pl.ds(pl.multiple_of((at.mp ^ bit) * rows, rows), rows)
        s.pair_send[number * rows : (number + 1) * rows, :] = r.slope[place, :pair_wide].astype(bf16)
    far_copy(4).start()
    s.offered[3] = r.mixed[...]
    far_copy(4).wait_recv()
    place = pl.ds(pl.multiple_of(across * rows, rows), rows)
    s.pair_across_send[...] = (
        r.slope[place, :pair_wide] + s.pair_came[rows:, :].astype(f32)
    ).astype(bf16)
    far_copy(5).start()
    attended_copy(0).wait_recv()
    attended_copy(2).start()

    arrive(r.hidden)

    def feed_tile(first, tile):
        return contract_cols(r.hidden[pl.ds(first, 2 * rows), :], r.down[part_of(tile), :])

    for tile in range(2):
        s.far_send[:, part_of(tile)] = feed_tile(2 * rows, tile).astype(bf16)
    far_copy(2).start()
    for tile in range(2):
        near_write(r.gelu, tile, feed_tile(0, tile))
    serve(0, 2)
    serve(1, 2)
    far_copy(5).wait_recv()
    place = pl.ds(pl.multiple_of(at.mp * rows, rows), rows)
    both = (
        r.slope[place, :pair_wide]
        + s.pair_came[:rows, :].astype(f32)
        + s.pair_across_came[...].astype(f32)
    ).astype(bf16)
    s.offered[1] = both[:, :INNER]
    s.offered[2] = both[:, INNER:]
    stage(4)

    def right_copy(number):
        partner = (across, beside, corner)[number - 1]
        return remote(
            s.offered.at[partner], s.right.at[block_rows(number)],
            s.right_sems.at[0, number], s.right_sems.at[1, number], at.dp, partner,
        )

    for number in range(1, line):
        right_copy(number).start()
    s.right[block_rows(0), :] = s.offered[at.mp]
    grad = (
        contract_cols(s.offered[0], r.heads[0])
        + contract_cols(s.offered[1], r.heads[1])
        + contract_cols(s.offered[2], r.heads[2])
    )
    arrive(r.wide_tokens)
    through, gain_one_grad = norm_backward(
        r.wide_tokens[...].astype(f32), r.full_gains[0:1, :], grad, depth
    )
    s.residual_grad[...] = s.residual_grad[...] + through

    offset_grad = jnp.concatenate(offsets + [jnp.zeros((8 - HEADS, span), f32)], axis=0)
    reach = lax.broadcasted_iota(jnp.int32, (8, span), 1) - (rows - 1) - first_row
    reach = bucket_ids(reach)
    table_grad = jnp.zeros((8, LANES), f32)
    buckets = table_ref.shape[1]
    for number in range(buckets):
        mass = jnp.sum(jnp.where(reach == number, offset_grad, 0.0), axis=1, keepdims=True)
        table_grad = jnp.where(norm_lane == number, mass, table_grad)
    s.small[0, :, wide:] = table_grad
    s.small[0, 0:1, :wide] = gain_one_grad
    s.small[0, 1:2, :wide] = gain_two_grad
    s.small[0, 2:, :wide] = jnp.zeros((6, wide), f32)

    def line_spread(source, slots, sems, first):
        copies = [
            remote(
                source, slots.at[at.mp], sems.at[first, step], sems.at[first + 1, step],
                at.dp, lax.rem(at.mp + step, line),
            )
            for step in range(1, line)
        ]
        for copy in copies:
            copy.start()
        slots[at.mp] = source[...]
        return copies

    def slot_total(slots, count):
        total = slots[0]
        for number in range(1, count):
            total = total + slots[number]
        return total

    small_copies = line_spread(s.small.at[0], s.small_line, s.small_sems, 0)
    serve(2, 2)
    far_copy(2).wait_recv()
    s.across_send[...] = (
        near_read(r.gelu, 1) + s.far_came[rows:, :].astype(f32)
    ).astype(bf16)
    far_copy(3).start()
    serve(3, 2)

    normed_load.wait()
    for number in range(1, 3):
        attended_copy(number).wait_recv()
    for number in range(1, line):
        right_copy(number).wait_recv()
    last = at.mp == line - 1
    for tile in range(tiles):
        lanes = slice(tile * tile_wide, (tile + 1) * tile_wide)
        left = jnp.where(last, r.upstream[:, lanes], r.normed_two[:, lanes])
        s.mine_grad[lanes, :] = contract_rows(left, s.right[...]).astype(bf16)
    mine_serve(0)

    for copy in small_copies:
        copy.wait()
    s.small[1] = slot_total(s.small_line, line)
    pair_slot = 2 * slot
    plane_copies = []
    for step in range(1, size):
        target = lax.rem(at.dp + step, size)
        lanes = pl.ds(pl.multiple_of(target // 2 * pair_slot, pair_slot), pair_slot)
        plane_copies.append(
            remote(
                s.small.at[1, :, lanes], s.small_gains.at[at.dp], s.small_sems.at[2, step],
                s.small_sems.at[3, step], target, at.mp,
            )
        )
        plane_copies.append(
            remote(
                s.small.at[1, :, pl.ds(wide, LANES)], s.small_table.at[at.dp],
                s.small_sems.at[4, step], s.small_sems.at[5, step], target, at.mp,
            )
        )
    for copy in plane_copies:
        copy.start()
    lanes = pl.ds(pl.multiple_of(at.dp // 2 * pair_slot, pair_slot), pair_slot)
    s.small_gains[at.dp] = s.small[1, :, lanes]
    s.small_table[at.dp] = s.small[1, :, wide:]

    serve(0, 3)
    mine_serve(1)
    serve(1, 3)
    down_total = jnp.concatenate([finish(4), finish(5)], axis=1)
    down_total = down_total[:shard]
    down_held[...] = down_total
    hands[2].start()
    staged(0)
    add_norms(
        6, s.down_stage[0], down_total, s.down_stage[1], s.down_stage[2], weight_decay
    )
    mine_serve(2)
    serve(2, 3)
    for copy in plane_copies:
        copy.wait()
    gains_total = slot_total(s.small_gains, size)
    odd = lax.rem(at.dp, 2) == 1
    gains_total = jnp.where(odd, pltpu.roll(gains_total, slot, 1), gains_total)[:2, :shard]
    out.gains_grad[...] = gains_total
    staged(5)
    for number in range(2):
        row = slice(number, number + 1)
        add_norms(
            7 + number, s.gains_stage[0, row], gains_total[row], s.gains_stage[1, row],
            s.gains_stage[2, row], 0.0, 1.0 / line,
        )
    table_total = slot_total(s.small_table, size)[:HEADS, :buckets]
    out.table_grad[...] = table_total
    staged(6)
    add_norms(
        9, s.table_stage[0], table_total, s.table_stage[1], s.table_stage[2], 0.0,
        1.0 / (line * size),
    )
    far_copy(3).wait_recv()
    layer_out = (
        r.residual[...]
        + (
            near_read(r.gelu, 0)
            + s.far_came[:rows, :].astype(f32)
            + s.across_came[...].astype(f32)
        )
    ).astype(bf16)
    stage(3)
    def grad_copy(matrix):
        held = (r.gelu, r.slope)[matrix]
        return pltpu.make_async_copy(
            held.at[pl.ds(3 * shard, shard)], out.gate_up_grad.at[matrix], s.stage_sems.at[21 + matrix]
        )

    def close(piece):
        total = finish(piece)
        lanes = piece_slice(piece)
        early = slot - shard
        shares = [(0, total[:shard], 0), (1, total[shard:], 0)] if piece < 2 else [(1, total, early)]
        for matrix, gradient, first in shares:
            held = (r.gelu, r.slope)[matrix]
            last_row = first + gradient.shape[0]
            rows_of = [slice(place * shard + first, place * shard + last_row) for place in range(4)]
            held[rows_of[3], lanes] = gradient
            add_norms(
                4 + matrix, held[rows_of[0], lanes], gradient, held[rows_of[1], lanes],
                held[rows_of[2], lanes], weight_decay,
            )
        if piece % 2 == 1:
            grad_copy(piece // 2).start()

    mine_serve(3)
    serve(3, 3)
    staged(3)
    staged(4)
    close(0)
    close(1)
    coarse = s.residual_grad[...].astype(bf16)
    fine = (s.residual_grad[...] - coarse.astype(f32)).astype(bf16)
    tile = 3 * LANES
    for low in range(0, depth, tile):
        high = min(low + tile, depth)
        layer_held[:, low:high] = gathered_tile(
            layer_out, None, low, high, shard, slot
        ).astype(bf16)
        tokens_held[:, low:high] = gathered_tile(coarse, fine, low, high, shard, slot)
    hands[0].start()
    hands[1].start()

    close(2)

    for side in range(2):
        mine_copy(side, half - 1).wait_recv()
    mine_total = (
        s.mine_grad[slab_rows(at.dp), :].astype(f32)
        + s.mine_came[0, half - 1].astype(f32)
        + s.mine_came[1, half - 1].astype(f32)
    ).astype(bf16)
    s.mine_sums[at.mp] = mine_total

    def sums_copy(number):
        partner = (across, beside, corner)[number - 1]
        return remote(
            s.mine_sums.at[at.mp], s.mine_sums.at[at.mp],
            s.sums_sems.at[0, number], s.sums_sems.at[1, number], at.dp, partner,
        )

    for number in range(1, line):
        sums_copy(number).start()
    staged(1)
    staged(2)

    def mine_state(index):
        return jnp.where(last, s.out_stage[index], s.mine_stage[index])

    add_norms(
        at.mp, mine_state(0), mine_total.astype(f32)[:shard], mine_state(1), mine_state(2),
        weight_decay,
    )

    close(3)

    spot = at.dp * line + at.mp
    norm_copies = []
    for step in range(1, size * line):
        target = lax.rem(spot + step, size * line)
        norm_copies.append(
            remote(
                s.norm_part, s.norm_plane.at[spot], s.norm_sems.at[0, step],
                s.norm_sems.at[1, step], target // line, lax.rem(target, line),
            )
        )
    for copy in norm_copies:
        copy.start()
    s.norm_plane[spot] = s.norm_part[...]

    for side in range(2):
        for hop in range(half):
            mine_copy(side, hop).wait_send()
            for piece in range(6):
                if piece_has(piece, side, hop):
                    piece_copy(piece, side, hop).wait_send()
    for number in range(2, 6):
        far_copy(number).wait_send()
    for number in range(3):
        attended_copy(number).wait_send()
    for number in range(1, line):
        right_copy(number).wait_send()
    for number in range(1, line):
        sums_copy(number).wait()
    hands.append(pltpu.make_async_copy(s.mine_sums, out.heads_grad, hand_sems.at[3]))
    hands[3].start()
    for copy in norm_copies:
        copy.wait()
    out.norms[...] = slot_total(s.norm_plane, size * line)
    for matrix in range(2):
        grad_copy(matrix).wait()
    for hand in hands:
        hand.wait()


def ring_backward(size, line, depth, slot, width, span, lens, table, got, states):
    rows = got.query.shape[0]
    wide, keys, half = size * slot, rows * line, size // 2
    shard, buckets = depth // size, table.shape[1]
    shapes = forward_shapes(rows, line, size, slot, width, span)
    dma = pltpu.SemaphoreType.DMA
    far = list(back_loads(got)) + [got.normed] + [array for state in states for array in state]
    operands = [lens, table] + far
    specs = [
        pl.BlockSpec(memory_space=pltpu.SMEM),
        pl.BlockSpec(memory_space=pltpu.VMEM),
    ] + [pl.BlockSpec(memory_space=pl.ANY)] * len(far)
    outs = BackwardOut(
        layer_out=((rows, depth), bf16),
        tokens_grad=((rows, depth), f32),
        heads_grad=((line, slot, INNER), bf16),
        gate_up_grad=((2, shard, width), f32),
        down_grad=((shard, width), f32),
        gains_grad=((2, shard), f32),
        table_grad=((HEADS, buckets), f32),
        norms=((8, LANES), f32),
    )
    handed = (outs.gate_up_grad, outs.heads_grad, outs.layer_out, outs.tokens_grad, outs.down_grad)
    half_rows = pltpu.VMEM((2 * rows, wide), bf16)
    block = pltpu.VMEM((rows, wide), bf16)
    loads = back_loads(shapes)
    scratch = BackwardScratch(
        load_sems=dma((len(loads) + 1,)),
        residual_grad=pltpu.VMEM((rows, wide), f32),
        both_grads=pltpu.VMEM((2, keys, width), bf16),
        fresh=pltpu.VMEM((2, 2 * shard, width), bf16),
        wide_came=pltpu.VMEM((2, half, 2 * shard, width), bf16),
        down_came=pltpu.VMEM((2, half, slot, width), bf16),
        far_send=half_rows,
        far_came=half_rows,
        across_send=block,
        across_came=block,
        pair_send=pltpu.VMEM((2 * rows, 2 * INNER), bf16),
        pair_came=pltpu.VMEM((2 * rows, 2 * INNER), bf16),
        pair_across_send=pltpu.VMEM((rows, 2 * INNER), bf16),
        pair_across_came=pltpu.VMEM((rows, 2 * INNER), bf16),
        offered=pltpu.VMEM((line, rows, INNER), bf16),
        right=pltpu.VMEM((keys, INNER), bf16),
        mine_grad=pltpu.VMEM((wide, INNER), bf16),
        mine_came=pltpu.VMEM((2, half, slot, INNER), bf16),
        mine_sums=pltpu.VMEM((line, slot, INNER), bf16),
        small=pltpu.VMEM((2, 8, wide + LANES), f32),
        small_line=pltpu.VMEM((line, 8, wide + LANES), f32),
        small_gains=pltpu.VMEM((size, 8, 2 * slot), f32),
        small_table=pltpu.VMEM((size, 8, LANES), f32),
        norm_part=pltpu.VMEM((8, LANES), f32),
        norm_line=pltpu.VMEM((line, 8, LANES), f32),
        norm_plane=pltpu.VMEM((size * line, 8, LANES), f32),
        down_stage=pltpu.VMEM((3, shard, width), f32),
        mine_stage=pltpu.VMEM((3, shard, INNER), f32),
        out_stage=pltpu.VMEM((3, shard, INNER), f32),
        gains_stage=pltpu.VMEM((3, 2, shard), f32),
        table_stage=pltpu.VMEM((3, HEADS, buckets), f32),
        wide_sems=dma((2, 6, 2, half)),
        line_sems=dma((2, 6)),
        attended_sems=dma((2, 3)),
        right_sems=dma((2, line)),
        mine_sems=dma((2, 2, half)),
        sums_sems=dma((2, line)),
        small_sems=dma((6, size)),
        norm_sems=dma((2, size * line)),
        stage_sems=dma((23,)),
    )
    flops = 2 * keys * wide * (6 * width + INNER) + 16 * rows * wide * INNER
    results = pl.pallas_call(
        partial(ring_backward_kernel, size, depth, span),
        out_shape=[jax.ShapeDtypeStruct(*shape) for shape in outs],
        in_specs=specs,
        out_specs=[
            pl.BlockSpec(memory_space=pl.ANY if any(shape is one for one in handed) else pltpu.VMEM)
            for shape in outs
        ],
        scratch_shapes=[pltpu.VMEM(*shape) for shape in loads]
        + list(scratch)
        + [pltpu.VMEM(*shape) for shape in handed[2:]]
        + [dma((4,))],
        compiler_params=pltpu.CompilerParams(
            collective_id=5, has_side_effects=True, vmem_limit_bytes=BACKWARD_BYTES
        ),
        cost_estimate=pl.CostEstimate(flops=flops, bytes_accessed=50 * 2**20, transcendentals=0),
        name="ring_backward",
    )(*operands)
    return BackwardOut(*results)


class UpdateOut(NamedTuple):
    layer_out: object
    tokens_grad: object
    first: object
    second: object
    new: object
    copy: object
    norms: object


def update_kernel(*refs):
    norms_ref, layer_source, tokens_source = refs[:3]
    sources = [refs[3 + 6 * kind : 9 + 6 * kind] for kind in range(4)]
    refs = refs[27:]
    layer_target, tokens_target = refs[:2]
    targets = [refs[2 + 6 * kind : 8 + 6 * kind] for kind in range(4)]
    norms_out = refs[26]
    refs = refs[27:]
    held = [refs[6 * kind : 6 * kind + 6] for kind in range(5)]
    layer_held, tokens_held, load_sems, store_sems = refs[30:]
    parts = [(number, None) for number in (5, 4, 1)]
    parts = parts + [(0, index) for index in range(held[1][0].shape[0])]
    parts = parts + [(2, 0), (2, 1), (3, None)]

    def view(ref, index):
        return ref if index is None else ref.at[index]

    def load_copy(spot, kind):
        number, index = parts[spot]
        source = view(sources[kind][number], index)
        if kind == 0 and number == 1:
            source = sources[0][1].at[sources[0][1].shape[0] - 1]
        return pltpu.make_async_copy(
            source, view(held[kind][number], index),
            load_sems.at[spot, kind],
        )

    def store_copy(spot, kind):
        number, index = parts[spot]
        return pltpu.make_async_copy(
            view(held[kind + 1][number], index), view(targets[kind][number], index),
            store_sems.at[spot, kind],
        )

    passed = [
        pltpu.make_async_copy(layer_source, layer_held, load_sems.at[len(parts), 0]),
        pltpu.make_async_copy(tokens_source, tokens_held, load_sems.at[len(parts), 1]),
    ]
    handed = [
        pltpu.make_async_copy(layer_held, layer_target, store_sems.at[len(parts), 0]),
        pltpu.make_async_copy(tokens_held, tokens_target, store_sems.at[len(parts), 1]),
    ]
    for spot in range(len(parts)):
        for kind in range(4):
            load_copy(spot, kind).start()
    for copy in passed:
        copy.start()
    roots = jnp.sqrt(norms_ref[...])
    count = norms_out.shape[1]
    steps = pltpu.roll(roots, LANES - count, 1)
    norms_out[...] = jnp.concatenate([roots[:1], steps[:1]], axis=0)[:, :count]
    lane = lax.broadcasted_iota(jnp.int32, roots.shape, 1)
    rates = learn_rate * roots / jnp.where(lane < count, steps, 1.0)
    starts = (0, 3, 4, 6, 7, 9)
    for spot, (number, index) in enumerate(parts):
        for kind in range(4):
            load_copy(spot, kind).wait()
        gradient, first, second, weight, copy = [view(held[kind][number], index) for kind in range(5)]
        decay = 0.0 if number > 3 else weight_decay
        rate = rates[:1, starts[number] + (index or 0) : starts[number] + (index or 0) + 1]
        if number == 4:
            rate = jnp.concatenate([rate, rates[:1, starts[number] + 1 : starts[number] + 2]], axis=0)
        old = weight[...]
        change = gradient[...].astype(f32)
        if number < 2:
            change = change[: old.shape[0]]
        new_first, new_second, step_dir = lamb_parts(old, change, first[...], second[...], decay)
        new = old - rate * step_dir
        first[...] = new_first
        second[...] = new_second
        weight[...] = new
        copy[...] = new.astype(bf16)
        for kind in range(4):
            store_copy(spot, kind).start()
    for number in range(2):
        passed[number].wait()
        handed[number].start()
    for copy in handed:
        copy.wait()
    for spot in range(len(parts)):
        for kind in range(4):
            store_copy(spot, kind).wait()


def update_all(norms, layer_out, tokens_grad, grads, firsts, seconds, weights, count):
    far = [layer_out, tokens_grad] + list(grads) + list(firsts) + list(seconds) + list(weights)
    shapes = [array.shape for array in weights]
    outs = [(layer_out.shape, bf16), (tokens_grad.shape, f32)]
    for kind in (f32, f32, f32, bf16):
        outs = outs + [(shape, kind) for shape in shapes]
    outs = outs + [((2, count), f32)]
    held = []
    filled = grads[0].shape[1:]
    held = [pltpu.VMEM((shapes[0][0],) + filled, bf16), pltpu.VMEM(filled, bf16)]
    held = held + [pltpu.VMEM(shape, f32) for shape in shapes[2:]]
    for kind in (f32, f32, f32, bf16):
        held = held + [pltpu.VMEM(shape, kind) for shape in shapes]
    held = held + [pltpu.VMEM(layer_out.shape, bf16), pltpu.VMEM(tokens_grad.shape, f32)]
    spots = 6 + shapes[0][0] + 1
    size = sum(array.size * 4 for array in far)
    any_spec = pl.BlockSpec(memory_space=pl.ANY)
    vmem_spec = pl.BlockSpec(memory_space=pltpu.VMEM)
    results = pl.pallas_call(
        update_kernel,
        out_shape=[jax.ShapeDtypeStruct(*out) for out in outs],
        in_specs=[vmem_spec] + [any_spec] * len(far),
        out_specs=[any_spec] * (len(outs) - 1) + [vmem_spec],
        scratch_shapes=held
        + [pltpu.SemaphoreType.DMA((spots, 4)), pltpu.SemaphoreType.DMA((spots, 4))],
        compiler_params=pltpu.CompilerParams(vmem_limit_bytes=VMEM_BYTES),
        cost_estimate=pl.CostEstimate(flops=size * 4, bytes_accessed=2 * size, transcendentals=size),
        name="update",
    )(norms, *far)
    kinds = [results[2 + 6 * kind : 8 + 6 * kind] for kind in range(4)]
    return UpdateOut(results[0], results[1], *kinds, results[26])


def plain_gradients(
    tokens,
    cotangent,
    lengths,
    heads_in,
    heads_out,
    expand_in,
    expand_out,
    norm_gains,
    bias_table,
):
    rows, depth = tokens.shape
    mp_size = lax.axis_size("mp")
    mp_spot = lax.axis_index("mp")
    keys = rows * mp_size
    span = -(-(keys + rows - 1) // LANES) * LANES
    first_row = mp_spot * rows
    shard_width = norm_gains.shape[1]
    buckets = bias_table.shape[0]

    four = jnp.concatenate([heads_in, heads_out.T[None]], axis=0).astype(bf16)
    mine = lax.dynamic_slice_in_dim(four, mp_spot, 1, axis=0)
    mine_all = gather_dp(mine)
    full_gains = gather_gains(norm_gains.astype(bf16).astype(f32))
    gain_one, gain_two = full_gains[0:1], full_gains[1:2]
    inputs = tokens.astype(f32)
    normed = rms_scale(inputs, gain_one, depth).astype(bf16)
    normed_parts = gather_mp(normed)
    used = first_row + jnp.arange(rows, dtype=jnp.int32) < lengths[0, 0] + lengths[0, 1]
    upstream = jnp.where(used[:, None], cotangent, jnp.zeros_like(cotangent))
    upstream_parts = gather_mp(upstream)

    mine_parts = gather_mp(mine_all)
    by_bit = jnp.concatenate([mine_parts[0], mine_parts[2], mine_parts[1], mine_parts[3]], axis=0)
    full_heads = jnp.concatenate(
        [lax.dynamic_slice_in_dim(by_bit, mp_spot ^ number, 1, axis=0) for number in range(mp_size)],
        axis=0,
    )
    wide_in = gather_dp(expand_in.astype(bf16))
    wide_out = gather_dp(expand_out.T.astype(bf16)[None])[0]

    table = jnp.pad(bias_table.T, ((0, 8 - HEADS), (0, 0)))
    attention_flops = rows * keys * LANES * HEADS
    mixed, query, key, value, logs, residual, normed_two = vmem_call(
        partial(forward_kernel, span, depth),
        [
            ((rows, INNER), bf16),
            ((rows, INNER), bf16),
            ((keys, INNER), bf16),
            ((keys, INNER), bf16),
            ((rows, LANES), f32),
            ((rows, depth), f32),
            ((rows, depth), bf16),
        ],
        (
            2 * depth * INNER * (2 * keys + 2 * rows) + 4 * attention_flops,
            2 * (4 * depth * INNER + 2 * keys * depth),
            rows * keys * HEADS,
        ),
        name="attention_forward",
        smem_first=True,
    )(lengths, *normed_parts, full_heads, table, tokens, gain_two)

    normed_all = jnp.concatenate(gather_mp(normed_two), axis=0)
    upstream_all = jnp.concatenate(upstream_parts, axis=0)
    gate_pre = matmul(normed_all, wide_in[0])
    up_pre = matmul(normed_all, wide_in[1])
    gelu_gate, gelu_pull = jax.vjp(partial(jax.nn.gelu, approximate=True), gate_pre)
    hidden = (gelu_gate * up_pre).astype(bf16)
    expand_out_grad = scatter_dp(contract_rows(upstream_all, hidden).astype(bf16)[None])[0].T
    feed_part = contract_cols(hidden, wide_out).astype(bf16)
    feed_near = feed_part[: 2 * rows].astype(f32) + swap(feed_part[2 * rows :], 1).astype(f32)
    feed_out = feed_near[:rows] + swap(feed_near[rows:].astype(bf16), 2).astype(f32)
    layer_out = (residual + feed_out).astype(bf16)

    hidden_grad = matmul(upstream_all, wide_out)
    up_grad = (hidden_grad * gelu_gate).astype(bf16)
    gate_grad = gelu_pull(hidden_grad * up_pre)[0].astype(bf16)
    normed_part = contract_cols(gate_grad, wide_in[0]) + contract_cols(up_grad, wide_in[1])
    normed_near = normed_part[: 2 * rows] + swap(normed_part[2 * rows :].astype(bf16), 1).astype(f32)
    normed_across = swap(normed_near[rows:].astype(bf16), 2)
    expand_in_grad = scatter_dp(
        jnp.stack(
            [
                contract_rows(normed_all, gate_grad).astype(bf16),
                contract_rows(normed_all, up_grad).astype(bf16),
            ]
        )
    )

    residual_grad, attended_grad, query_grad, near, far, offset_grad, gain_two_grad = vmem_call(
        partial(backward_kernel, span, depth),
        [
            ((rows, depth), f32),
            ((rows, depth), bf16),
            ((rows, INNER), bf16),
            ((2 * rows, 2 * INNER), f32),
            ((2 * rows, 2 * INNER), bf16),
            ((8, span), f32),
            ((1, depth), f32),
        ],
        (
            2 * depth * INNER * rows + 10 * attention_flops,
            rows * depth * 16 + 2 * (4 * depth * INNER + 2 * keys * INNER),
            rows * keys * HEADS,
        ),
        scratch=[pltpu.VMEM((keys, 2 * INNER), f32)],
        name="attention_backward",
        smem_first=True,
    )(
        lengths,
        normed_near[:rows],
        normed_across,
        residual,
        upstream,
        gain_two,
        full_heads,
        query,
        key,
        value,
        logs,
        table,
    )
    attended_parts = gather_mp(attended_grad)
    beside = swap(far, 1)
    across = swap((near[rows:] + beside[rows:].astype(f32)).astype(bf16), 2)
    tokens_grad, both, gain_one_grad = vmem_call(
        partial(input_kernel, depth),
        [((rows, depth), f32), ((rows, 2 * INNER), bf16), ((1, depth), f32)],
        (6 * rows * depth * INNER, rows * depth * 14 + 8 * depth * INNER, 0),
        name="input_backward",
    )(near, beside, across, query_grad, full_heads, tokens, gain_one, residual_grad)

    offered = jnp.stack([query_grad, both[:, :INNER], both[:, INNER:], mixed])

    def for_bit(bit):
        return lax.dynamic_slice_in_dim(offered, mp_spot ^ bit, 1, axis=0)

    from_beside = swap(jnp.concatenate([for_bit(1), for_bit(3)], axis=0), 1)
    from_across = swap(jnp.concatenate([for_bit(2), from_beside[1:]], axis=0), 2)
    right = jnp.concatenate(
        [for_bit(0)[0], from_across[0], from_beside[0], from_across[1]], axis=0
    )
    left = jnp.where(
        mp_spot == mp_size - 1,
        jnp.concatenate(attended_parts, axis=0),
        jnp.concatenate(normed_parts, axis=0),
    )
    mine_grad = scatter_dp(contract_rows(left, right).astype(bf16)[None]).astype(bf16)
    grad_parts = gather_mp(mine_grad)
    grads_by_bit = jnp.concatenate(
        [grad_parts[0], grad_parts[2], grad_parts[1], grad_parts[3]], axis=0
    )
    heads_grad = [
        lax.dynamic_slice_in_dim(grads_by_bit, mp_spot ^ number, 1, axis=0)
        for number in range(mp_size)
    ]
    head_in_grad = jnp.concatenate(heads_grad[:3], axis=0).astype(f32)
    head_out_grad = heads_grad[3][0].T.astype(f32)

    reach = jnp.arange(span, dtype=jnp.int32) - (rows - 1) - first_row
    onehot = (bucket_ids(reach)[:, None] == jnp.arange(buckets, dtype=jnp.int32)[None, :]).astype(f32)
    table_part = jnp.dot(offset_grad, onehot, precision=highest)[:HEADS].T
    gain_parts = jnp.concatenate([gain_one_grad, gain_two_grad], axis=0)
    small = total_all(pack_rows([gain_parts, table_part]), 1).reshape(-1)
    gains_total = small[: 2 * depth].reshape(2, depth)
    table_grad = small[2 * depth : 2 * depth + buckets * HEADS].reshape(buckets, HEADS)
    gains_grad = lax.dynamic_slice_in_dim(
        gains_total, lax.axis_index("dp") * shard_width, shard_width, 1
    )

    return layer_out, tokens_grad, (
        head_in_grad,
        head_out_grad,
        expand_in_grad,
        expand_out_grad,
        gains_grad,
        table_grad,
    )


def ring_step(
    tokens, cotangent, lengths, heads_in, heads_out, expand_in, expand_out, norm_gains, bias_table, firsts, seconds
):
    rows, depth = tokens.shape
    size, line = lax.axis_size("dp"), lax.axis_size("mp")
    span = -(-(rows * line + rows - 1) // LANES) * LANES
    width = expand_in.shape[2]
    slot = -(-norm_gains.shape[1] // 16) * 16
    weights = Moments(heads_in, heads_out, expand_in, expand_out, norm_gains, bias_table)
    weights, firsts, seconds = [
        Moments(state[0], state[1].T, state[2], state[3].T, state[4], state[5].T)
        for state in (weights, firsts, seconds)
    ]
    got = ring_forward(
        size, line, depth, slot, width, span,
        (lengths, tokens, cotangent, norm_gains, weights.bias_table) + tuple(weights[:4]),
    )
    back = ring_backward(
        size, line, depth, slot, width, span, lengths, weights.bias_table, got,
        (weights, firsts, seconds),
    )
    grads = Moments(
        back.heads_grad,
        back.heads_grad,
        back.gate_up_grad,
        back.down_grad,
        back.gains_grad,
        back.table_grad,
    )
    update = update_all(
        back.norms, back.layer_out, back.tokens_grad, grads, firsts, seconds, weights, 10
    )
    outputs = [update.layer_out, update.tokens_grad]
    for number in range(6):
        for kind in (update.first, update.second, update.new, update.copy):
            outputs.append(kind[number].T if number in (1, 3, 5) else kind[number])
    return tuple(outputs + [update.norms])


def shards(
    tokens,
    cotangent,
    lengths,
    heads_in,
    heads_out,
    expand_in,
    expand_out,
    norm_gains,
    bias_table,
    heads_in_first,
    heads_out_first,
    expand_in_first,
    expand_out_first,
    gains_first,
    table_first,
    heads_in_second,
    heads_out_second,
    expand_in_second,
    expand_out_second,
    gains_second,
    table_second,
):
    given = (
        tokens, cotangent, lengths, heads_in, heads_out, expand_in, expand_out, norm_gains, bias_table
    )
    weight_list = (heads_in, heads_out, expand_in, expand_out, norm_gains, bias_table)
    first_list = (
        heads_in_first,
        heads_out_first,
        expand_in_first,
        expand_out_first,
        gains_first,
        table_first,
    )
    second_list = (
        heads_in_second,
        heads_out_second,
        expand_in_second,
        expand_out_second,
        gains_second,
        table_second,
    )
    decay_list = (weight_decay, weight_decay, weight_decay, weight_decay, 0.0, 0.0)
    sub_list = (3, 1, 2, 1, 2, 1)
    if lax.axis_size("dp") <= RING_LIMIT:
        return ring_step(*given, first_list, second_list)
    layer_out, tokens_grad, grad_list = plain_gradients(*given)
    results = [
        lamb_parts(
            weight_list[number],
            grad_list[number],
            first_list[number],
            second_list[number],
            decay_list[number],
        )
        for number in range(6)
    ]
    count = sum(sub_list)
    shared = 1.0 / lax.axis_size("mp")
    share_list = (shared, shared, 1.0, 1.0, shared, shared / lax.axis_size("dp"))
    parts = [weight_list, [result[2] for result in results]]
    sums = lax.psum(
        jnp.concatenate(
            [
                sub_squares(part[number], sub_list[number]) * share_list[number]
                for part in parts
                for number in range(6)
            ]
        ),
        ("dp", "mp"),
    )
    weight_norm = jnp.sqrt(sums[:count])
    step_norm = jnp.sqrt(sums[count : 2 * count])
    ratios = weight_norm / step_norm
    starts = (0, 3, 4, 6, 7, 9)
    outputs = [layer_out, tokens_grad]
    for number in range(6):
        weight = weight_list[number]
        sub_count = sub_list[number]
        ratio_part = ratios[starts[number] : starts[number] + sub_count]
        shape = (sub_count,) + (1,) * (weight.ndim - 1) if sub_count > 1 else (1,) * weight.ndim
        new_weight = weight - learn_rate * ratio_part.reshape(shape) * results[number][2]
        outputs = outputs + [
            results[number][0],
            results[number][1],
            new_weight,
            new_weight.astype(bf16),
        ]
    outputs = outputs + [jnp.stack([weight_norm, step_norm])]
    return tuple(outputs)


def solution(mesh):
    return jax.shard_map(
        shards,
        mesh=mesh,
        in_specs=(
            P(("dp", "mp"), None),
            P(("dp", "mp"), None),
            P("dp", None),
            P(None, "dp", None),
            P(None, "dp"),
            P(None, "dp", "mp"),
            P("mp", "dp"),
            P(None, "dp"),
            P(),
            P(None, "dp", None),
            P(None, "dp"),
            P(None, "dp", "mp"),
            P("mp", "dp"),
            P(None, "dp"),
            P(),
            P(None, "dp", None),
            P(None, "dp"),
            P(None, "dp", "mp"),
            P("mp", "dp"),
            P(None, "dp"),
            P(),
        ),
        out_specs=(
            P(("dp", "mp"), None),
            P(("dp", "mp"), None),
            P(None, "dp", None),
            P(None, "dp", None),
            P(None, "dp", None),
            P(None, "dp", None),
            P(None, "dp"),
            P(None, "dp"),
            P(None, "dp"),
            P(None, "dp"),
            P(None, "dp", "mp"),
            P(None, "dp", "mp"),
            P(None, "dp", "mp"),
            P(None, "dp", "mp"),
            P("mp", "dp"),
            P("mp", "dp"),
            P("mp", "dp"),
            P("mp", "dp"),
            P(None, "dp"),
            P(None, "dp"),
            P(None, "dp"),
            P(None, "dp"),
            P(),
            P(),
            P(),
            P(),
            P(),
        ),
        check_vma=False,
    )
```
